256 devices in a mesh: row: 16 (over x, y), col: 8 (over z), seq: 2 (over core).
Axes of the slice: x: 4, y: 4, z: 8, core: 2. Of those that a mesh axis runs over, the one named last changes fastest.
Arguments:
- hidden: float32 [8192, 1536], P(('row', 'seq')), may hold values from -6 to 6
- cotangent: bfloat16 [8192, 1536], P(('row', 'seq')), may hold values from -6 to 6
- segments: int32 [8192], P(('row', 'seq')), may hold values from 0 to 15, never falling along the last dimension, each value on 1 to 2000 neighbouring positions
- routes: int32 [8192, 6], P(('row', 'seq')), may hold values from 0 to 15, all different within a row; in each aligned block of 256 rows (0 to 255, 256 to 511, ...) at most 144 rows name the same one
- gain_mix: float32 [1536], replicated, may hold values from 0.5 to 1.5
- w_z: bfloat16 [1536, 3072], P(('row', 'seq'), 'col'), may hold values from -0.15625 to 0.15625
- w_x: bfloat16 [1536, 3072], P(('row', 'seq'), 'col'), may hold values from -0.15625 to 0.15625
- w_bc: bfloat16 [1536, 256], P(('row', 'seq')), may hold values from -0.15625 to 0.15625
- w_dt: bfloat16 [1536, 48], P(('row', 'seq'), 'col'), may hold values from -0.15625 to 0.15625
- conv_x: float32 [4, 3072], P(None, 'col'), may hold values from -3 to 3
- conv_bc: float32 [4, 256], replicated, may hold values from -3 to 3
- dt_bias: float32 [48], P('col'), may hold values from -7 to -2.5
- a_log: float32 [48], P('col'), may hold values from 0 to 2.7
- d_skip: float32 [48], P('col'), may hold values from 0.5 to 1.5
- gain_gate: float32 [3072], P('col'), may hold values from 0.5 to 1.5
- out_t: bfloat16 [1536, 3072], P(('row', 'seq'), 'col'), may hold values from -0.109375 to 0.109375
- gain_moe: float32 [1536], replicated, may hold values from 0.5 to 1.5
- w_router: bfloat16 [1536, 16], P(('row', 'seq')), may hold values from -0.078125 to 0.078125
- w_gate_t: bfloat16 [1536, 16, 512], P(('row', 'seq'), 'col'), may hold values from -0.15625 to 0.15625
- w_up_t: bfloat16 [1536, 16, 512], P(('row', 'seq'), 'col'), may hold values from -0.15625 to 0.15625
- w_down_t: bfloat16 [1536, 16, 512], P(('row', 'seq'), 'col'), may hold values from -0.5 to 0.5
- ws_gate: bfloat16 [1536, 1024], P(('row', 'seq'), 'col'), may hold values from -0.15625 to 0.15625
- ws_up: bfloat16 [1536, 1024], P(('row', 'seq'), 'col'), may hold values from -0.15625 to 0.15625
- ws_down_t: bfloat16 [1536, 1024], P(('row', 'seq'), 'col'), may hold values from -0.375 to 0.375
Outputs:
- output: float32 [8192, 1536], P(('row', 'seq'))
- grad_hidden: float32 [8192, 1536], P(('row', 'seq'))
- inv_rms_mix: float32 [8192], P(('row', 'seq'))
- inv_rms_moe: float32 [8192], P(('row', 'seq'))
- g_gain_mix: float32 [1536], replicated
- g_w_z: float32 [1536, 3072], P(('row', 'seq'), 'col')
- g_w_x: float32 [1536, 3072], P(('row', 'seq'), 'col')
- g_w_bc: float32 [1536, 256], P(('row', 'seq'))
- g_w_dt: float32 [1536, 48], P(('row', 'seq'), 'col')
- g_conv_x: float32 [4, 3072], P(None, 'col')
- g_conv_bc: float32 [4, 256], replicated
- g_dt_bias: float32 [48], P('col')
- g_a_log: float32 [48], P('col')
- g_d_skip: float32 [48], P('col')
- g_gain_gate: float32 [3072], P('col')
- g_out_t: float32 [1536, 3072], P(('row', 'seq'), 'col')
- g_gain_moe: float32 [1536], replicated
- g_w_router: float32 [1536, 16], P(('row', 'seq'))
- g_w_gate_t: float32 [1536, 16, 512], P(('row', 'seq'), 'col')
- g_w_up_t: float32 [1536, 16, 512], P(('row', 'seq'), 'col')
- g_w_down_t: float32 [1536, 16, 512], P(('row', 'seq'), 'col')
- g_ws_gate: float32 [1536, 1024], P(('row', 'seq'), 'col')
- g_ws_up: float32 [1536, 1024], P(('row', 'seq'), 'col')
- g_ws_down_t: float32 [1536, 1024], P(('row', 'seq'), 'col')
The draws below stay inside these ranges and needn't reach their ends.
Inputs may be any that keep to these rules, and one draw needn't show every extreme that they name: `segments`: segment numbers never fall along the tokens; a document is a run of equal numbers inside one sequence of 512 tokens. The 6 routes of a token name different experts; in each aligned block of 256 tokens (the tokens of one device) no expert is named by more than 144 routes, a bound that some block reaches.
All inputs are finite; a program needn't handle non-finite values.
Results may differ from the reference program's by a relative error of at most 0.018.
Values may be sent and summed in bfloat16 or wider, within the bound.
No kernel may reach another device: no remote copies, remote signals or barrier semaphores. Data moves between devices by JAX's collectives and lax.ppermute only.
A program may use at most 128 MiB of HBM per device.

```python
import math
import jax
import jax.numpy as jnp
import numpy as np
from jax import lax

D = 1536
H = 48
P_SIZE = 64
N = 128
CONV = 4
EXPERTS = 16
TOP = 6
F = 512
S = 1024
Q = 128
TD = 256
E = 3072
LENGTH = 512
TOKENS = 8192
C = 144


def levels(own_key, extent, split, low, top_value):
    level, own = 1.0, jax.random.fold_in(own_key, 6)
    for position, blocks in split:
        draws = jnp.exp(jax.random.uniform(jax.random.fold_in(own, position), (blocks,), jnp.float32, low / len(split), top_value / len(split)))
        level = level * jnp.repeat(draws, extent[position] // blocks).reshape([-1 if axis == position else 1 for axis in range(len(extent))])
    return level


def length_profile(number_of, total, most, skew):
    weights = [(1 << 20) // math.isqrt(rank ** skew) + 1 for rank in range(2, number_of + 1)]
    surplus, given = total - most - (number_of - 1), [1] * (number_of - 1)
    while surplus > 0:
        free = [i for i in range(number_of - 1) if given[i] < most]
        mass, remaining = sum([weights[i] for i in free]), surplus
        for i in free:
            more = min(most - given[i], max(1, remaining * weights[i] // mass), surplus)
            given[i] = given[i] + more
            surplus = surplus - more
    return np.array([most] + given)


def uneven_parts(stream_key, count, total, reach, skew):
    if count == 2:
        one = jax.random.randint(stream_key, (), max(1, total - reach), min(reach, total - 1) + 1)
        return jnp.stack([one, total - one])
    tallies = jnp.asarray(length_profile(count, total, reach, skew), jnp.int32)
    twos = (count - 1) // 2
    source_of, taker = tallies[1:1 + 2 * twos:2], tallies[2:2 + 2 * twos:2]
    room = jnp.minimum(source_of - 1, reach - taker)
    moved = jax.random.randint(jax.random.fold_in(stream_key, 1), (twos,), 0, 1 << 20) % (room + 1)
    tallies = tallies.at[1:1 + 2 * twos:2].set(source_of - moved).at[2:2 + 2 * twos:2].set(taker + moved)
    return tallies[jax.random.permutation(jax.random.fold_in(stream_key, 2), count)]


def assign_block(own_key, own, number, rows, amount, top, limit, lean):
    sequence = jax.random.permutation(own_key, amount)
    heavy_load, common = portions_of(amount, rows * top, limit, lean, True), portions_of(amount, rows * top, limit, lean, False)
    places = jnp.arange(amount)

    def named(lengths, rotation):
        used = int((lengths > 0).sum())
        fixed = max(1, used // 4)
        passed = fixed + (places - fixed + rotation * (used - fixed)) % max(1, amount - fixed)
        return jnp.zeros((amount,), jnp.int32).at[sequence[jnp.where(places < fixed, places, passed)]].set(jnp.asarray(lengths, jnp.int32))

    lengths = jnp.where(number % 4 == 0, named(heavy_load, number // 4), named(common, number - number // 4 - 1))
    mixed = jax.random.permutation(jax.random.fold_in(own, 3), amount)
    source_of, receiver = mixed[0:amount // 2 * 2:2], mixed[1:amount // 2 * 2:2]
    room = jnp.minimum(lengths[source_of] - 1, limit - lengths[receiver]) // 2
    room = jnp.where((source_of == sequence[0]) | (receiver == sequence[0]) | (lengths[receiver] == 0), 0, jnp.maximum(room, 0))
    passed = jax.random.randint(jax.random.fold_in(own, 4), (amount // 2,), 0, 1 << 20) % (room + 1)
    lengths = lengths.at[source_of].add(-passed).at[receiver].add(passed)
    labels = jnp.searchsorted(jnp.cumsum(lengths), jnp.arange(rows * top), side="right").astype(jnp.int32)
    table = labels.reshape(top, rows).T
    table = table[jax.random.permutation(jax.random.fold_in(own, 1), rows)]
    rotation = jax.random.randint(jax.random.fold_in(own, 2), (rows, 1), 0, top)
    return jnp.take_along_axis(table, (jnp.arange(top)[None, :] + rotation) % top, axis=1)


def portions_of(count, total, reach, lean, full):
    weights = [(1 << 20) // math.isqrt(rank ** lean) + 1 for rank in range(1, count + 1)]
    largest = reach if full else min(reach, max(-(-total // count), total * weights[0] // sum(weights)))
    least = 1 if total - largest >= count - 1 else 0
    counts, surplus = [largest] + [least] * (count - 1), total - largest - least * (count - 1)
    while surplus > 0:
        free = [i for i in range(1, count) if counts[i] < largest] or [i for i in range(1, count) if counts[i] < reach]
        whole, budget = sum([weights[i] for i in free]), surplus
        for i in free:
            more = min(reach - counts[i], max(1, budget * weights[i] // whole), surplus)
            counts[i] = counts[i] + more
            surplus = surplus - more
    return np.array(counts)


def normal_values(key, shape, deviation, most, split=(), kind=jnp.bfloat16):
    entries = jax.random.normal(key, shape, jnp.float32) * deviation
    if len(split) > 0:
        entries = levels(key, shape, split, -0.22, 0.18) * entries
    return jnp.clip(entries, min=-most, max=most).astype(kind)


def setup_inputs(seed: int = 0) -> dict:
    splits = jax.random.split(jax.random.key(seed), 25)
    hidden = normal_values(splits[0], (TOKENS, D), 1.0, 6.0, ((0, 32),), jnp.float32)
    cotangent = normal_values(splits[1], (TOKENS, D), 1.0, 6.0, ((0, 32),))
    segments = jnp.searchsorted(jnp.cumsum(uneven_parts(splits[2], max(TOKENS // 512, 2), TOKENS, min(2000, TOKENS // 2), 0)), jnp.arange(TOKENS), side="right").astype(jnp.int32)
    routes_keys = jax.random.split(jax.random.fold_in(splits[3], 1), TOKENS // TD)
    routes_turns = jax.random.permutation(jax.random.fold_in(splits[3], 3), TOKENS // TD)
    routes = jax.vmap(lambda own, number: assign_block(jax.random.fold_in(splits[3], 2), own, number, TD, EXPERTS, TOP, C, 1))(routes_keys, routes_turns).reshape((TOKENS, TOP))
    gain_mix = jnp.clip(1.0 + 0.1 * jax.random.normal(splits[4], (D,), jnp.float32), 0.5, 1.5)
    w_z = normal_values(splits[5], (D, E), D ** -0.5, 0.15625, ((0, 32), (1, 8)))
    w_x = normal_values(splits[6], (D, E), D ** -0.5, 0.15625, ((0, 32), (1, 8)))
    w_bc = normal_values(splits[7], (D, 2 * N), D ** -0.5, 0.15625, ((0, 32),))
    w_dt = normal_values(splits[8], (D, H), D ** -0.5, 0.15625, ((0, 32), (1, 8)))
    conv_x = normal_values(splits[9], (CONV, E), CONV ** -0.5, 3.0, ((1, 8),), jnp.float32)
    conv_bc = normal_values(splits[10], (CONV, 2 * N), CONV ** -0.5, 3.0, (), jnp.float32)
    dt_bias = jnp.clip(-7.0 + 4.5 * jax.random.uniform(splits[11], (H,), jnp.float32) ** levels(splits[11], (H,), ((0, 8),), -0.2, 0.2), -7.0, -2.5)
    a_log = jnp.clip(2.7 * jax.random.uniform(splits[12], (H,), jnp.float32) ** levels(splits[12], (H,), ((0, 8),), -0.2, 0.2), 0.0, 2.7)
    d_skip = jnp.clip(0.5 + 1.0 * jax.random.uniform(splits[13], (H,), jnp.float32) ** levels(splits[13], (H,), ((0, 8),), -0.2, 0.2), 0.5, 1.5)
    gain_gate = jnp.clip(1.0 + 0.1 * jax.random.normal(splits[14], (E,), jnp.float32), 0.5, 1.5)
    out_t = normal_values(splits[15], (D, E), E ** -0.5, 0.109375, ((0, 32), (1, 8)))
    gain_moe = jnp.clip(1.0 + 0.1 * jax.random.normal(splits[16], (D,), jnp.float32), 0.5, 1.5)
    w_router = normal_values(splits[17], (D, EXPERTS), (0.5 / D ** 0.5), 0.078125, ((0, 32),))
    w_gate_t = normal_values(splits[18], (D, EXPERTS, F), D ** -0.5, 0.15625, ((0, 32), (1, 8)))
    w_up_t = normal_values(splits[19], (D, EXPERTS, F), D ** -0.5, 0.15625, ((0, 32), (1, 8)))
    w_down_t = normal_values(splits[20], (D, EXPERTS, F), (F // 4) ** -0.5, 0.5, ((0, 32), (1, 8)))
    ws_gate = normal_values(splits[21], (D, S), D ** -0.5, 0.15625, ((0, 32), (1, 8)))
    ws_up = normal_values(splits[22], (D, S), D ** -0.5, 0.15625, ((0, 32), (1, 8)))
    ws_down_t = normal_values(splits[23], (D, S), (S // 4) ** -0.5, 0.375, ((0, 32), (1, 8)))
    return dict(hidden=hidden, cotangent=cotangent, segments=segments, routes=routes, gain_mix=gain_mix, w_z=w_z, w_x=w_x, w_bc=w_bc, w_dt=w_dt, conv_x=conv_x, conv_bc=conv_bc, dt_bias=dt_bias, a_log=a_log, d_skip=d_skip, gain_gate=gain_gate, out_t=out_t, gain_moe=gain_moe, w_router=w_router, w_gate_t=w_gate_t, w_up_t=w_up_t, w_down_t=w_down_t, ws_gate=ws_gate, ws_up=ws_up, ws_down_t=ws_down_t)


EPS = 1e-05
PRECISE = lax.Precision.HIGHEST

@jax.custom_vjp
def low(v):
    return lax.optimization_barrier(v.astype(jnp.bfloat16)).astype(jnp.float32)

@jax.custom_vjp
def low_back(v):
    return v

def low_keep(v):
    return (low(v), None)

def low_pass(kept, grad):
    return (grad,)

def back_keep(v):
    return (v, None)

def back_low(kept, grad):
    return (low(grad),)
low.defvjp(low_keep, low_pass)
low_back.defvjp(back_keep, back_low)

def matmul(left, right):
    return jnp.dot(left, right, precision=PRECISE, preferred_element_type=jnp.float32)

def silu_value(values):
    return values * jax.nn.sigmoid(values)

def conv_reset(extended, kernel, starts_ext):
    kernel_taps = kernel.shape[0]
    tok_rows = extended.shape[0] - kernel_taps + 1
    totals = kernel[kernel_taps - 1][None, :] * extended[kernel_taps - 1:]
    keeping = jnp.ones((tok_rows,), jnp.float32)
    for lag_steps in range(1, kernel_taps):
        keeping = keeping * (1.0 - starts_ext[kernel_taps - lag_steps:kernel_taps - lag_steps + tok_rows])
        totals = totals + kernel[kernel_taps - 1 - lag_steps][None, :] * extended[kernel_taps - 1 - lag_steps:kernel_taps - 1 - lag_steps + tok_rows] * keeping[:, None]
    return totals

def ssd_block(state_in, block):
    head_inputs, step_size, log_decay, b_matrix, c_matrix, starts = block
    block_rows = starts.shape[0]
    cum_decay = jnp.cumsum(log_decay, axis=0)
    doc_index = jnp.cumsum(starts)
    positions = jnp.arange(block_rows)
    same_doc = (doc_index[:, None] == doc_index[None, :]) & (positions[:, None] >= positions[None, :])
    decay_gap = cum_decay[:, None, :] - cum_decay[None, :, :]
    decay_mask = jnp.where(same_doc[:, :, None], jnp.exp(jnp.where(same_doc[:, :, None], decay_gap, 0.0)), 0.0)
    scores = jnp.einsum('in,jn->ij', c_matrix, b_matrix, precision=PRECISE)
    weights = decay_mask * scores[:, :, None] * step_size[None, :, :]
    inner_out = jnp.einsum('ijh,jhp->ihp', weights, head_inputs, precision=PRECISE)
    enter_weight = jnp.exp(cum_decay) * jnp.where(doc_index == 0.0, 1.0, 0.0)[:, None]
    carried = jnp.einsum('in,hpn->ihp', c_matrix, state_in, precision=PRECISE) * enter_weight[:, :, None]
    tail_weight = jnp.where((doc_index == doc_index[-1])[:, None], jnp.exp(cum_decay[-1][None, :] - cum_decay), 0.0) * step_size
    fresh_state = jnp.einsum('jh,jhp,jn->hpn', tail_weight, head_inputs, b_matrix, precision=PRECISE)
    return (state_in * enter_weight[-1][:, None, None] + fresh_state, inner_out + carried)

def scan_all(head_inputs, step_size, log_decay, b_matrix, c_matrix, starts):
    blocks = starts.shape[0] // Q
    pieces = (head_inputs.reshape(blocks, Q, H, P_SIZE), step_size.reshape(blocks, Q, H), log_decay.reshape(blocks, Q, H), b_matrix.reshape(blocks, Q, N), c_matrix.reshape(blocks, Q, N), starts.reshape(blocks, Q))
    _, outputs = lax.scan(jax.checkpoint(ssd_block), jnp.zeros((H, P_SIZE, N), jnp.float32), pieces)
    return outputs.reshape(-1, H, P_SIZE)

def doc_starts(segments):
    positions = jnp.arange(segments.shape[0])
    before = jnp.concatenate([segments[:1], segments[:-1]])
    opening = (positions % LENGTH == 0) | (segments != before)
    return jnp.where(opening, 1.0, 0.0).astype(jnp.float32)

def layer_forward(hidden, gain_mix, w_z, w_x, w_bc, w_dt, conv_x, conv_bc, dt_bias, a_log, d_skip, gain_gate, out_t, gain_moe, w_router, w_gate_t, w_up_t, w_down_t, ws_gate, ws_up, ws_down_t, starts, routes):
    tok_total = hidden.shape[0]
    inv_mix = lax.rsqrt(lax.optimization_barrier(jnp.mean(hidden * hidden, axis=1)) + EPS)
    normed_mix = low(hidden * inv_mix[:, None] * gain_mix)
    z_pre = low_back(matmul(normed_mix, w_z))
    x_pre = low_back(matmul(normed_mix, w_x))
    bc_pre = low_back(matmul(normed_mix, w_bc))
    dt_pre = low_back(matmul(normed_mix, w_dt))
    tail_len = CONV - 1
    starts_ext = jnp.concatenate([jnp.ones((tail_len,), jnp.float32), starts])
    x_conv = silu_value(conv_reset(jnp.concatenate([jnp.zeros((tail_len, E), jnp.float32), x_pre]), conv_x, starts_ext))
    bc_conv = silu_value(conv_reset(jnp.concatenate([jnp.zeros((tail_len, 2 * N), jnp.float32), bc_pre]), conv_bc, starts_ext))
    step_size = jax.nn.softplus(dt_pre + dt_bias)
    log_decay = -step_size * jnp.exp(a_log)
    head_inputs = x_conv.reshape(tok_total, H, P_SIZE)
    scanned = scan_all(head_inputs, step_size, log_decay, bc_conv[:, :N], bc_conv[:, N:], starts)
    mixer_out = (scanned + d_skip[None, :, None] * head_inputs).reshape(tok_total, E)
    gated = mixer_out * silu_value(z_pre)
    inv_gate = lax.rsqrt(lax.optimization_barrier(jnp.mean(gated * gated, axis=1)) + EPS)
    normed_gate = low(gated * inv_gate[:, None] * gain_gate)
    mix_out = low_back(matmul(normed_gate, out_t.T))
    residual = hidden + mix_out
    inv_moe = lax.rsqrt(lax.optimization_barrier(jnp.mean(residual * residual, axis=1)) + EPS)
    normed_moe = low(residual * inv_moe[:, None] * gain_moe)
    logits = low_back(matmul(normed_moe, w_router))
    picks = (routes[:, :, None] == jnp.arange(EXPERTS, dtype=jnp.int32)[None, None, :]).astype(jnp.float32)
    chosen = lax.optimization_barrier(jnp.sum(picks * logits[:, None, :], axis=2))
    route_gates = jax.nn.softmax(chosen, axis=1)

    def expert_block(inputs):
        block_moe, block_routes, block_gates = inputs
        flat_routes = block_routes.reshape(-1)
        marks = (flat_routes[:, None] == jnp.arange(EXPERTS, dtype=jnp.int32)[None, :]).astype(jnp.int32)
        slot_place = lax.optimization_barrier(jnp.sum((jnp.cumsum(marks, axis=0) - 1) * marks, axis=1))
        slot_index = (flat_routes * C + slot_place).astype(jnp.int32)
        token_of = (jnp.arange(flat_routes.shape[0]) // TOP).astype(jnp.int32)
        slot_owner = jnp.zeros((EXPERTS * C,), jnp.int32).at[slot_index].set(token_of)
        slot_filled = jnp.zeros((EXPERTS * C,), jnp.float32).at[slot_index].set(1.0)
        buffer_rows = (block_moe[slot_owner] * slot_filled[:, None]).reshape(EXPERTS, C, D)
        gate_pre = low_back(jnp.einsum('ecd,def->ecf', buffer_rows, w_gate_t, precision=PRECISE))
        up_pre = low_back(jnp.einsum('ecd,def->ecf', buffer_rows, w_up_t, precision=PRECISE))
        activ = low(silu_value(gate_pre) * up_pre)
        expert_out = low_back(jnp.einsum('ecf,def->ecd', activ, w_down_t, precision=PRECISE)).reshape(EXPERTS * C, D)
        picked = expert_out[slot_index].reshape(-1, TOP, D)
        return jnp.einsum('tk,tkd->td', block_gates, picked, precision=PRECISE)
    blocks = tok_total // TD
    routed = lax.map(jax.checkpoint(expert_block), (normed_moe.reshape(blocks, TD, D), routes.reshape(blocks, TD, TOP), route_gates.reshape(blocks, TD, TOP)))
    shared_gate = low_back(matmul(normed_moe, ws_gate))
    shared_up = low_back(matmul(normed_moe, ws_up))
    shared_act = low(silu_value(shared_gate) * shared_up)
    shared_out = matmul(shared_act, ws_down_t.T)
    output = residual + routed.reshape(tok_total, D) + shared_out
    return (output, (inv_mix, inv_moe))

def reference(hidden, cotangent, segments, routes, gain_mix, w_z, w_x, w_bc, w_dt, conv_x, conv_bc, dt_bias, a_log, d_skip, gain_gate, out_t, gain_moe, w_router, w_gate_t, w_up_t, w_down_t, ws_gate, ws_up, ws_down_t):
    starts = doc_starts(segments)

    def closed(*params):
        return layer_forward(*params, starts, routes)
    params = (hidden, gain_mix, w_z.astype(jnp.float32), w_x.astype(jnp.float32), w_bc.astype(jnp.float32), w_dt.astype(jnp.float32), conv_x, conv_bc, dt_bias, a_log, d_skip, gain_gate, out_t.astype(jnp.float32), gain_moe, w_router.astype(jnp.float32), w_gate_t.astype(jnp.float32), w_up_t.astype(jnp.float32), w_down_t.astype(jnp.float32), ws_gate.astype(jnp.float32), ws_up.astype(jnp.float32), ws_down_t.astype(jnp.float32))
    output, pullback, stats = jax.vjp(closed, *params, has_aux=True)
    grads = pullback(cotangent.astype(jnp.float32))
    return (output, grads[0], stats[0], stats[1], grads[1], grads[2], grads[3], grads[4], grads[5], grads[6], grads[7], grads[8], grads[9], grads[10], grads[11], grads[12], grads[13], grads[14], grads[15], grads[16], grads[17], grads[18], grads[19], grads[20])
```

```python
import jax
import jax.numpy as jnp
from jax import lax
from jax.sharding import PartitionSpec as P

EPS = 1e-05
PRECISE = lax.Precision.HIGHEST
BF = jnp.bfloat16
F32 = jnp.float32


def silu(v):
    return v * jax.nn.sigmoid(v)


def silu_slope(v):
    s = jax.nn.sigmoid(v)
    return s * (1.0 + v * (1.0 - s))


def nn(left, right):
    return lax.dot_general(left, right, (((1,), (0,)), ((), ())), preferred_element_type=F32)


def nt(left, right):
    return lax.dot_general(left, right, (((1,), (1,)), ((), ())), preferred_element_type=F32)


def tn(left, right):
    return lax.dot_general(left, right, (((0,), (0,)), ((), ())), preferred_element_type=F32)


def swap(value):
    return lax.ppermute(value, "seq", [(0, 1), (1, 0)])


def half(value, axis, which):
    size = value.shape[axis] // 2
    return lax.slice_in_dim(value, which * size, (which + 1) * size, axis=axis)


def own_half(value, axis):
    first = lax.axis_index("seq") == 0
    return jnp.where(first, half(value, axis, 0), half(value, axis, 1))


def other_half(value, axis):
    first = lax.axis_index("seq") == 0
    return jnp.where(first, half(value, axis, 1), half(value, axis, 0))


def join(own, other, axis):
    first = lax.axis_index("seq") == 0
    return jnp.where(
        first, jnp.concatenate([own, other], axis), jnp.concatenate([other, own], axis)
    )


def both(own):
    return jnp.concatenate([own, swap(own)], 0)


def low(value):
    return lax.reduce_precision(value, 8, 7)


def two(value):
    high = low(value)
    return high.astype(BF), (value - high).astype(BF)


def one(high, low_term):
    return high.astype(F32) + low_term.astype(F32)


def after(value, *others):
    return lax.optimization_barrier((value, *others))[0]


def exchange_rows(part, axis):
    count = lax.axis_size(axis)
    blocks = part.reshape(count, part.shape[0] // count, part.shape[1])
    return lax.all_to_all(blocks, axis, 0, 0, tiled=False)


def sum_to_tokens(part, *extra):
    rows = part.shape[0] // 2
    chip = (part[:rows].astype(F32) + swap(part[rows:]).astype(F32)).astype(BF)
    if extra:
        beside = jnp.concatenate(extra, 1)
        beside = beside[:rows] + swap(beside[rows:])
        chip = jnp.concatenate([chip, *two(beside)], 1)
    total = jnp.sum(exchange_rows(chip, "col").astype(F32), axis=0)
    if not extra:
        return total
    width, more = part.shape[1], beside.shape[1]
    return total[:, :width], total[:, width : width + more] + total[:, width + more :]


def from_tokens(own):
    return lax.all_gather(own, "col", axis=0, tiled=True)


def on_device(
    hidden,
    cotangent,
    segments,
    routes,
    gain_mix,
    w_z,
    w_x,
    w_bc,
    w_dt,
    conv_x,
    conv_bc,
    dt_bias,
    a_log,
    d_skip,
    gain_gate,
    out_t,
    gain_moe,
    w_router,
    w_gate_t,
    w_up_t,
    w_down_t,
    ws_gate,
    ws_up,
    ws_down_t,
):
    half_tokens, width = hidden.shape
    rows = lax.axis_size("row")
    cols = lax.axis_size("col")
    seq = lax.axis_index("seq")
    col = lax.axis_index("col")
    tokens = 2 * half_tokens
    inner = conv_x.shape[1] // 2
    heads = dt_bias.shape[0] // 2
    head_width = inner // heads
    state = conv_bc.shape[1] // 2
    experts = w_router.shape[1]
    hidden_units = w_gate_t.shape[2]
    shared_units = ws_gate.shape[1] // 2
    inner_all = conv_x.shape[1] * cols
    shard = half_tokens // cols

    mixer_half = lambda s: jnp.concatenate(
        [half(w_z, 1, s), half(w_x, 1, s), w_bc, half(out_t, 1, s), half(w_dt, 1, s)], 1
    )
    mixer_rows = jnp.stack([mixer_half(0), mixer_half(1)])
    mixer_width = mixer_rows.shape[2]
    mixer_whole = lax.all_to_all(
        jnp.broadcast_to(mixer_rows[None], (rows, *mixer_rows.shape)).reshape(
            2 * rows, -1, mixer_width
        ),
        ("row", "seq"),
        0,
        0,
    ).reshape(width, mixer_width)
    out_at = 2 * inner + 2 * state
    dt_at = out_at + inner
    out_whole = mixer_whole[:, out_at:dt_at]

    def expert_half(pick):
        parts = [
            pick(w_gate_t, 1)[:, 0],
            pick(w_up_t, 1)[:, 0],
            pick(ws_gate, 1),
            pick(ws_up, 1),
            w_router,
            jnp.zeros((w_router.shape[0], 128 - w_router.shape[1]), BF),
            pick(w_down_t, 1)[:, 0],
            pick(ws_down_t, 1),
        ]
        return jnp.concatenate(parts, 1)

    expert_rows = join(expert_half(own_half), swap(expert_half(other_half)), 0)
    expert_whole = lax.all_gather(expert_rows, "row", axis=0, tiled=True)
    down_units = hidden_units + shared_units
    in_units = 2 * down_units
    first_whole = expert_whole[:, : in_units + experts]
    down_whole = expert_whole[:, in_units + 128 :]

    inv_mix = lax.rsqrt(jnp.mean(hidden * hidden, axis=1) + EPS)
    normed_mix = both((hidden * inv_mix[:, None] * gain_mix).astype(BF))
    cot = both(cotangent)
    named = jnp.max(
        jnp.where(
            routes[:, :, None] == jnp.arange(experts, dtype=jnp.int32)[None, None, :], 1.0, 0.0
        ),
        axis=1,
    )
    marks = both(jnp.concatenate([named, segments.astype(F32)[:, None]], 1).astype(BF)).astype(F32)
    named = marks[:, :experts] > 0.0
    seg = marks[:, experts]
    place = (jnp.arange(tokens) + seq * half_tokens) % tokens
    hold = ((seg == jnp.roll(seg, 1)) & (place > 0)).astype(F32)[:, None]
    keep = [None, hold]
    for lag in range(2, 4):
        keep.append(keep[-1] * jnp.roll(hold, lag - 1, 0))

    taps = jnp.concatenate([own_half(conv_x, 1), conv_bc], 1)
    bias_here = own_half(dt_bias, 0)
    rate = jnp.exp(own_half(a_log, 0))
    skip_here = own_half(d_skip, 0)
    gain_here = own_half(gain_gate, 0)
    skip_wide = jnp.repeat(skip_here, head_width)[None, :]

    pre = nn(normed_mix, mixer_whole)
    z_pre = pre[:, :inner]
    conv_in = pre[:, inner:out_at]
    dt_in = pre[:, dt_at:] + bias_here
    conv_sum = taps[3][None, :] * conv_in
    for lag in range(1, 4):
        conv_sum = conv_sum + taps[3 - lag][None, :] * jnp.roll(conv_in, lag, 0) * keep[lag]
    conv_out = silu(conv_sum)
    x_conv = conv_out[:, :inner]
    b_map = conv_out[:, inner : inner + state].astype(BF)
    c_map = conv_out[:, inner + state :].astype(BF)
    step = jax.nn.softplus(dt_in)
    log_decay = -step * rate
    lower = place[:, None] >= place[None, :]
    triangle = lower.astype(F32)
    cum = jnp.dot(triangle, log_decay, precision=PRECISE)
    cum_t = cum.T
    mask = lower & (seg[:, None] == seg[None, :])
    scores = nt(c_map, b_map)
    decays, mixes, scaled, outs = [], [], [], []
    for h in range(heads):
        here = slice(h * head_width, (h + 1) * head_width)
        decay = jnp.exp(jnp.where(mask, cum[:, h : h + 1] - cum_t[h : h + 1, :], -jnp.inf))
        mix = (decay * scores).astype(BF)
        scale = low(x_conv[:, here] * step[:, h : h + 1])
        decays.append(decay)
        mixes.append(mix)
        scaled.append(scale)
        outs.append(nn(mix, scale.astype(BF)))
    scanned = jnp.concatenate(outs, 1)
    mixer_out = scanned + skip_wide * x_conv
    gated = mixer_out * silu(z_pre)
    square = jnp.sum(gated * gated, axis=1, keepdims=True)
    mix_part = nt((gated * gain_here).astype(BF), out_whole).astype(BF)
    mix_sum, square = sum_to_tokens(mix_part, square)

    here = lax.dynamic_slice_in_dim(hidden, col * shard, shard, 0)
    inv_gate_here = lax.rsqrt(square / inner_all + EPS)
    mix_out = mix_sum * inv_gate_here
    residual = here + mix_out
    inv_moe_here = lax.rsqrt(jnp.mean(residual * residual, axis=1, keepdims=True) + EPS)
    moe_here = (residual * inv_moe_here * gain_moe).astype(BF)
    moe_half = from_tokens(
        jnp.concatenate([moe_here, *two(inv_gate_here), *two(inv_moe_here)], 1)
    )
    inv_moe = one(moe_half[:, width + 2], moe_half[:, width + 3])
    moe_all = both(moe_half)
    normed_moe = moe_all[:, :width]
    inv_gate = one(moe_all[:, width : width + 1], moe_all[:, width + 1 : width + 2])

    pre = nn(normed_moe, first_whole)
    gate_pre = pre[:, :hidden_units]
    up_pre = pre[:, hidden_units : 2 * hidden_units]
    shared_gate = pre[:, 2 * hidden_units : 2 * hidden_units + shared_units]
    shared_up = pre[:, 2 * hidden_units + shared_units : in_units]
    logits = jnp.where(named, pre[:, in_units:], -jnp.inf)
    raised = jnp.exp(logits - jnp.max(logits, axis=1, keepdims=True))
    gates = raised / jnp.sum(raised, axis=1, keepdims=True)
    mine = (jnp.arange(experts) == 2 * col + seq).astype(F32)[None, :]
    weight = jnp.sum(gates * mine, axis=1, keepdims=True)
    act = silu(gate_pre) * up_pre
    shared_act = silu(shared_gate) * shared_up
    acts = jnp.concatenate([(act * weight).astype(BF), shared_act.astype(BF)], 1)
    moe_part = nt(acts, down_whole).astype(BF)
    back = nn(cot, down_whole)
    act_back = back[:, :hidden_units]
    shared_back = back[:, hidden_units:]
    gates_grad = jnp.sum(act * act_back, axis=1, keepdims=True) * mine
    act_grad = act_back * weight
    in_grads = jnp.concatenate(
        [
            (act_grad * up_pre * silu_slope(gate_pre)).astype(BF),
            (act_grad * silu(gate_pre)).astype(BF),
            (shared_back * shared_up * silu_slope(shared_gate)).astype(BF),
            (shared_back * silu(shared_gate)).astype(BF),
        ],
        1,
    )
    moe_in_part = nt(in_grads, first_whole[:, :in_units]).astype(BF)
    moe_in_sum, gates_grad = sum_to_tokens(moe_in_part, gates_grad)
    expert_sums = jnp.concatenate([tn(normed_moe, in_grads), tn(cot, acts)], 1).astype(BF)
    moe_in_sum, expert_sums = lax.optimization_barrier((moe_in_sum, expert_sums))
    expert_sums = lax.psum_scatter(expert_sums, "row", scatter_dimension=0, tiled=True)

    gates_here = lax.dynamic_slice_in_dim(gates, col * shard, shard, 0)
    cot_here = lax.dynamic_slice_in_dim(cotangent, col * shard, shard, 0).astype(F32)
    logits_grad = (
        gates_here * (gates_grad - jnp.sum(gates_here * gates_grad, axis=1, keepdims=True))
    ).astype(BF)
    moe_in_grad = moe_in_sum + nt(logits_grad, first_whole[:, in_units:])
    scaled_moe = moe_in_grad * gain_moe
    residual_grad = (
        cot_here
        + inv_moe_here * scaled_moe
        - residual
        * (inv_moe_here**3 * jnp.mean(scaled_moe * residual, axis=1, keepdims=True))
    )
    gain_moe_grad = jnp.sum(moe_in_grad * residual * inv_moe_here, axis=0)
    mix_grad_here = residual_grad.astype(BF)
    gate_dot = jnp.sum(mix_grad_here.astype(F32) * mix_out, axis=1, keepdims=True)
    mix_all = both(
        from_tokens(jnp.concatenate([mix_grad_here, logits_grad, *two(gate_dot)], 1))
    )
    mix_grad = mix_all[:, :width]
    logits_all = mix_all[:, width : width + experts]
    gate_dot = one(
        mix_all[:, width + experts : width + experts + 1], mix_all[:, width + experts + 1 :]
    )

    output_here = residual + sum_to_tokens(after(moe_part, mix_all))
    output = lax.all_gather(output_here, "col", axis=0, tiled=True)

    gate_norm_grad = nn(mix_grad, out_whole)
    normed = gated * inv_gate
    gain_gate_grad = jnp.sum(gate_norm_grad * normed, axis=0)
    normed_gate = (normed * gain_here).astype(BF)
    gated_grad = inv_gate * (gate_norm_grad * gain_here) - gated * (
        inv_gate * inv_gate * gate_dot / inner_all
    )
    ssm_grad = gated_grad * silu(z_pre)
    z_grad = (gated_grad * mixer_out * silu_slope(z_pre)).astype(BF)
    by_head = lambda v: jnp.sum(v.reshape(tokens, heads, head_width), axis=2)
    skip_grad = jnp.sum(by_head(ssm_grad * x_conv), axis=0)
    ssm_round = low(ssm_grad)
    ssm_low = ssm_round.astype(BF)
    scores_grad = jnp.zeros((tokens, tokens), F32)
    spread = []
    for h in range(heads):
        here = slice(h * head_width, (h + 1) * head_width)
        spread.append(tn(mixes[h], ssm_low[:, here]))
        scores_grad = scores_grad + decays[h] * nt(ssm_low[:, here], scaled[h].astype(BF))
    scores_low = scores_grad.astype(BF)
    scaled_grad = jnp.concatenate(spread, 1)
    step_grad = by_head(x_conv * scaled_grad)
    cum_grad = by_head(ssm_round * scanned) - by_head(
        jnp.concatenate(scaled, 1) * scaled_grad
    )
    decay_grad = lax.dot_general(
        triangle, cum_grad, (((0,), (0,)), ((), ())), precision=PRECISE
    )
    step_wide = jnp.repeat(step, head_width, axis=1)
    inputs_grad = scaled_grad * step_wide + ssm_grad * skip_wide
    b_grad = tn(scores_low, c_map)
    c_grad = nn(scores_low, b_map)
    step_grad = step_grad - decay_grad * rate
    a_log_grad = jnp.sum(decay_grad * log_decay, axis=0)
    dt_float = step_grad * jax.nn.sigmoid(dt_in)
    dt_bias_grad = jnp.sum(dt_float, axis=0)
    conv_grad = jnp.concatenate([inputs_grad, b_grad, c_grad], 1) * silu_slope(conv_sum)
    taps_grad = [jnp.sum(conv_grad * conv_in, axis=0)]
    conv_in_grad = taps[3][None, :] * conv_grad
    for lag in range(1, 4):
        kept = conv_grad * keep[lag]
        taps_grad.append(jnp.sum(kept * jnp.roll(conv_in, lag, 0), axis=0))
        conv_in_grad = conv_in_grad + taps[3 - lag][None, :] * jnp.roll(kept, -lag, 0)
    taps_grad = jnp.stack(taps_grad[::-1])
    mixer_grads = jnp.concatenate([z_grad, conv_in_grad.astype(BF), dt_float.astype(BF)], 1)
    mixer_in = jnp.concatenate([mixer_whole[:, :out_at], mixer_whole[:, dt_at:]], 1)
    mix_in_grad = sum_to_tokens(nt(mixer_grads, mixer_in).astype(BF))
    mixer_sums = jnp.concatenate(
        [tn(mix_grad, normed_gate), tn(normed_mix, mixer_grads), tn(normed_moe, logits_all)], 1
    ).astype(BF)

    here = lax.dynamic_slice_in_dim(hidden, col * shard, shard, 0)
    inv_here = lax.dynamic_slice_in_dim(inv_mix, col * shard, shard, 0)[:, None]
    scaled_mix = mix_in_grad * gain_mix
    grad_hidden_here = (
        residual_grad
        + inv_here * scaled_mix
        - here * (inv_here**3 * jnp.mean(scaled_mix * here, axis=1, keepdims=True))
    )
    gain_mix_grad = jnp.sum(mix_in_grad * here * inv_here, axis=0)

    small = jnp.concatenate(
        [
            gain_mix_grad,
            gain_moe_grad,
            taps_grad[:, inner:].reshape(-1),
            gain_gate_grad,
            taps_grad[:, :inner].reshape(-1),
            dt_bias_grad,
            a_log_grad,
            skip_grad,
        ]
    )
    for_all = 2 * width + conv_bc.size
    sums_width = mixer_sums.shape[1]
    small_rows = -(-2 * small.shape[0] // sums_width)
    small_flat = jnp.concatenate(
        [*two(small), jnp.zeros((small_rows * sums_width - 2 * small.shape[0],), BF)]
    ).reshape(1, small_rows, sums_width)
    sent = jnp.concatenate(
        [
            mixer_sums.reshape(2 * rows, -1, sums_width),
            jnp.broadcast_to(small_flat, (2 * rows, small_rows, sums_width)),
        ],
        1,
    )
    got = lax.all_to_all(sent, ("row", "seq"), 0, 0).astype(F32)
    got = jnp.sum(got.reshape(rows, 2, -1, sums_width), axis=0)
    mine = w_z.shape[0]
    sums, small_sums = got[:, :mine], got[:, mine:].reshape(2, -1)
    count = small.shape[0]
    small_sums = small_sums[:, :count] + small_sums[:, count : 2 * count]

    def columns(at, size):
        return jnp.concatenate([sums[0, :, at : at + size], sums[1, :, at : at + size]], 1)

    bc_at = 3 * inner
    end = bc_at + 2 * state
    bc_sum = sums[0, :, bc_at:end] + sums[1, :, bc_at:end]
    pieces = [
        grad_hidden_here.astype(BF).reshape(-1),
        bc_sum.astype(BF).reshape(-1),
        *two(small_sums[0, :for_all] + small_sums[1, :for_all]),
    ]
    sizes = [p.shape[0] for p in pieces]
    whole = from_tokens(jnp.concatenate(pieces).reshape(1, -1))
    ends = [sum(sizes[: i + 1]) for i in range(len(sizes))]
    grad_hidden = whole[:, : ends[0]].reshape(half_tokens, width).astype(F32)
    g_w_bc = jnp.sum(whole[:, ends[0] : ends[1]].astype(F32), axis=0).reshape(-1, 2 * state)
    small_all = jnp.sum(whole[:, ends[1] :].astype(F32), axis=0)
    small_all = small_all[:for_all] + small_all[for_all:]

    g_out_t = columns(0, inner)
    g_w_z = columns(inner, inner)
    g_w_x = columns(2 * inner, inner)
    g_w_dt = columns(end, heads)
    g_w_router = sums[0, :, end + heads :]
    rest = small_sums[:, for_all:]

    def pairs(at, size, first=1):
        part = rest[:, at : at + size].reshape(2, first, -1)
        return jnp.concatenate([part[0], part[1]], 1)

    g_gain_gate = pairs(0, inner).reshape(-1)
    g_conv_x = pairs(inner, 4 * inner, 4)
    g_dt_bias = pairs(5 * inner, heads).reshape(-1)
    g_a_log = pairs(5 * inner + heads, heads).reshape(-1)
    g_d_skip = pairs(5 * inner + 2 * heads, heads).reshape(-1)
    g_gain_mix = small_all[:width]
    g_gain_moe = small_all[width : 2 * width]
    g_conv_bc = small_all[2 * width :].reshape(4, -1)

    own = own_half(expert_sums, 0)
    other = swap(other_half(expert_sums, 0))

    def expert(at):
        a = own[:, None, at : at + hidden_units]
        return join(a, other[:, None, at : at + hidden_units], 1).astype(F32)

    def shared(at):
        return join(
            own[:, at : at + shared_units], other[:, at : at + shared_units], 1
        ).astype(F32)

    g_w_gate_t = expert(0)
    g_w_up_t = expert(hidden_units)
    g_w_down_t = expert(in_units)
    g_ws_gate = shared(2 * hidden_units)
    g_ws_up = shared(2 * hidden_units + shared_units)
    g_ws_down_t = shared(in_units + hidden_units)
    return (
        output,
        grad_hidden,
        inv_mix,
        inv_moe,
        g_gain_mix,
        g_w_z,
        g_w_x,
        g_w_bc,
        g_w_dt,
        g_conv_x,
        g_conv_bc,
        g_dt_bias,
        g_a_log,
        g_d_skip,
        g_gain_gate,
        g_out_t,
        g_gain_moe,
        g_w_router,
        g_w_gate_t,
        g_w_up_t,
        g_w_down_t,
        g_ws_gate,
        g_ws_up,
        g_ws_down_t,
    )


def solution(mesh):
    placed = (
        P(("row", "seq"), None),
        P(("row", "seq"), None),
        P(("row", "seq")),
        P(("row", "seq"), None),
        P(),
        P(("row", "seq"), "col"),
        P(("row", "seq"), "col"),
        P(("row", "seq"), None),
        P(("row", "seq"), "col"),
        P(None, "col"),
        P(),
        P("col"),
        P("col"),
        P("col"),
        P("col"),
        P(("row", "seq"), "col"),
        P(),
        P(("row", "seq"), None),
        P(("row", "seq"), "col", None),
        P(("row", "seq"), "col", None),
        P(("row", "seq"), "col", None),
        P(("row", "seq"), "col"),
        P(("row", "seq"), "col"),
        P(("row", "seq"), "col"),
    )
    return jax.shard_map(
        on_device,
        mesh=mesh,
        in_specs=placed,
        out_specs=(
            P(("row", "seq"), None),
            P(("row", "seq"), None),
            P(("row", "seq")),
            P(("row", "seq")),
            P(),
            P(("row", "seq"), "col"),
            P(("row", "seq"), "col"),
            P(("row", "seq"), None),
            P(("row", "seq"), "col"),
            P(None, "col"),
            P(),
            P("col"),
            P("col"),
            P("col"),
            P("col"),
            P(("row", "seq"), "col"),
            P(),
            P(("row", "seq"), None),
            P(("row", "seq"), "col", None),
            P(("row", "seq"), "col", None),
            P(("row", "seq"), "col", None),
            P(("row", "seq"), "col"),
            P(("row", "seq"), "col"),
            P(("row", "seq"), "col"),
        ),
        check_vma=False,
    )
```

```python
import functools

import jax
import jax.numpy as jnp
from jax import lax
from jax.experimental import pallas as pl
from jax.experimental.pallas import tpu as pltpu
from jax.sharding import PartitionSpec as P

EPS = 1e-05
BF = jnp.bfloat16
F32 = jnp.float32
FAR = -1e30


def silu(v):
    return v * jax.nn.sigmoid(v)


def nn(left, right):
    return lax.dot_general(left, right, (((1,), (0,)), ((), ())), preferred_element_type=F32)


def nt(left, right):
    return lax.dot_general(left, right, (((1,), (1,)), ((), ())), preferred_element_type=F32)


def tn(left, right):
    return lax.dot_general(left, right, (((0,), (0,)), ((), ())), preferred_element_type=F32)


def swap(value):
    return lax.ppermute(value, "seq", [(0, 1), (1, 0)])


def half(value, axis, which):
    size = value.shape[axis] // 2
    return lax.slice_in_dim(value, which * size, (which + 1) * size, axis=axis)


def own_half(value, axis):
    first = lax.axis_index("seq") == 0
    return jnp.where(first, half(value, axis, 0), half(value, axis, 1))


def other_half(value, axis):
    first = lax.axis_index("seq") == 0
    return jnp.where(first, half(value, axis, 1), half(value, axis, 0))


def join(own, other, axis):
    first = lax.axis_index("seq") == 0
    return jnp.where(
        first, jnp.concatenate([own, other], axis), jnp.concatenate([other, own], axis)
    )


def low(value):
    return lax.reduce_precision(value, 8, 7)


def two(value):
    high = low(value)
    return high.astype(BF), (value - high).astype(BF)


def three(value):
    high = value.astype(BF)
    rest = value - high.astype(F32)
    middle = rest.astype(BF)
    return high, middle, (rest - middle.astype(F32)).astype(BF)


def exact(left, value):
    high, middle, last = three(value)
    return (nn(left, last) + nn(left, middle)) + nn(left, high)


def one(high, low_term):
    return high.astype(F32) + low_term.astype(F32)


def after(value, *others):
    return lax.optimization_barrier((value, *others))[0]


def call(kernel, outs, args, flops, name):
    whole = pl.BlockSpec(memory_space=pltpu.VMEM)
    shapes = [jax.ShapeDtypeStruct(shape, kind) for shape, kind in outs]
    size = lambda a: a.size * jnp.dtype(a.dtype).itemsize
    return pl.pallas_call(
        kernel,
        out_shape=shapes,
        in_specs=[whole] * len(args),
        out_specs=[whole] * len(outs),
        compiler_params=pltpu.CompilerParams(vmem_limit_bytes=56 * 2**20),
        cost_estimate=pl.CostEstimate(
            flops=flops,
            bytes_accessed=sum(size(a) for a in args) + sum(size(a) for a in shapes),
            transcendentals=0,
        ),
        name=name,
    )(*args)


def causal(marks, marks_row, rows):
    return (marks[rows, 1:2] >= marks_row[1:2, :]) & (marks[rows, 0:1] == marks_row[0:1, :])


def convolved(value, taps, marks):
    total = taps[3:4, :] * value
    for lag in range(1, 4):
        rolled = pltpu.roll(value, lag, 0) * marks[:, 1 + lag : 2 + lag]
        total = total + taps[3 - lag : 4 - lag, :] * rolled
    return total


def head_columns(inner, lanes, head_width):
    down = lax.broadcasted_iota(jnp.int32, (inner, lanes), 0)
    across = lax.broadcasted_iota(jnp.int32, (inner, lanes), 1) * head_width
    return jnp.where((down >= across) & (down < across + head_width), 1.0, 0.0).astype(BF)


def by_head(value, columns):
    high, middle, last = three(value)
    return (nn(last, columns) + nn(middle, columns)) + nn(high, columns)


def softplus(v):
    return jnp.maximum(v, 0.0) + jnp.log1p(jnp.exp(-jnp.abs(v)))


def mixer_forward(
    inner,
    head_width,
    own_ref,
    other_ref,
    w_ref,
    marks_ref,
    row_ref,
    taps_x_ref,
    taps_bc_ref,
    head_ref,
    wide_ref,
    pre_ref,
    dt_ref,
    cum_ref,
    scanned_ref,
    part_own_ref,
    part_other_ref,
    square_ref,
    scaled_ref,
):
    half_tokens, width = own_ref.shape
    tokens = 2 * half_tokens
    heads = inner // head_width
    bc_at, out_at, dt_at = 2 * inner, pre_ref.shape[1], pre_ref.shape[1] + inner
    state = (out_at - bc_at) // 2
    for part, src in ((0, own_ref), (1, other_ref)):
        rows = slice(part * half_tokens, (part + 1) * half_tokens)
        pre_ref[rows, :] = nn(src[...], w_ref[:, :out_at])
        dt_ref[rows, :] = nn(src[...], w_ref[:, dt_at:]) + head_ref[0:1, :]
    marks, marks_row = marks_ref[...], row_ref[...]
    x_conv = silu(convolved(pre_ref[:, :inner], taps_x_ref[...], marks))
    bc = silu(convolved(pre_ref[:, bc_at:out_at], taps_bc_ref[...], marks)).astype(BF)
    b_map, c_map = bc[:, :state], bc[:, state:]
    step = softplus(dt_ref[...])
    lower = jnp.where(marks[:, 1:2] >= marks_row[1:2, :], 1.0, 0.0).astype(BF)
    cum = exact(lower, -step * head_ref[1:2, :])
    cum_ref[...] = cum
    cum_row = jnp.concatenate([cum, jnp.zeros_like(cum)], 1).T
    for h in range(heads):
        here = slice(h * head_width, (h + 1) * head_width)
        scaled_ref[:, here] = (x_conv[:, here] * step[:, h : h + 1]).astype(BF)
    block = 128
    for at in range(0, tokens, block):
        rows = slice(at, at + block)
        scores = nt(c_map[rows, :], b_map)
        mask = causal(marks, marks_row, rows)
        for h in range(heads):
            here = slice(h * head_width, (h + 1) * head_width)
            gap = cum[rows, h : h + 1] - cum_row[h : h + 1, :]
            mix = (jnp.exp(jnp.where(mask, gap, FAR)) * scores).astype(BF)
            scanned_ref[rows, here] = nn(mix, scaled_ref[:, here])
    mixer_out = scanned_ref[...] + wide_ref[0:1, :] * x_conv
    gated = mixer_out * silu(pre_ref[:, inner:bc_at])
    square_ref[...] = jnp.sum(gated * gated, axis=1, keepdims=True)
    sent = (gated * wide_ref[1:2, :]).astype(BF)
    out_w = w_ref[:, out_at:dt_at]
    part_own_ref[...] = nt(sent[:half_tokens], out_w).astype(BF)
    part_other_ref[...] = nt(sent[half_tokens:], out_w).astype(BF)


def mixer_backward(
    inner,
    inner_all,
    head_width,
    own_ref,
    other_ref,
    moe_own_ref,
    moe_other_ref,
    w_ref,
    marks_ref,
    row_ref,
    taps_x_ref,
    taps_bc_ref,
    head_ref,
    wide_ref,
    pre_ref,
    dt_ref,
    cum_ref,
    scanned_ref,
    grads_ref,
    dt_grad_ref,
    normed_ref,
    part_own_ref,
    part_other_ref,
    small_ref,
    scaled_ref,
    low_ref,
    spread_ref,
    c_grad_ref,
    b_grad_ref,
):
    half_tokens = own_ref.shape[0]
    width = w_ref.shape[0]
    tokens = 2 * half_tokens
    heads = inner // head_width
    bc_at, out_at, dt_at = 2 * inner, pre_ref.shape[1], pre_ref.shape[1] + inner
    state = (out_at - bc_at) // 2
    experts = own_ref.shape[1] - width - 2
    marks, marks_row = marks_ref[...], row_ref[...]
    stack = lambda a, b: jnp.concatenate([a, b], 0)
    conv_x = convolved(pre_ref[:, :inner], taps_x_ref[...], marks)
    conv_bc = convolved(pre_ref[:, bc_at:out_at], taps_bc_ref[...], marks)
    x_conv = silu(conv_x)
    bc = silu(conv_bc).astype(BF)
    b_map, c_map = bc[:, :state], bc[:, state:]
    z_pre = pre_ref[:, inner:bc_at]
    step = softplus(dt_ref[...])
    rate = head_ref[1:2, :]
    skip_wide, gain = wide_ref[0:1, :], wide_ref[1:2, :]
    out_w = w_ref[:, out_at:dt_at]
    gate_norm_grad = stack(
        nn(own_ref[:, :width], out_w), nn(other_ref[:, :width], out_w)
    )
    at = width + experts
    dots = lambda ref: one(ref[:, at : at + 1], ref[:, at + 1 : at + 2])
    gate_dot = stack(dots(own_ref), dots(other_ref))
    gates = lambda ref: one(ref[:, width : width + 1], ref[:, width + 1 : width + 2])
    inv_gate = stack(gates(moe_own_ref), gates(moe_other_ref))
    sig = jax.nn.sigmoid(z_pre)
    silu_z = z_pre * sig
    mixer_out = scanned_ref[...] + skip_wide * x_conv
    gated = mixer_out * silu_z
    normed = gated * inv_gate
    small_ref[...] = jnp.zeros_like(small_ref)
    misc = 4 * 128
    small_ref[4:5, misc : misc + inner] = jnp.sum(gate_norm_grad * normed, axis=0, keepdims=True)
    normed_ref[...] = (normed * gain).astype(BF)
    gated_grad = inv_gate * (gate_norm_grad * gain) - gated * (
        inv_gate * inv_gate * gate_dot * (1.0 / inner_all)
    )
    ssm_grad = gated_grad * silu_z
    grads_ref[:, inner:bc_at] = (
        gated_grad * mixer_out * (sig * (1.0 + z_pre * (1.0 - sig)))
    ).astype(BF)
    columns = head_columns(inner, dt_ref.shape[1], head_width)
    skips = by_head(
        jnp.broadcast_to(jnp.sum(ssm_grad * x_conv, axis=0, keepdims=True), (8, inner)), columns
    )
    small_ref[7:8, misc : misc + heads] = skips[0:1, :heads]
    low_ref[...] = ssm_grad.astype(BF)
    for h in range(heads):
        here = slice(h * head_width, (h + 1) * head_width)
        scaled_ref[:, here] = (x_conv[:, here] * step[:, h : h + 1]).astype(BF)
    cum = cum_ref[...]
    cum_row = jnp.concatenate([cum, jnp.zeros_like(cum)], 1).T
    c_grad_ref[...] = jnp.zeros_like(c_grad_ref)
    block = 128
    for start in range(0, tokens, block):
        rows = slice(start, start + block)
        scores = nt(b_map[rows, :], c_map)
        mask = (marks_row[1:2, :] >= marks[rows, 1:2]) & (
            marks_row[0:1, :] == marks[rows, 0:1]
        )
        scores_grad = jnp.zeros((block, tokens), F32)
        for h in range(heads):
            here = slice(h * head_width, (h + 1) * head_width)
            gap = cum_row[h : h + 1, :] - cum[rows, h : h + 1]
            decay = jnp.exp(jnp.where(mask, gap, FAR))
            spread_ref[rows, here] = nn((decay * scores).astype(BF), low_ref[:, here])
            scores_grad = scores_grad + decay * nt(scaled_ref[rows, here], low_ref[:, here])
        scores_low = scores_grad.astype(BF)
        b_grad_ref[rows, :] = nn(scores_low, c_map)
        c_grad_ref[...] += tn(scores_low, b_map[rows, :])
    spread = spread_ref[...]
    step_grad = by_head(x_conv * spread, columns)
    cum_grad = by_head(
        low_ref[...].astype(F32) * scanned_ref[...] - scaled_ref[...].astype(F32) * spread, columns
    )
    upper = jnp.where(marks_row[1:2, :] >= marks[:, 1:2], 1.0, 0.0).astype(BF)
    decay_grad = exact(upper, cum_grad)
    dt_float = (step_grad - decay_grad * rate) * jax.nn.sigmoid(dt_ref[...])
    small_ref[5:6, misc : misc + heads] = jnp.sum(dt_float, axis=0, keepdims=True)[:, :heads]
    small_ref[6:7, misc : misc + heads] = jnp.sum(
        decay_grad * (-step * rate), axis=0, keepdims=True
    )[:, :heads]
    dt_low = dt_float.astype(BF)
    dt_grad_ref[...] = dt_low
    for h in range(heads):
        here = slice(h * head_width, (h + 1) * head_width)
        spread_ref[:, here] = spread[:, here] * step[:, h : h + 1]

    def back(value_grad, total, value, taps, lanes, to):
        sig_c = jax.nn.sigmoid(total)
        grad = value_grad * (sig_c * (1.0 + total * (1.0 - sig_c)))
        small_ref[7:8, lanes] = small_ref[7:8, lanes] + jnp.sum(
            grad * value, axis=0, keepdims=True
        )
        result = taps[3:4, :] * grad
        for lag in range(1, 4):
            kept = grad * marks[:, 1 + lag : 2 + lag]
            small_ref[7 - lag : 8 - lag, lanes] = jnp.sum(
                kept * pltpu.roll(value, lag, 0), axis=0, keepdims=True
            )
            result = result + taps[3 - lag : 4 - lag, :] * pltpu.roll(kept, tokens - lag, 0)
        grads_ref[:, to] = result.astype(BF)

    back(
        spread_ref[...] + ssm_grad * skip_wide,
        conv_x,
        pre_ref[:, :inner],
        taps_x_ref[...],
        slice(0, inner),
        slice(0, inner),
    )
    back(
        jnp.concatenate([b_grad_ref[...], c_grad_ref[...]], 1),
        conv_bc,
        pre_ref[:, bc_at:out_at],
        taps_bc_ref[...],
        slice(inner, inner + 2 * state),
        slice(bc_at, out_at),
    )
    for part, dst in ((0, part_own_ref), (1, part_other_ref)):
        rows = slice(part * half_tokens, (part + 1) * half_tokens)
        dst[...] = (
            nt(grads_ref[rows, :], w_ref[:, :out_at]) + nt(dt_low[rows, :], w_ref[:, dt_at:])
        ).astype(BF)


def mixer_products(
    inner,
    own_ref,
    other_ref,
    mix_own_ref,
    mix_other_ref,
    moe_own_ref,
    moe_other_ref,
    grads_ref,
    dt_grad_ref,
    normed_ref,
    sums_ref,
):
    half_tokens, width = own_ref.shape
    out_at = grads_ref.shape[1]
    dt_at = out_at + inner
    experts = mix_own_ref.shape[1] - width - 2
    count = sums_ref.shape[0]
    rows = width // count
    group = min(8, count)
    first, second = slice(0, half_tokens), slice(half_tokens, 2 * half_tokens)
    logits = slice(width, width + experts)
    for at in range(0, count, group):
        here = slice(at * rows, (at + group) * rows)
        mine, others = own_ref[:, here], other_ref[:, here]
        a = tn(mine, grads_ref[first, :]) + tn(others, grads_ref[second, :])
        b = tn(mix_own_ref[:, here], normed_ref[first, :]) + tn(
            mix_other_ref[:, here], normed_ref[second, :]
        )
        c = tn(mine, dt_grad_ref[first, :]) + tn(others, dt_grad_ref[second, :])
        d = tn(moe_own_ref[:, here], mix_own_ref[:, logits]) + tn(
            moe_other_ref[:, here], mix_other_ref[:, logits]
        )
        a, b, c, d = a.astype(BF), b.astype(BF), c.astype(BF), d.astype(BF)
        for k in range(group):
            part = slice(k * rows, (k + 1) * rows)
            sums_ref[at + k, :rows, :out_at] = a[part]
            sums_ref[at + k, :rows, out_at:dt_at] = b[part]
            sums_ref[at + k, :rows, dt_at:] = c[part]
            sums_ref[at + k, :rows, dt_at + 16 : dt_at + 16 + experts] = d[part]
    sums_ref[:, rows:, :] = jnp.zeros(
        (count, sums_ref.shape[1] - rows, sums_ref.shape[2]), BF
    )


def experts_both_ways(
    units,
    shared,
    own_ref,
    other_ref,
    cot_own_ref,
    cot_other_ref,
    w_ref,
    named_ref,
    mine_ref,
    in_own_ref,
    in_other_ref,
    out_own_ref,
    out_other_ref,
    grads_ref,
    acts_ref,
    gates_ref,
    gates_grad_ref,
):
    half_tokens = own_ref.shape[0]
    width = w_ref.shape[0]
    experts = named_ref.shape[1]
    in_units = 2 * (units + shared)
    down_at = in_units + 128
    mine = mine_ref[...]
    parts = (
        (own_ref, cot_own_ref, in_own_ref, out_own_ref),
        (other_ref, cot_other_ref, in_other_ref, out_other_ref),
    )
    for part, (src, cot, in_dst, out_dst) in enumerate(parts):
        rows = slice(part * half_tokens, (part + 1) * half_tokens)
        pre = nn(src[:, :width], w_ref[:, :down_at])
        back = nn(cot[...], w_ref[:, down_at:])
        logits = jnp.where(named_ref[rows, :] > 0.0, pre[:, in_units : in_units + experts], FAR)
        raised = jnp.exp(logits - jnp.max(logits, axis=1, keepdims=True))
        gates = raised / jnp.sum(raised, axis=1, keepdims=True)
        gates_ref[rows, :] = gates
        weight = jnp.sum(gates * mine, axis=1, keepdims=True)
        gate, up = pre[:, :units], pre[:, units : 2 * units]
        sig = jax.nn.sigmoid(gate)
        silu_gate = gate * sig
        act = silu_gate * up
        acts_ref[rows, :units] = (act * weight).astype(BF)
        act_back = back[:, :units]
        gates_grad_ref[rows, :] = jnp.sum(act * act_back, axis=1, keepdims=True) * mine
        act_grad = act_back * weight
        grads_ref[rows, :units] = (
            act_grad * up * (sig * (1.0 + gate * (1.0 - sig)))
        ).astype(BF)
        grads_ref[rows, units : 2 * units] = (act_grad * silu_gate).astype(BF)
        gate, up = pre[:, 2 * units : 2 * units + shared], pre[:, 2 * units + shared : in_units]
        sig = jax.nn.sigmoid(gate)
        silu_gate = gate * sig
        acts_ref[rows, units:] = (silu_gate * up).astype(BF)
        act_grad = back[:, units:]
        grads_ref[rows, 2 * units : 2 * units + shared] = (
            act_grad * up * (sig * (1.0 + gate * (1.0 - sig)))
        ).astype(BF)
        grads_ref[rows, 2 * units + shared :] = (act_grad * silu_gate).astype(BF)
        in_dst[...] = nt(grads_ref[rows, :], w_ref[:, :in_units]).astype(BF)
        out_dst[...] = nt(acts_ref[rows, :], w_ref[:, down_at:]).astype(BF)


def expert_products(
    own_ref, other_ref, cot_own_ref, cot_other_ref, grads_ref, acts_ref, sums_ref
):
    half_tokens, width = cot_own_ref.shape
    split = grads_ref.shape[1]
    first, second = slice(0, half_tokens), slice(half_tokens, 2 * half_tokens)
    block = 256
    for at in range(0, width, block):
        here = slice(at, at + block)
        sums_ref[here, :split] = (
            tn(own_ref[:, here], grads_ref[first, :]) + tn(other_ref[:, here], grads_ref[second, :])
        ).astype(BF)
        sums_ref[here, split:] = (
            tn(cot_own_ref[:, here], acts_ref[first, :])
            + tn(cot_other_ref[:, here], acts_ref[second, :])
        ).astype(BF)


def tail_sums(
    inner,
    heads,
    got_ref,
    out_ref,
    z_ref,
    x_ref,
    dt_ref,
    router_ref,
    conv_ref,
    gain_ref,
    head_ref,
    sent_ref,
):
    count, rows = got_ref.shape[0], out_ref.shape[0]
    experts = router_ref.shape[1]
    bc_at = 2 * inner
    out_at = got_ref.shape[2] - 64 - inner
    dt_at = out_at + inner
    totals = []
    for core in range(2):
        total = got_ref[core].astype(F32)
        for at in range(core + 2, count, 2):
            total = total + got_ref[at].astype(F32)
        totals.append(total)
        here = slice(core * inner, (core + 1) * inner)
        x_ref[:, here] = total[:rows, :inner]
        z_ref[:, here] = total[:rows, inner:bc_at]
        out_ref[:, here] = total[:rows, out_at:dt_at]
        dt_ref[:, core * heads : (core + 1) * heads] = total[:rows, dt_at : dt_at + heads]
        small = total[rows : rows + 8] + total[rows + 8 :]
        conv_ref[:, here] = small[4:8, :inner]
        gain_ref[:, here] = small[4:5, 512 : 512 + inner]
        for k in range(3):
            head_ref[k : k + 1, core * heads : (core + 1) * heads] = small[
                5 + k : 6 + k, 512 : 512 + heads
            ]
    router_ref[...] = totals[0][:rows, dt_at + 16 : dt_at + 16 + experts]
    both = totals[0] + totals[1]
    span = out_at - bc_at
    sent_ref[:rows, :] = both[:rows, bc_at:out_at].astype(BF)
    small = both[rows : rows + 8] + both[rows + 8 :]
    pieces = [small[0:4, k * span : (k + 1) * span] for k in range(3)]
    pieces.append(small[4:8, inner : inner + span])
    for k, piece in enumerate(pieces):
        high = piece.astype(BF)
        sent_ref[rows + 4 * k : rows + 4 * k + 4, :] = high
        sent_ref[rows + 16 + 4 * k : rows + 20 + 4 * k, :] = (
            piece - high.astype(F32)
        ).astype(BF)


def last_sums(got_ref, bc_ref, mix_ref, moe_ref, conv_ref):
    rows, span = bc_ref.shape
    total = got_ref[0].astype(F32)
    for at in range(1, got_ref.shape[0]):
        total = total + got_ref[at].astype(F32)
    bc_ref[...] = total[:rows]
    small = total[rows : rows + 16] + total[rows + 16 :]
    for k in range(3):
        for part, dst in ((0, mix_ref), (1, moe_ref)):
            for row in range(2):
                at = row * 3 * span + k * span
                dst[:, at : at + span] = small[4 * k + 2 * part + row : 4 * k + 2 * part + row + 1]
    conv_ref[...] = small[12:16]


def exchange_rows(part, axis):
    count = lax.axis_size(axis)
    blocks = part.reshape(count, part.shape[0] // count, part.shape[1])
    return lax.all_to_all(blocks, axis, 0, 0, tiled=False)


def sum_to_tokens(own, other, *extra):
    rows = own.shape[0]
    chip = (own.astype(F32) + swap(other).astype(F32)).astype(BF)
    if extra:
        beside = jnp.concatenate(extra, 1)
        beside = beside[:rows] + swap(beside[rows:])
        chip = jnp.concatenate([chip, *two(beside)], 1)
    total = jnp.sum(exchange_rows(chip, "col").astype(F32), axis=0)
    if not extra:
        return total
    width, more = own.shape[1], beside.shape[1]
    return total[:, :width], total[:, width : width + more] + total[:, width + more :]


def from_tokens(own):
    return lax.all_gather(own, "col", axis=0, tiled=True)


def on_device(
    hidden,
    cotangent,
    segments,
    routes,
    gain_mix,
    w_z,
    w_x,
    w_bc,
    w_dt,
    conv_x,
    conv_bc,
    dt_bias,
    a_log,
    d_skip,
    gain_gate,
    out_t,
    gain_moe,
    w_router,
    w_gate_t,
    w_up_t,
    w_down_t,
    ws_gate,
    ws_up,
    ws_down_t,
):
    half_tokens, width = hidden.shape
    rows = lax.axis_size("row")
    cols = lax.axis_size("col")
    seq = lax.axis_index("seq")
    col = lax.axis_index("col")
    tokens = 2 * half_tokens
    inner = conv_x.shape[1] // 2
    heads = dt_bias.shape[0] // 2
    head_width = inner // heads
    state = conv_bc.shape[1] // 2
    experts = w_router.shape[1]
    hidden_units = w_gate_t.shape[2]
    shared_units = ws_gate.shape[1] // 2
    lanes = 64
    inner_all = conv_x.shape[1] * cols
    shard = half_tokens // cols

    out_at = 2 * inner + 2 * state
    dt_at = out_at + inner
    mixer_width = dt_at + lanes
    zeros = jnp.zeros((w_z.shape[0], lanes - heads), BF)
    mixer_half = lambda s: jnp.concatenate(
        [half(w_x, 1, s), half(w_z, 1, s), w_bc, half(out_t, 1, s), half(w_dt, 1, s), zeros], 1
    )
    mixer_rows = jnp.stack([mixer_half(0), mixer_half(1)])
    spread_rows = jnp.broadcast_to(mixer_rows[None], (rows, *mixer_rows.shape)).reshape(
        2 * rows, -1, mixer_width
    )
    (
        spread_rows,
        w_gate_t,
        w_up_t,
        w_down_t,
        ws_gate,
        ws_up,
        ws_down_t,
        conv_x,
        dt_bias,
        a_log,
        d_skip,
        gain_gate,
        segments,
        routes,
    ) = lax.optimization_barrier(
        (
            spread_rows,
            w_gate_t,
            w_up_t,
            w_down_t,
            ws_gate,
            ws_up,
            ws_down_t,
            conv_x,
            dt_bias,
            a_log,
            d_skip,
            gain_gate,
            segments,
            routes,
        )
    )
    mixer_whole = lax.all_to_all(spread_rows, ("row", "seq"), 0, 0).reshape(width, mixer_width)

    def expert_half(pick):
        parts = [
            pick(w_gate_t, 1)[:, 0],
            pick(w_up_t, 1)[:, 0],
            pick(ws_gate, 1),
            pick(ws_up, 1),
            w_router,
            jnp.zeros((w_router.shape[0], 128 - w_router.shape[1]), BF),
            pick(w_down_t, 1)[:, 0],
            pick(ws_down_t, 1),
        ]
        return jnp.concatenate(parts, 1)

    expert_rows = join(expert_half(own_half), swap(expert_half(other_half)), 0)
    expert_whole = lax.all_gather(expert_rows, "row", axis=0, tiled=True)
    down_units = hidden_units + shared_units
    in_units = 2 * down_units
    down_at = in_units + 128

    inv_mix = lax.rsqrt(jnp.mean(hidden * hidden, axis=1) + EPS)
    mix_own = (hidden * inv_mix[:, None] * gain_mix).astype(BF)
    mix_other = swap(mix_own)
    cot_other = swap(cotangent)
    named = jnp.max(
        jnp.where(
            routes[:, :, None] == jnp.arange(experts, dtype=jnp.int32)[None, None, :], 1.0, 0.0
        ),
        axis=1,
    )
    aside = jnp.concatenate([named, segments.astype(F32)[:, None]], 1).astype(BF)
    aside = jnp.concatenate([aside, swap(aside)], 0).astype(F32)
    named = aside[:, :experts]
    seg = aside[:, experts]
    place = (jnp.arange(tokens) + seq * half_tokens) % tokens
    hold = ((seg == jnp.roll(seg, 1)) & (place > 0)).astype(F32)
    kept_two = hold * jnp.roll(hold, 1)
    kept_three = kept_two * jnp.roll(hold, 2)
    blank = jnp.zeros_like(seg)
    marks_row = jnp.stack(
        [seg, place.astype(F32), hold, kept_two, kept_three, blank, blank, blank]
    )
    marks = marks_row.T
    taps_x = own_half(conv_x, 1)
    fill = jnp.zeros((lanes - heads,), F32)
    wide_head = lambda v: jnp.concatenate([own_half(v, 0), fill])
    head_rows = jnp.stack(
        [wide_head(dt_bias), jnp.concatenate([jnp.exp(own_half(a_log, 0)), fill])]
    )
    wide_rows = jnp.stack([jnp.repeat(own_half(d_skip, 0), head_width), own_half(gain_gate, 0)])

    fixed = (mixer_whole, marks, marks_row, taps_x, conv_bc, head_rows, wide_rows)
    pre, dt_in, cum, scanned, part_own, part_other, square, _ = call(
        functools.partial(mixer_forward, inner, head_width),
        [
            ((tokens, out_at), F32),
            ((tokens, lanes), F32),
            ((tokens, lanes), F32),
            ((tokens, inner), F32),
            ((half_tokens, width), BF),
            ((half_tokens, width), BF),
            ((tokens, 1), F32),
            ((tokens, inner), BF),
        ],
        (mix_own, mix_other, *fixed),
        4 * 10**9,
        "mixer_forward",
    )
    mix_sum, square = sum_to_tokens(part_own, part_other, square)

    here = lax.dynamic_slice_in_dim(hidden, col * shard, shard, 0)
    inv_gate_here = lax.rsqrt(square / inner_all + EPS)
    mix_out = mix_sum * inv_gate_here
    residual = here + mix_out
    inv_moe_here = lax.rsqrt(jnp.mean(residual * residual, axis=1, keepdims=True) + EPS)
    moe_here = (residual * inv_moe_here * gain_moe).astype(BF)
    moe_own = from_tokens(
        jnp.concatenate([moe_here, *two(inv_gate_here), *two(inv_moe_here)], 1)
    )
    inv_moe = one(moe_own[:, width + 2], moe_own[:, width + 3])
    moe_other = swap(moe_own)

    mine = (jnp.arange(experts) == 2 * col + seq).astype(F32)[None, :]
    in_own, in_other, out_own, out_other, in_grads, acts, gates, gates_grad = call(
        functools.partial(experts_both_ways, hidden_units, shared_units),
        [
            ((half_tokens, width), BF),
            ((half_tokens, width), BF),
            ((half_tokens, width), BF),
            ((half_tokens, width), BF),
            ((tokens, in_units), BF),
            ((tokens, down_units), BF),
            ((tokens, experts), F32),
            ((tokens, experts), F32),
        ],
        (moe_own, moe_other, cotangent, cot_other, expert_whole, named, mine),
        6 * 10**9,
        "experts_both_ways",
    )
    moe_in_sum, gates_grad = sum_to_tokens(in_own, in_other, gates_grad)
    (expert_sums,) = call(
        expert_products,
        [((width, in_units + down_units), BF)],
        (moe_own, moe_other, cotangent, cot_other, in_grads, acts),
        3 * 10**9,
        "expert_products",
    )
    moe_in_sum, expert_sums = lax.optimization_barrier((moe_in_sum, expert_sums))
    expert_sums = lax.psum_scatter(expert_sums, "row", scatter_dimension=0, tiled=True)

    gates_here = lax.dynamic_slice_in_dim(gates, col * shard, shard, 0)
    cot_here = lax.dynamic_slice_in_dim(cotangent, col * shard, shard, 0).astype(F32)
    logits_grad = (
        gates_here * (gates_grad - jnp.sum(gates_here * gates_grad, axis=1, keepdims=True))
    ).astype(BF)
    moe_in_grad = moe_in_sum + nt(logits_grad, expert_whole[:, in_units : in_units + experts])
    scaled_moe = moe_in_grad * gain_moe
    residual_grad = (
        cot_here
        + inv_moe_here * scaled_moe
        - residual
        * (inv_moe_here**3 * jnp.mean(scaled_moe * residual, axis=1, keepdims=True))
    )
    gain_moe_grad = jnp.sum(moe_in_grad * residual * inv_moe_here, axis=0)
    mix_grad_here = residual_grad.astype(BF)
    gate_dot = jnp.sum(mix_grad_here.astype(F32) * mix_out, axis=1, keepdims=True)
    grad_own = from_tokens(jnp.concatenate([mix_grad_here, logits_grad, *two(gate_dot)], 1))
    grad_other = swap(grad_own)

    output_here = residual + sum_to_tokens(after(out_own, grad_own), out_other)
    output = lax.all_gather(after(output_here, expert_sums), "col", axis=0, tiled=True)

    grads, dt_grad, normed_gate, part_own, part_other, small, *_ = call(
        functools.partial(mixer_backward, inner, inner_all, head_width),
        [
            ((tokens, out_at), BF),
            ((tokens, lanes), BF),
            ((tokens, inner), BF),
            ((half_tokens, width), BF),
            ((half_tokens, width), BF),
            ((8, mixer_width), F32),
            ((tokens, inner), BF),
            ((tokens, inner), BF),
            ((tokens, inner), F32),
            ((tokens, state), F32),
            ((tokens, state), F32),
        ],
        (grad_own, grad_other, moe_own, moe_other, *fixed, pre, dt_in, cum, scanned),
        5 * 10**9,
        "mixer_backward",
    )
    mix_in_grad = sum_to_tokens(part_own, part_other)
    (mixer_sums,) = call(
        functools.partial(mixer_products, inner),
        [((2 * rows, w_z.shape[0] + 16, mixer_width), BF)],
        (
            mix_own,
            mix_other,
            grad_own,
            grad_other,
            moe_own,
            moe_other,
            grads,
            dt_grad,
            normed_gate,
        ),
        2 * 10**9,
        "mixer_products",
    )
    mix_in_grad, mixer_sums = lax.optimization_barrier((mix_in_grad, mixer_sums))

    inv_here = lax.dynamic_slice_in_dim(inv_mix, col * shard, shard, 0)[:, None]
    scaled_mix = mix_in_grad * gain_mix
    grad_hidden_here = (
        residual_grad
        + inv_here * scaled_mix
        - here * (inv_here**3 * jnp.mean(scaled_mix * here, axis=1, keepdims=True))
    )
    gain_mix_grad = jnp.sum(mix_in_grad * here * inv_here, axis=0)

    gains = jnp.concatenate([gain_mix_grad, gain_moe_grad]).reshape(4, width // 2)
    small = small + jnp.pad(gains, ((0, 4), (0, mixer_width - width // 2)))
    small = jnp.concatenate(two(small), 0)
    mixer_sums = lax.dynamic_update_slice(
        mixer_sums,
        jnp.broadcast_to(small[None], (2 * rows, *small.shape)),
        (0, w_z.shape[0], 0),
    )
    got = lax.all_to_all(mixer_sums, ("row", "seq"), 0, 0)
    grad_hidden = from_tokens(grad_hidden_here.astype(BF))
    got, grad_hidden = lax.optimization_barrier((got, grad_hidden))
    grad_hidden = grad_hidden.astype(F32)
    weight_rows = w_z.shape[0]
    (
        g_out_t,
        g_w_z,
        g_w_x,
        g_w_dt,
        g_w_router,
        g_conv_x,
        g_gain_gate,
        by_heads,
        sent,
    ) = call(
        functools.partial(tail_sums, inner, heads),
        [
            ((weight_rows, 2 * inner), F32),
            ((weight_rows, 2 * inner), F32),
            ((weight_rows, 2 * inner), F32),
            ((weight_rows, 2 * heads), F32),
            ((weight_rows, experts), F32),
            ((4, 2 * inner), F32),
            ((1, 2 * inner), F32),
            ((3, 2 * heads), F32),
            ((weight_rows + 32, 2 * state), BF),
        ],
        (got,),
        10**7,
        "tail_sums",
    )
    g_gain_gate = g_gain_gate.reshape(-1)
    g_dt_bias, g_a_log, g_d_skip = by_heads[0], by_heads[1], by_heads[2]
    got = lax.all_to_all(jnp.broadcast_to(sent[None], (cols, *sent.shape)), "col", 0, 0)
    g_w_bc, g_gain_mix, g_gain_moe, g_conv_bc = call(
        last_sums,
        [
            ((weight_rows, 2 * state), F32),
            ((1, width), F32),
            ((1, width), F32),
            ((4, 2 * state), F32),
        ],
        (got,),
        10**6,
        "last_sums",
    )
    g_gain_mix, g_gain_moe = g_gain_mix.reshape(-1), g_gain_moe.reshape(-1)

    own = own_half(expert_sums, 0)
    other = swap(other_half(expert_sums, 0))

    def expert(at):
        a = own[:, None, at : at + hidden_units]
        return join(a, other[:, None, at : at + hidden_units], 1).astype(F32)

    def shared(at):
        return join(
            own[:, at : at + shared_units], other[:, at : at + shared_units], 1
        ).astype(F32)

    g_w_gate_t = expert(0)
    g_w_up_t = expert(hidden_units)
    g_w_down_t = expert(in_units)
    g_ws_gate = shared(2 * hidden_units)
    g_ws_up = shared(2 * hidden_units + shared_units)
    g_ws_down_t = shared(in_units + hidden_units)
    return (
        output,
        grad_hidden,
        inv_mix,
        inv_moe,
        g_gain_mix,
        g_w_z,
        g_w_x,
        g_w_bc,
        g_w_dt,
        g_conv_x,
        g_conv_bc,
        g_dt_bias,
        g_a_log,
        g_d_skip,
        g_gain_gate,
        g_out_t,
        g_gain_moe,
        g_w_router,
        g_w_gate_t,
        g_w_up_t,
        g_w_down_t,
        g_ws_gate,
        g_ws_up,
        g_ws_down_t,
    )


def solution(mesh):
    placed = (
        P(("row", "seq"), None),
        P(("row", "seq"), None),
        P(("row", "seq")),
        P(("row", "seq"), None),
        P(),
        P(("row", "seq"), "col"),
        P(("row", "seq"), "col"),
        P(("row", "seq"), None),
        P(("row", "seq"), "col"),
        P(None, "col"),
        P(),
        P("col"),
        P("col"),
        P("col"),
        P("col"),
        P(("row", "seq"), "col"),
        P(),
        P(("row", "seq"), None),
        P(("row", "seq"), "col", None),
        P(("row", "seq"), "col", None),
        P(("row", "seq"), "col", None),
        P(("row", "seq"), "col"),
        P(("row", "seq"), "col"),
        P(("row", "seq"), "col"),
    )
    return jax.shard_map(
        on_device,
        mesh=mesh,
        in_specs=placed,
        out_specs=(
            P(("row", "seq"), None),
            P(("row", "seq"), None),
            P(("row", "seq")),
            P(("row", "seq")),
            P(),
            P(("row", "seq"), "col"),
            P(("row", "seq"), "col"),
            P(("row", "seq"), None),
            P(("row", "seq"), "col"),
            P(None, "col"),
            P(),
            P("col"),
            P("col"),
            P("col"),
            P("col"),
            P(("row", "seq"), "col"),
            P(),
            P(("row", "seq"), None),
            P(("row", "seq"), "col", None),
            P(("row", "seq"), "col", None),
            P(("row", "seq"), "col", None),
            P(("row", "seq"), "col"),
            P(("row", "seq"), "col"),
            P(("row", "seq"), "col"),
        ),
        check_vma=False,
    )
```

```python
import functools

import jax
import jax.numpy as jnp
from jax import lax
from jax.experimental import pallas as pl
from jax.experimental.pallas import tpu as pltpu
from jax.sharding import PartitionSpec as P

EPS = 1e-05
BF = jnp.bfloat16
F32 = jnp.float32
FAR = -1e30
TAPS_BC_ROW, TAPS_X_ROW, GATE_ROW, HEAD_ROW, SMALL_ROWS = 24, 32, 40, 42, 48


def silu(v):
    return v * jax.nn.sigmoid(v)


def nn(left, right):
    return lax.dot_general(left, right, (((1,), (0,)), ((), ())), preferred_element_type=F32)


def nt(left, right):
    return lax.dot_general(left, right, (((1,), (1,)), ((), ())), preferred_element_type=F32)


def tn(left, right):
    return lax.dot_general(left, right, (((0,), (0,)), ((), ())), preferred_element_type=F32)


def swap(value):
    return lax.ppermute(value, "seq", [(0, 1), (1, 0)])


def half(value, axis, which):
    size = value.shape[axis] // 2
    return lax.slice_in_dim(value, which * size, (which + 1) * size, axis=axis)


def own_half(value, axis):
    first = lax.axis_index("seq") == 0
    return jnp.where(first, half(value, axis, 0), half(value, axis, 1))


def other_half(value, axis):
    first = lax.axis_index("seq") == 0
    return jnp.where(first, half(value, axis, 1), half(value, axis, 0))


def join(own, other, axis):
    first = lax.axis_index("seq") == 0
    return jnp.where(
        first, jnp.concatenate([own, other], axis), jnp.concatenate([other, own], axis)
    )


def low(value):
    return lax.reduce_precision(value, 8, 7)


def two(value):
    high = low(value)
    return high.astype(BF), (value - high).astype(BF)


def three(value):
    high = value.astype(BF)
    rest = value - high.astype(F32)
    middle = rest.astype(BF)
    return high, middle, (rest - middle.astype(F32)).astype(BF)


def exact(left, value):
    high, middle, last = three(value)
    return (nn(left, last) + nn(left, middle)) + nn(left, high)


def one(high, low_term):
    return high.astype(F32) + low_term.astype(F32)


def after(value, *others):
    return lax.optimization_barrier((value, *others))[0]


def call(kernel, outs, args, flops, name, room=12, scratch=()):
    whole = pl.BlockSpec(memory_space=pltpu.VMEM)
    shapes = [jax.ShapeDtypeStruct(shape, kind) for shape, kind in outs]
    size = lambda a: a.size * jnp.dtype(a.dtype).itemsize
    return pl.pallas_call(
        kernel,
        out_shape=shapes,
        in_specs=[whole] * len(args),
        out_specs=[whole] * len(outs),
        scratch_shapes=[pltpu.VMEM(shape, kind) for shape, kind in scratch],
        compiler_params=pltpu.CompilerParams(vmem_limit_bytes=room * 2**20),
        cost_estimate=pl.CostEstimate(
            flops=flops,
            bytes_accessed=sum(size(a) for a in args) + sum(size(a) for a in shapes),
            transcendentals=0,
        ),
        name=name,
    )(*args)


def causal(marks, marks_row, rows):
    return (marks[rows, 1:2] >= marks_row[1:2, :]) & (marks[rows, 0:1] == marks_row[0:1, :])


def convolved(value, taps, marks):
    total = taps[3:4, :] * value
    for lag in range(1, 4):
        rolled = pltpu.roll(value, lag, 0) * marks[:, 1 + lag : 2 + lag]
        total = total + taps[3 - lag : 4 - lag, :] * rolled
    return total


def head_columns(inner, lanes, head_width):
    down = lax.broadcasted_iota(jnp.int32, (inner, lanes), 0)
    across = lax.broadcasted_iota(jnp.int32, (inner, lanes), 1) * head_width
    return jnp.where((down >= across) & (down < across + head_width), 1.0, 0.0).astype(BF)


def by_head(value, columns):
    high, middle, last = three(value)
    return (nn(last, columns) + nn(middle, columns)) + nn(high, columns)


def softplus(v):
    return jnp.maximum(v, 0.0) + jnp.log1p(jnp.exp(-jnp.abs(v)))


def mixer_forward(
    inner,
    head_width,
    own_ref,
    other_ref,
    w_ref,
    marks_ref,
    row_ref,
    taps_x_ref,
    taps_bc_ref,
    head_ref,
    wide_ref,
    pre_ref,
    dt_ref,
    cum_ref,
    scanned_ref,
    part_own_ref,
    part_other_ref,
    square_own_ref,
    square_other_ref,
    scaled_ref,
):
    half_tokens, width = own_ref.shape
    tokens = 2 * half_tokens
    heads = inner // head_width
    bc_at, out_at, dt_at = 2 * inner, pre_ref.shape[1], pre_ref.shape[1] + inner
    state = (out_at - bc_at) // 2
    for part, src in ((0, own_ref), (1, other_ref)):
        rows = slice(part * half_tokens, (part + 1) * half_tokens)
        pre_ref[rows, :] = nn(src[...], w_ref[:, :out_at])
        dt_ref[rows, :] = nn(src[...], w_ref[:, dt_at:]) + head_ref[0:1, :]
    marks, marks_row = marks_ref[...], row_ref[...]
    x_conv = silu(convolved(pre_ref[:, :inner], taps_x_ref[...], marks))
    bc = silu(convolved(pre_ref[:, bc_at:out_at], taps_bc_ref[...], marks)).astype(BF)
    b_map, c_map = bc[:, :state], bc[:, state:]
    step = softplus(dt_ref[...])
    lower = jnp.where(marks[:, 1:2] >= marks_row[1:2, :], 1.0, 0.0).astype(BF)
    cum = exact(lower, -step * head_ref[1:2, :])
    cum_ref[...] = cum
    cum_row = jnp.concatenate([cum, jnp.zeros_like(cum)], 1).T
    for h in range(heads):
        here = slice(h * head_width, (h + 1) * head_width)
        scaled_ref[:, here] = (x_conv[:, here] * step[:, h : h + 1]).astype(BF)
    block = 128
    for at in range(0, tokens, block):
        rows = slice(at, at + block)
        scores = nt(c_map[rows, :], b_map)
        mask = causal(marks, marks_row, rows)
        for h in range(heads):
            here = slice(h * head_width, (h + 1) * head_width)
            gap = cum[rows, h : h + 1] - cum_row[h : h + 1, :]
            mix = (jnp.exp(jnp.where(mask, gap, FAR)) * scores).astype(BF)
            scanned_ref[rows, here] = nn(mix, scaled_ref[:, here])
    mixer_out = scanned_ref[...] + wide_ref[0:1, :] * x_conv
    gated = mixer_out * silu(pre_ref[:, inner:bc_at])
    square = jnp.sum(gated * gated, axis=1, keepdims=True)
    square_own_ref[...] = square[:half_tokens]
    square_other_ref[...] = square[half_tokens:]
    sent = (gated * wide_ref[1:2, :]).astype(BF)
    out_w = w_ref[:, out_at:dt_at]
    part_own_ref[...] = nt(sent[:half_tokens], out_w).astype(BF)
    part_other_ref[...] = nt(sent[half_tokens:], out_w).astype(BF)


def mixer_backward(
    inner,
    inner_all,
    head_width,
    experts,
    own_ref,
    other_ref,
    moe_own_ref,
    moe_other_ref,
    w_ref,
    marks_ref,
    row_ref,
    taps_x_ref,
    taps_bc_ref,
    head_ref,
    wide_ref,
    pre_ref,
    dt_ref,
    cum_ref,
    scanned_ref,
    grads_ref,
    dt_grad_ref,
    normed_ref,
    part_own_ref,
    part_other_ref,
    small_ref,
    scaled_ref,
    low_ref,
    spread_ref,
    c_grad_ref,
    b_grad_ref,
):
    half_tokens = own_ref.shape[0]
    width = w_ref.shape[0]
    tokens = 2 * half_tokens
    heads = inner // head_width
    bc_at, out_at, dt_at = 2 * inner, pre_ref.shape[1], pre_ref.shape[1] + inner
    state = (out_at - bc_at) // 2
    marks, marks_row = marks_ref[...], row_ref[...]
    stack = lambda a, b: jnp.concatenate([a, b], 0)
    conv_x = convolved(pre_ref[:, :inner], taps_x_ref[...], marks)
    conv_bc = convolved(pre_ref[:, bc_at:out_at], taps_bc_ref[...], marks)
    x_conv = silu(conv_x)
    bc = silu(conv_bc).astype(BF)
    b_map, c_map = bc[:, :state], bc[:, state:]
    z_pre = pre_ref[:, inner:bc_at]
    step = softplus(dt_ref[...])
    rate = head_ref[1:2, :]
    skip_wide, gain = wide_ref[0:1, :], wide_ref[1:2, :]
    out_w = w_ref[:, out_at:dt_at]
    gate_norm_grad = stack(
        nn(own_ref[:, :width], out_w), nn(other_ref[:, :width], out_w)
    )
    at = width + experts
    dots = lambda ref: one(ref[:, at : at + 1], ref[:, at + 1 : at + 2])
    gate_dot = stack(dots(own_ref), dots(other_ref))
    gates = lambda ref: one(ref[:, width : width + 1], ref[:, width + 1 : width + 2])
    inv_gate = stack(gates(moe_own_ref), gates(moe_other_ref))
    sig = jax.nn.sigmoid(z_pre)
    silu_z = z_pre * sig
    mixer_out = scanned_ref[...] + skip_wide * x_conv
    gated = mixer_out * silu_z
    normed = gated * inv_gate
    small_ref[...] = jnp.zeros_like(small_ref)

    def keep_small(row, value):
        for at in range(0, value.shape[1], 128):
            piece = value[:, at : at + 128]
            small_ref[row : row + 1, : piece.shape[1]] = piece
            row = row + 1

    keep_small(GATE_ROW, jnp.sum(gate_norm_grad * normed, axis=0, keepdims=True))
    normed_ref[...] = (normed * gain).astype(BF)
    gated_grad = inv_gate * (gate_norm_grad * gain) - gated * (
        inv_gate * inv_gate * gate_dot * (1.0 / inner_all)
    )
    ssm_grad = gated_grad * silu_z
    grads_ref[:, inner:bc_at] = (
        gated_grad * mixer_out * (sig * (1.0 + z_pre * (1.0 - sig)))
    ).astype(BF)
    columns = head_columns(inner, dt_ref.shape[1], head_width)
    skips = by_head(
        jnp.broadcast_to(jnp.sum(ssm_grad * x_conv, axis=0, keepdims=True), (8, inner)), columns
    )
    keep_small(HEAD_ROW + 2, skips[0:1, :heads])
    low_ref[...] = ssm_grad.astype(BF)
    for h in range(heads):
        here = slice(h * head_width, (h + 1) * head_width)
        scaled_ref[:, here] = (x_conv[:, here] * step[:, h : h + 1]).astype(BF)
    cum = cum_ref[...]
    cum_row = jnp.concatenate([cum, jnp.zeros_like(cum)], 1).T
    c_grad_ref[...] = jnp.zeros_like(c_grad_ref)
    block = 128
    for start in range(0, tokens, block):
        rows = slice(start, start + block)
        scores = nt(b_map[rows, :], c_map)
        mask = (marks_row[1:2, :] >= marks[rows, 1:2]) & (
            marks_row[0:1, :] == marks[rows, 0:1]
        )
        scores_grad = jnp.zeros((block, tokens), F32)
        for h in range(heads):
            here = slice(h * head_width, (h + 1) * head_width)
            gap = cum_row[h : h + 1, :] - cum[rows, h : h + 1]
            decay = jnp.exp(jnp.where(mask, gap, FAR))
            spread_ref[rows, here] = nn((decay * scores).astype(BF), low_ref[:, here])
            scores_grad = scores_grad + decay * nt(scaled_ref[rows, here], low_ref[:, here])
        scores_low = scores_grad.astype(BF)
        b_grad_ref[rows, :] = nn(scores_low, c_map)
        c_grad_ref[...] += tn(scores_low, b_map[rows, :])
    spread = spread_ref[...]
    step_grad = by_head(x_conv * spread, columns)
    cum_grad = by_head(
        low_ref[...].astype(F32) * scanned_ref[...] - scaled_ref[...].astype(F32) * spread, columns
    )
    upper = jnp.where(marks_row[1:2, :] >= marks[:, 1:2], 1.0, 0.0).astype(BF)
    decay_grad = exact(upper, cum_grad)
    dt_float = (step_grad - decay_grad * rate) * jax.nn.sigmoid(dt_ref[...])
    keep_small(HEAD_ROW, jnp.sum(dt_float, axis=0, keepdims=True)[:, :heads])
    keep_small(
        HEAD_ROW + 1, jnp.sum(decay_grad * (-step * rate), axis=0, keepdims=True)[:, :heads]
    )
    dt_low = dt_float.astype(BF)
    dt_grad_ref[...] = dt_low
    for h in range(heads):
        here = slice(h * head_width, (h + 1) * head_width)
        spread_ref[:, here] = spread[:, here] * step[:, h : h + 1]

    def back(value_grad, total, value, taps, small_row, to):
        sig_c = jax.nn.sigmoid(total)
        grad = value_grad * (sig_c * (1.0 + total * (1.0 - sig_c)))
        keep_small(small_row + 6, jnp.sum(grad * value, axis=0, keepdims=True))
        result = taps[3:4, :] * grad
        for lag in range(1, 4):
            kept = grad * marks[:, 1 + lag : 2 + lag]
            keep_small(
                small_row + 2 * (3 - lag),
                jnp.sum(kept * pltpu.roll(value, lag, 0), axis=0, keepdims=True),
            )
            result = result + taps[3 - lag : 4 - lag, :] * pltpu.roll(kept, tokens - lag, 0)
        grads_ref[:, to] = result.astype(BF)

    back(
        spread_ref[...] + ssm_grad * skip_wide,
        conv_x,
        pre_ref[:, :inner],
        taps_x_ref[...],
        TAPS_X_ROW,
        slice(0, inner),
    )
    back(
        jnp.concatenate([b_grad_ref[...], c_grad_ref[...]], 1),
        conv_bc,
        pre_ref[:, bc_at:out_at],
        taps_bc_ref[...],
        TAPS_BC_ROW,
        slice(bc_at, out_at),
    )
    for part, dst in ((0, part_own_ref), (1, part_other_ref)):
        rows = slice(part * half_tokens, (part + 1) * half_tokens)
        dst[...] = (
            nt(grads_ref[rows, :], w_ref[:, :out_at]) + nt(dt_low[rows, :], w_ref[:, dt_at:])
        ).astype(BF)


def mixer_products(
    inner,
    experts,
    own_ref,
    other_ref,
    mix_own_ref,
    mix_other_ref,
    moe_own_ref,
    moe_other_ref,
    grads_ref,
    dt_grad_ref,
    normed_ref,
    sums_ref,
):
    half_tokens, width = own_ref.shape
    out_at = grads_ref.shape[1]
    dt_at = out_at + inner
    count = sums_ref.shape[0]
    rows = width // count
    group = min(8, count)
    first, second = slice(0, half_tokens), slice(half_tokens, 2 * half_tokens)
    logits = slice(width, width + experts)
    for at in range(0, count, group):
        here = slice(at * rows, (at + group) * rows)
        mine, others = own_ref[:, here], other_ref[:, here]
        a = tn(mine, grads_ref[first, :]) + tn(others, grads_ref[second, :])
        b = tn(mix_own_ref[:, here], normed_ref[first, :]) + tn(
            mix_other_ref[:, here], normed_ref[second, :]
        )
        c = tn(mine, dt_grad_ref[first, :]) + tn(others, dt_grad_ref[second, :])
        d = tn(moe_own_ref[:, here], mix_own_ref[:, logits]) + tn(
            moe_other_ref[:, here], mix_other_ref[:, logits]
        )
        a, b, c, d = a.astype(BF), b.astype(BF), c.astype(BF), d.astype(BF)
        for k in range(group):
            part = slice(k * rows, (k + 1) * rows)
            sums_ref[at + k, :, :out_at] = a[part]
            sums_ref[at + k, :, out_at:dt_at] = b[part]
            sums_ref[at + k, :, dt_at : dt_at + 64] = c[part]
            sums_ref[at + k, :, dt_at + 16 : dt_at + 16 + experts] = d[part]
            sums_ref[at + k, :, dt_at + 64 :] = jnp.zeros((rows, 128), BF)


def experts_both_ways(
    units,
    shared,
    own_ref,
    other_ref,
    cot_own_ref,
    cot_other_ref,
    w_ref,
    named_ref,
    mine_ref,
    in_own_ref,
    in_other_ref,
    out_own_ref,
    out_other_ref,
    grads_ref,
    acts_ref,
    gates_ref,
    gates_grad_own_ref,
    gates_grad_other_ref,
):
    half_tokens = own_ref.shape[0]
    width = w_ref.shape[0]
    experts = named_ref.shape[1]
    in_units = 2 * (units + shared)
    down_at = in_units + 128
    mine = mine_ref[...]
    parts = (
        (own_ref, cot_own_ref, in_own_ref, out_own_ref, gates_grad_own_ref),
        (other_ref, cot_other_ref, in_other_ref, out_other_ref, gates_grad_other_ref),
    )
    for part, (src, cot, in_dst, out_dst, gates_dst) in enumerate(parts):
        rows = slice(part * half_tokens, (part + 1) * half_tokens)
        pre = nn(src[:, :width], w_ref[:, :down_at])
        back = nn(cot[...], w_ref[:, down_at:])
        logits = jnp.where(named_ref[rows, :] > 0.0, pre[:, in_units : in_units + experts], FAR)
        raised = jnp.exp(logits - jnp.max(logits, axis=1, keepdims=True))
        gates = raised / jnp.sum(raised, axis=1, keepdims=True)
        gates_ref[rows, :] = gates
        weight = jnp.sum(gates * mine, axis=1, keepdims=True)
        gate, up = pre[:, :units], pre[:, units : 2 * units]
        sig = jax.nn.sigmoid(gate)
        silu_gate = gate * sig
        act = silu_gate * up
        acts_ref[rows, :units] = (act * weight).astype(BF)
        act_back = back[:, :units]
        gates_dst[...] = jnp.sum(act * act_back, axis=1, keepdims=True) * mine
        act_grad = act_back * weight
        grads_ref[rows, :units] = (
            act_grad * up * (sig * (1.0 + gate * (1.0 - sig)))
        ).astype(BF)
        grads_ref[rows, units : 2 * units] = (act_grad * silu_gate).astype(BF)
        gate, up = pre[:, 2 * units : 2 * units + shared], pre[:, 2 * units + shared : in_units]
        sig = jax.nn.sigmoid(gate)
        silu_gate = gate * sig
        acts_ref[rows, units:] = (silu_gate * up).astype(BF)
        act_grad = back[:, units:]
        grads_ref[rows, 2 * units : 2 * units + shared] = (
            act_grad * up * (sig * (1.0 + gate * (1.0 - sig)))
        ).astype(BF)
        grads_ref[rows, 2 * units + shared :] = (act_grad * silu_gate).astype(BF)
        in_dst[...] = nt(grads_ref[rows, :], w_ref[:, :in_units]).astype(BF)
        out_dst[...] = nt(acts_ref[rows, :], w_ref[:, down_at:]).astype(BF)


def expert_products(
    own_ref, other_ref, cot_own_ref, cot_other_ref, grads_ref, acts_ref, sums_ref
):
    half_tokens, width = cot_own_ref.shape
    split = grads_ref.shape[1]
    first, second = slice(0, half_tokens), slice(half_tokens, 2 * half_tokens)
    block = 256
    for at in range(0, width, block):
        here = slice(at, at + block)
        sums_ref[here, :split] = (
            tn(own_ref[:, here], grads_ref[first, :]) + tn(other_ref[:, here], grads_ref[second, :])
        ).astype(BF)
        sums_ref[here, split:] = (
            tn(cot_own_ref[:, here], acts_ref[first, :])
            + tn(cot_other_ref[:, here], acts_ref[second, :])
        ).astype(BF)


def tail_sums(
    inner,
    heads,
    got_ref,
    out_ref,
    z_ref,
    x_ref,
    dt_ref,
    router_ref,
    conv_ref,
    gain_ref,
    head_ref,
    sent_ref,
):
    count, rows = got_ref.shape[0], out_ref.shape[0]
    experts = router_ref.shape[1]
    bc_at = 2 * inner
    small_at = got_ref.shape[2] - 128
    dt_at = small_at - 64
    out_at = dt_at - inner
    totals = []
    for core in range(2):
        total = got_ref[core].astype(F32)
        for at in range(core + 2, count, 2):
            total = total + got_ref[at].astype(F32)
        totals.append(total)
        here = slice(core * inner, (core + 1) * inner)
        x_ref[:, here] = total[:, :inner]
        z_ref[:, here] = total[:, inner:bc_at]
        out_ref[:, here] = total[:, out_at:dt_at]
        dt_ref[:, core * heads : (core + 1) * heads] = total[:, dt_at : dt_at + heads]
        small = total[:SMALL_ROWS, small_at:]

        def row_of(at):
            return jnp.concatenate([small[at : at + 1], small[at + 1 : at + 2, : inner - 128]], 1)

        for k in range(conv_ref.shape[0]):
            conv_ref[k : k + 1, here] = row_of(TAPS_X_ROW + 2 * k)
        gain_ref[:, here] = row_of(GATE_ROW)
        for k in range(3):
            head_ref[k : k + 1, core * heads : (core + 1) * heads] = small[
                HEAD_ROW + k : HEAD_ROW + k + 1, :heads
            ]
    router_ref[...] = totals[0][:, dt_at + 16 : dt_at + 16 + experts]
    sent_ref[:rows, :] = (totals[0][:, bc_at:out_at] + totals[1][:, bc_at:out_at]).astype(BF)
    small = totals[0][:TAPS_X_ROW, small_at:] + totals[1][:TAPS_X_ROW, small_at:]
    high = small.astype(BF)
    sent_ref[rows:, :128] = high
    sent_ref[rows:, 128:] = (small - high.astype(F32)).astype(BF)


def last_sums(got_ref, bc_ref, mix_ref, moe_ref, conv_ref):
    rows = bc_ref.shape[0]
    total = got_ref[0].astype(F32)
    for at in range(1, got_ref.shape[0]):
        total = total + got_ref[at].astype(F32)
    bc_ref[...] = total[:rows]
    small = total[rows:, :128] + total[rows:, 128:]
    half_rows = TAPS_BC_ROW // 2
    mix_ref[...] = small[:half_rows]
    moe_ref[...] = small[half_rows:TAPS_BC_ROW]
    for k in range(conv_ref.shape[0]):
        for part in range(2):
            at = TAPS_BC_ROW + 2 * k + part
            conv_ref[k : k + 1, part * 128 : (part + 1) * 128] = small[at : at + 1]


def chip_sum(own_ref, other_ref, extra_own_ref, extra_other_ref, sum_ref):
    width, more = own_ref.shape[1], extra_own_ref.shape[1]
    sum_ref[:, :width] = (own_ref[...].astype(F32) + other_ref[...].astype(F32)).astype(BF)
    extra = extra_own_ref[...] + extra_other_ref[...]
    high = extra.astype(BF)
    sum_ref[:, width:] = jnp.zeros((own_ref.shape[0], sum_ref.shape[1] - width), BF)
    sum_ref[:, width : width + more] = high
    sum_ref[:, width + more : width + 2 * more] = (extra - high.astype(F32)).astype(BF)


def second_shard(
    got_ref,
    residual_ref,
    mix_out_ref,
    cot_ref,
    gates_ref,
    router_ref,
    inv_ref,
    gain_ref,
    sent_ref,
    grad_ref,
    gain_grad_ref,
):
    width, experts = residual_ref.shape[1], gates_ref.shape[1]
    total = got_ref[0].astype(F32)
    for at in range(1, got_ref.shape[0]):
        total = total + got_ref[at].astype(F32)
    gates = gates_ref[...]
    gates_grad = total[:, width : width + experts] + total[:, width + experts : width + 2 * experts]
    logits_grad = (
        gates * (gates_grad - jnp.sum(gates * gates_grad, axis=1, keepdims=True))
    ).astype(BF)
    moe_in_grad = total[:, :width] + nt(logits_grad, router_ref[...])
    residual, inv = residual_ref[...], inv_ref[...]
    scaled = moe_in_grad * gain_ref[...]
    mean = jnp.sum(scaled * residual, axis=1, keepdims=True) * (1.0 / width)
    grad = cot_ref[...].astype(F32) + inv * scaled - residual * (inv * inv * inv * mean)
    grad_ref[...] = grad
    gain_grad_ref[...] = jnp.sum(moe_in_grad * residual * inv, axis=0, keepdims=True)
    grad_low = grad.astype(BF)
    gate_dot = jnp.sum(grad_low.astype(F32) * mix_out_ref[...], axis=1, keepdims=True)
    high = gate_dot.astype(BF)
    sent_ref[:, :width] = grad_low
    sent_ref[:, width:] = jnp.zeros((residual.shape[0], sent_ref.shape[1] - width), BF)
    sent_ref[:, width : width + experts] = logits_grad
    sent_ref[:, width + experts : width + experts + 1] = high
    sent_ref[:, width + experts + 1 : width + experts + 2] = (
        gate_dot - high.astype(F32)
    ).astype(BF)


def mixer_rows(inner, heads, x_ref, z_ref, bc_ref, out_ref, dt_ref, rows_ref):
    bc_at, state = 2 * inner, bc_ref.shape[1]
    out_at = bc_at + state
    dt_at = out_at + inner
    for core in range(2):
        here = slice(core * inner, (core + 1) * inner)
        parts = (
            (0, x_ref[:, here]),
            (inner, z_ref[:, here]),
            (bc_at, bc_ref[...]),
            (out_at, out_ref[:, here]),
            (dt_at, jnp.zeros((x_ref.shape[0], rows_ref.shape[2] - dt_at), BF)),
            (dt_at, dt_ref[:, core * heads : (core + 1) * heads]),
        )
        for at, value in parts:
            rows_ref[core, :, at : at + value.shape[1]] = value
        for at in range(core + 2, rows_ref.shape[0], 2):
            rows_ref[at] = rows_ref[core]


def exchange_rows(part, axis):
    count = lax.axis_size(axis)
    blocks = part.reshape(count, part.shape[0] // count, part.shape[1])
    return lax.all_to_all(blocks, axis, 0, 0, tiled=False)


def chip(own, other, extra_own, extra_other):
    rows, width = own.shape
    extra = call(
        chip_sum,
        [((rows, width + 128), BF)],
        (own, swap(other), extra_own, swap(extra_other)),
        10**6,
        "chip_sum",
    )
    return extra[0]


def from_tokens(own):
    return lax.all_gather(own, "col", axis=0, tiled=True)


def on_device(
    hidden,
    cotangent,
    segments,
    routes,
    gain_mix,
    w_z,
    w_x,
    w_bc,
    w_dt,
    conv_x,
    conv_bc,
    dt_bias,
    a_log,
    d_skip,
    gain_gate,
    out_t,
    gain_moe,
    w_router,
    w_gate_t,
    w_up_t,
    w_down_t,
    ws_gate,
    ws_up,
    ws_down_t,
):
    half_tokens, width = hidden.shape
    rows = lax.axis_size("row")
    cols = lax.axis_size("col")
    seq = lax.axis_index("seq")
    col = lax.axis_index("col")
    tokens = 2 * half_tokens
    inner = conv_x.shape[1] // 2
    heads = dt_bias.shape[0] // 2
    head_width = inner // heads
    state = conv_bc.shape[1] // 2
    experts = w_router.shape[1]
    hidden_units = w_gate_t.shape[2]
    shared_units = ws_gate.shape[1] // 2
    lanes = 64
    inner_all = conv_x.shape[1] * cols
    shard = half_tokens // cols

    out_at = 2 * inner + 2 * state
    dt_at = out_at + inner
    mixer_width = dt_at + lanes
    (spread_rows,) = call(
        functools.partial(mixer_rows, inner, heads),
        [((2 * rows, w_z.shape[0], mixer_width), BF)],
        (w_x, w_z, w_bc, out_t, w_dt),
        10**6,
        "mixer_rows",
        12,
    )
    (
        spread_rows,
        w_gate_t,
        w_up_t,
        w_down_t,
        ws_gate,
        ws_up,
        ws_down_t,
        conv_x,
        dt_bias,
        a_log,
        d_skip,
        gain_gate,
        segments,
        routes,
    ) = lax.optimization_barrier(
        (
            spread_rows,
            w_gate_t,
            w_up_t,
            w_down_t,
            ws_gate,
            ws_up,
            ws_down_t,
            conv_x,
            dt_bias,
            a_log,
            d_skip,
            gain_gate,
            segments,
            routes,
        )
    )
    mixer_whole = lax.all_to_all(spread_rows, ("row", "seq"), 0, 0).reshape(width, mixer_width)

    def expert_half(pick):
        parts = [
            pick(w_gate_t, 1)[:, 0],
            pick(w_up_t, 1)[:, 0],
            pick(ws_gate, 1),
            pick(ws_up, 1),
            w_router,
            jnp.zeros((w_router.shape[0], 128 - w_router.shape[1]), BF),
            pick(w_down_t, 1)[:, 0],
            pick(ws_down_t, 1),
        ]
        return jnp.concatenate(parts, 1)

    expert_rows = join(expert_half(own_half), swap(expert_half(other_half)), 0)
    expert_rows = after(expert_rows, mixer_whole)
    expert_whole = lax.all_gather(expert_rows, "row", axis=0, tiled=True)
    down_units = hidden_units + shared_units
    in_units = 2 * down_units
    down_at = in_units + 128

    inv_mix = lax.rsqrt(jnp.mean(hidden * hidden, axis=1) + EPS)
    mix_own = (hidden * inv_mix[:, None] * gain_mix).astype(BF)
    mix_other = swap(mix_own)
    cot_other = swap(cotangent)
    named = jnp.max(
        jnp.where(
            routes[:, :, None] == jnp.arange(experts, dtype=jnp.int32)[None, None, :], 1.0, 0.0
        ),
        axis=1,
    )
    aside = jnp.concatenate([named, segments.astype(F32)[:, None]], 1).astype(BF)
    aside = jnp.concatenate([aside, swap(aside)], 0).astype(F32)
    named = aside[:, :experts]
    seg = aside[:, experts]
    place = (jnp.arange(tokens) + seq * half_tokens) % tokens
    hold = ((seg == jnp.roll(seg, 1)) & (place > 0)).astype(F32)
    kept_two = hold * jnp.roll(hold, 1)
    kept_three = kept_two * jnp.roll(hold, 2)
    blank = jnp.zeros_like(seg)
    marks_row = jnp.stack(
        [seg, place.astype(F32), hold, kept_two, kept_three, blank, blank, blank]
    )
    marks = marks_row.T
    taps_x = own_half(conv_x, 1)
    fill = jnp.zeros((lanes - heads,), F32)
    wide_head = lambda v: jnp.concatenate([own_half(v, 0), fill])
    head_rows = jnp.stack(
        [wide_head(dt_bias), jnp.concatenate([jnp.exp(own_half(a_log, 0)), fill])]
    )
    wide_rows = jnp.stack([jnp.repeat(own_half(d_skip, 0), head_width), own_half(gain_gate, 0)])

    fixed = (mixer_whole, marks, marks_row, taps_x, conv_bc, head_rows, wide_rows)
    pre, dt_in, cum, scanned, part_own, part_other, square_own, square_other = call(
        functools.partial(mixer_forward, inner, head_width),
        [
            ((tokens, out_at), F32),
            ((tokens, lanes), F32),
            ((tokens, lanes), F32),
            ((tokens, inner), F32),
            ((half_tokens, width), BF),
            ((half_tokens, width), BF),
            ((half_tokens, 1), F32),
            ((half_tokens, 1), F32),
        ],
        (mix_own, mix_other, *fixed),
        4 * 10**9,
        "mixer_forward",
        28,
        [((tokens, inner), BF)],
    )
    mix_sum = exchange_rows(chip(part_own, part_other, square_own, square_other), "col")
    mix_sum = jnp.sum(mix_sum.astype(F32), axis=0)
    square = mix_sum[:, width : width + 1] + mix_sum[:, width + 1 : width + 2]
    mix_sum = mix_sum[:, :width]

    here = lax.dynamic_slice_in_dim(hidden, col * shard, shard, 0)
    inv_gate_here = lax.rsqrt(square / inner_all + EPS)
    mix_out = mix_sum * inv_gate_here
    residual = here + mix_out
    inv_moe_here = lax.rsqrt(jnp.mean(residual * residual, axis=1, keepdims=True) + EPS)
    moe_here = (residual * inv_moe_here * gain_moe).astype(BF)
    moe_own = from_tokens(
        jnp.concatenate(
            [moe_here, *two(inv_gate_here), *two(inv_moe_here), jnp.zeros((shard, 124), BF)], 1
        )
    )
    inv_moe = one(moe_own[:, width + 2], moe_own[:, width + 3])
    moe_other = swap(moe_own)

    mine = (jnp.arange(experts) == 2 * col + seq).astype(F32)[None, :]
    in_own, in_other, out_own, out_other, in_grads, acts, gates, *gates_grad = call(
        functools.partial(experts_both_ways, hidden_units, shared_units),
        [
            ((half_tokens, width), BF),
            ((half_tokens, width), BF),
            ((half_tokens, width), BF),
            ((half_tokens, width), BF),
            ((tokens, in_units), BF),
            ((tokens, down_units), BF),
            ((tokens, experts), F32),
            ((half_tokens, experts), F32),
            ((half_tokens, experts), F32),
        ],
        (moe_own, moe_other, cotangent, cot_other, expert_whole, named, mine),
        6 * 10**9,
        "experts_both_ways",
        36,
    )
    moe_got = exchange_rows(chip(in_own, in_other, *gates_grad), "col")
    (expert_sums,) = call(
        expert_products,
        [((width, in_units + down_units), BF)],
        (moe_own, moe_other, cotangent, cot_other, in_grads, acts),
        3 * 10**9,
        "expert_products",
        28,
    )
    moe_got, expert_sums = lax.optimization_barrier((moe_got, expert_sums))
    expert_sums = lax.psum_scatter(expert_sums, "row", scatter_dimension=0, tiled=True)

    sent, residual_grad, gain_moe_grad = call(
        second_shard,
        [((shard, width + 128), BF), ((shard, width), F32), ((1, width), F32)],
        (
            moe_got,
            residual,
            mix_out,
            lax.dynamic_slice_in_dim(cotangent, col * shard, shard, 0),
            lax.dynamic_slice_in_dim(gates, col * shard, shard, 0),
            expert_whole[:, in_units : in_units + experts],
            inv_moe_here,
            gain_moe[None],
        ),
        10**7,
        "second_shard",
    )
    grad_own = from_tokens(sent)

    chip_out = (out_own.astype(F32) + swap(out_other).astype(F32)).astype(BF)
    grad_own, chip_out = lax.optimization_barrier((grad_own, chip_out))
    grad_other = swap(grad_own)
    out_got = exchange_rows(chip_out, "col")

    grads, dt_grad, normed_gate, part_own, part_other, small = call(
        functools.partial(mixer_backward, inner, inner_all, head_width, experts),
        [
            ((tokens, out_at), BF),
            ((tokens, lanes), BF),
            ((tokens, inner), BF),
            ((half_tokens, width), BF),
            ((half_tokens, width), BF),
            ((SMALL_ROWS, 128), F32),
        ],
        (grad_own, grad_other, moe_own, moe_other, *fixed, pre, dt_in, cum, scanned),
        5 * 10**9,
        "mixer_backward",
        36,
        [
            ((tokens, inner), BF),
            ((tokens, inner), BF),
            ((tokens, inner), F32),
            ((tokens, state), F32),
            ((tokens, state), F32),
        ],
    )
    chip_in = (part_own.astype(F32) + swap(part_other).astype(F32)).astype(BF)
    chip_in, out_got = lax.optimization_barrier((chip_in, out_got))
    output_here = residual + jnp.sum(out_got.astype(F32), axis=0)
    output = lax.all_gather(after(output_here, expert_sums), "col", axis=0, tiled=True)
    mix_in_got = exchange_rows(chip_in, "col")
    (mixer_sums,) = call(
        functools.partial(mixer_products, inner, experts),
        [((2 * rows, w_z.shape[0], mixer_width + 128), BF)],
        (
            mix_own,
            mix_other,
            grad_own,
            grad_other,
            moe_own,
            moe_other,
            grads,
            dt_grad,
            normed_gate,
        ),
        2 * 10**9,
        "mixer_products",
        28,
    )
    mix_in_got, mixer_sums = lax.optimization_barrier((mix_in_got, mixer_sums))
    mix_in_grad = jnp.sum(mix_in_got.astype(F32), axis=0)

    inv_here = lax.dynamic_slice_in_dim(inv_mix, col * shard, shard, 0)[:, None]
    scaled_mix = mix_in_grad * gain_mix
    grad_hidden_here = (
        residual_grad
        + inv_here * scaled_mix
        - here * (inv_here**3 * jnp.mean(scaled_mix * here, axis=1, keepdims=True))
    )
    gain_mix_grad = jnp.sum(mix_in_grad * here * inv_here, axis=0)

    gains = jnp.concatenate([gain_mix_grad.reshape(-1, 128), gain_moe_grad.reshape(-1, 128)])
    small = jnp.concatenate([gains, small[TAPS_BC_ROW:]]).astype(BF)
    mixer_sums = lax.dynamic_update_slice(
        mixer_sums, jnp.broadcast_to(small[None], (2 * rows, *small.shape)), (0, 0, mixer_width)
    )
    got = lax.all_to_all(mixer_sums, ("row", "seq"), 0, 0)
    grad_hidden = from_tokens(grad_hidden_here.astype(BF))
    grad_hidden = grad_hidden.astype(F32)

    own = own_half(expert_sums, 0)
    other = swap(other_half(expert_sums, 0))

    def expert(at):
        a = own[:, None, at : at + hidden_units]
        return join(a, other[:, None, at : at + hidden_units], 1).astype(F32)

    def shared(at):
        return join(
            own[:, at : at + shared_units], other[:, at : at + shared_units], 1
        ).astype(F32)

    g_w_gate_t = expert(0)
    g_w_up_t = expert(hidden_units)
    g_w_down_t = expert(in_units)
    g_ws_gate = shared(2 * hidden_units)
    g_ws_up = shared(2 * hidden_units + shared_units)
    g_ws_down_t = shared(in_units + hidden_units)
    (
        got,
        grad_hidden,
        g_w_gate_t,
        g_w_up_t,
        g_w_down_t,
        g_ws_gate,
        g_ws_up,
        g_ws_down_t,
        inv_moe,
    ) = lax.optimization_barrier(
        (
            got,
            grad_hidden,
            g_w_gate_t,
            g_w_up_t,
            g_w_down_t,
            g_ws_gate,
            g_ws_up,
            g_ws_down_t,
            inv_moe,
        )
    )
    weight_rows = w_z.shape[0]
    (
        g_out_t,
        g_w_z,
        g_w_x,
        g_w_dt,
        g_w_router,
        g_conv_x,
        g_gain_gate,
        by_heads,
        sent,
    ) = call(
        functools.partial(tail_sums, inner, heads),
        [
            ((weight_rows, 2 * inner), F32),
            ((weight_rows, 2 * inner), F32),
            ((weight_rows, 2 * inner), F32),
            ((weight_rows, 2 * heads), F32),
            ((weight_rows, experts), F32),
            ((4, 2 * inner), F32),
            ((1, 2 * inner), F32),
            ((3, 2 * heads), F32),
            ((weight_rows + 32, 2 * state), BF),
        ],
        (got,),
        10**7,
        "tail_sums",
        16,
    )
    g_gain_gate = g_gain_gate.reshape(-1)
    g_dt_bias, g_a_log, g_d_skip = by_heads[0], by_heads[1], by_heads[2]
    got = lax.all_to_all(jnp.broadcast_to(sent[None], (cols, *sent.shape)), "col", 0, 0)
    g_w_bc, g_gain_mix, g_gain_moe, g_conv_bc = call(
        last_sums,
        [
            ((weight_rows, 2 * state), F32),
            ((width // 128, 128), F32),
            ((width // 128, 128), F32),
            ((4, 2 * state), F32),
        ],
        (got,),
        10**6,
        "last_sums",
    )
    g_gain_mix, g_gain_moe = g_gain_mix.reshape(-1), g_gain_moe.reshape(-1)

    return (
        output,
        grad_hidden,
        inv_mix,
        inv_moe,
        g_gain_mix,
        g_w_z,
        g_w_x,
        g_w_bc,
        g_w_dt,
        g_conv_x,
        g_conv_bc,
        g_dt_bias,
        g_a_log,
        g_d_skip,
        g_gain_gate,
        g_out_t,
        g_gain_moe,
        g_w_router,
        g_w_gate_t,
        g_w_up_t,
        g_w_down_t,
        g_ws_gate,
        g_ws_up,
        g_ws_down_t,
    )


def solution(mesh):
    placed = (
        P(("row", "seq"), None),
        P(("row", "seq"), None),
        P(("row", "seq")),
        P(("row", "seq"), None),
        P(),
        P(("row", "seq"), "col"),
        P(("row", "seq"), "col"),
        P(("row", "seq"), None),
        P(("row", "seq"), "col"),
        P(None, "col"),
        P(),
        P("col"),
        P("col"),
        P("col"),
        P("col"),
        P(("row", "seq"), "col"),
        P(),
        P(("row", "seq"), None),
        P(("row", "seq"), "col", None),
        P(("row", "seq"), "col", None),
        P(("row", "seq"), "col", None),
        P(("row", "seq"), "col"),
        P(("row", "seq"), "col"),
        P(("row", "seq"), "col"),
    )
    return jax.shard_map(
        on_device,
        mesh=mesh,
        in_specs=placed,
        out_specs=(
            P(("row", "seq"), None),
            P(("row", "seq"), None),
            P(("row", "seq")),
            P(("row", "seq")),
            P(),
            P(("row", "seq"), "col"),
            P(("row", "seq"), "col"),
            P(("row", "seq"), None),
            P(("row", "seq"), "col"),
            P(None, "col"),
            P(),
            P("col"),
            P("col"),
            P("col"),
            P("col"),
            P(("row", "seq"), "col"),
            P(),
            P(("row", "seq"), None),
            P(("row", "seq"), "col", None),
            P(("row", "seq"), "col", None),
            P(("row", "seq"), "col", None),
            P(("row", "seq"), "col"),
            P(("row", "seq"), "col"),
            P(("row", "seq"), "col"),
        ),
        check_vma=False,
    )
```

```python
import functools

import jax
import jax.numpy as jnp
from jax import lax
from jax.experimental import pallas as pl
from jax.experimental.pallas import tpu as pltpu
from jax.sharding import PartitionSpec as P

EPS = 1e-05
BF = jnp.bfloat16
F32 = jnp.float32
FAR = -1e30
TAPS_BC_ROW, TAPS_X_ROW, GATE_ROW, HEAD_ROW, SMALL_ROWS = 24, 32, 40, 42, 48


def silu(v):
    return v * jax.nn.sigmoid(v)


def nn(left, right):
    return lax.dot_general(left, right, (((1,), (0,)), ((), ())), preferred_element_type=F32)


def nt(left, right):
    return lax.dot_general(left, right, (((1,), (1,)), ((), ())), preferred_element_type=F32)


def tn(left, right):
    return lax.dot_general(left, right, (((0,), (0,)), ((), ())), preferred_element_type=F32)


def swap(value):
    return lax.ppermute(value, "seq", [(0, 1), (1, 0)])


def half(value, axis, which):
    size = value.shape[axis] // 2
    return lax.slice_in_dim(value, which * size, (which + 1) * size, axis=axis)


def own_half(value, axis):
    first = lax.axis_index("seq") == 0
    return jnp.where(first, half(value, axis, 0), half(value, axis, 1))


def other_half(value, axis):
    first = lax.axis_index("seq") == 0
    return jnp.where(first, half(value, axis, 1), half(value, axis, 0))


def join(own, other, axis):
    first = lax.axis_index("seq") == 0
    return jnp.where(
        first, jnp.concatenate([own, other], axis), jnp.concatenate([other, own], axis)
    )


def low(value):
    return lax.reduce_precision(value, 8, 7)


def two(value):
    high = low(value)
    return high.astype(BF), (value - high).astype(BF)


def halved(value):
    high = value.astype(BF)
    return high, (value - high.astype(F32)).astype(BF)


def three(value):
    high = value.astype(BF)
    rest = value - high.astype(F32)
    middle = rest.astype(BF)
    return high, middle, (rest - middle.astype(F32)).astype(BF)


def exact(left, value):
    high, middle, last = three(value)
    return (nn(left, last) + nn(left, middle)) + nn(left, high)


def one(high, low_term):
    return high.astype(F32) + low_term.astype(F32)


def after(value, *others):
    return lax.optimization_barrier((value, *others))[0]


def call(kernel, outs, args, flops, name, room=12, scratch=()):
    whole = pl.BlockSpec(memory_space=pltpu.VMEM)
    shapes = [jax.ShapeDtypeStruct(shape, kind) for shape, kind in outs]
    size = lambda a: a.size * jnp.dtype(a.dtype).itemsize
    return pl.pallas_call(
        kernel,
        out_shape=shapes,
        in_specs=[whole] * len(args),
        out_specs=[whole] * len(outs),
        scratch_shapes=[pltpu.VMEM(shape, kind) for shape, kind in scratch],
        compiler_params=pltpu.CompilerParams(vmem_limit_bytes=room * 2**20),
        cost_estimate=pl.CostEstimate(
            flops=flops,
            bytes_accessed=sum(size(a) for a in args) + sum(size(a) for a in shapes),
            transcendentals=0,
        ),
        name=name,
    )(*args)


def causal(marks, marks_row, rows):
    return (marks[rows, 1:2] >= marks_row[1:2, :]) & (marks[rows, 0:1] == marks_row[0:1, :])


def convolved(value, taps, marks):
    total = taps[3:4, :] * value
    for lag in range(1, 4):
        rolled = pltpu.roll(value, lag, 0) * marks[:, 1 + lag : 2 + lag]
        total = total + taps[3 - lag : 4 - lag, :] * rolled
    return total


def head_columns(inner, lanes, head_width):
    down = lax.broadcasted_iota(jnp.int32, (inner, lanes), 0)
    across = lax.broadcasted_iota(jnp.int32, (inner, lanes), 1) * head_width
    return jnp.where((down >= across) & (down < across + head_width), 1.0, 0.0).astype(BF)


def by_head(value, columns):
    high, middle, last = three(value)
    return (nn(last, columns) + nn(middle, columns)) + nn(high, columns)


def softplus(v):
    return jnp.maximum(v, 0.0) + jnp.log1p(jnp.exp(-jnp.abs(v)))


def mixer_forward(
    inner,
    head_width,
    own_ref,
    other_ref,
    w_ref,
    marks_ref,
    row_ref,
    taps_x_ref,
    taps_bc_ref,
    head_ref,
    wide_ref,
    pre_ref,
    dt_ref,
    cum_ref,
    scanned_ref,
    part_own_ref,
    part_other_ref,
    square_own_ref,
    square_other_ref,
    scaled_ref,
):
    half_tokens, width = own_ref.shape
    tokens = 2 * half_tokens
    heads = inner // head_width
    bc_at, out_at, dt_at = 2 * inner, pre_ref.shape[1], pre_ref.shape[1] + inner
    state = (out_at - bc_at) // 2
    for part, src in ((0, own_ref), (1, other_ref)):
        rows = slice(part * half_tokens, (part + 1) * half_tokens)
        pre_ref[rows, :] = nn(src[...], w_ref[:, :out_at])
        dt_ref[rows, :] = nn(src[...], w_ref[:, dt_at:]) + head_ref[0:1, :]
    marks, marks_row = marks_ref[...], row_ref[...]
    x_conv = silu(convolved(pre_ref[:, :inner], taps_x_ref[...], marks))
    bc = silu(convolved(pre_ref[:, bc_at:out_at], taps_bc_ref[...], marks)).astype(BF)
    b_map, c_map = bc[:, :state], bc[:, state:]
    step = softplus(dt_ref[...])
    lower = jnp.where(marks[:, 1:2] >= marks_row[1:2, :], 1.0, 0.0).astype(BF)
    cum = exact(lower, -step * head_ref[1:2, :])
    cum_ref[...] = cum
    cum_row = jnp.concatenate([cum, jnp.zeros_like(cum)], 1).T
    for h in range(heads):
        here = slice(h * head_width, (h + 1) * head_width)
        scaled_ref[:, here] = (x_conv[:, here] * step[:, h : h + 1]).astype(BF)
    block = 128
    for at in range(0, tokens, block):
        rows = slice(at, at + block)
        scores = nt(c_map[rows, :], b_map)
        mask = causal(marks, marks_row, rows)
        for h in range(heads):
            here = slice(h * head_width, (h + 1) * head_width)
            gap = cum[rows, h : h + 1] - cum_row[h : h + 1, :]
            mix = (jnp.exp(jnp.where(mask, gap, FAR)) * scores).astype(BF)
            scanned_ref[rows, here] = nn(mix, scaled_ref[:, here])
    mixer_out = scanned_ref[...] + wide_ref[0:1, :] * x_conv
    gated = mixer_out * silu(pre_ref[:, inner:bc_at])
    square = jnp.sum(gated * gated, axis=1, keepdims=True)
    square_own_ref[...] = square[:half_tokens]
    square_other_ref[...] = square[half_tokens:]
    sent = (gated * wide_ref[1:2, :]).astype(BF)
    out_w = w_ref[:, out_at:dt_at]
    part_own_ref[...] = nt(sent[:half_tokens], out_w).astype(BF)
    part_other_ref[...] = nt(sent[half_tokens:], out_w).astype(BF)


def mixer_backward(
    inner,
    inner_all,
    head_width,
    experts,
    own_ref,
    other_ref,
    moe_own_ref,
    moe_other_ref,
    w_ref,
    marks_ref,
    row_ref,
    taps_x_ref,
    taps_bc_ref,
    head_ref,
    wide_ref,
    pre_ref,
    dt_ref,
    cum_ref,
    scanned_ref,
    grads_ref,
    dt_grad_ref,
    normed_ref,
    part_own_ref,
    part_other_ref,
    small_ref,
    scaled_ref,
    low_ref,
    spread_ref,
    c_grad_ref,
    b_grad_ref,
):
    half_tokens = own_ref.shape[0]
    width = w_ref.shape[0]
    tokens = 2 * half_tokens
    heads = inner // head_width
    bc_at, out_at, dt_at = 2 * inner, pre_ref.shape[1], pre_ref.shape[1] + inner
    state = (out_at - bc_at) // 2
    marks, marks_row = marks_ref[...], row_ref[...]
    stack = lambda a, b: jnp.concatenate([a, b], 0)
    conv_x = convolved(pre_ref[:, :inner], taps_x_ref[...], marks)
    conv_bc = convolved(pre_ref[:, bc_at:out_at], taps_bc_ref[...], marks)
    x_conv = silu(conv_x)
    bc = silu(conv_bc).astype(BF)
    b_map, c_map = bc[:, :state], bc[:, state:]
    z_pre = pre_ref[:, inner:bc_at]
    step = softplus(dt_ref[...])
    rate = head_ref[1:2, :]
    skip_wide, gain = wide_ref[0:1, :], wide_ref[1:2, :]
    out_w = w_ref[:, out_at:dt_at]
    gate_norm_grad = stack(
        nn(own_ref[:, :width], out_w), nn(other_ref[:, :width], out_w)
    )
    at = width + experts
    dots = lambda ref: one(ref[:, at : at + 1], ref[:, at + 1 : at + 2])
    gate_dot = stack(dots(own_ref), dots(other_ref))
    gates = lambda ref: one(ref[:, width : width + 1], ref[:, width + 1 : width + 2])
    inv_gate = stack(gates(moe_own_ref), gates(moe_other_ref))
    sig = jax.nn.sigmoid(z_pre)
    silu_z = z_pre * sig
    mixer_out = scanned_ref[...] + skip_wide * x_conv
    gated = mixer_out * silu_z
    normed = gated * inv_gate
    small_ref[...] = jnp.zeros_like(small_ref)

    def keep_small(row, value):
        for at in range(0, value.shape[1], 128):
            piece = value[:, at : at + 128]
            small_ref[row : row + 1, : piece.shape[1]] = piece
            row = row + 1

    keep_small(GATE_ROW, jnp.sum(gate_norm_grad * normed, axis=0, keepdims=True))
    normed_ref[...] = (normed * gain).astype(BF)
    gated_grad = inv_gate * (gate_norm_grad * gain) - gated * (
        inv_gate * inv_gate * gate_dot * (1.0 / inner_all)
    )
    ssm_grad = gated_grad * silu_z
    grads_ref[:, inner:bc_at] = (
        gated_grad * mixer_out * (sig * (1.0 + z_pre * (1.0 - sig)))
    ).astype(BF)
    columns = head_columns(inner, dt_ref.shape[1], head_width)
    skips = by_head(
        jnp.broadcast_to(jnp.sum(ssm_grad * x_conv, axis=0, keepdims=True), (8, inner)), columns
    )
    keep_small(HEAD_ROW + 2, skips[0:1, :heads])
    low_ref[...] = ssm_grad.astype(BF)
    for h in range(heads):
        here = slice(h * head_width, (h + 1) * head_width)
        scaled_ref[:, here] = (x_conv[:, here] * step[:, h : h + 1]).astype(BF)
    cum = cum_ref[...]
    cum_row = jnp.concatenate([cum, jnp.zeros_like(cum)], 1).T
    c_grad_ref[...] = jnp.zeros_like(c_grad_ref)
    block = 128
    for start in range(0, tokens, block):
        rows = slice(start, start + block)
        scores = nt(b_map[rows, :], c_map)
        mask = (marks_row[1:2, :] >= marks[rows, 1:2]) & (
            marks_row[0:1, :] == marks[rows, 0:1]
        )
        scores_grad = jnp.zeros((block, tokens), F32)
        for h in range(heads):
            here = slice(h * head_width, (h + 1) * head_width)
            gap = cum_row[h : h + 1, :] - cum[rows, h : h + 1]
            decay = jnp.exp(jnp.where(mask, gap, FAR))
            spread_ref[rows, here] = nn((decay * scores).astype(BF), low_ref[:, here])
            scores_grad = scores_grad + decay * nt(scaled_ref[rows, here], low_ref[:, here])
        scores_low = scores_grad.astype(BF)
        b_grad_ref[rows, :] = nn(scores_low, c_map)
        c_grad_ref[...] += tn(scores_low, b_map[rows, :])
    spread = spread_ref[...]
    step_grad = by_head(x_conv * spread, columns)
    cum_grad = by_head(
        low_ref[...].astype(F32) * scanned_ref[...] - scaled_ref[...].astype(F32) * spread, columns
    )
    upper = jnp.where(marks_row[1:2, :] >= marks[:, 1:2], 1.0, 0.0).astype(BF)
    decay_grad = exact(upper, cum_grad)
    dt_float = (step_grad - decay_grad * rate) * jax.nn.sigmoid(dt_ref[...])
    keep_small(HEAD_ROW, jnp.sum(dt_float, axis=0, keepdims=True)[:, :heads])
    keep_small(
        HEAD_ROW + 1, jnp.sum(decay_grad * (-step * rate), axis=0, keepdims=True)[:, :heads]
    )
    dt_low = dt_float.astype(BF)
    dt_grad_ref[...] = dt_low
    for h in range(heads):
        here = slice(h * head_width, (h + 1) * head_width)
        spread_ref[:, here] = spread[:, here] * step[:, h : h + 1]

    def back(value_grad, total, value, taps, small_row, to):
        sig_c = jax.nn.sigmoid(total)
        grad = value_grad * (sig_c * (1.0 + total * (1.0 - sig_c)))
        keep_small(small_row + 6, jnp.sum(grad * value, axis=0, keepdims=True))
        result = taps[3:4, :] * grad
        for lag in range(1, 4):
            kept = grad * marks[:, 1 + lag : 2 + lag]
            keep_small(
                small_row + 2 * (3 - lag),
                jnp.sum(kept * pltpu.roll(value, lag, 0), axis=0, keepdims=True),
            )
            result = result + taps[3 - lag : 4 - lag, :] * pltpu.roll(kept, tokens - lag, 0)
        grads_ref[:, to] = result.astype(BF)

    back(
        spread_ref[...] + ssm_grad * skip_wide,
        conv_x,
        pre_ref[:, :inner],
        taps_x_ref[...],
        TAPS_X_ROW,
        slice(0, inner),
    )
    back(
        jnp.concatenate([b_grad_ref[...], c_grad_ref[...]], 1),
        conv_bc,
        pre_ref[:, bc_at:out_at],
        taps_bc_ref[...],
        TAPS_BC_ROW,
        slice(bc_at, out_at),
    )
    for part, dst in ((0, part_own_ref), (1, part_other_ref)):
        rows = slice(part * half_tokens, (part + 1) * half_tokens)
        dst[...] = (
            nt(grads_ref[rows, :], w_ref[:, :out_at]) + nt(dt_low[rows, :], w_ref[:, dt_at:])
        ).astype(BF)


def mixer_products(
    inner,
    experts,
    own_ref,
    other_ref,
    mix_own_ref,
    mix_other_ref,
    moe_own_ref,
    moe_other_ref,
    grads_ref,
    dt_grad_ref,
    normed_ref,
    sums_ref,
):
    half_tokens, width = own_ref.shape
    out_at = grads_ref.shape[1]
    dt_at = out_at + inner
    count = sums_ref.shape[0]
    rows = width // count
    group = min(8, count)
    first, second = slice(0, half_tokens), slice(half_tokens, 2 * half_tokens)
    logits = slice(width, width + experts)
    for at in range(0, count, group):
        here = slice(at * rows, (at + group) * rows)
        mine, others = own_ref[:, here], other_ref[:, here]
        a = tn(mine, grads_ref[first, :]) + tn(others, grads_ref[second, :])
        b = tn(mix_own_ref[:, here], normed_ref[first, :]) + tn(
            mix_other_ref[:, here], normed_ref[second, :]
        )
        c = tn(mine, dt_grad_ref[first, :]) + tn(others, dt_grad_ref[second, :])
        d = tn(moe_own_ref[:, here], mix_own_ref[:, logits]) + tn(
            moe_other_ref[:, here], mix_other_ref[:, logits]
        )
        a, b, c, d = a.astype(BF), b.astype(BF), c.astype(BF), d.astype(BF)
        for k in range(group):
            part = slice(k * rows, (k + 1) * rows)
            sums_ref[at + k, :, :out_at] = a[part]
            sums_ref[at + k, :, out_at:dt_at] = b[part]
            sums_ref[at + k, :, dt_at : dt_at + 64] = c[part]
            sums_ref[at + k, :, dt_at + 16 : dt_at + 16 + experts] = d[part]
            sums_ref[at + k, :, dt_at + 64 :] = jnp.zeros((rows, 128), BF)


def experts_both_ways(
    units,
    shared,
    own_ref,
    other_ref,
    cot_own_ref,
    cot_other_ref,
    w_ref,
    named_ref,
    mine_ref,
    in_own_ref,
    in_other_ref,
    out_own_ref,
    out_other_ref,
    grads_ref,
    acts_ref,
    gates_ref,
    gates_grad_own_ref,
    gates_grad_other_ref,
):
    half_tokens = own_ref.shape[0]
    width = w_ref.shape[0]
    experts = named_ref.shape[1]
    in_units = 2 * (units + shared)
    down_at = in_units + 128
    mine = mine_ref[...]
    parts = (
        (own_ref, cot_own_ref, in_own_ref, out_own_ref, gates_grad_own_ref),
        (other_ref, cot_other_ref, in_other_ref, out_other_ref, gates_grad_other_ref),
    )
    for part, (src, cot, in_dst, out_dst, gates_dst) in enumerate(parts):
        rows = slice(part * half_tokens, (part + 1) * half_tokens)
        pre = nn(src[:, :width], w_ref[:, :down_at])
        back = nn(cot[...], w_ref[:, down_at:])
        logits = jnp.where(named_ref[rows, :] > 0.0, pre[:, in_units : in_units + experts], FAR)
        raised = jnp.exp(logits - jnp.max(logits, axis=1, keepdims=True))
        gates = raised / jnp.sum(raised, axis=1, keepdims=True)
        gates_ref[rows, :] = gates
        weight = jnp.sum(gates * mine, axis=1, keepdims=True)
        gate, up = pre[:, :units], pre[:, units : 2 * units]
        sig = jax.nn.sigmoid(gate)
        silu_gate = gate * sig
        act = silu_gate * up
        acts_ref[rows, :units] = (act * weight).astype(BF)
        act_back = back[:, :units]
        gates_dst[...] = jnp.sum(act * act_back, axis=1, keepdims=True) * mine
        act_grad = act_back * weight
        grads_ref[rows, :units] = (
            act_grad * up * (sig * (1.0 + gate * (1.0 - sig)))
        ).astype(BF)
        grads_ref[rows, units : 2 * units] = (act_grad * silu_gate).astype(BF)
        gate, up = pre[:, 2 * units : 2 * units + shared], pre[:, 2 * units + shared : in_units]
        sig = jax.nn.sigmoid(gate)
        silu_gate = gate * sig
        acts_ref[rows, units:] = (silu_gate * up).astype(BF)
        act_grad = back[:, units:]
        grads_ref[rows, 2 * units : 2 * units + shared] = (
            act_grad * up * (sig * (1.0 + gate * (1.0 - sig)))
        ).astype(BF)
        grads_ref[rows, 2 * units + shared :] = (act_grad * silu_gate).astype(BF)
        in_dst[...] = nt(grads_ref[rows, :], w_ref[:, :in_units]).astype(BF)
        out_dst[...] = nt(acts_ref[rows, :], w_ref[:, down_at:]).astype(BF)


def expert_products(
    own_ref, other_ref, cot_own_ref, cot_other_ref, grads_ref, acts_ref, sums_ref
):
    half_tokens, width = cot_own_ref.shape
    split = grads_ref.shape[1]
    first, second = slice(0, half_tokens), slice(half_tokens, 2 * half_tokens)
    block = 256
    for at in range(0, width, block):
        here = slice(at, at + block)
        sums_ref[here, :split] = (
            tn(own_ref[:, here], grads_ref[first, :]) + tn(other_ref[:, here], grads_ref[second, :])
        ).astype(BF)
        sums_ref[here, split:] = (
            tn(cot_own_ref[:, here], acts_ref[first, :])
            + tn(cot_other_ref[:, here], acts_ref[second, :])
        ).astype(BF)


def tail_sums(
    inner,
    heads,
    got_ref,
    w_x_ref,
    w_z_ref,
    w_bc_ref,
    w_dt_ref,
    out_ref,
    z_ref,
    x_ref,
    dt_ref,
    router_ref,
    conv_ref,
    gain_ref,
    head_ref,
    sent_ref,
):
    count, rows = got_ref.shape[0], out_ref.shape[0]
    experts = router_ref.shape[1]
    bc_at = 2 * inner
    small_at = got_ref.shape[2] - 128
    dt_at = small_at - 64
    out_at = dt_at - inner
    totals = []
    for core in range(2):
        total = got_ref[core].astype(F32)
        for at in range(core + 2, count, 2):
            total = total + got_ref[at].astype(F32)
        totals.append(total)
        here = slice(core * inner, (core + 1) * inner)
        x_ref[:, here] = total[:, :inner]
        z_ref[:, here] = total[:, inner:bc_at]
        out_ref[:, here] = total[:, out_at:dt_at]
        dt_ref[:, core * heads : (core + 1) * heads] = total[:, dt_at : dt_at + heads]
        small = total[:SMALL_ROWS, small_at:]

        def row_of(at):
            return jnp.concatenate([small[at : at + 1], small[at + 1 : at + 2, : inner - 128]], 1)

        for k in range(conv_ref.shape[0]):
            conv_ref[k : k + 1, here] = row_of(TAPS_X_ROW + 2 * k)
        gain_ref[:, here] = row_of(GATE_ROW)
        for k in range(3):
            head_ref[k : k + 1, core * heads : (core + 1) * heads] = small[
                HEAD_ROW + k : HEAD_ROW + k + 1, :heads
            ]
    router_ref[...] = totals[0][:, dt_at + 16 : dt_at + 16 + experts]
    span = out_at - bc_at
    bc = totals[0][:, bc_at:out_at] + totals[1][:, bc_at:out_at]
    small = totals[0][:TAPS_X_ROW, small_at:] + totals[1][:TAPS_X_ROW, small_at:]
    sent_ref[...] = jnp.zeros_like(sent_ref)
    sent_ref[:rows, :span] = bc.astype(BF)
    sent_ref[rows:, :128], sent_ref[rows:, 128:256] = halved(small)
    dot = lambda a, b: jnp.sum(a.astype(F32) * b, axis=1, keepdims=True)
    by_gain = (
        dot(w_x_ref[...], x_ref[...])
        + dot(w_z_ref[...], z_ref[...])
        + dot(w_bc_ref[...], bc)
        + dot(w_dt_ref[...], dt_ref[...])
    )
    sent_ref[:rows, span : span + 1], sent_ref[:rows, span + 1 : span + 2] = halved(by_gain)


def last_sums(got_ref, gain_ref, bc_ref, mix_ref, moe_ref, conv_ref):
    rows, span = bc_ref.shape
    total = got_ref[0].astype(F32)
    for at in range(1, got_ref.shape[0]):
        total = total + got_ref[at].astype(F32)
    bc_ref[...] = total[:rows, :span]
    by_gain = total[:rows, span : span + 1] + total[:rows, span + 1 : span + 2]
    wide = jnp.broadcast_to(by_gain / gain_ref[...], (rows, 128))
    full = jnp.concatenate([wide, jnp.zeros((mix_ref.shape[1] - rows, 128), F32)], 0)
    mix_ref[...] = full.T[:8]
    small = total[rows:, :128] + total[rows:, 128:256]
    half_rows = TAPS_BC_ROW // 2
    moe_ref[...] = small[half_rows:TAPS_BC_ROW]
    for k in range(conv_ref.shape[0]):
        for part in range(2):
            at = TAPS_BC_ROW + 2 * k + part
            conv_ref[k : k + 1, part * 128 : (part + 1) * 128] = small[at : at + 1]


def chip_sum(own_ref, other_ref, extra_own_ref, extra_other_ref, sum_ref):
    width, more = own_ref.shape[1], extra_own_ref.shape[1]
    sum_ref[:, :width] = (own_ref[...].astype(F32) + other_ref[...].astype(F32)).astype(BF)
    extra = extra_own_ref[...] + extra_other_ref[...]
    high = extra.astype(BF)
    sum_ref[:, width:] = jnp.zeros((own_ref.shape[0], sum_ref.shape[1] - width), BF)
    sum_ref[:, width : width + more] = high
    sum_ref[:, width + more : width + 2 * more] = (extra - high.astype(F32)).astype(BF)


def second_shard(
    got_ref,
    residual_ref,
    mix_out_ref,
    cot_ref,
    gates_ref,
    router_ref,
    inv_ref,
    gain_ref,
    sent_ref,
    grad_ref,
    gain_grad_ref,
):
    width, experts = residual_ref.shape[1], gates_ref.shape[1]
    total = got_ref[0].astype(F32)
    for at in range(1, got_ref.shape[0]):
        total = total + got_ref[at].astype(F32)
    gates = gates_ref[...]
    gates_grad = total[:, width : width + experts] + total[:, width + experts : width + 2 * experts]
    logits_grad = (
        gates * (gates_grad - jnp.sum(gates * gates_grad, axis=1, keepdims=True))
    ).astype(BF)
    moe_in_grad = total[:, :width] + nt(logits_grad, router_ref[...])
    residual, inv = residual_ref[...], inv_ref[...]
    scaled = moe_in_grad * gain_ref[...]
    mean = jnp.sum(scaled * residual, axis=1, keepdims=True) * (1.0 / width)
    grad = cot_ref[...].astype(F32) + inv * scaled - residual * (inv * inv * inv * mean)
    grad_ref[...] = grad
    gain_grad_ref[...] = jnp.sum(moe_in_grad * residual * inv, axis=0, keepdims=True)
    grad_low = grad.astype(BF)
    gate_dot = jnp.sum(grad_low.astype(F32) * mix_out_ref[...], axis=1, keepdims=True)
    high = gate_dot.astype(BF)
    sent_ref[:, :width] = grad_low
    sent_ref[:, width:] = jnp.zeros((residual.shape[0], sent_ref.shape[1] - width), BF)
    sent_ref[:, width : width + experts] = logits_grad
    sent_ref[:, width + experts : width + experts + 1] = high
    sent_ref[:, width + experts + 1 : width + experts + 2] = (
        gate_dot - high.astype(F32)
    ).astype(BF)


def mixer_rows(inner, heads, x_ref, z_ref, bc_ref, out_ref, dt_ref, rows_ref):
    bc_at, state = 2 * inner, bc_ref.shape[1]
    out_at = bc_at + state
    dt_at = out_at + inner
    for core in range(2):
        here = slice(core * inner, (core + 1) * inner)
        parts = (
            (0, x_ref[:, here]),
            (inner, z_ref[:, here]),
            (bc_at, bc_ref[...]),
            (out_at, out_ref[:, here]),
            (dt_at, jnp.zeros((x_ref.shape[0], rows_ref.shape[2] - dt_at), BF)),
            (dt_at, dt_ref[:, core * heads : (core + 1) * heads]),
        )
        for at, value in parts:
            rows_ref[core, :, at : at + value.shape[1]] = value
        for at in range(core + 2, rows_ref.shape[0], 2):
            rows_ref[at] = rows_ref[core]


def exchange_rows(part, axis):
    count = lax.axis_size(axis)
    blocks = part.reshape(count, part.shape[0] // count, part.shape[1])
    return lax.all_to_all(blocks, axis, 0, 0, tiled=False)


def chip(own, other, extra_own, extra_other):
    rows, width = own.shape
    extra = call(
        chip_sum,
        [((rows, width + 128), BF)],
        (own, swap(other), extra_own, swap(extra_other)),
        10**6,
        "chip_sum",
    )
    return extra[0]


def ring_sum(part):
    count = lax.axis_size("col")
    here, size = lax.axis_index("col"), part.shape[0] // count
    take = lambda ahead: lax.dynamic_slice_in_dim(
        part, (here + ahead + count) % count * size, size, 0
    ).astype(F32)
    step = lambda value, way: lax.ppermute(
        value.astype(BF), "col", [(i, (i + way) % count) for i in range(count)]
    ).astype(F32)
    up, down = take(count // 2), take(1 - count // 2)
    for left in range(count // 2 - 1, 0, -1):
        up = step(up, 1) + take(left)
        if left > 1:
            down = step(down, -1) + take(1 - left)
    return step(up, 1) + step(down, -1) + take(0)


def from_tokens(own):
    return lax.all_gather(own, "col", axis=0, tiled=True)


def on_device(
    hidden,
    cotangent,
    segments,
    routes,
    gain_mix,
    w_z,
    w_x,
    w_bc,
    w_dt,
    conv_x,
    conv_bc,
    dt_bias,
    a_log,
    d_skip,
    gain_gate,
    out_t,
    gain_moe,
    w_router,
    w_gate_t,
    w_up_t,
    w_down_t,
    ws_gate,
    ws_up,
    ws_down_t,
):
    half_tokens, width = hidden.shape
    rows = lax.axis_size("row")
    cols = lax.axis_size("col")
    seq = lax.axis_index("seq")
    col = lax.axis_index("col")
    tokens = 2 * half_tokens
    inner = conv_x.shape[1] // 2
    heads = dt_bias.shape[0] // 2
    head_width = inner // heads
    state = conv_bc.shape[1] // 2
    experts = w_router.shape[1]
    hidden_units = w_gate_t.shape[2]
    shared_units = ws_gate.shape[1] // 2
    lanes = 64
    inner_all = conv_x.shape[1] * cols
    shard = half_tokens // cols

    out_at = 2 * inner + 2 * state
    dt_at = out_at + inner
    mixer_width = dt_at + lanes
    (spread_rows,) = call(
        functools.partial(mixer_rows, inner, heads),
        [((2 * rows, w_z.shape[0], mixer_width), BF)],
        (w_x, w_z, w_bc, out_t, w_dt),
        10**6,
        "mixer_rows",
        12,
    )
    (
        spread_rows,
        w_gate_t,
        w_up_t,
        w_down_t,
        ws_gate,
        ws_up,
        ws_down_t,
        conv_x,
        dt_bias,
        a_log,
        d_skip,
        gain_gate,
        segments,
        routes,
    ) = lax.optimization_barrier(
        (
            spread_rows,
            w_gate_t,
            w_up_t,
            w_down_t,
            ws_gate,
            ws_up,
            ws_down_t,
            conv_x,
            dt_bias,
            a_log,
            d_skip,
            gain_gate,
            segments,
            routes,
        )
    )
    mixer_whole = lax.all_to_all(spread_rows, ("row", "seq"), 0, 0).reshape(width, mixer_width)

    def expert_half(pick):
        parts = [
            pick(w_gate_t, 1)[:, 0],
            pick(w_up_t, 1)[:, 0],
            pick(ws_gate, 1),
            pick(ws_up, 1),
            w_router,
            jnp.zeros((w_router.shape[0], 128 - w_router.shape[1]), BF),
            pick(w_down_t, 1)[:, 0],
            pick(ws_down_t, 1),
        ]
        return jnp.concatenate(parts, 1)

    expert_rows = join(expert_half(own_half), swap(expert_half(other_half)), 0)
    down_units = hidden_units + shared_units
    in_units = 2 * down_units
    down_at = in_units + 128

    inv_mix = lax.rsqrt(jnp.mean(hidden * hidden, axis=1) + EPS)
    mix_own = (hidden * inv_mix[:, None] * gain_mix).astype(BF)
    mix_other = swap(mix_own)
    cot_other = swap(cotangent)
    named = jnp.max(
        jnp.where(
            routes[:, :, None] == jnp.arange(experts, dtype=jnp.int32)[None, None, :], 1.0, 0.0
        ),
        axis=1,
    )
    aside = jnp.concatenate([named, segments.astype(F32)[:, None]], 1).astype(BF)
    aside = jnp.concatenate([aside, swap(aside)], 0).astype(F32)
    named = aside[:, :experts]
    seg = aside[:, experts]
    place = (jnp.arange(tokens) + seq * half_tokens) % tokens
    hold = ((seg == jnp.roll(seg, 1)) & (place > 0)).astype(F32)
    kept_two = hold * jnp.roll(hold, 1)
    kept_three = kept_two * jnp.roll(hold, 2)
    blank = jnp.zeros_like(seg)
    marks_row = jnp.stack(
        [seg, place.astype(F32), hold, kept_two, kept_three, blank, blank, blank]
    )
    marks = marks_row.T
    taps_x = own_half(conv_x, 1)
    fill = jnp.zeros((lanes - heads,), F32)
    wide_head = lambda v: jnp.concatenate([own_half(v, 0), fill])
    head_rows = jnp.stack(
        [wide_head(dt_bias), jnp.concatenate([jnp.exp(own_half(a_log, 0)), fill])]
    )
    wide_rows = jnp.stack([jnp.repeat(own_half(d_skip, 0), head_width), own_half(gain_gate, 0)])

    expert_rows, mixer_whole, mix_own, mix_other, cot_other, named, marks, marks_row = (
        lax.optimization_barrier(
            (expert_rows, mixer_whole, mix_own, mix_other, cot_other, named, marks, marks_row)
        )
    )
    expert_whole = lax.all_gather(expert_rows, "row", axis=0, tiled=True)

    fixed = (mixer_whole, marks, marks_row, taps_x, conv_bc, head_rows, wide_rows)
    pre, dt_in, cum, scanned, part_own, part_other, square_own, square_other = call(
        functools.partial(mixer_forward, inner, head_width),
        [
            ((tokens, out_at), F32),
            ((tokens, lanes), F32),
            ((tokens, lanes), F32),
            ((tokens, inner), F32),
            ((half_tokens, width), BF),
            ((half_tokens, width), BF),
            ((half_tokens, 1), F32),
            ((half_tokens, 1), F32),
        ],
        (mix_own, mix_other, *fixed),
        4 * 10**9,
        "mixer_forward",
        28,
        [((tokens, inner), BF)],
    )
    mix_sum = exchange_rows(chip(part_own, part_other, square_own, square_other), "col")
    mix_sum = jnp.sum(mix_sum.astype(F32), axis=0)
    square = mix_sum[:, width : width + 1] + mix_sum[:, width + 1 : width + 2]
    mix_sum = mix_sum[:, :width]

    here = lax.dynamic_slice_in_dim(hidden, col * shard, shard, 0)
    inv_gate_here = lax.rsqrt(square / inner_all + EPS)
    mix_out = mix_sum * inv_gate_here
    residual = here + mix_out
    inv_moe_here = lax.rsqrt(jnp.mean(residual * residual, axis=1, keepdims=True) + EPS)
    moe_here = (residual * inv_moe_here * gain_moe).astype(BF)
    moe_own = from_tokens(
        jnp.concatenate(
            [moe_here, *two(inv_gate_here), *two(inv_moe_here), jnp.zeros((shard, 124), BF)], 1
        )
    )
    inv_moe = one(moe_own[:, width + 2], moe_own[:, width + 3])
    moe_other = swap(moe_own)

    mine = (jnp.arange(experts) == 2 * col + seq).astype(F32)[None, :]
    in_own, in_other, out_own, out_other, in_grads, acts, gates, *gates_grad = call(
        functools.partial(experts_both_ways, hidden_units, shared_units),
        [
            ((half_tokens, width), BF),
            ((half_tokens, width), BF),
            ((half_tokens, width), BF),
            ((half_tokens, width), BF),
            ((tokens, in_units), BF),
            ((tokens, down_units), BF),
            ((tokens, experts), F32),
            ((half_tokens, experts), F32),
            ((half_tokens, experts), F32),
        ],
        (moe_own, moe_other, cotangent, cot_other, expert_whole, named, mine),
        6 * 10**9,
        "experts_both_ways",
        36,
    )
    moe_got = exchange_rows(chip(in_own, in_other, *gates_grad), "col")
    (expert_sums,) = call(
        expert_products,
        [((width, in_units + down_units), BF)],
        (moe_own, moe_other, cotangent, cot_other, in_grads, acts),
        3 * 10**9,
        "expert_products",
        28,
    )
    chip_out = (out_own.astype(F32) + swap(out_other).astype(F32)).astype(BF)
    moe_got, expert_sums, chip_out, cot_here, gates_here, router, gain_row = (
        lax.optimization_barrier(
            (
                moe_got,
                expert_sums,
                chip_out,
                lax.dynamic_slice_in_dim(cotangent, col * shard, shard, 0),
                lax.dynamic_slice_in_dim(gates, col * shard, shard, 0),
                expert_whole[:, in_units : in_units + experts],
                gain_moe[None],
            )
        )
    )
    expert_sums = lax.psum_scatter(expert_sums, "row", scatter_dimension=0, tiled=True)

    sent, residual_grad, gain_moe_grad = call(
        second_shard,
        [((shard, width + 128), BF), ((shard, width), F32), ((1, width), F32)],
        (
            moe_got,
            residual,
            mix_out,
            cot_here,
            gates_here,
            router,
            inv_moe_here,
            gain_row,
        ),
        10**7,
        "second_shard",
    )
    grad_own = from_tokens(sent)

    grad_own, chip_out = lax.optimization_barrier((grad_own, chip_out))
    grad_other = swap(grad_own)
    out_got = exchange_rows(chip_out, "col")

    grads, dt_grad, normed_gate, part_own, part_other, small = call(
        functools.partial(mixer_backward, inner, inner_all, head_width, experts),
        [
            ((tokens, out_at), BF),
            ((tokens, lanes), BF),
            ((tokens, inner), BF),
            ((half_tokens, width), BF),
            ((half_tokens, width), BF),
            ((SMALL_ROWS, 128), F32),
        ],
        (grad_own, grad_other, moe_own, moe_other, *fixed, pre, dt_in, cum, scanned),
        5 * 10**9,
        "mixer_backward",
        36,
        [
            ((tokens, inner), BF),
            ((tokens, inner), BF),
            ((tokens, inner), F32),
            ((tokens, state), F32),
            ((tokens, state), F32),
        ],
    )
    chip_in = (part_own.astype(F32) + swap(part_other).astype(F32)).astype(BF)
    (mixer_sums,) = call(
        functools.partial(mixer_products, inner, experts),
        [((2 * rows, w_z.shape[0], mixer_width + 128), BF)],
        (
            mix_own,
            mix_other,
            grad_own,
            grad_other,
            moe_own,
            moe_other,
            grads,
            dt_grad,
            normed_gate,
        ),
        2 * 10**9,
        "mixer_products",
        28,
    )
    gains = jnp.concatenate([jnp.zeros((width // 128, 128), F32), gain_moe_grad.reshape(-1, 128)])
    small = jnp.concatenate([gains, small[TAPS_BC_ROW:]]).astype(BF)
    mixer_sums = lax.dynamic_update_slice(
        mixer_sums, jnp.broadcast_to(small[None], (2 * rows, *small.shape)), (0, 0, mixer_width)
    )
    chip_in, out_got, mixer_sums = lax.optimization_barrier((chip_in, out_got, mixer_sums))
    got = lax.all_to_all(mixer_sums, ("row", "seq"), 0, 0)

    mix_in_grad = ring_sum(chip_in)
    output_here = residual + jnp.sum(out_got.astype(F32), axis=0)
    inv_here = lax.dynamic_slice_in_dim(inv_mix, col * shard, shard, 0)[:, None]
    scaled_mix = mix_in_grad * gain_mix
    grad_hidden_here = (
        residual_grad
        + inv_here * scaled_mix
        - here * (inv_here**3 * jnp.mean(scaled_mix * here, axis=1, keepdims=True))
    )
    sent = jnp.concatenate([grad_hidden_here, output_here]).astype(BF)
    sent, expert_sums = lax.optimization_barrier((sent, expert_sums))
    gathered = lax.all_gather(sent, "col", axis=0)
    weight_rows = w_z.shape[0]
    device = 2 * lax.axis_index("row") + seq
    gain_here = lax.dynamic_slice_in_dim(gain_mix, device * weight_rows, weight_rows, 0)[:, None]

    own = own_half(expert_sums, 0)
    other = swap(other_half(expert_sums, 0))

    def expert(at):
        a = own[:, None, at : at + hidden_units]
        return join(a, other[:, None, at : at + hidden_units], 1).astype(F32)

    def shared(at):
        return join(
            own[:, at : at + shared_units], other[:, at : at + shared_units], 1
        ).astype(F32)

    g_w_gate_t = expert(0)
    g_w_up_t = expert(hidden_units)
    g_w_down_t = expert(in_units)
    g_ws_gate = shared(2 * hidden_units)
    g_ws_up = shared(2 * hidden_units + shared_units)
    g_ws_down_t = shared(in_units + hidden_units)
    got, sent, g_w_gate_t, g_w_up_t, g_w_down_t, g_ws_gate, g_ws_up, g_ws_down_t, inv_moe = (
        lax.optimization_barrier(
            (
                got,
                sent,
                g_w_gate_t,
                g_w_up_t,
                g_w_down_t,
                g_ws_gate,
                g_ws_up,
                g_ws_down_t,
                inv_moe,
            )
        )
    )
    (
        g_out_t,
        g_w_z,
        g_w_x,
        g_w_dt,
        g_w_router,
        g_conv_x,
        g_gain_gate,
        by_heads,
        sent,
    ) = call(
        functools.partial(tail_sums, inner, heads),
        [
            ((weight_rows, 2 * inner), F32),
            ((weight_rows, 2 * inner), F32),
            ((weight_rows, 2 * inner), F32),
            ((weight_rows, 2 * heads), F32),
            ((weight_rows, experts), F32),
            ((4, 2 * inner), F32),
            ((1, 2 * inner), F32),
            ((3, 2 * heads), F32),
            ((weight_rows + 32, 2 * state + 128), BF),
        ],
        (got, w_x, w_z, w_bc, w_dt),
        10**7,
        "tail_sums",
        16,
    )
    g_gain_gate = g_gain_gate.reshape(-1)
    g_dt_bias, g_a_log, g_d_skip = by_heads[0], by_heads[1], by_heads[2]
    got = lax.all_to_all(jnp.broadcast_to(sent[None], (cols, *sent.shape)), "col", 0, 0)
    g_w_bc, gain_mix_here, g_gain_moe, g_conv_bc = call(
        last_sums,
        [
            ((weight_rows, 2 * state), F32),
            ((8, -(-weight_rows // 128) * 128), F32),
            ((width // 128, 128), F32),
            ((4, 2 * state), F32),
        ],
        (got, gain_here),
        10**6,
        "last_sums",
    )
    g_gain_moe = g_gain_moe.reshape(-1)
    gain_mix_all = lax.all_to_all(
        jnp.broadcast_to(gain_mix_here[None], (2 * rows, *gain_mix_here.shape)),
        ("row", "seq"),
        0,
        0,
    )
    g_gain_mix = gain_mix_all[:, 0, :weight_rows].reshape(-1)
    grad_hidden = gathered[:, :shard].reshape(half_tokens, width).astype(F32)
    output = gathered[:, shard:].reshape(half_tokens, width).astype(F32)

    return (
        output,
        grad_hidden,
        inv_mix,
        inv_moe,
        g_gain_mix,
        g_w_z,
        g_w_x,
        g_w_bc,
        g_w_dt,
        g_conv_x,
        g_conv_bc,
        g_dt_bias,
        g_a_log,
        g_d_skip,
        g_gain_gate,
        g_out_t,
        g_gain_moe,
        g_w_router,
        g_w_gate_t,
        g_w_up_t,
        g_w_down_t,
        g_ws_gate,
        g_ws_up,
        g_ws_down_t,
    )


def solution(mesh):
    placed = (
        P(("row", "seq"), None),
        P(("row", "seq"), None),
        P(("row", "seq")),
        P(("row", "seq"), None),
        P(),
        P(("row", "seq"), "col"),
        P(("row", "seq"), "col"),
        P(("row", "seq"), None),
        P(("row", "seq"), "col"),
        P(None, "col"),
        P(),
        P("col"),
        P("col"),
        P("col"),
        P("col"),
        P(("row", "seq"), "col"),
        P(),
        P(("row", "seq"), None),
        P(("row", "seq"), "col", None),
        P(("row", "seq"), "col", None),
        P(("row", "seq"), "col", None),
        P(("row", "seq"), "col"),
        P(("row", "seq"), "col"),
        P(("row", "seq"), "col"),
    )
    return jax.shard_map(
        on_device,
        mesh=mesh,
        in_specs=placed,
        out_specs=(
            P(("row", "seq"), None),
            P(("row", "seq"), None),
            P(("row", "seq")),
            P(("row", "seq")),
            P(),
            P(("row", "seq"), "col"),
            P(("row", "seq"), "col"),
            P(("row", "seq"), None),
            P(("row", "seq"), "col"),
            P(None, "col"),
            P(),
            P("col"),
            P("col"),
            P("col"),
            P("col"),
            P(("row", "seq"), "col"),
            P(),
            P(("row", "seq"), None),
            P(("row", "seq"), "col", None),
            P(("row", "seq"), "col", None),
            P(("row", "seq"), "col", None),
            P(("row", "seq"), "col"),
            P(("row", "seq"), "col"),
            P(("row", "seq"), "col"),
        ),
        check_vma=False,
    )
```

```python
import functools

import jax
import jax.numpy as jnp
from jax import lax
from jax.experimental import pallas as pl
from jax.experimental.pallas import tpu as pltpu
from jax.sharding import PartitionSpec as P

EPS = 1e-05
BF = jnp.bfloat16
F32 = jnp.float32
FAR = -1e30
TAPS_BC_ROW, TAPS_X_ROW, GATE_ROW, HEAD_ROW, SMALL_ROWS = 24, 32, 40, 42, 48


def silu(v):
    return v * jax.nn.sigmoid(v)


def nn(left, right):
    return lax.dot_general(left, right, (((1,), (0,)), ((), ())), preferred_element_type=F32)


def nt(left, right):
    return lax.dot_general(left, right, (((1,), (1,)), ((), ())), preferred_element_type=F32)


def tn(left, right):
    return lax.dot_general(left, right, (((0,), (0,)), ((), ())), preferred_element_type=F32)


def swap(value):
    return lax.ppermute(value, "seq", [(0, 1), (1, 0)])


def half(value, axis, which):
    size = value.shape[axis] // 2
    return lax.slice_in_dim(value, which * size, (which + 1) * size, axis=axis)


def own_half(value, axis):
    first = lax.axis_index("seq") == 0
    return jnp.where(first, half(value, axis, 0), half(value, axis, 1))


def other_half(value, axis):
    first = lax.axis_index("seq") == 0
    return jnp.where(first, half(value, axis, 1), half(value, axis, 0))


def join(own, other, axis):
    first = lax.axis_index("seq") == 0
    return jnp.where(
        first, jnp.concatenate([own, other], axis), jnp.concatenate([other, own], axis)
    )


def low(value):
    return lax.reduce_precision(value, 8, 7)


def two(value):
    high = low(value)
    return high.astype(BF), (value - high).astype(BF)


def three(value):
    high = value.astype(BF)
    rest = value - high.astype(F32)
    middle = rest.astype(BF)
    return high, middle, (rest - middle.astype(F32)).astype(BF)


def exact(left, value):
    high, middle, last = three(value)
    return (nn(left, last) + nn(left, middle)) + nn(left, high)


def one(high, low_term):
    return high.astype(F32) + low_term.astype(F32)


def after(value, *others):
    return lax.optimization_barrier((value, *others))[0]


def call(kernel, outs, args, flops, name, room=12, scratch=(), apart=(), scalars=()):
    whole = pl.BlockSpec(memory_space=pltpu.VMEM)
    spec = {i: pl.BlockSpec(memory_space=pltpu.HBM) for i in apart}
    spec.update({i: pl.BlockSpec(memory_space=pltpu.SMEM) for i in scalars})
    shapes = [jax.ShapeDtypeStruct(shape, kind) for shape, kind in outs]
    size = lambda a: a.size * jnp.dtype(a.dtype).itemsize
    held = [pltpu.VMEM(args[i].shape, args[i].dtype) for i in apart]
    if apart:
        held.append(pltpu.SemaphoreType.DMA((len(apart) + 1,)))
    return pl.pallas_call(
        kernel,
        out_shape=shapes,
        in_specs=[spec.get(i, whole) for i in range(len(args))],
        out_specs=[whole] * len(outs),
        scratch_shapes=[pltpu.VMEM(shape, kind) for shape, kind in scratch] + held,
        compiler_params=pltpu.CompilerParams(vmem_limit_bytes=room * 2**20),
        cost_estimate=pl.CostEstimate(
            flops=flops,
            bytes_accessed=sum(size(a) for a in args) + sum(size(a) for a in shapes),
            transcendentals=0,
        ),
        name=name,
    )(*args)


def fetched(pairs, sems):
    copies = [
        pltpu.make_async_copy(src, dst, sems.at[k]) for k, (src, dst) in enumerate(pairs)
    ]
    for copy in copies:
        copy.start()
    return copies


def causal(marks, marks_row, rows):
    return (marks[rows, 1:2] >= marks_row[1:2, :]) & (marks[rows, 0:1] == marks_row[0:1, :])


def convolved(value, taps, marks):
    total = taps[3:4, :] * value
    for lag in range(1, 4):
        rolled = pltpu.roll(value, lag, 0) * marks[:, 1 + lag : 2 + lag]
        total = total + taps[3 - lag : 4 - lag, :] * rolled
    return total


def head_columns(inner, lanes, head_width):
    down = lax.broadcasted_iota(jnp.int32, (inner, lanes), 0)
    across = lax.broadcasted_iota(jnp.int32, (inner, lanes), 1) * head_width
    return jnp.where((down >= across) & (down < across + head_width), 1.0, 0.0).astype(BF)


def by_head(value, columns):
    high, middle, last = three(value)
    return (nn(last, columns) + nn(middle, columns)) + nn(high, columns)


def softplus(v):
    return jnp.maximum(v, 0.0) + jnp.log1p(jnp.exp(-jnp.abs(v)))


def mixer_forward(
    inner,
    head_width,
    own_ref,
    other_ref,
    w_src,
    marks_ref,
    row_ref,
    taps_x_ref,
    taps_bc_ref,
    head_ref,
    wide_ref,
    pre_ref,
    dt_ref,
    cum_ref,
    scanned_ref,
    part_own_ref,
    part_other_ref,
    square_own_ref,
    square_other_ref,
    scaled_ref,
    w_ref,
    sems,
):
    half_tokens, width = own_ref.shape
    tokens = 2 * half_tokens
    heads = inner // head_width
    bc_at, out_at, dt_at = 2 * inner, pre_ref.shape[1], pre_ref.shape[1] + inner
    state = (out_at - bc_at) // 2
    copies = fetched(
        (
            (w_src.at[:, :out_at], w_ref.at[:, :out_at]),
            (w_src.at[:, out_at:], w_ref.at[:, out_at:]),
        ),
        sems,
    )
    for part, src in ((0, own_ref), (1, other_ref)):
        rows = slice(part * half_tokens, (part + 1) * half_tokens)
        if part == 0:
            copies[0].wait()
        pre_ref[rows, :] = nn(src[...], w_ref[:, :out_at])
        if part == 0:
            copies[1].wait()
        dt_ref[rows, :] = nn(src[...], w_ref[:, dt_at:]) + head_ref[0:1, :]
    marks, marks_row = marks_ref[...], row_ref[...]
    x_conv = silu(convolved(pre_ref[:, :inner], taps_x_ref[...], marks))
    bc = silu(convolved(pre_ref[:, bc_at:out_at], taps_bc_ref[...], marks)).astype(BF)
    b_map, c_map = bc[:, :state], bc[:, state:]
    step = softplus(dt_ref[...])
    lower = jnp.where(marks[:, 1:2] >= marks_row[1:2, :], 1.0, 0.0).astype(BF)
    cum = exact(lower, -step * head_ref[1:2, :])
    cum_ref[...] = cum
    cum_row = jnp.concatenate([cum, jnp.zeros_like(cum)], 1).T
    for h in range(heads):
        here = slice(h * head_width, (h + 1) * head_width)
        scaled_ref[:, here] = (x_conv[:, here] * step[:, h : h + 1]).astype(BF)
    block = 128
    for at in range(0, tokens, block):
        rows = slice(at, at + block)
        scores = nt(c_map[rows, :], b_map)
        mask = causal(marks, marks_row, rows)
        for h in range(heads):
            here = slice(h * head_width, (h + 1) * head_width)
            gap = cum[rows, h : h + 1] - cum_row[h : h + 1, :]
            mix = (jnp.exp(jnp.where(mask, gap, FAR)) * scores).astype(BF)
            scanned_ref[rows, here] = nn(mix, scaled_ref[:, here])
    mixer_out = scanned_ref[...] + wide_ref[0:1, :] * x_conv
    gated = mixer_out * silu(pre_ref[:, inner:bc_at])
    square = jnp.sum(gated * gated, axis=1, keepdims=True)
    square_own_ref[...] = square[:half_tokens]
    square_other_ref[...] = square[half_tokens:]
    sent = (gated * wide_ref[1:2, :]).astype(BF)
    out_w = w_ref[:, out_at:dt_at]
    part_own_ref[...] = nt(sent[:half_tokens], out_w).astype(BF)
    part_other_ref[...] = nt(sent[half_tokens:], out_w).astype(BF)


def mixer_backward(
    inner,
    inner_all,
    head_width,
    experts,
    own_src,
    other_src,
    moe_own_src,
    moe_other_src,
    w_src,
    marks_ref,
    row_ref,
    taps_x_ref,
    taps_bc_ref,
    head_ref,
    wide_ref,
    pre_src,
    dt_src,
    cum_src,
    scanned_src,
    grads_ref,
    dt_grad_ref,
    normed_ref,
    part_own_ref,
    part_other_ref,
    small_ref,
    scaled_ref,
    low_ref,
    spread_ref,
    c_grad_ref,
    b_grad_ref,
    own_ref,
    other_ref,
    moe_own_ref,
    moe_other_ref,
    w_ref,
    pre_ref,
    dt_ref,
    cum_ref,
    scanned_ref,
    sems,
):
    half_tokens = own_ref.shape[0]
    width = w_ref.shape[0]
    split = pre_ref.shape[1]
    copies = fetched(
        (
            (w_src.at[:, split:], w_ref.at[:, split:]),
            (own_src, own_ref),
            (other_src, other_ref),
            (moe_own_src.at[:, width:], moe_own_ref.at[:, width:]),
            (moe_other_src.at[:, width:], moe_other_ref.at[:, width:]),
            (pre_src, pre_ref),
            (scanned_src, scanned_ref),
            (dt_src, dt_ref),
            (cum_src, cum_ref),
            (w_src.at[:, :split], w_ref.at[:, :split]),
        ),
        sems,
    )
    tokens = 2 * half_tokens
    heads = inner // head_width
    bc_at, out_at, dt_at = 2 * inner, pre_ref.shape[1], pre_ref.shape[1] + inner
    state = (out_at - bc_at) // 2
    marks, marks_row = marks_ref[...], row_ref[...]
    stack = lambda a, b: jnp.concatenate([a, b], 0)
    for copy in copies[:3]:
        copy.wait()
    out_w = w_ref[:, out_at:dt_at]
    gate_norm_grad = stack(
        nn(own_ref[:, :width], out_w), nn(other_ref[:, :width], out_w)
    )
    for copy in copies[3:9]:
        copy.wait()
    conv_x = convolved(pre_ref[:, :inner], taps_x_ref[...], marks)
    conv_bc = convolved(pre_ref[:, bc_at:out_at], taps_bc_ref[...], marks)
    x_conv = silu(conv_x)
    bc = silu(conv_bc).astype(BF)
    b_map, c_map = bc[:, :state], bc[:, state:]
    z_pre = pre_ref[:, inner:bc_at]
    step = softplus(dt_ref[...])
    rate = head_ref[1:2, :]
    skip_wide, gain = wide_ref[0:1, :], wide_ref[1:2, :]
    at = width + experts
    dots = lambda ref: one(ref[:, at : at + 1], ref[:, at + 1 : at + 2])
    gate_dot = stack(dots(own_ref), dots(other_ref))
    gates = lambda ref: one(ref[:, width : width + 1], ref[:, width + 1 : width + 2])
    inv_gate = stack(gates(moe_own_ref), gates(moe_other_ref))
    sig = jax.nn.sigmoid(z_pre)
    silu_z = z_pre * sig
    mixer_out = scanned_ref[...] + skip_wide * x_conv
    gated = mixer_out * silu_z
    normed = gated * inv_gate
    small_ref[...] = jnp.zeros_like(small_ref)

    def keep_small(row, value):
        for at in range(0, value.shape[1], 128):
            piece = value[:, at : at + 128]
            small_ref[row : row + 1, : piece.shape[1]] = piece
            row = row + 1

    keep_small(GATE_ROW, jnp.sum(gate_norm_grad * normed, axis=0, keepdims=True))
    normed_ref[...] = (normed * gain).astype(BF)
    gated_grad = inv_gate * (gate_norm_grad * gain) - gated * (
        inv_gate * inv_gate * gate_dot * (1.0 / inner_all)
    )
    ssm_grad = gated_grad * silu_z
    grads_ref[:, inner:bc_at] = (
        gated_grad * mixer_out * (sig * (1.0 + z_pre * (1.0 - sig)))
    ).astype(BF)
    columns = head_columns(inner, dt_ref.shape[1], head_width)
    skips = by_head(
        jnp.broadcast_to(jnp.sum(ssm_grad * x_conv, axis=0, keepdims=True), (8, inner)), columns
    )
    keep_small(HEAD_ROW + 2, skips[0:1, :heads])
    low_ref[...] = ssm_grad.astype(BF)
    for h in range(heads):
        here = slice(h * head_width, (h + 1) * head_width)
        scaled_ref[:, here] = (x_conv[:, here] * step[:, h : h + 1]).astype(BF)
    cum = cum_ref[...]
    cum_row = jnp.concatenate([cum, jnp.zeros_like(cum)], 1).T
    c_grad_ref[...] = jnp.zeros_like(c_grad_ref)
    block = 128
    for start in range(0, tokens, block):
        rows = slice(start, start + block)
        scores = nt(b_map[rows, :], c_map)
        mask = (marks_row[1:2, :] >= marks[rows, 1:2]) & (
            marks_row[0:1, :] == marks[rows, 0:1]
        )
        scores_grad = jnp.zeros((block, tokens), F32)
        for h in range(heads):
            here = slice(h * head_width, (h + 1) * head_width)
            gap = cum_row[h : h + 1, :] - cum[rows, h : h + 1]
            decay = jnp.exp(jnp.where(mask, gap, FAR))
            spread_ref[rows, here] = nn((decay * scores).astype(BF), low_ref[:, here])
            scores_grad = scores_grad + decay * nt(scaled_ref[rows, here], low_ref[:, here])
        scores_low = scores_grad.astype(BF)
        b_grad_ref[rows, :] = nn(scores_low, c_map)
        c_grad_ref[...] += tn(scores_low, b_map[rows, :])
    spread = spread_ref[...]
    step_grad = by_head(x_conv * spread, columns)
    cum_grad = by_head(
        low_ref[...].astype(F32) * scanned_ref[...] - scaled_ref[...].astype(F32) * spread, columns
    )
    upper = jnp.where(marks_row[1:2, :] >= marks[:, 1:2], 1.0, 0.0).astype(BF)
    decay_grad = exact(upper, cum_grad)
    dt_float = (step_grad - decay_grad * rate) * jax.nn.sigmoid(dt_ref[...])
    keep_small(HEAD_ROW, jnp.sum(dt_float, axis=0, keepdims=True)[:, :heads])
    keep_small(
        HEAD_ROW + 1, jnp.sum(decay_grad * (-step * rate), axis=0, keepdims=True)[:, :heads]
    )
    dt_low = dt_float.astype(BF)
    dt_grad_ref[...] = dt_low
    for h in range(heads):
        here = slice(h * head_width, (h + 1) * head_width)
        spread_ref[:, here] = spread[:, here] * step[:, h : h + 1]

    def back(value_grad, total, value, taps, small_row, to):
        sig_c = jax.nn.sigmoid(total)
        grad = value_grad * (sig_c * (1.0 + total * (1.0 - sig_c)))
        keep_small(small_row + 6, jnp.sum(grad * value, axis=0, keepdims=True))
        result = taps[3:4, :] * grad
        for lag in range(1, 4):
            kept = grad * marks[:, 1 + lag : 2 + lag]
            keep_small(
                small_row + 2 * (3 - lag),
                jnp.sum(kept * pltpu.roll(value, lag, 0), axis=0, keepdims=True),
            )
            result = result + taps[3 - lag : 4 - lag, :] * pltpu.roll(kept, tokens - lag, 0)
        grads_ref[:, to] = result.astype(BF)

    back(
        spread_ref[...] + ssm_grad * skip_wide,
        conv_x,
        pre_ref[:, :inner],
        taps_x_ref[...],
        TAPS_X_ROW,
        slice(0, inner),
    )
    back(
        jnp.concatenate([b_grad_ref[...], c_grad_ref[...]], 1),
        conv_bc,
        pre_ref[:, bc_at:out_at],
        taps_bc_ref[...],
        TAPS_BC_ROW,
        slice(bc_at, out_at),
    )
    copies[9].wait()
    for part, dst in ((0, part_own_ref), (1, part_other_ref)):
        rows = slice(part * half_tokens, (part + 1) * half_tokens)
        dst[...] = (
            nt(grads_ref[rows, :], w_ref[:, :out_at]) + nt(dt_low[rows, :], w_ref[:, dt_at:])
        ).astype(BF)


def mixer_products(
    inner,
    experts,
    own_ref,
    other_ref,
    mix_own_ref,
    mix_other_ref,
    moe_own_ref,
    moe_other_ref,
    grads_ref,
    dt_grad_ref,
    normed_ref,
    sums_ref,
):
    half_tokens, width = own_ref.shape
    out_at = grads_ref.shape[1]
    dt_at = out_at + inner
    count = sums_ref.shape[0]
    rows = width // count
    group = min(8, count)
    first, second = slice(0, half_tokens), slice(half_tokens, 2 * half_tokens)
    logits = slice(width, width + experts)
    for at in range(0, count, group):
        here = slice(at * rows, (at + group) * rows)
        mine, others = own_ref[:, here], other_ref[:, here]
        a = tn(mine, grads_ref[first, :]) + tn(others, grads_ref[second, :])
        b = tn(mix_own_ref[:, here], normed_ref[first, :]) + tn(
            mix_other_ref[:, here], normed_ref[second, :]
        )
        c = tn(mine, dt_grad_ref[first, :]) + tn(others, dt_grad_ref[second, :])
        d = tn(moe_own_ref[:, here], mix_own_ref[:, logits]) + tn(
            moe_other_ref[:, here], mix_other_ref[:, logits]
        )
        a, b, c, d = a.astype(BF), b.astype(BF), c.astype(BF), d.astype(BF)
        for k in range(group):
            part = slice(k * rows, (k + 1) * rows)
            sums_ref[at + k, :, :out_at] = a[part]
            sums_ref[at + k, :, out_at:dt_at] = b[part]
            sums_ref[at + k, :, dt_at : dt_at + 64] = c[part]
            sums_ref[at + k, :, dt_at + 16 : dt_at + 16 + experts] = d[part]
            sums_ref[at + k, :, dt_at + 64 :] = jnp.zeros((rows, 128), BF)


def experts_both_ways(
    units,
    shared,
    own_src,
    other_src,
    cot_own_src,
    cot_other_src,
    w_src,
    routes_own_ref,
    routes_other_ref,
    mine_ref,
    in_own_ref,
    in_other_ref,
    out_own_ref,
    out_other_ref,
    grads_ref,
    acts_ref,
    gates_ref,
    gates_grad_own_ref,
    gates_grad_other_ref,
    own_ref,
    other_ref,
    cot_own_ref,
    cot_other_ref,
    w_ref,
    sems,
):
    half_tokens = own_ref.shape[0]
    width = w_ref.shape[0]
    experts = mine_ref.shape[1]
    in_units = 2 * (units + shared)
    down_at = in_units + 128
    late, cot_one, one_own, first, cot_two, two_own = fetched(
        (
            (w_src.at[:, down_at:], w_ref.at[:, down_at:]),
            (cot_own_src, cot_own_ref),
            (own_src, own_ref),
            (w_src.at[:, :down_at], w_ref.at[:, :down_at]),
            (cot_other_src, cot_other_ref),
            (other_src, other_ref),
        ),
        sems,
    )
    mine = mine_ref[...]
    number = lax.broadcasted_iota(jnp.int32, (half_tokens, experts), 1)
    down_end = down_at + units + shared
    parts = (
        (own_ref, cot_own_ref, routes_own_ref, in_own_ref, out_own_ref, gates_grad_own_ref),
        (
            other_ref,
            cot_other_ref,
            routes_other_ref,
            in_other_ref,
            out_other_ref,
            gates_grad_other_ref,
        ),
    )
    for part, (src, cot, routes, in_dst, out_dst, gates_dst) in enumerate(parts):
        rows = slice(part * half_tokens, (part + 1) * half_tokens)
        if part == 0:
            late.wait()
        (cot_one, cot_two)[part].wait()
        back = nn(cot[...], w_ref[:, down_at:down_end])
        if part == 0:
            first.wait()
        (one_own, two_own)[part].wait()
        pre = nn(src[:, :width], w_ref[:, :down_at])
        named = number == routes[:, 0:1]
        for k in range(1, routes.shape[1]):
            named = named | (number == routes[:, k : k + 1])
        logits = jnp.where(named, pre[:, in_units : in_units + experts], FAR)
        raised = jnp.exp(logits - jnp.max(logits, axis=1, keepdims=True))
        gates = raised / jnp.sum(raised, axis=1, keepdims=True)
        gates_ref[rows, :] = gates
        weight = jnp.sum(gates * mine, axis=1, keepdims=True)
        gate, up = pre[:, :units], pre[:, units : 2 * units]
        sig = jax.nn.sigmoid(gate)
        silu_gate = gate * sig
        act = silu_gate * up
        acts_ref[rows, :units] = (act * weight).astype(BF)
        act_back = back[:, :units]
        gates_dst[...] = jnp.sum(act * act_back, axis=1, keepdims=True) * mine
        act_grad = act_back * weight
        grads_ref[rows, :units] = (
            act_grad * up * (sig * (1.0 + gate * (1.0 - sig)))
        ).astype(BF)
        grads_ref[rows, units : 2 * units] = (act_grad * silu_gate).astype(BF)
        gate, up = pre[:, 2 * units : 2 * units + shared], pre[:, 2 * units + shared : in_units]
        sig = jax.nn.sigmoid(gate)
        silu_gate = gate * sig
        acts_ref[rows, units:] = (silu_gate * up).astype(BF)
        act_grad = back[:, units:]
        grads_ref[rows, 2 * units : 2 * units + shared] = (
            act_grad * up * (sig * (1.0 + gate * (1.0 - sig)))
        ).astype(BF)
        grads_ref[rows, 2 * units + shared :] = (act_grad * silu_gate).astype(BF)
        in_dst[...] = nt(grads_ref[rows, :], w_ref[:, :in_units]).astype(BF)
        out_dst[...] = nt(acts_ref[rows, :], w_ref[:, down_at:down_end]).astype(BF)


def expert_products(
    own_ref, other_ref, cot_own_ref, cot_other_ref, grads_ref, acts_ref, sums_ref
):
    half_tokens, width = cot_own_ref.shape
    split = grads_ref.shape[1]
    first, second = slice(0, half_tokens), slice(half_tokens, 2 * half_tokens)
    block = 256
    for at in range(0, width, block):
        here = slice(at, at + block)
        sums_ref[here, :split] = (
            tn(own_ref[:, here], grads_ref[first, :]) + tn(other_ref[:, here], grads_ref[second, :])
        ).astype(BF)
        sums_ref[here, split:] = (
            tn(cot_own_ref[:, here], acts_ref[first, :])
            + tn(cot_other_ref[:, here], acts_ref[second, :])
        ).astype(BF)


def tail_sums(
    inner,
    heads,
    got_ref,
    out_ref,
    z_ref,
    x_ref,
    dt_ref,
    router_ref,
    conv_ref,
    gain_ref,
    head_ref,
    sent_ref,
):
    count, rows = got_ref.shape[0], out_ref.shape[0]
    experts = router_ref.shape[1]
    bc_at = 2 * inner
    small_at = got_ref.shape[2] - 128
    dt_at = small_at - 64
    out_at = dt_at - inner
    totals = []
    for core in range(2):
        total = got_ref[core].astype(F32)
        for at in range(core + 2, count, 2):
            total = total + got_ref[at].astype(F32)
        totals.append(total)
        here = slice(core * inner, (core + 1) * inner)
        x_ref[:, here] = total[:, :inner]
        z_ref[:, here] = total[:, inner:bc_at]
        out_ref[:, here] = total[:, out_at:dt_at]
        dt_ref[:, core * heads : (core + 1) * heads] = total[:, dt_at : dt_at + heads]
        small = total[:SMALL_ROWS, small_at:]

        def row_of(at):
            return jnp.concatenate([small[at : at + 1], small[at + 1 : at + 2, : inner - 128]], 1)

        for k in range(conv_ref.shape[0]):
            conv_ref[k : k + 1, here] = row_of(TAPS_X_ROW + 2 * k)
        gain_ref[:, here] = row_of(GATE_ROW)
        for k in range(3):
            head_ref[k : k + 1, core * heads : (core + 1) * heads] = small[
                HEAD_ROW + k : HEAD_ROW + k + 1, :heads
            ]
    router_ref[...] = totals[0][:, dt_at + 16 : dt_at + 16 + experts]
    sent_ref[:rows, :] = (totals[0][:, bc_at:out_at] + totals[1][:, bc_at:out_at]).astype(BF)
    small = totals[0][:TAPS_X_ROW, small_at:] + totals[1][:TAPS_X_ROW, small_at:]
    high = small.astype(BF)
    sent_ref[rows:, :128] = high
    sent_ref[rows:, 128:] = (small - high.astype(F32)).astype(BF)


def last_sums(got_ref, bc_ref, mix_ref, moe_ref, conv_ref):
    rows = bc_ref.shape[0]
    total = got_ref[0].astype(F32)
    for at in range(1, got_ref.shape[0]):
        total = total + got_ref[at].astype(F32)
    bc_ref[...] = total[:rows]
    small = total[rows:, :128] + total[rows:, 128:]
    half_rows = TAPS_BC_ROW // 2
    mix_ref[...] = small[:half_rows]
    moe_ref[...] = small[half_rows:TAPS_BC_ROW]
    for k in range(conv_ref.shape[0]):
        for part in range(2):
            at = TAPS_BC_ROW + 2 * k + part
            conv_ref[k : k + 1, part * 128 : (part + 1) * 128] = small[at : at + 1]


def chip_sum(own_ref, other_ref, extra_own_ref, extra_other_ref, sum_ref):
    width, more = own_ref.shape[1], extra_own_ref.shape[1]
    sum_ref[:, :width] = (own_ref[...].astype(F32) + other_ref[...].astype(F32)).astype(BF)
    extra = extra_own_ref[...] + extra_other_ref[...]
    high = extra.astype(BF)
    sum_ref[:, width:] = jnp.zeros((own_ref.shape[0], sum_ref.shape[1] - width), BF)
    sum_ref[:, width : width + more] = high
    sum_ref[:, width + more : width + 2 * more] = (extra - high.astype(F32)).astype(BF)


def second_shard(
    got_ref,
    residual_ref,
    mix_out_ref,
    cot_ref,
    gates_ref,
    router_ref,
    inv_ref,
    gain_ref,
    sent_ref,
    grad_ref,
    gain_grad_ref,
):
    width, experts = residual_ref.shape[1], gates_ref.shape[1]
    total = got_ref[0].astype(F32)
    for at in range(1, got_ref.shape[0]):
        total = total + got_ref[at].astype(F32)
    gates = gates_ref[...]
    gates_grad = total[:, width : width + experts] + total[:, width + experts : width + 2 * experts]
    logits_grad = (
        gates * (gates_grad - jnp.sum(gates * gates_grad, axis=1, keepdims=True))
    ).astype(BF)
    moe_in_grad = total[:, :width] + nt(logits_grad, router_ref[...])
    residual, inv = residual_ref[...], inv_ref[...]
    scaled = moe_in_grad * gain_ref[...]
    mean = jnp.sum(scaled * residual, axis=1, keepdims=True) * (1.0 / width)
    grad = cot_ref[...].astype(F32) + inv * scaled - residual * (inv * inv * inv * mean)
    grad_ref[...] = grad
    gain_grad_ref[...] = jnp.sum(moe_in_grad * residual * inv, axis=0, keepdims=True)
    grad_low = grad.astype(BF)
    gate_dot = jnp.sum(grad_low.astype(F32) * mix_out_ref[...], axis=1, keepdims=True)
    high = gate_dot.astype(BF)
    sent_ref[:, :width] = grad_low
    sent_ref[:, width:] = jnp.zeros((residual.shape[0], sent_ref.shape[1] - width), BF)
    sent_ref[:, width : width + experts] = logits_grad
    sent_ref[:, width + experts : width + experts + 1] = high
    sent_ref[:, width + experts + 1 : width + experts + 2] = (
        gate_dot - high.astype(F32)
    ).astype(BF)


def mixer_rows(inner, heads, x_ref, z_ref, bc_ref, out_ref, dt_ref, rows_ref):
    bc_at, state = 2 * inner, bc_ref.shape[1]
    out_at = bc_at + state
    dt_at = out_at + inner
    for core in range(2):
        here = slice(core * inner, (core + 1) * inner)
        parts = (
            (0, x_ref[:, here]),
            (inner, z_ref[:, here]),
            (bc_at, bc_ref[...]),
            (out_at, out_ref[:, here]),
            (dt_at, jnp.zeros((x_ref.shape[0], rows_ref.shape[2] - dt_at), BF)),
            (dt_at, dt_ref[:, core * heads : (core + 1) * heads]),
        )
        for at, value in parts:
            rows_ref[core, :, at : at + value.shape[1]] = value
        for at in range(core + 2, rows_ref.shape[0], 2):
            rows_ref[at] = rows_ref[core]


def expert_packs(
    units, shared, flag_ref, gate_ref, up_ref, sg_ref, su_ref, router_ref, down_ref, sd_ref, *packs
):
    first = flag_ref[0] == 0
    router_at = 2 * (units + shared)
    down_at = router_at + 128
    for which, dst in enumerate(packs):
        dst[...] = jnp.zeros_like(dst)
        lead = first if which == 0 else jnp.logical_not(first)

        def pick(a, b):
            return jnp.where(lead, a.astype(F32), b.astype(F32)).astype(BF)

        for ref, at in ((gate_ref, 0), (up_ref, units), (down_ref, down_at)):
            dst[:, at : at + units] = pick(ref[:, :units], ref[:, units:])
        for ref, at in (
            (sg_ref, 2 * units),
            (su_ref, 2 * units + shared),
            (sd_ref, down_at + units),
        ):
            dst[:, at : at + shared] = pick(ref[:, :shared], ref[:, shared:])
        dst[:, router_at : router_at + router_ref.shape[1]] = router_ref[...]


def joined(flag_ref, own_ref, other_ref, rows_ref):
    first = flag_ref[0] == 0
    rows = own_ref.shape[0]
    own, other = own_ref[...].astype(F32), other_ref[...].astype(F32)
    rows_ref[:rows] = jnp.where(first, own, other).astype(BF)
    rows_ref[rows:] = jnp.where(first, other, own).astype(BF)


def small_set(
    inner,
    heads,
    head_width,
    flag_ref,
    bias_ref,
    log_ref,
    skip_ref,
    seg_own_ref,
    seg_other_ref,
    taps_ref,
    gain_ref,
    marks_ref,
    row_ref,
    taps_x_ref,
    head_ref,
    wide_ref,
):
    first = flag_ref[0] == 0
    half_tokens = seg_own_ref.shape[1]
    tokens = 2 * half_tokens
    seg = jnp.concatenate([seg_own_ref[...], seg_other_ref[...]], 1).astype(F32)
    seg = jnp.broadcast_to(seg, (8, tokens))
    place = lax.broadcasted_iota(jnp.int32, (8, tokens), 1)
    turned = jnp.where(place < half_tokens, place + half_tokens, place - half_tokens)
    place = jnp.where(first, place, turned).astype(F32)
    before = pltpu.roll(seg, 1, 1)
    hold = jnp.where((seg == before) & (place > 0.0), 1.0, 0.0)
    kept_two = hold * pltpu.roll(hold, 1, 1)
    kept_three = kept_two * pltpu.roll(hold, 2, 1)
    which = lax.broadcasted_iota(jnp.int32, (8, tokens), 0)
    rows = jnp.where(which == 0, seg, 0.0)
    for k, value in enumerate((place, hold, kept_two, kept_three)):
        rows = jnp.where(which == k + 1, value, rows)
    row_ref[...] = rows
    tall = jnp.concatenate([rows, jnp.zeros((120, tokens), F32)], 0)
    marks_ref[...] = tall.T[:, :8]
    taps_x_ref[...] = jnp.where(first, taps_ref[:, :inner], taps_ref[:, inner:])
    lanes = head_ref.shape[1]
    lane = lax.broadcasted_iota(jnp.int32, (1, lanes), 1)
    bias, log, on = jnp.zeros((1, lanes), F32), jnp.zeros((1, lanes), F32), lane < heads
    across = lax.broadcasted_iota(jnp.int32, (1, inner), 1)
    skip = jnp.zeros((1, inner), F32)
    for h in range(heads):
        own = lambda ref: jnp.where(first, ref[h], ref[heads + h])
        bias = jnp.where(lane == h, own(bias_ref), bias)
        log = jnp.where(lane == h, own(log_ref), log)
        skip = jnp.where(
            (across >= h * head_width) & (across < (h + 1) * head_width), own(skip_ref), skip
        )
    head_ref[0:1, :] = bias
    head_ref[1:2, :] = jnp.where(on, jnp.exp(log), 0.0)
    wide_ref[0:1, :] = skip
    wide_ref[1:2, :] = jnp.where(first, gain_ref[:, :inner], gain_ref[:, inner:])


def exchange_rows(part, axis):
    count = lax.axis_size(axis)
    blocks = part.reshape(count, part.shape[0] // count, part.shape[1])
    return lax.all_to_all(blocks, axis, 0, 0, tiled=False)


def chip(own, other, extra_own, extra_other):
    rows, width = own.shape
    extra = call(
        chip_sum,
        [((rows, width + 128), BF)],
        (own, swap(other), extra_own, swap(extra_other)),
        10**6,
        "chip_sum",
    )
    return extra[0]


def from_tokens(own):
    return lax.all_gather(own, "col", axis=0, tiled=True)


def on_device(
    hidden,
    cotangent,
    segments,
    routes,
    gain_mix,
    w_z,
    w_x,
    w_bc,
    w_dt,
    conv_x,
    conv_bc,
    dt_bias,
    a_log,
    d_skip,
    gain_gate,
    out_t,
    gain_moe,
    w_router,
    w_gate_t,
    w_up_t,
    w_down_t,
    ws_gate,
    ws_up,
    ws_down_t,
):
    half_tokens, width = hidden.shape
    rows = lax.axis_size("row")
    cols = lax.axis_size("col")
    seq = lax.axis_index("seq")
    col = lax.axis_index("col")
    tokens = 2 * half_tokens
    inner = conv_x.shape[1] // 2
    heads = dt_bias.shape[0] // 2
    head_width = inner // heads
    state = conv_bc.shape[1] // 2
    experts = w_router.shape[1]
    hidden_units = w_gate_t.shape[2]
    shared_units = ws_gate.shape[1] // 2
    lanes = 64
    inner_all = conv_x.shape[1] * cols
    shard = half_tokens // cols

    out_at = 2 * inner + 2 * state
    dt_at = out_at + inner
    mixer_width = dt_at + lanes
    (spread_rows,) = call(
        functools.partial(mixer_rows, inner, heads),
        [((2 * rows, w_z.shape[0], mixer_width), BF)],
        (w_x, w_z, w_bc, out_t, w_dt),
        10**6,
        "mixer_rows",
        12,
    )
    (
        spread_rows,
        hidden,
        cotangent,
        w_gate_t,
        w_up_t,
        w_down_t,
        ws_gate,
        ws_up,
        ws_down_t,
        w_router,
        conv_x,
        gain_gate,
        segments,
        routes,
    ) = lax.optimization_barrier(
        (
            spread_rows,
            hidden,
            cotangent,
            w_gate_t,
            w_up_t,
            w_down_t,
            ws_gate,
            ws_up,
            ws_down_t,
            w_router,
            conv_x,
            gain_gate,
            segments,
            routes,
        )
    )
    mixer_whole = lax.all_to_all(spread_rows, ("row", "seq"), 0, 0).reshape(width, mixer_width)

    inv_mix = lax.rsqrt(jnp.mean(hidden * hidden, axis=1) + EPS)
    mix_own = (hidden * inv_mix[:, None] * gain_mix).astype(BF)
    mix_other = swap(mix_own)
    cot_other = swap(cotangent)
    routes_other = swap(routes)
    flag = seq.astype(jnp.int32)[None]

    down_units = hidden_units + shared_units
    in_units = 2 * down_units
    down_at = in_units + 128
    weight_rows = w_z.shape[0]
    packed = -(-(down_at + down_units) // 128) * 128
    flat = lambda a: a.reshape(weight_rows, 2 * hidden_units)
    pack_own, pack_other = call(
        functools.partial(expert_packs, hidden_units, shared_units),
        [((weight_rows, packed), BF)] * 2,
        (
            flag,
            flat(w_gate_t),
            flat(w_up_t),
            ws_gate,
            ws_up,
            w_router,
            flat(w_down_t),
            ws_down_t,
        ),
        10**6,
        "expert_packs",
        scalars=(0,),
    )
    (expert_rows,) = call(
        joined,
        [((2 * weight_rows, packed), BF)],
        (flag, pack_own, swap(pack_other)),
        10**6,
        "expert_rows",
        scalars=(0,),
    )
    seg_own = segments[None]
    marks, marks_row, taps_x, head_rows, wide_rows = call(
        functools.partial(small_set, inner, heads, head_width),
        [
            ((tokens, 8), F32),
            ((8, tokens), F32),
            ((4, inner), F32),
            ((2, lanes), F32),
            ((2, inner), F32),
        ],
        (flag, dt_bias, a_log, d_skip, seg_own, swap(seg_own), conv_x, gain_gate[None]),
        10**6,
        "small_set",
        scalars=(0, 1, 2, 3),
    )
    expert_rows, mixer_whole, mix_own, mix_other, cot_other, routes_other, marks, marks_row = (
        lax.optimization_barrier(
            (
                expert_rows,
                mixer_whole,
                mix_own,
                mix_other,
                cot_other,
                routes_other,
                marks,
                marks_row,
            )
        )
    )
    expert_whole = lax.all_gather(expert_rows, "row", axis=0, tiled=True)

    fixed = (mixer_whole, marks, marks_row, taps_x, conv_bc, head_rows, wide_rows)
    pre, dt_in, cum, scanned, part_own, part_other, square_own, square_other = call(
        functools.partial(mixer_forward, inner, head_width),
        [
            ((tokens, out_at), F32),
            ((tokens, lanes), F32),
            ((tokens, lanes), F32),
            ((tokens, inner), F32),
            ((half_tokens, width), BF),
            ((half_tokens, width), BF),
            ((half_tokens, 1), F32),
            ((half_tokens, 1), F32),
        ],
        (mix_own, mix_other, *fixed),
        4 * 10**9,
        "mixer_forward",
        28,
        [((tokens, inner), BF)],
        (2,),
    )
    mix_sum = exchange_rows(chip(part_own, part_other, square_own, square_other), "col")
    mix_sum = jnp.sum(mix_sum.astype(F32), axis=0)
    square = mix_sum[:, width : width + 1] + mix_sum[:, width + 1 : width + 2]
    mix_sum = mix_sum[:, :width]

    here = lax.dynamic_slice_in_dim(hidden, col * shard, shard, 0)
    inv_gate_here = lax.rsqrt(square / inner_all + EPS)
    mix_out = mix_sum * inv_gate_here
    residual = here + mix_out
    inv_moe_here = lax.rsqrt(jnp.mean(residual * residual, axis=1, keepdims=True) + EPS)
    moe_here = (residual * inv_moe_here * gain_moe).astype(BF)
    moe_own = from_tokens(
        jnp.concatenate(
            [moe_here, *two(inv_gate_here), *two(inv_moe_here), jnp.zeros((shard, 124), BF)], 1
        )
    )
    inv_moe = one(moe_own[:, width + 2], moe_own[:, width + 3])
    moe_other = swap(moe_own)

    mine = (jnp.arange(experts) == 2 * col + seq).astype(F32)[None, :]
    in_own, in_other, out_own, out_other, in_grads, acts, gates, *gates_grad = call(
        functools.partial(experts_both_ways, hidden_units, shared_units),
        [
            ((half_tokens, width), BF),
            ((half_tokens, width), BF),
            ((half_tokens, width), BF),
            ((half_tokens, width), BF),
            ((tokens, in_units), BF),
            ((tokens, down_units), BF),
            ((tokens, experts), F32),
            ((half_tokens, experts), F32),
            ((half_tokens, experts), F32),
        ],
        (moe_own, moe_other, cotangent, cot_other, expert_whole, routes, routes_other, mine),
        6 * 10**9,
        "experts_both_ways",
        56,
        (),
        (0, 1, 2, 3, 4),
    )
    moe_got = exchange_rows(chip(in_own, in_other, *gates_grad), "col")
    (expert_sums,) = call(
        expert_products,
        [((width, in_units + down_units), BF)],
        (moe_own, moe_other, cotangent, cot_other, in_grads, acts),
        3 * 10**9,
        "expert_products",
        28,
    )
    chip_out = (out_own.astype(F32) + swap(out_other).astype(F32)).astype(BF)
    moe_got, expert_sums, chip_out, cot_here, gates_here, router, gain_row = (
        lax.optimization_barrier(
            (
                moe_got,
                expert_sums,
                chip_out,
                lax.dynamic_slice_in_dim(cotangent, col * shard, shard, 0),
                lax.dynamic_slice_in_dim(gates, col * shard, shard, 0),
                expert_whole[:, in_units : in_units + experts],
                gain_moe[None],
            )
        )
    )
    expert_sums = lax.psum_scatter(expert_sums, "row", scatter_dimension=0, tiled=True)

    sent, residual_grad, gain_moe_grad = call(
        second_shard,
        [((shard, width + 128), BF), ((shard, width), F32), ((1, width), F32)],
        (
            moe_got,
            residual,
            mix_out,
            cot_here,
            gates_here,
            router,
            inv_moe_here,
            gain_row,
        ),
        10**7,
        "second_shard",
    )
    grad_own = from_tokens(sent)

    grad_own, chip_out = lax.optimization_barrier((grad_own, chip_out))
    grad_other = swap(grad_own)
    out_got = exchange_rows(chip_out, "col")

    grads, dt_grad, normed_gate, part_own, part_other, small = call(
        functools.partial(mixer_backward, inner, inner_all, head_width, experts),
        [
            ((tokens, out_at), BF),
            ((tokens, lanes), BF),
            ((tokens, inner), BF),
            ((half_tokens, width), BF),
            ((half_tokens, width), BF),
            ((SMALL_ROWS, 128), F32),
        ],
        (grad_own, grad_other, moe_own, moe_other, *fixed, pre, dt_in, cum, scanned),
        5 * 10**9,
        "mixer_backward",
        56,
        [
            ((tokens, inner), BF),
            ((tokens, inner), BF),
            ((tokens, inner), F32),
            ((tokens, state), F32),
            ((tokens, state), F32),
        ],
        (0, 1, 2, 3, 4, 11, 12, 13, 14),
    )
    chip_in = (part_own.astype(F32) + swap(part_other).astype(F32)).astype(BF)
    chip_in, out_got = lax.optimization_barrier((chip_in, out_got))
    output_here = residual + jnp.sum(out_got.astype(F32), axis=0)
    output = 2.0 * lax.all_gather(
        after(0.5 * output_here, expert_sums), "col", axis=0, tiled=True
    )
    mix_in_got = exchange_rows(chip_in, "col")
    (mixer_sums,) = call(
        functools.partial(mixer_products, inner, experts),
        [((2 * rows, w_z.shape[0], mixer_width + 128), BF)],
        (
            mix_own,
            mix_other,
            grad_own,
            grad_other,
            moe_own,
            moe_other,
            grads,
            dt_grad,
            normed_gate,
        ),
        2 * 10**9,
        "mixer_products",
        28,
    )
    mix_in_got, mixer_sums = lax.optimization_barrier((mix_in_got, mixer_sums))
    mix_in_grad = jnp.sum(mix_in_got.astype(F32), axis=0)

    inv_here = lax.dynamic_slice_in_dim(inv_mix, col * shard, shard, 0)[:, None]
    scaled_mix = mix_in_grad * gain_mix
    grad_hidden_here = (
        residual_grad
        + inv_here * scaled_mix
        - here * (inv_here**3 * jnp.mean(scaled_mix * here, axis=1, keepdims=True))
    )
    gain_mix_grad = jnp.sum(mix_in_grad * here * inv_here, axis=0)

    gains = jnp.concatenate([gain_mix_grad.reshape(-1, 128), gain_moe_grad.reshape(-1, 128)])
    small = jnp.concatenate([gains, small[TAPS_BC_ROW:]]).astype(BF)
    mixer_sums = lax.dynamic_update_slice(
        mixer_sums, jnp.broadcast_to(small[None], (2 * rows, *small.shape)), (0, 0, mixer_width)
    )
    got = lax.all_to_all(mixer_sums, ("row", "seq"), 0, 0)
    grad_hidden = from_tokens(grad_hidden_here.astype(BF))
    grad_hidden = grad_hidden.astype(F32)

    own = own_half(expert_sums, 0)
    other = swap(other_half(expert_sums, 0))

    def expert(at):
        a = own[:, None, at : at + hidden_units]
        return join(a, other[:, None, at : at + hidden_units], 1).astype(F32)

    def shared(at):
        return join(
            own[:, at : at + shared_units], other[:, at : at + shared_units], 1
        ).astype(F32)

    g_w_gate_t = expert(0)
    g_w_up_t = expert(hidden_units)
    g_w_down_t = expert(in_units)
    g_ws_gate = shared(2 * hidden_units)
    g_ws_up = shared(2 * hidden_units + shared_units)
    g_ws_down_t = shared(in_units + hidden_units)
    (
        got,
        grad_hidden,
        g_w_gate_t,
        g_w_up_t,
        g_w_down_t,
        g_ws_gate,
        g_ws_up,
        g_ws_down_t,
        inv_moe,
    ) = lax.optimization_barrier(
        (
            got,
            grad_hidden,
            g_w_gate_t,
            g_w_up_t,
            g_w_down_t,
            g_ws_gate,
            g_ws_up,
            g_ws_down_t,
            inv_moe,
        )
    )
    (
        g_out_t,
        g_w_z,
        g_w_x,
        g_w_dt,
        g_w_router,
        g_conv_x,
        g_gain_gate,
        by_heads,
        sent,
    ) = call(
        functools.partial(tail_sums, inner, heads),
        [
            ((weight_rows, 2 * inner), F32),
            ((weight_rows, 2 * inner), F32),
            ((weight_rows, 2 * inner), F32),
            ((weight_rows, 2 * heads), F32),
            ((weight_rows, experts), F32),
            ((4, 2 * inner), F32),
            ((1, 2 * inner), F32),
            ((3, 2 * heads), F32),
            ((weight_rows + 32, 2 * state), BF),
        ],
        (got,),
        10**7,
        "tail_sums",
        16,
    )
    g_gain_gate = g_gain_gate.reshape(-1)
    g_dt_bias, g_a_log, g_d_skip = by_heads[0], by_heads[1], by_heads[2]
    got = lax.all_to_all(jnp.broadcast_to(sent[None], (cols, *sent.shape)), "col", 0, 0)
    got, output = lax.optimization_barrier((got, output))
    g_w_bc, g_gain_mix, g_gain_moe, g_conv_bc = call(
        last_sums,
        [
            ((weight_rows, 2 * state), F32),
            ((width // 128, 128), F32),
            ((width // 128, 128), F32),
            ((4, 2 * state), F32),
        ],
        (got,),
        10**6,
        "last_sums",
    )
    g_gain_mix, g_gain_moe = g_gain_mix.reshape(-1), g_gain_moe.reshape(-1)

    return (
        output,
        grad_hidden,
        inv_mix,
        inv_moe,
        g_gain_mix,
        g_w_z,
        g_w_x,
        g_w_bc,
        g_w_dt,
        g_conv_x,
        g_conv_bc,
        g_dt_bias,
        g_a_log,
        g_d_skip,
        g_gain_gate,
        g_out_t,
        g_gain_moe,
        g_w_router,
        g_w_gate_t,
        g_w_up_t,
        g_w_down_t,
        g_ws_gate,
        g_ws_up,
        g_ws_down_t,
    )


def solution(mesh):
    placed = (
        P(("row", "seq"), None),
        P(("row", "seq"), None),
        P(("row", "seq")),
        P(("row", "seq"), None),
        P(),
        P(("row", "seq"), "col"),
        P(("row", "seq"), "col"),
        P(("row", "seq"), None),
        P(("row", "seq"), "col"),
        P(None, "col"),
        P(),
        P("col"),
        P("col"),
        P("col"),
        P("col"),
        P(("row", "seq"), "col"),
        P(),
        P(("row", "seq"), None),
        P(("row", "seq"), "col", None),
        P(("row", "seq"), "col", None),
        P(("row", "seq"), "col", None),
        P(("row", "seq"), "col"),
        P(("row", "seq"), "col"),
        P(("row", "seq"), "col"),
    )
    return jax.shard_map(
        on_device,
        mesh=mesh,
        in_specs=placed,
        out_specs=(
            P(("row", "seq"), None),
            P(("row", "seq"), None),
            P(("row", "seq")),
            P(("row", "seq")),
            P(),
            P(("row", "seq"), "col"),
            P(("row", "seq"), "col"),
            P(("row", "seq"), None),
            P(("row", "seq"), "col"),
            P(None, "col"),
            P(),
            P("col"),
            P("col"),
            P("col"),
            P("col"),
            P(("row", "seq"), "col"),
            P(),
            P(("row", "seq"), None),
            P(("row", "seq"), "col", None),
            P(("row", "seq"), "col", None),
            P(("row", "seq"), "col", None),
            P(("row", "seq"), "col"),
            P(("row", "seq"), "col"),
            P(("row", "seq"), "col"),
        ),
        check_vma=False,
    )
```

```python
import functools

import jax
import jax.numpy as jnp
from jax import lax
from jax.experimental import pallas as pl
from jax.experimental.pallas import tpu as pltpu
from jax.sharding import PartitionSpec as P

EPS = 1e-05
BF = jnp.bfloat16
F32 = jnp.float32
FAR = -1e30
TAPS_BC_ROW, TAPS_X_ROW, GATE_ROW, HEAD_ROW, SMALL_ROWS = 24, 32, 40, 42, 48


def silu(v):
    return v * jax.nn.sigmoid(v)


def nn(left, right):
    return lax.dot_general(left, right, (((1,), (0,)), ((), ())), preferred_element_type=F32)


def nt(left, right):
    return lax.dot_general(left, right, (((1,), (1,)), ((), ())), preferred_element_type=F32)


def tn(left, right):
    return lax.dot_general(left, right, (((0,), (0,)), ((), ())), preferred_element_type=F32)


def swap(value):
    return lax.ppermute(value, "seq", [(0, 1), (1, 0)])


def half(value, axis, which):
    size = value.shape[axis] // 2
    return lax.slice_in_dim(value, which * size, (which + 1) * size, axis=axis)


def own_half(value, axis):
    first = lax.axis_index("seq") == 0
    return jnp.where(first, half(value, axis, 0), half(value, axis, 1))


def other_half(value, axis):
    first = lax.axis_index("seq") == 0
    return jnp.where(first, half(value, axis, 1), half(value, axis, 0))


def join(own, other, axis):
    first = lax.axis_index("seq") == 0
    return jnp.where(
        first, jnp.concatenate([own, other], axis), jnp.concatenate([other, own], axis)
    )


def low(value):
    return lax.reduce_precision(value, 8, 7)


def two(value):
    high = low(value)
    return high.astype(BF), (value - high).astype(BF)


def three(value):
    high = value.astype(BF)
    rest = value - high.astype(F32)
    middle = rest.astype(BF)
    return high, middle, (rest - middle.astype(F32)).astype(BF)


def exact(left, value):
    high, middle, last = three(value)
    return (nn(left, last) + nn(left, middle)) + nn(left, high)


def one(high, low_term):
    return high.astype(F32) + low_term.astype(F32)


def after(value, *others):
    return lax.optimization_barrier((value, *others))[0]


def call(kernel, outs, args, flops, name, room=12, scratch=(), apart=(), scalars=()):
    whole = pl.BlockSpec(memory_space=pltpu.VMEM)
    spec = {i: pl.BlockSpec(memory_space=pltpu.HBM) for i in apart}
    spec.update({i: pl.BlockSpec(memory_space=pltpu.SMEM) for i in scalars})
    shapes = [jax.ShapeDtypeStruct(shape, kind) for shape, kind in outs]
    size = lambda a: a.size * jnp.dtype(a.dtype).itemsize
    held = [pltpu.VMEM(args[i].shape, args[i].dtype) for i in apart]
    if apart:
        held.append(pltpu.SemaphoreType.DMA((len(apart) + 1,)))
    return pl.pallas_call(
        kernel,
        out_shape=shapes,
        in_specs=[spec.get(i, whole) for i in range(len(args))],
        out_specs=[whole] * len(outs),
        scratch_shapes=[pltpu.VMEM(shape, kind) for shape, kind in scratch] + held,
        compiler_params=pltpu.CompilerParams(vmem_limit_bytes=room * 2**20),
        cost_estimate=pl.CostEstimate(
            flops=flops,
            bytes_accessed=sum(size(a) for a in args) + sum(size(a) for a in shapes),
            transcendentals=0,
        ),
        name=name,
    )(*args)


def fetched(pairs, sems):
    copies = [
        pltpu.make_async_copy(src, dst, sems.at[k]) for k, (src, dst) in enumerate(pairs)
    ]
    for copy in copies:
        copy.start()
    return copies


def causal(marks, marks_row, rows):
    return (marks[rows, 1:2] >= marks_row[1:2, :]) & (marks[rows, 0:1] == marks_row[0:1, :])


def convolved(value, taps, marks):
    total = taps[3:4, :] * value
    for lag in range(1, 4):
        rolled = pltpu.roll(value, lag, 0) * marks[:, 1 + lag : 2 + lag]
        total = total + taps[3 - lag : 4 - lag, :] * rolled
    return total


def head_columns(inner, lanes, head_width):
    down = lax.broadcasted_iota(jnp.int32, (inner, lanes), 0)
    across = lax.broadcasted_iota(jnp.int32, (inner, lanes), 1) * head_width
    return jnp.where((down >= across) & (down < across + head_width), 1.0, 0.0).astype(BF)


def by_head(value, columns):
    high, middle, last = three(value)
    return (nn(last, columns) + nn(middle, columns)) + nn(high, columns)


def softplus(v):
    return jnp.maximum(v, 0.0) + jnp.log1p(jnp.exp(-jnp.abs(v)))


def mixer_forward(
    inner,
    head_width,
    own_ref,
    other_ref,
    w_src,
    w_bc_src,
    marks_ref,
    row_ref,
    taps_x_ref,
    taps_bc_ref,
    head_ref,
    wide_ref,
    pre_ref,
    dt_ref,
    cum_ref,
    scanned_ref,
    part_own_ref,
    part_other_ref,
    square_own_ref,
    square_other_ref,
    scaled_ref,
    w_ref,
    w_bc_ref,
    sems,
):
    half_tokens, width = own_ref.shape
    tokens = 2 * half_tokens
    heads = inner // head_width
    bc_at, out_at = 2 * inner, pre_ref.shape[1]
    dt_at = bc_at + inner
    state = (out_at - bc_at) // 2
    copies = fetched(
        (
            (w_src.at[:, :bc_at], w_ref.at[:, :bc_at]),
            (w_bc_src, w_bc_ref),
            (w_src.at[:, bc_at:], w_ref.at[:, bc_at:]),
        ),
        sems,
    )
    for part, src in ((0, own_ref), (1, other_ref)):
        rows = slice(part * half_tokens, (part + 1) * half_tokens)
        if part == 0:
            copies[0].wait()
        pre_ref[rows, :bc_at] = nn(src[...], w_ref[:, :bc_at])
        if part == 0:
            copies[1].wait()
        pre_ref[rows, bc_at:] = nn(src[...], w_bc_ref[...])
        if part == 0:
            copies[2].wait()
        dt_ref[rows, :] = nn(src[...], w_ref[:, dt_at:]) + head_ref[0:1, :]
    marks, marks_row = marks_ref[...], row_ref[...]
    x_conv = silu(convolved(pre_ref[:, :inner], taps_x_ref[...], marks))
    bc = silu(convolved(pre_ref[:, bc_at:out_at], taps_bc_ref[...], marks)).astype(BF)
    b_map, c_map = bc[:, :state], bc[:, state:]
    step = softplus(dt_ref[...])
    lower = jnp.where(marks[:, 1:2] >= marks_row[1:2, :], 1.0, 0.0).astype(BF)
    cum = exact(lower, -step * head_ref[1:2, :])
    cum_ref[...] = cum
    cum_row = jnp.concatenate([cum, jnp.zeros_like(cum)], 1).T
    for h in range(heads):
        here = slice(h * head_width, (h + 1) * head_width)
        scaled_ref[:, here] = (x_conv[:, here] * step[:, h : h + 1]).astype(BF)
    block = 128
    for at in range(0, tokens, block):
        rows = slice(at, at + block)
        scores = nt(c_map[rows, :], b_map)
        mask = causal(marks, marks_row, rows)
        for h in range(heads):
            here = slice(h * head_width, (h + 1) * head_width)
            gap = cum[rows, h : h + 1] - cum_row[h : h + 1, :]
            mix = (jnp.exp(jnp.where(mask, gap, FAR)) * scores).astype(BF)
            scanned_ref[rows, here] = nn(mix, scaled_ref[:, here])
    mixer_out = scanned_ref[...] + wide_ref[0:1, :] * x_conv
    gated = mixer_out * silu(pre_ref[:, inner:bc_at])
    square = jnp.sum(gated * gated, axis=1, keepdims=True)
    square_own_ref[...] = square[:half_tokens]
    square_other_ref[...] = square[half_tokens:]
    sent = (gated * wide_ref[1:2, :]).astype(BF)
    out_w = w_ref[:, bc_at:dt_at]
    part_own_ref[...] = nt(sent[:half_tokens], out_w).astype(BF)
    part_other_ref[...] = nt(sent[half_tokens:], out_w).astype(BF)


def mixer_backward(
    inner,
    inner_all,
    head_width,
    experts,
    own_src,
    other_src,
    moe_own_src,
    moe_other_src,
    w_src,
    w_bc_src,
    marks_src,
    row_src,
    taps_x_src,
    taps_bc_src,
    head_src,
    wide_src,
    pre_src,
    dt_src,
    cum_src,
    scanned_src,
    grads_ref,
    dt_grad_ref,
    normed_ref,
    part_own_ref,
    part_other_ref,
    small_ref,
    scaled_ref,
    low_ref,
    spread_ref,
    c_grad_ref,
    b_grad_ref,
    own_ref,
    other_ref,
    moe_own_ref,
    moe_other_ref,
    w_ref,
    w_bc_ref,
    marks_ref,
    row_ref,
    taps_x_ref,
    taps_bc_ref,
    head_ref,
    wide_ref,
    pre_ref,
    dt_ref,
    cum_ref,
    scanned_ref,
    sems,
):
    half_tokens = own_ref.shape[0]
    width = w_ref.shape[0]
    split = 2 * inner
    copies = fetched(
        (
            (w_src.at[:, split:], w_ref.at[:, split:]),
            (own_src, own_ref),
            (other_src, other_ref),
            (moe_own_src.at[:, width:], moe_own_ref.at[:, width:]),
            (moe_other_src.at[:, width:], moe_other_ref.at[:, width:]),
            (pre_src, pre_ref),
            (scanned_src, scanned_ref),
            (dt_src, dt_ref),
            (cum_src, cum_ref),
            (marks_src, marks_ref),
            (row_src, row_ref),
            (taps_x_src, taps_x_ref),
            (taps_bc_src, taps_bc_ref),
            (head_src, head_ref),
            (wide_src, wide_ref),
            (w_src.at[:, :split], w_ref.at[:, :split]),
            (w_bc_src, w_bc_ref),
        ),
        sems,
    )
    tokens = 2 * half_tokens
    heads = inner // head_width
    bc_at, out_at = 2 * inner, pre_ref.shape[1]
    dt_at = bc_at + inner
    state = (out_at - bc_at) // 2
    stack = lambda a, b: jnp.concatenate([a, b], 0)
    for copy in copies[:3]:
        copy.wait()
    out_w = w_ref[:, bc_at:dt_at]
    gate_norm_grad = stack(
        nn(own_ref[:, :width], out_w), nn(other_ref[:, :width], out_w)
    )
    for copy in copies[3:15]:
        copy.wait()
    marks, marks_row = marks_ref[...], row_ref[...]
    conv_x = convolved(pre_ref[:, :inner], taps_x_ref[...], marks)
    conv_bc = convolved(pre_ref[:, bc_at:out_at], taps_bc_ref[...], marks)
    x_conv = silu(conv_x)
    bc = silu(conv_bc).astype(BF)
    b_map, c_map = bc[:, :state], bc[:, state:]
    z_pre = pre_ref[:, inner:bc_at]
    step = softplus(dt_ref[...])
    rate = head_ref[1:2, :]
    skip_wide, gain = wide_ref[0:1, :], wide_ref[1:2, :]
    at = width + experts
    dots = lambda ref: one(ref[:, at : at + 1], ref[:, at + 1 : at + 2])
    gate_dot = stack(dots(own_ref), dots(other_ref))
    gates = lambda ref: one(ref[:, width : width + 1], ref[:, width + 1 : width + 2])
    inv_gate = stack(gates(moe_own_ref), gates(moe_other_ref))
    sig = jax.nn.sigmoid(z_pre)
    silu_z = z_pre * sig
    mixer_out = scanned_ref[...] + skip_wide * x_conv
    gated = mixer_out * silu_z
    normed = gated * inv_gate
    small_ref[...] = jnp.zeros_like(small_ref)

    def keep_small(row, value):
        for at in range(0, value.shape[1], 128):
            piece = value[:, at : at + 128]
            small_ref[row : row + 1, : piece.shape[1]] = piece
            row = row + 1

    keep_small(GATE_ROW, jnp.sum(gate_norm_grad * normed, axis=0, keepdims=True))
    normed_ref[...] = (normed * gain).astype(BF)
    gated_grad = inv_gate * (gate_norm_grad * gain) - gated * (
        inv_gate * inv_gate * gate_dot * (1.0 / inner_all)
    )
    ssm_grad = gated_grad * silu_z
    grads_ref[:, inner:bc_at] = (
        gated_grad * mixer_out * (sig * (1.0 + z_pre * (1.0 - sig)))
    ).astype(BF)
    columns = head_columns(inner, dt_ref.shape[1], head_width)
    skips = by_head(
        jnp.broadcast_to(jnp.sum(ssm_grad * x_conv, axis=0, keepdims=True), (8, inner)), columns
    )
    keep_small(HEAD_ROW + 2, skips[0:1, :heads])
    low_ref[...] = ssm_grad.astype(BF)
    for h in range(heads):
        here = slice(h * head_width, (h + 1) * head_width)
        scaled_ref[:, here] = (x_conv[:, here] * step[:, h : h + 1]).astype(BF)
    cum = cum_ref[...]
    cum_row = jnp.concatenate([cum, jnp.zeros_like(cum)], 1).T
    c_grad_ref[...] = jnp.zeros_like(c_grad_ref)
    block = 128
    for start in range(0, tokens, block):
        rows = slice(start, start + block)
        scores = nt(b_map[rows, :], c_map)
        mask = (marks_row[1:2, :] >= marks[rows, 1:2]) & (
            marks_row[0:1, :] == marks[rows, 0:1]
        )
        scores_grad = jnp.zeros((block, tokens), F32)
        for h in range(heads):
            here = slice(h * head_width, (h + 1) * head_width)
            gap = cum_row[h : h + 1, :] - cum[rows, h : h + 1]
            decay = jnp.exp(jnp.where(mask, gap, FAR))
            spread_ref[rows, here] = nn((decay * scores).astype(BF), low_ref[:, here])
            scores_grad = scores_grad + decay * nt(scaled_ref[rows, here], low_ref[:, here])
        scores_low = scores_grad.astype(BF)
        b_grad_ref[rows, :] = nn(scores_low, c_map)
        c_grad_ref[...] += tn(scores_low, b_map[rows, :])
    spread = spread_ref[...]
    step_grad = by_head(x_conv * spread, columns)
    cum_grad = by_head(
        low_ref[...].astype(F32) * scanned_ref[...] - scaled_ref[...].astype(F32) * spread, columns
    )
    upper = jnp.where(marks_row[1:2, :] >= marks[:, 1:2], 1.0, 0.0).astype(BF)
    decay_grad = exact(upper, cum_grad)
    dt_float = (step_grad - decay_grad * rate) * jax.nn.sigmoid(dt_ref[...])
    keep_small(HEAD_ROW, jnp.sum(dt_float, axis=0, keepdims=True)[:, :heads])
    keep_small(
        HEAD_ROW + 1, jnp.sum(decay_grad * (-step * rate), axis=0, keepdims=True)[:, :heads]
    )
    dt_low = dt_float.astype(BF)
    dt_grad_ref[...] = dt_low
    for h in range(heads):
        here = slice(h * head_width, (h + 1) * head_width)
        spread_ref[:, here] = spread[:, here] * step[:, h : h + 1]

    def back(value_grad, total, value, taps, small_row, to):
        sig_c = jax.nn.sigmoid(total)
        grad = value_grad * (sig_c * (1.0 + total * (1.0 - sig_c)))
        keep_small(small_row + 6, jnp.sum(grad * value, axis=0, keepdims=True))
        result = taps[3:4, :] * grad
        for lag in range(1, 4):
            kept = grad * marks[:, 1 + lag : 2 + lag]
            keep_small(
                small_row + 2 * (3 - lag),
                jnp.sum(kept * pltpu.roll(value, lag, 0), axis=0, keepdims=True),
            )
            result = result + taps[3 - lag : 4 - lag, :] * pltpu.roll(kept, tokens - lag, 0)
        grads_ref[:, to] = result.astype(BF)

    back(
        spread_ref[...] + ssm_grad * skip_wide,
        conv_x,
        pre_ref[:, :inner],
        taps_x_ref[...],
        TAPS_X_ROW,
        slice(0, inner),
    )
    back(
        jnp.concatenate([b_grad_ref[...], c_grad_ref[...]], 1),
        conv_bc,
        pre_ref[:, bc_at:out_at],
        taps_bc_ref[...],
        TAPS_BC_ROW,
        slice(bc_at, out_at),
    )
    copies[15].wait()
    copies[16].wait()
    for part, dst in ((0, part_own_ref), (1, part_other_ref)):
        rows = slice(part * half_tokens, (part + 1) * half_tokens)
        dst[...] = (
            nt(grads_ref[rows, :bc_at], w_ref[:, :bc_at])
            + nt(grads_ref[rows, bc_at:], w_bc_ref[...])
            + nt(dt_low[rows, :], w_ref[:, dt_at:])
        ).astype(BF)


def mixer_products(
    inner,
    experts,
    own_ref,
    other_ref,
    mix_own_ref,
    mix_other_ref,
    moe_own_ref,
    moe_other_ref,
    grads_ref,
    dt_grad_ref,
    normed_ref,
    sums_ref,
):
    half_tokens, width = own_ref.shape
    out_at = grads_ref.shape[1]
    dt_at = out_at + inner
    count = sums_ref.shape[0]
    rows = width // count
    group = min(8, count)
    first, second = slice(0, half_tokens), slice(half_tokens, 2 * half_tokens)
    logits = slice(width, width + experts)
    for at in range(0, count, group):
        here = slice(at * rows, (at + group) * rows)
        mine, others = own_ref[:, here], other_ref[:, here]
        a = tn(mine, grads_ref[first, :]) + tn(others, grads_ref[second, :])
        b = tn(mix_own_ref[:, here], normed_ref[first, :]) + tn(
            mix_other_ref[:, here], normed_ref[second, :]
        )
        c = tn(mine, dt_grad_ref[first, :]) + tn(others, dt_grad_ref[second, :])
        d = tn(moe_own_ref[:, here], mix_own_ref[:, logits]) + tn(
            moe_other_ref[:, here], mix_other_ref[:, logits]
        )
        a, b, c, d = a.astype(BF), b.astype(BF), c.astype(BF), d.astype(BF)
        for k in range(group):
            part = slice(k * rows, (k + 1) * rows)
            sums_ref[at + k, :, :out_at] = a[part]
            sums_ref[at + k, :, out_at:dt_at] = b[part]
            sums_ref[at + k, :, dt_at : dt_at + 64] = c[part]
            sums_ref[at + k, :, dt_at + 16 : dt_at + 16 + experts] = d[part]
            sums_ref[at + k, :, dt_at + 64 :] = jnp.zeros((rows, 128), BF)


def experts_both_ways(
    units,
    shared,
    own_ref,
    other_ref,
    cot_own_ref,
    cot_other_ref,
    w_ref,
    routes_own_ref,
    routes_other_ref,
    mine_ref,
    in_own_ref,
    in_other_ref,
    out_own_ref,
    out_other_ref,
    grads_ref,
    acts_ref,
    gates_ref,
    gates_grad_own_ref,
    gates_grad_other_ref,
):
    half_tokens = own_ref.shape[0]
    width = w_ref.shape[0]
    experts = mine_ref.shape[1]
    in_units = 2 * (units + shared)
    down_at = in_units + 128
    mine = mine_ref[...]
    number = lax.broadcasted_iota(jnp.int32, (half_tokens, experts), 1)
    down_end = down_at + units + shared
    parts = (
        (own_ref, cot_own_ref, routes_own_ref, in_own_ref, out_own_ref, gates_grad_own_ref),
        (
            other_ref,
            cot_other_ref,
            routes_other_ref,
            in_other_ref,
            out_other_ref,
            gates_grad_other_ref,
        ),
    )
    for part, (src, cot, routes, in_dst, out_dst, gates_dst) in enumerate(parts):
        rows = slice(part * half_tokens, (part + 1) * half_tokens)
        back = nn(cot[...], w_ref[:, down_at:down_end])
        pre = nn(src[:, :width], w_ref[:, :down_at])
        named = number == routes[:, 0:1]
        for k in range(1, routes.shape[1]):
            named = named | (number == routes[:, k : k + 1])
        logits = jnp.where(named, pre[:, in_units : in_units + experts], FAR)
        raised = jnp.exp(logits - jnp.max(logits, axis=1, keepdims=True))
        gates = raised / jnp.sum(raised, axis=1, keepdims=True)
        gates_ref[rows, :] = gates
        weight = jnp.sum(gates * mine, axis=1, keepdims=True)
        gate, up = pre[:, :units], pre[:, units : 2 * units]
        sig = jax.nn.sigmoid(gate)
        silu_gate = gate * sig
        act = silu_gate * up
        acts_ref[rows, :units] = (act * weight).astype(BF)
        act_back = back[:, :units]
        gates_dst[...] = jnp.sum(act * act_back, axis=1, keepdims=True) * mine
        act_grad = act_back * weight
        grads_ref[rows, :units] = (
            act_grad * up * (sig * (1.0 + gate * (1.0 - sig)))
        ).astype(BF)
        grads_ref[rows, units : 2 * units] = (act_grad * silu_gate).astype(BF)
        gate, up = pre[:, 2 * units : 2 * units + shared], pre[:, 2 * units + shared : in_units]
        sig = jax.nn.sigmoid(gate)
        silu_gate = gate * sig
        acts_ref[rows, units:] = (silu_gate * up).astype(BF)
        act_grad = back[:, units:]
        grads_ref[rows, 2 * units : 2 * units + shared] = (
            act_grad * up * (sig * (1.0 + gate * (1.0 - sig)))
        ).astype(BF)
        grads_ref[rows, 2 * units + shared :] = (act_grad * silu_gate).astype(BF)
        in_dst[...] = nt(grads_ref[rows, :], w_ref[:, :in_units]).astype(BF)
        out_dst[...] = nt(acts_ref[rows, :], w_ref[:, down_at:down_end]).astype(BF)


def expert_products(
    own_ref, other_ref, cot_own_ref, cot_other_ref, grads_ref, acts_ref, sums_ref
):
    half_tokens, width = cot_own_ref.shape
    split = grads_ref.shape[1]
    first, second = slice(0, half_tokens), slice(half_tokens, 2 * half_tokens)
    block = 256
    for at in range(0, width, block):
        here = slice(at, at + block)
        sums_ref[here, :split] = (
            tn(own_ref[:, here], grads_ref[first, :]) + tn(other_ref[:, here], grads_ref[second, :])
        ).astype(BF)
        sums_ref[here, split:] = (
            tn(cot_own_ref[:, here], acts_ref[first, :])
            + tn(cot_other_ref[:, here], acts_ref[second, :])
        ).astype(BF)


def tail_sums(
    inner,
    heads,
    got_ref,
    out_ref,
    z_ref,
    x_ref,
    dt_ref,
    router_ref,
    conv_ref,
    gain_ref,
    head_ref,
    sent_ref,
):
    count, rows = got_ref.shape[0], out_ref.shape[0]
    experts = router_ref.shape[1]
    bc_at = 2 * inner
    small_at = got_ref.shape[2] - 128
    dt_at = small_at - 64
    out_at = dt_at - inner
    totals = []
    for core in range(2):
        total = got_ref[core].astype(F32)
        for at in range(core + 2, count, 2):
            total = total + got_ref[at].astype(F32)
        totals.append(total)
        here = slice(core * inner, (core + 1) * inner)
        x_ref[:, here] = total[:, :inner]
        z_ref[:, here] = total[:, inner:bc_at]
        out_ref[:, here] = total[:, out_at:dt_at]
        dt_ref[:, core * heads : (core + 1) * heads] = total[:, dt_at : dt_at + heads]
        small = total[:SMALL_ROWS, small_at:]

        def row_of(at):
            return jnp.concatenate([small[at : at + 1], small[at + 1 : at + 2, : inner - 128]], 1)

        for k in range(conv_ref.shape[0]):
            conv_ref[k : k + 1, here] = row_of(TAPS_X_ROW + 2 * k)
        gain_ref[:, here] = row_of(GATE_ROW)
        for k in range(3):
            head_ref[k : k + 1, core * heads : (core + 1) * heads] = small[
                HEAD_ROW + k : HEAD_ROW + k + 1, :heads
            ]
    router_ref[...] = totals[0][:, dt_at + 16 : dt_at + 16 + experts]
    sent_ref[:rows, :] = (totals[0][:, bc_at:out_at] + totals[1][:, bc_at:out_at]).astype(BF)
    small = totals[0][:TAPS_X_ROW, small_at:] + totals[1][:TAPS_X_ROW, small_at:]
    high = small.astype(BF)
    sent_ref[rows:, :128] = high
    sent_ref[rows:, 128:] = (small - high.astype(F32)).astype(BF)


def last_sums(got_ref, bc_ref, mix_ref, moe_ref, conv_ref):
    rows = bc_ref.shape[0]
    total = got_ref[0].astype(F32)
    for at in range(1, got_ref.shape[0]):
        total = total + got_ref[at].astype(F32)
    bc_ref[...] = total[:rows]
    small = total[rows:, :128] + total[rows:, 128:]
    half_rows = TAPS_BC_ROW // 2
    mix_ref[...] = small[:half_rows]
    moe_ref[...] = small[half_rows:TAPS_BC_ROW]
    for k in range(conv_ref.shape[0]):
        for part in range(2):
            at = TAPS_BC_ROW + 2 * k + part
            conv_ref[k : k + 1, part * 128 : (part + 1) * 128] = small[at : at + 1]


def chip_sum(own_ref, other_ref, extra_own_ref, extra_other_ref, sum_ref):
    width, more = own_ref.shape[1], extra_own_ref.shape[1]
    sum_ref[:, :width] = (own_ref[...].astype(F32) + other_ref[...].astype(F32)).astype(BF)
    extra = extra_own_ref[...] + extra_other_ref[...]
    high = extra.astype(BF)
    sum_ref[:, width:] = jnp.zeros((own_ref.shape[0], sum_ref.shape[1] - width), BF)
    sum_ref[:, width : width + more] = high
    sum_ref[:, width + more : width + 2 * more] = (extra - high.astype(F32)).astype(BF)


def second_shard(
    got_ref,
    residual_ref,
    mix_out_ref,
    cot_ref,
    gates_ref,
    router_ref,
    inv_ref,
    gain_ref,
    sent_ref,
    grad_ref,
    gain_grad_ref,
):
    width, experts = residual_ref.shape[1], gates_ref.shape[1]
    total = got_ref[0].astype(F32)
    for at in range(1, got_ref.shape[0]):
        total = total + got_ref[at].astype(F32)
    gates = gates_ref[...]
    gates_grad = total[:, width : width + experts] + total[:, width + experts : width + 2 * experts]
    logits_grad = (
        gates * (gates_grad - jnp.sum(gates * gates_grad, axis=1, keepdims=True))
    ).astype(BF)
    moe_in_grad = total[:, :width] + nt(logits_grad, router_ref[...])
    residual, inv = residual_ref[...], inv_ref[...]
    scaled = moe_in_grad * gain_ref[...]
    mean = jnp.sum(scaled * residual, axis=1, keepdims=True) * (1.0 / width)
    grad = cot_ref[...].astype(F32) + inv * scaled - residual * (inv * inv * inv * mean)
    grad_ref[...] = grad
    gain_grad_ref[...] = jnp.sum(moe_in_grad * residual * inv, axis=0, keepdims=True)
    grad_low = grad.astype(BF)
    gate_dot = jnp.sum(grad_low.astype(F32) * mix_out_ref[...], axis=1, keepdims=True)
    high = gate_dot.astype(BF)
    sent_ref[:, :width] = grad_low
    sent_ref[:, width:] = jnp.zeros((residual.shape[0], sent_ref.shape[1] - width), BF)
    sent_ref[:, width : width + experts] = logits_grad
    sent_ref[:, width + experts : width + experts + 1] = high
    sent_ref[:, width + experts + 1 : width + experts + 2] = (
        gate_dot - high.astype(F32)
    ).astype(BF)


def mixer_rows(
    inner,
    heads,
    x_src,
    z_src,
    out_src,
    dt_src,
    rows_ref,
    x_ref,
    z_ref,
    out_ref,
    dt_ref,
    sems,
):
    copies = fetched(
        ((x_src, x_ref), (z_src, z_ref), (out_src, out_ref), (dt_src, dt_ref)), sems
    )
    for copy in copies:
        copy.wait()
    dt_at = 3 * inner
    for core in range(2):
        here = slice(core * inner, (core + 1) * inner)
        parts = (
            (0, x_ref[:, here]),
            (inner, z_ref[:, here]),
            (2 * inner, out_ref[:, here]),
            (dt_at, jnp.zeros((x_ref.shape[0], rows_ref.shape[2] - dt_at), BF)),
            (dt_at, dt_ref[:, core * heads : (core + 1) * heads]),
        )
        for at, value in parts:
            rows_ref[core, :, at : at + value.shape[1]] = value
        for at in range(core + 2, rows_ref.shape[0], 2):
            rows_ref[at] = rows_ref[core]


def expert_packs(
    units, shared, flag_ref, gate_ref, up_ref, sg_ref, su_ref, router_ref, down_ref, sd_ref, *packs
):
    first = flag_ref[0] == 0
    router_at = 2 * (units + shared)
    down_at = router_at + 128
    for which, dst in enumerate(packs):
        dst[...] = jnp.zeros_like(dst)
        lead = first if which == 0 else jnp.logical_not(first)

        def pick(a, b):
            return jnp.where(lead, a.astype(F32), b.astype(F32)).astype(BF)

        for ref, at in ((gate_ref, 0), (up_ref, units), (down_ref, down_at)):
            dst[:, at : at + units] = pick(ref[:, :units], ref[:, units:])
        for ref, at in (
            (sg_ref, 2 * units),
            (su_ref, 2 * units + shared),
            (sd_ref, down_at + units),
        ):
            dst[:, at : at + shared] = pick(ref[:, :shared], ref[:, shared:])
        dst[:, router_at : router_at + router_ref.shape[1]] = router_ref[...]


def joined(flag_ref, own_ref, other_ref, rows_ref):
    first = flag_ref[0] == 0
    rows = own_ref.shape[0]
    own, other = own_ref[...].astype(F32), other_ref[...].astype(F32)
    rows_ref[:rows] = jnp.where(first, own, other).astype(BF)
    rows_ref[rows:] = jnp.where(first, other, own).astype(BF)


def small_set(
    inner,
    heads,
    head_width,
    flag_ref,
    bias_ref,
    log_ref,
    skip_ref,
    seg_own_ref,
    seg_other_ref,
    taps_ref,
    gain_ref,
    marks_ref,
    row_ref,
    taps_x_ref,
    head_ref,
    wide_ref,
):
    first = flag_ref[0] == 0
    half_tokens = seg_own_ref.shape[1]
    tokens = 2 * half_tokens
    seg = jnp.concatenate([seg_own_ref[...], seg_other_ref[...]], 1).astype(F32)
    seg = jnp.broadcast_to(seg, (8, tokens))
    place = lax.broadcasted_iota(jnp.int32, (8, tokens), 1)
    turned = jnp.where(place < half_tokens, place + half_tokens, place - half_tokens)
    place = jnp.where(first, place, turned).astype(F32)
    before = pltpu.roll(seg, 1, 1)
    hold = jnp.where((seg == before) & (place > 0.0), 1.0, 0.0)
    kept_two = hold * pltpu.roll(hold, 1, 1)
    kept_three = kept_two * pltpu.roll(hold, 2, 1)
    which = lax.broadcasted_iota(jnp.int32, (8, tokens), 0)
    rows = jnp.where(which == 0, seg, 0.0)
    for k, value in enumerate((place, hold, kept_two, kept_three)):
        rows = jnp.where(which == k + 1, value, rows)
    row_ref[...] = rows
    tall = jnp.concatenate([rows, jnp.zeros((120, tokens), F32)], 0)
    marks_ref[...] = tall.T[:, :8]
    taps_x_ref[...] = jnp.where(first, taps_ref[:, :inner], taps_ref[:, inner:])
    lanes = head_ref.shape[1]
    lane = lax.broadcasted_iota(jnp.int32, (1, lanes), 1)
    bias, log, on = jnp.zeros((1, lanes), F32), jnp.zeros((1, lanes), F32), lane < heads
    across = lax.broadcasted_iota(jnp.int32, (1, inner), 1)
    skip = jnp.zeros((1, inner), F32)
    for h in range(heads):
        own = lambda ref: jnp.where(first, ref[h], ref[heads + h])
        bias = jnp.where(lane == h, own(bias_ref), bias)
        log = jnp.where(lane == h, own(log_ref), log)
        skip = jnp.where(
            (across >= h * head_width) & (across < (h + 1) * head_width), own(skip_ref), skip
        )
    head_ref[0:1, :] = bias
    head_ref[1:2, :] = jnp.where(on, jnp.exp(log), 0.0)
    wide_ref[0:1, :] = skip
    wide_ref[1:2, :] = jnp.where(first, gain_ref[:, :inner], gain_ref[:, inner:])


def exchange_rows(part, axis):
    count = lax.axis_size(axis)
    blocks = part.reshape(count, part.shape[0] // count, part.shape[1])
    return lax.all_to_all(blocks, axis, 0, 0, tiled=False)


def chip(own, other, extra_own, extra_other):
    rows, width = own.shape
    extra = call(
        chip_sum,
        [((rows, width + 128), BF)],
        (own, swap(other), extra_own, swap(extra_other)),
        10**6,
        "chip_sum",
    )
    return extra[0]


def from_tokens(own):
    return lax.all_gather(own, "col", axis=0, tiled=True)


def on_device(
    hidden,
    cotangent,
    segments,
    routes,
    gain_mix,
    w_z,
    w_x,
    w_bc,
    w_dt,
    conv_x,
    conv_bc,
    dt_bias,
    a_log,
    d_skip,
    gain_gate,
    out_t,
    gain_moe,
    w_router,
    w_gate_t,
    w_up_t,
    w_down_t,
    ws_gate,
    ws_up,
    ws_down_t,
):
    half_tokens, width = hidden.shape
    rows = lax.axis_size("row")
    cols = lax.axis_size("col")
    seq = lax.axis_index("seq")
    col = lax.axis_index("col")
    tokens = 2 * half_tokens
    inner = conv_x.shape[1] // 2
    heads = dt_bias.shape[0] // 2
    head_width = inner // heads
    state = conv_bc.shape[1] // 2
    experts = w_router.shape[1]
    hidden_units = w_gate_t.shape[2]
    shared_units = ws_gate.shape[1] // 2
    lanes = 64
    inner_all = conv_x.shape[1] * cols
    shard = half_tokens // cols

    out_at = 2 * inner + 2 * state
    dt_at = out_at + inner
    mixer_width = dt_at + lanes
    rows_width = 3 * inner + lanes
    (spread_rows,) = call(
        functools.partial(mixer_rows, inner, heads),
        [((2 * rows, w_z.shape[0], rows_width), BF)],
        (w_x, w_z, out_t, w_dt),
        10**6,
        "mixer_rows",
        56,
        (),
        (0, 1, 2, 3),
    )
    (
        spread_rows,
        w_bc,
        hidden,
        cotangent,
        w_gate_t,
        w_up_t,
        w_down_t,
        ws_gate,
        ws_up,
        ws_down_t,
        w_router,
        conv_x,
        gain_gate,
        segments,
        routes,
    ) = lax.optimization_barrier(
        (
            spread_rows,
            w_bc,
            hidden,
            cotangent,
            w_gate_t,
            w_up_t,
            w_down_t,
            ws_gate,
            ws_up,
            ws_down_t,
            w_router,
            conv_x,
            gain_gate,
            segments,
            routes,
        )
    )
    mixer_whole = lax.all_to_all(spread_rows, ("row", "seq"), 0, 0).reshape(width, rows_width)
    bc_whole = lax.all_gather(w_bc, ("row", "seq"), axis=0, tiled=True)

    inv_mix = lax.rsqrt(jnp.mean(hidden * hidden, axis=1) + EPS)
    mix_own = (hidden * inv_mix[:, None] * gain_mix).astype(BF)
    mix_other = swap(mix_own)
    cot_other = swap(cotangent)
    routes_other = swap(routes)
    flag = seq.astype(jnp.int32)[None]

    down_units = hidden_units + shared_units
    in_units = 2 * down_units
    down_at = in_units + 128
    weight_rows = w_z.shape[0]
    packed = -(-(down_at + down_units) // 128) * 128
    flat = lambda a: a.reshape(weight_rows, 2 * hidden_units)
    pack_own, pack_other = call(
        functools.partial(expert_packs, hidden_units, shared_units),
        [((weight_rows, packed), BF)] * 2,
        (
            flag,
            flat(w_gate_t),
            flat(w_up_t),
            ws_gate,
            ws_up,
            w_router,
            flat(w_down_t),
            ws_down_t,
        ),
        10**6,
        "expert_packs",
        scalars=(0,),
    )
    (expert_rows,) = call(
        joined,
        [((2 * weight_rows, packed), BF)],
        (flag, pack_own, swap(pack_other)),
        10**6,
        "expert_rows",
        scalars=(0,),
    )
    seg_own = segments[None]
    marks, marks_row, taps_x, head_rows, wide_rows = call(
        functools.partial(small_set, inner, heads, head_width),
        [
            ((tokens, 8), F32),
            ((8, tokens), F32),
            ((4, inner), F32),
            ((2, lanes), F32),
            ((2, inner), F32),
        ],
        (flag, dt_bias, a_log, d_skip, seg_own, swap(seg_own), conv_x, gain_gate[None]),
        10**6,
        "small_set",
        scalars=(0, 1, 2, 3),
    )
    (
        expert_rows,
        mixer_whole,
        bc_whole,
        mix_own,
        mix_other,
        cot_other,
        routes_other,
        marks,
        marks_row,
    ) = (
        lax.optimization_barrier(
            (
                expert_rows,
                mixer_whole,
                bc_whole,
                mix_own,
                mix_other,
                cot_other,
                routes_other,
                marks,
                marks_row,
            )
        )
    )
    expert_whole = lax.all_gather(expert_rows, "row", axis=0, tiled=True)

    fixed = (mixer_whole, bc_whole, marks, marks_row, taps_x, conv_bc, head_rows, wide_rows)
    pre, dt_in, cum, scanned, part_own, part_other, square_own, square_other = call(
        functools.partial(mixer_forward, inner, head_width),
        [
            ((tokens, out_at), F32),
            ((tokens, lanes), F32),
            ((tokens, lanes), F32),
            ((tokens, inner), F32),
            ((half_tokens, width), BF),
            ((half_tokens, width), BF),
            ((half_tokens, 1), F32),
            ((half_tokens, 1), F32),
        ],
        (mix_own, mix_other, *fixed),
        4 * 10**9,
        "mixer_forward",
        28,
        [((tokens, inner), BF)],
        (2, 3),
    )
    mix_sum = exchange_rows(chip(part_own, part_other, square_own, square_other), "col")
    mix_sum = jnp.sum(mix_sum.astype(F32), axis=0)
    square = mix_sum[:, width : width + 1] + mix_sum[:, width + 1 : width + 2]
    mix_sum = mix_sum[:, :width]

    here = lax.dynamic_slice_in_dim(hidden, col * shard, shard, 0)
    inv_gate_here = lax.rsqrt(square / inner_all + EPS)
    mix_out = mix_sum * inv_gate_here
    residual = here + mix_out
    inv_moe_here = lax.rsqrt(jnp.mean(residual * residual, axis=1, keepdims=True) + EPS)
    moe_here = (residual * inv_moe_here * gain_moe).astype(BF)
    moe_own = from_tokens(
        jnp.concatenate(
            [moe_here, *two(inv_gate_here), *two(inv_moe_here), jnp.zeros((shard, 124), BF)], 1
        )
    )
    moe_own, expert_whole = lax.optimization_barrier((moe_own, expert_whole))
    inv_moe = one(moe_own[:, width + 2], moe_own[:, width + 3])
    moe_other = swap(moe_own)

    mine = (jnp.arange(experts) == 2 * col + seq).astype(F32)[None, :]
    in_own, in_other, out_own, out_other, in_grads, acts, gates, *gates_grad = call(
        functools.partial(experts_both_ways, hidden_units, shared_units),
        [
            ((half_tokens, width), BF),
            ((half_tokens, width), BF),
            ((half_tokens, width), BF),
            ((half_tokens, width), BF),
            ((tokens, in_units), BF),
            ((tokens, down_units), BF),
            ((tokens, experts), F32),
            ((half_tokens, experts), F32),
            ((half_tokens, experts), F32),
        ],
        (moe_own, moe_other, cotangent, cot_other, expert_whole, routes, routes_other, mine),
        6 * 10**9,
        "experts_both_ways",
        30,
    )
    moe_got = exchange_rows(chip(in_own, in_other, *gates_grad), "col")
    (expert_sums,) = call(
        expert_products,
        [((width, in_units + down_units), BF)],
        (moe_own, moe_other, cotangent, cot_other, in_grads, acts),
        3 * 10**9,
        "expert_products",
        28,
    )
    chip_out = (out_own.astype(F32) + swap(out_other).astype(F32)).astype(BF)
    moe_got, expert_sums, chip_out, cot_here, gates_here, router, gain_row = (
        lax.optimization_barrier(
            (
                moe_got,
                expert_sums,
                chip_out,
                lax.dynamic_slice_in_dim(cotangent, col * shard, shard, 0),
                lax.dynamic_slice_in_dim(gates, col * shard, shard, 0),
                expert_whole[:, in_units : in_units + experts],
                gain_moe[None],
            )
        )
    )
    expert_sums = lax.psum_scatter(expert_sums, "row", scatter_dimension=0, tiled=True)

    sent, residual_grad, gain_moe_grad = call(
        second_shard,
        [((shard, width + 128), BF), ((shard, width), F32), ((1, width), F32)],
        (
            moe_got,
            residual,
            mix_out,
            cot_here,
            gates_here,
            router,
            inv_moe_here,
            gain_row,
        ),
        10**7,
        "second_shard",
    )
    grad_own = from_tokens(sent)

    grad_own, chip_out = lax.optimization_barrier((grad_own, chip_out))
    grad_other = swap(grad_own)
    out_got = exchange_rows(chip_out, "col")

    grads, dt_grad, normed_gate, part_own, part_other, small = call(
        functools.partial(mixer_backward, inner, inner_all, head_width, experts),
        [
            ((tokens, out_at), BF),
            ((tokens, lanes), BF),
            ((tokens, inner), BF),
            ((half_tokens, width), BF),
            ((half_tokens, width), BF),
            ((SMALL_ROWS, 128), F32),
        ],
        (grad_own, grad_other, moe_own, moe_other, *fixed, pre, dt_in, cum, scanned),
        5 * 10**9,
        "mixer_backward",
        56,
        [
            ((tokens, inner), BF),
            ((tokens, inner), BF),
            ((tokens, inner), F32),
            ((tokens, state), F32),
            ((tokens, state), F32),
        ],
        tuple(range(16)),
    )
    chip_in = (part_own.astype(F32) + swap(part_other).astype(F32)).astype(BF)
    chip_in, out_got = lax.optimization_barrier((chip_in, out_got))
    output_here = residual + jnp.sum(out_got.astype(F32), axis=0)
    output = 2.0 * lax.all_gather(
        after(0.5 * output_here, expert_sums), "col", axis=0, tiled=True
    )
    mix_in_got = exchange_rows(chip_in, "col")
    (mixer_sums,) = call(
        functools.partial(mixer_products, inner, experts),
        [((2 * rows, w_z.shape[0], mixer_width + 128), BF)],
        (
            mix_own,
            mix_other,
            grad_own,
            grad_other,
            moe_own,
            moe_other,
            grads,
            dt_grad,
            normed_gate,
        ),
        2 * 10**9,
        "mixer_products",
        28,
    )
    mix_in_got, mixer_sums = lax.optimization_barrier((mix_in_got, mixer_sums))
    mix_in_grad = jnp.sum(mix_in_got.astype(F32), axis=0)

    inv_here = lax.dynamic_slice_in_dim(inv_mix, col * shard, shard, 0)[:, None]
    scaled_mix = mix_in_grad * gain_mix
    grad_hidden_here = (
        residual_grad
        + inv_here * scaled_mix
        - here * (inv_here**3 * jnp.mean(scaled_mix * here, axis=1, keepdims=True))
    )
    gain_mix_grad = jnp.sum(mix_in_grad * here * inv_here, axis=0)

    gains = jnp.concatenate([gain_mix_grad.reshape(-1, 128), gain_moe_grad.reshape(-1, 128)])
    small = jnp.concatenate([gains, small[TAPS_BC_ROW:]]).astype(BF)
    mixer_sums = lax.dynamic_update_slice(
        mixer_sums, jnp.broadcast_to(small[None], (2 * rows, *small.shape)), (0, 0, mixer_width)
    )
    got = lax.all_to_all(mixer_sums, ("row", "seq"), 0, 0)
    grad_hidden = from_tokens(grad_hidden_here.astype(BF))
    grad_hidden = grad_hidden.astype(F32)

    own = own_half(expert_sums, 0)
    other = swap(other_half(expert_sums, 0))

    def expert(at):
        a = own[:, None, at : at + hidden_units]
        return join(a, other[:, None, at : at + hidden_units], 1).astype(F32)

    def shared(at):
        return join(
            own[:, at : at + shared_units], other[:, at : at + shared_units], 1
        ).astype(F32)

    g_w_gate_t = expert(0)
    g_w_up_t = expert(hidden_units)
    g_w_down_t = expert(in_units)
    g_ws_gate = shared(2 * hidden_units)
    g_ws_up = shared(2 * hidden_units + shared_units)
    g_ws_down_t = shared(in_units + hidden_units)
    (
        got,
        grad_hidden,
        g_w_gate_t,
        g_w_up_t,
        g_w_down_t,
        g_ws_gate,
        g_ws_up,
        g_ws_down_t,
        inv_moe,
    ) = lax.optimization_barrier(
        (
            got,
            grad_hidden,
            g_w_gate_t,
            g_w_up_t,
            g_w_down_t,
            g_ws_gate,
            g_ws_up,
            g_ws_down_t,
            inv_moe,
        )
    )
    (
        g_out_t,
        g_w_z,
        g_w_x,
        g_w_dt,
        g_w_router,
        g_conv_x,
        g_gain_gate,
        by_heads,
        sent,
    ) = call(
        functools.partial(tail_sums, inner, heads),
        [
            ((weight_rows, 2 * inner), F32),
            ((weight_rows, 2 * inner), F32),
            ((weight_rows, 2 * inner), F32),
            ((weight_rows, 2 * heads), F32),
            ((weight_rows, experts), F32),
            ((4, 2 * inner), F32),
            ((1, 2 * inner), F32),
            ((3, 2 * heads), F32),
            ((weight_rows + 32, 2 * state), BF),
        ],
        (got,),
        10**7,
        "tail_sums",
        16,
    )
    g_gain_gate = g_gain_gate.reshape(-1)
    g_dt_bias, g_a_log, g_d_skip = by_heads[0], by_heads[1], by_heads[2]
    got = lax.all_to_all(jnp.broadcast_to(sent[None], (cols, *sent.shape)), "col", 0, 0)
    got, output = lax.optimization_barrier((got, output))
    g_w_bc, g_gain_mix, g_gain_moe, g_conv_bc = call(
        last_sums,
        [
            ((weight_rows, 2 * state), F32),
            ((width // 128, 128), F32),
            ((width // 128, 128), F32),
            ((4, 2 * state), F32),
        ],
        (got,),
        10**6,
        "last_sums",
    )
    g_gain_mix, g_gain_moe = g_gain_mix.reshape(-1), g_gain_moe.reshape(-1)

    return (
        output,
        grad_hidden,
        inv_mix,
        inv_moe,
        g_gain_mix,
        g_w_z,
        g_w_x,
        g_w_bc,
        g_w_dt,
        g_conv_x,
        g_conv_bc,
        g_dt_bias,
        g_a_log,
        g_d_skip,
        g_gain_gate,
        g_out_t,
        g_gain_moe,
        g_w_router,
        g_w_gate_t,
        g_w_up_t,
        g_w_down_t,
        g_ws_gate,
        g_ws_up,
        g_ws_down_t,
    )


def solution(mesh):
    placed = (
        P(("row", "seq"), None),
        P(("row", "seq"), None),
        P(("row", "seq")),
        P(("row", "seq"), None),
        P(),
        P(("row", "seq"), "col"),
        P(("row", "seq"), "col"),
        P(("row", "seq"), None),
        P(("row", "seq"), "col"),
        P(None, "col"),
        P(),
        P("col"),
        P("col"),
        P("col"),
        P("col"),
        P(("row", "seq"), "col"),
        P(),
        P(("row", "seq"), None),
        P(("row", "seq"), "col", None),
        P(("row", "seq"), "col", None),
        P(("row", "seq"), "col", None),
        P(("row", "seq"), "col"),
        P(("row", "seq"), "col"),
        P(("row", "seq"), "col"),
    )
    return jax.shard_map(
        on_device,
        mesh=mesh,
        in_specs=placed,
        out_specs=(
            P(("row", "seq"), None),
            P(("row", "seq"), None),
            P(("row", "seq")),
            P(("row", "seq")),
            P(),
            P(("row", "seq"), "col"),
            P(("row", "seq"), "col"),
            P(("row", "seq"), None),
            P(("row", "seq"), "col"),
            P(None, "col"),
            P(),
            P("col"),
            P("col"),
            P("col"),
            P("col"),
            P(("row", "seq"), "col"),
            P(),
            P(("row", "seq"), None),
            P(("row", "seq"), "col", None),
            P(("row", "seq"), "col", None),
            P(("row", "seq"), "col", None),
            P(("row", "seq"), "col"),
            P(("row", "seq"), "col"),
            P(("row", "seq"), "col"),
        ),
        check_vma=False,
    )
```

```python
import functools

import jax
import jax.numpy as jnp
from jax import lax
from jax.experimental import pallas as pl
from jax.experimental.pallas import tpu as pltpu
from jax.sharding import PartitionSpec as P

EPS = 1e-05
BF = jnp.bfloat16
F32 = jnp.float32
FAR = -1e30
TAPS_BC_ROW, TAPS_X_ROW, GATE_ROW, HEAD_ROW, SMALL_ROWS = 24, 32, 40, 42, 48


def silu(v):
    return v * jax.nn.sigmoid(v)


def nn(left, right):
    return lax.dot_general(left, right, (((1,), (0,)), ((), ())), preferred_element_type=F32)


def nt(left, right):
    return lax.dot_general(left, right, (((1,), (1,)), ((), ())), preferred_element_type=F32)


def tn(left, right):
    return lax.dot_general(left, right, (((0,), (0,)), ((), ())), preferred_element_type=F32)


def swap(value):
    return lax.ppermute(value, "seq", [(0, 1), (1, 0)])


def half(value, axis, which):
    size = value.shape[axis] // 2
    return lax.slice_in_dim(value, which * size, (which + 1) * size, axis=axis)


def own_half(value, axis):
    first = lax.axis_index("seq") == 0
    return jnp.where(first, half(value, axis, 0), half(value, axis, 1))


def other_half(value, axis):
    first = lax.axis_index("seq") == 0
    return jnp.where(first, half(value, axis, 1), half(value, axis, 0))


def join(own, other, axis):
    first = lax.axis_index("seq") == 0
    return jnp.where(
        first, jnp.concatenate([own, other], axis), jnp.concatenate([other, own], axis)
    )


def low(value):
    return lax.reduce_precision(value, 8, 7)


def two(value):
    high = low(value)
    return high.astype(BF), (value - high).astype(BF)


def three(value):
    high = value.astype(BF)
    rest = value - high.astype(F32)
    middle = rest.astype(BF)
    return high, middle, (rest - middle.astype(F32)).astype(BF)


def exact(left, value):
    high, middle, last = three(value)
    return (nn(left, last) + nn(left, middle)) + nn(left, high)


def one(high, low_term):
    return high.astype(F32) + low_term.astype(F32)


def after(value, *others):
    return lax.optimization_barrier((value, *others))[0]


def call(kernel, outs, args, flops, name, room=12, scratch=(), apart=(), scalars=()):
    whole = pl.BlockSpec(memory_space=pltpu.VMEM)
    spec = {i: pl.BlockSpec(memory_space=pltpu.HBM) for i in apart}
    spec.update({i: pl.BlockSpec(memory_space=pltpu.SMEM) for i in scalars})
    shapes = [jax.ShapeDtypeStruct(shape, kind) for shape, kind in outs]
    size = lambda a: a.size * jnp.dtype(a.dtype).itemsize
    held = [pltpu.VMEM(args[i].shape, args[i].dtype) for i in apart]
    if apart:
        held.append(pltpu.SemaphoreType.DMA((len(apart) + 1,)))
    return pl.pallas_call(
        kernel,
        out_shape=shapes,
        in_specs=[spec.get(i, whole) for i in range(len(args))],
        out_specs=[whole] * len(outs),
        scratch_shapes=[pltpu.VMEM(shape, kind) for shape, kind in scratch] + held,
        compiler_params=pltpu.CompilerParams(vmem_limit_bytes=room * 2**20),
        cost_estimate=pl.CostEstimate(
            flops=flops,
            bytes_accessed=sum(size(a) for a in args) + sum(size(a) for a in shapes),
            transcendentals=0,
        ),
        name=name,
    )(*args)


def fetched(pairs, sems):
    copies = [
        pltpu.make_async_copy(src, dst, sems.at[k]) for k, (src, dst) in enumerate(pairs)
    ]
    for copy in copies:
        copy.start()
    return copies


def causal(marks, marks_row, rows):
    return (marks[rows, 1:2] >= marks_row[1:2, :]) & (marks[rows, 0:1] == marks_row[0:1, :])


def convolved(value, taps, marks):
    total = taps[3:4, :] * value
    for lag in range(1, 4):
        rolled = pltpu.roll(value, lag, 0) * marks[:, 1 + lag : 2 + lag]
        total = total + taps[3 - lag : 4 - lag, :] * rolled
    return total


def head_columns(inner, lanes, head_width):
    down = lax.broadcasted_iota(jnp.int32, (inner, lanes), 0)
    across = lax.broadcasted_iota(jnp.int32, (inner, lanes), 1) * head_width
    return jnp.where((down >= across) & (down < across + head_width), 1.0, 0.0).astype(BF)


def by_head(value, columns):
    high, middle, last = three(value)
    return (nn(last, columns) + nn(middle, columns)) + nn(high, columns)


def softplus(v):
    return jnp.maximum(v, 0.0) + jnp.log1p(jnp.exp(-jnp.abs(v)))


def mixer_forward(
    inner,
    head_width,
    own_ref,
    other_ref,
    w_src,
    marks_ref,
    row_ref,
    taps_x_ref,
    taps_bc_ref,
    head_ref,
    wide_ref,
    pre_ref,
    dt_ref,
    cum_ref,
    scanned_ref,
    part_own_ref,
    part_other_ref,
    square_own_ref,
    square_other_ref,
    scaled_ref,
    w_ref,
    sems,
):
    half_tokens, width = own_ref.shape
    tokens = 2 * half_tokens
    heads = inner // head_width
    bc_at, out_at, dt_at = 2 * inner, pre_ref.shape[1], pre_ref.shape[1] + inner
    state = (out_at - bc_at) // 2
    copies = fetched(
        (
            (w_src.at[:, :out_at], w_ref.at[:, :out_at]),
            (w_src.at[:, out_at:], w_ref.at[:, out_at:]),
        ),
        sems,
    )
    for part, src in ((0, own_ref), (1, other_ref)):
        rows = slice(part * half_tokens, (part + 1) * half_tokens)
        if part == 0:
            copies[0].wait()
        pre_ref[rows, :] = nn(src[...], w_ref[:, :out_at])
        if part == 0:
            copies[1].wait()
        dt_ref[rows, :] = nn(src[...], w_ref[:, dt_at:]) + head_ref[0:1, :]
    marks, marks_row = marks_ref[...], row_ref[...]
    x_conv = silu(convolved(pre_ref[:, :inner], taps_x_ref[...], marks))
    bc = silu(convolved(pre_ref[:, bc_at:out_at], taps_bc_ref[...], marks)).astype(BF)
    b_map, c_map = bc[:, :state], bc[:, state:]
    step = softplus(dt_ref[...])
    lower = jnp.where(marks[:, 1:2] >= marks_row[1:2, :], 1.0, 0.0).astype(BF)
    cum = exact(lower, -step * head_ref[1:2, :])
    cum_ref[...] = cum
    cum_row = jnp.concatenate([cum, jnp.zeros_like(cum)], 1).T
    for h in range(heads):
        here = slice(h * head_width, (h + 1) * head_width)
        scaled_ref[:, here] = (x_conv[:, here] * step[:, h : h + 1]).astype(BF)
    block = 128
    for at in range(0, tokens, block):
        rows = slice(at, at + block)
        scores = nt(c_map[rows, :], b_map)
        mask = causal(marks, marks_row, rows)
        for h in range(heads):
            here = slice(h * head_width, (h + 1) * head_width)
            gap = cum[rows, h : h + 1] - cum_row[h : h + 1, :]
            mix = (jnp.exp(jnp.where(mask, gap, FAR)) * scores).astype(BF)
            scanned_ref[rows, here] = nn(mix, scaled_ref[:, here])
    mixer_out = scanned_ref[...] + wide_ref[0:1, :] * x_conv
    gated = mixer_out * silu(pre_ref[:, inner:bc_at])
    square = jnp.sum(gated * gated, axis=1, keepdims=True)
    square_own_ref[...] = square[:half_tokens]
    square_other_ref[...] = square[half_tokens:]
    sent = (gated * wide_ref[1:2, :]).astype(BF)
    out_w = w_ref[:, out_at:dt_at]
    part_own_ref[...] = nt(sent[:half_tokens], out_w).astype(BF)
    part_other_ref[...] = nt(sent[half_tokens:], out_w).astype(BF)


def mixer_backward(
    inner,
    inner_all,
    head_width,
    experts,
    own_src,
    other_src,
    moe_own_src,
    moe_other_src,
    w_src,
    marks_src,
    row_src,
    taps_x_src,
    taps_bc_src,
    head_src,
    wide_src,
    pre_src,
    dt_src,
    cum_src,
    scanned_src,
    grads_ref,
    dt_grad_ref,
    normed_ref,
    part_own_ref,
    part_other_ref,
    small_ref,
    scaled_ref,
    low_ref,
    spread_ref,
    c_grad_ref,
    b_grad_ref,
    own_ref,
    other_ref,
    moe_own_ref,
    moe_other_ref,
    w_ref,
    marks_ref,
    row_ref,
    taps_x_ref,
    taps_bc_ref,
    head_ref,
    wide_ref,
    pre_ref,
    dt_ref,
    cum_ref,
    scanned_ref,
    sems,
):
    half_tokens = own_ref.shape[0]
    width = w_ref.shape[0]
    split = pre_ref.shape[1]
    copies = fetched(
        (
            (w_src.at[:, split:], w_ref.at[:, split:]),
            (own_src, own_ref),
            (other_src, other_ref),
            (moe_own_src.at[:, width:], moe_own_ref.at[:, width:]),
            (moe_other_src.at[:, width:], moe_other_ref.at[:, width:]),
            (pre_src, pre_ref),
            (scanned_src, scanned_ref),
            (dt_src, dt_ref),
            (cum_src, cum_ref),
            (marks_src, marks_ref),
            (row_src, row_ref),
            (taps_x_src, taps_x_ref),
            (taps_bc_src, taps_bc_ref),
            (head_src, head_ref),
            (wide_src, wide_ref),
            (w_src.at[:, :split], w_ref.at[:, :split]),
        ),
        sems,
    )
    tokens = 2 * half_tokens
    heads = inner // head_width
    bc_at, out_at, dt_at = 2 * inner, pre_ref.shape[1], pre_ref.shape[1] + inner
    state = (out_at - bc_at) // 2
    stack = lambda a, b: jnp.concatenate([a, b], 0)
    for copy in copies[:3]:
        copy.wait()
    out_w = w_ref[:, out_at:dt_at]
    gate_norm_grad = stack(
        nn(own_ref[:, :width], out_w), nn(other_ref[:, :width], out_w)
    )
    for copy in copies[3:15]:
        copy.wait()
    marks, marks_row = marks_ref[...], row_ref[...]
    conv_x = convolved(pre_ref[:, :inner], taps_x_ref[...], marks)
    conv_bc = convolved(pre_ref[:, bc_at:out_at], taps_bc_ref[...], marks)
    x_conv = silu(conv_x)
    bc = silu(conv_bc).astype(BF)
    b_map, c_map = bc[:, :state], bc[:, state:]
    z_pre = pre_ref[:, inner:bc_at]
    step = softplus(dt_ref[...])
    rate = head_ref[1:2, :]
    skip_wide, gain = wide_ref[0:1, :], wide_ref[1:2, :]
    at = width + experts
    dots = lambda ref: one(ref[:, at : at + 1], ref[:, at + 1 : at + 2])
    gate_dot = stack(dots(own_ref), dots(other_ref))
    gates = lambda ref: one(ref[:, width : width + 1], ref[:, width + 1 : width + 2])
    inv_gate = stack(gates(moe_own_ref), gates(moe_other_ref))
    sig = jax.nn.sigmoid(z_pre)
    silu_z = z_pre * sig
    mixer_out = scanned_ref[...] + skip_wide * x_conv
    gated = mixer_out * silu_z
    normed = gated * inv_gate
    small_ref[...] = jnp.zeros_like(small_ref)

    def keep_small(row, value):
        for at in range(0, value.shape[1], 128):
            piece = value[:, at : at + 128]
            small_ref[row : row + 1, : piece.shape[1]] = piece
            row = row + 1

    keep_small(GATE_ROW, jnp.sum(gate_norm_grad * normed, axis=0, keepdims=True))
    normed_ref[...] = (normed * gain).astype(BF)
    gated_grad = inv_gate * (gate_norm_grad * gain) - gated * (
        inv_gate * inv_gate * gate_dot * (1.0 / inner_all)
    )
    ssm_grad = gated_grad * silu_z
    grads_ref[:, inner:bc_at] = (
        gated_grad * mixer_out * (sig * (1.0 + z_pre * (1.0 - sig)))
    ).astype(BF)
    columns = head_columns(inner, dt_ref.shape[1], head_width)
    skips = by_head(
        jnp.broadcast_to(jnp.sum(ssm_grad * x_conv, axis=0, keepdims=True), (8, inner)), columns
    )
    keep_small(HEAD_ROW + 2, skips[0:1, :heads])
    low_ref[...] = ssm_grad.astype(BF)
    for h in range(heads):
        here = slice(h * head_width, (h + 1) * head_width)
        scaled_ref[:, here] = (x_conv[:, here] * step[:, h : h + 1]).astype(BF)
    cum = cum_ref[...]
    cum_row = jnp.concatenate([cum, jnp.zeros_like(cum)], 1).T
    c_grad_ref[...] = jnp.zeros_like(c_grad_ref)
    block = 128
    for start in range(0, tokens, block):
        rows = slice(start, start + block)
        scores = nt(b_map[rows, :], c_map)
        mask = (marks_row[1:2, :] >= marks[rows, 1:2]) & (
            marks_row[0:1, :] == marks[rows, 0:1]
        )
        scores_grad = jnp.zeros((block, tokens), F32)
        for h in range(heads):
            here = slice(h * head_width, (h + 1) * head_width)
            gap = cum_row[h : h + 1, :] - cum[rows, h : h + 1]
            decay = jnp.exp(jnp.where(mask, gap, FAR))
            spread_ref[rows, here] = nn((decay * scores).astype(BF), low_ref[:, here])
            scores_grad = scores_grad + decay * nt(scaled_ref[rows, here], low_ref[:, here])
        scores_low = scores_grad.astype(BF)
        b_grad_ref[rows, :] = nn(scores_low, c_map)
        c_grad_ref[...] += tn(scores_low, b_map[rows, :])
    spread = spread_ref[...]
    step_grad = by_head(x_conv * spread, columns)
    cum_grad = by_head(
        low_ref[...].astype(F32) * scanned_ref[...] - scaled_ref[...].astype(F32) * spread, columns
    )
    upper = jnp.where(marks_row[1:2, :] >= marks[:, 1:2], 1.0, 0.0).astype(BF)
    decay_grad = exact(upper, cum_grad)
    dt_float = (step_grad - decay_grad * rate) * jax.nn.sigmoid(dt_ref[...])
    keep_small(HEAD_ROW, jnp.sum(dt_float, axis=0, keepdims=True)[:, :heads])
    keep_small(
        HEAD_ROW + 1, jnp.sum(decay_grad * (-step * rate), axis=0, keepdims=True)[:, :heads]
    )
    dt_low = dt_float.astype(BF)
    dt_grad_ref[...] = dt_low
    for h in range(heads):
        here = slice(h * head_width, (h + 1) * head_width)
        spread_ref[:, here] = spread[:, here] * step[:, h : h + 1]

    def back(value_grad, total, value, taps, small_row, to):
        sig_c = jax.nn.sigmoid(total)
        grad = value_grad * (sig_c * (1.0 + total * (1.0 - sig_c)))
        keep_small(small_row + 6, jnp.sum(grad * value, axis=0, keepdims=True))
        result = taps[3:4, :] * grad
        for lag in range(1, 4):
            kept = grad * marks[:, 1 + lag : 2 + lag]
            keep_small(
                small_row + 2 * (3 - lag),
                jnp.sum(kept * pltpu.roll(value, lag, 0), axis=0, keepdims=True),
            )
            result = result + taps[3 - lag : 4 - lag, :] * pltpu.roll(kept, tokens - lag, 0)
        grads_ref[:, to] = result.astype(BF)

    back(
        spread_ref[...] + ssm_grad * skip_wide,
        conv_x,
        pre_ref[:, :inner],
        taps_x_ref[...],
        TAPS_X_ROW,
        slice(0, inner),
    )
    back(
        jnp.concatenate([b_grad_ref[...], c_grad_ref[...]], 1),
        conv_bc,
        pre_ref[:, bc_at:out_at],
        taps_bc_ref[...],
        TAPS_BC_ROW,
        slice(bc_at, out_at),
    )
    copies[15].wait()
    for part, dst in ((0, part_own_ref), (1, part_other_ref)):
        rows = slice(part * half_tokens, (part + 1) * half_tokens)
        dst[...] = (
            nt(grads_ref[rows, :], w_ref[:, :out_at]) + nt(dt_low[rows, :], w_ref[:, dt_at:])
        ).astype(BF)


def mixer_products(
    inner,
    experts,
    own_ref,
    other_ref,
    mix_own_ref,
    mix_other_ref,
    moe_own_ref,
    moe_other_ref,
    grads_ref,
    dt_grad_ref,
    normed_ref,
    sums_ref,
):
    half_tokens, width = own_ref.shape
    out_at = grads_ref.shape[1]
    dt_at = out_at + inner
    count = sums_ref.shape[0]
    rows = width // count
    group = min(8, count)
    first, second = slice(0, half_tokens), slice(half_tokens, 2 * half_tokens)
    logits = slice(width, width + experts)
    for at in range(0, count, group):
        here = slice(at * rows, (at + group) * rows)
        mine, others = own_ref[:, here], other_ref[:, here]
        a = tn(mine, grads_ref[first, :]) + tn(others, grads_ref[second, :])
        b = tn(mix_own_ref[:, here], normed_ref[first, :]) + tn(
            mix_other_ref[:, here], normed_ref[second, :]
        )
        c = tn(mine, dt_grad_ref[first, :]) + tn(others, dt_grad_ref[second, :])
        d = tn(moe_own_ref[:, here], mix_own_ref[:, logits]) + tn(
            moe_other_ref[:, here], mix_other_ref[:, logits]
        )
        a, b, c, d = a.astype(BF), b.astype(BF), c.astype(BF), d.astype(BF)
        for k in range(group):
            part = slice(k * rows, (k + 1) * rows)
            sums_ref[at + k, :, :out_at] = a[part]
            sums_ref[at + k, :, out_at:dt_at] = b[part]
            sums_ref[at + k, :, dt_at : dt_at + 64] = c[part]
            sums_ref[at + k, :, dt_at + 16 : dt_at + 16 + experts] = d[part]
            sums_ref[at + k, :, dt_at + 64 :] = jnp.zeros((rows, 128), BF)


def experts_both_ways(
    units,
    shared,
    own_ref,
    other_ref,
    cot_own_ref,
    cot_other_ref,
    w_ref,
    routes_own_ref,
    routes_other_ref,
    mine_ref,
    in_own_ref,
    in_other_ref,
    out_own_ref,
    out_other_ref,
    grads_ref,
    acts_ref,
    gates_ref,
    gates_grad_own_ref,
    gates_grad_other_ref,
):
    half_tokens = own_ref.shape[0]
    width = w_ref.shape[0]
    experts = mine_ref.shape[1]
    in_units = 2 * (units + shared)
    down_at = in_units + 128
    mine = mine_ref[...]
    number = lax.broadcasted_iota(jnp.int32, (half_tokens, experts), 1)
    down_end = down_at + units + shared
    parts = (
        (own_ref, cot_own_ref, routes_own_ref, in_own_ref, out_own_ref, gates_grad_own_ref),
        (
            other_ref,
            cot_other_ref,
            routes_other_ref,
            in_other_ref,
            out_other_ref,
            gates_grad_other_ref,
        ),
    )
    for part, (src, cot, routes, in_dst, out_dst, gates_dst) in enumerate(parts):
        rows = slice(part * half_tokens, (part + 1) * half_tokens)
        back = nn(cot[...], w_ref[:, down_at:down_end])
        pre = nn(src[:, :width], w_ref[:, :down_at])
        named = number == routes[:, 0:1]
        for k in range(1, routes.shape[1]):
            named = named | (number == routes[:, k : k + 1])
        logits = jnp.where(named, pre[:, in_units : in_units + experts], FAR)
        raised = jnp.exp(logits - jnp.max(logits, axis=1, keepdims=True))
        gates = raised / jnp.sum(raised, axis=1, keepdims=True)
        gates_ref[rows, :] = gates
        weight = jnp.sum(gates * mine, axis=1, keepdims=True)
        gate, up = pre[:, :units], pre[:, units : 2 * units]
        sig = jax.nn.sigmoid(gate)
        silu_gate = gate * sig
        act = silu_gate * up
        acts_ref[rows, :units] = (act * weight).astype(BF)
        act_back = back[:, :units]
        gates_dst[...] = jnp.sum(act * act_back, axis=1, keepdims=True) * mine
        act_grad = act_back * weight
        grads_ref[rows, :units] = (
            act_grad * up * (sig * (1.0 + gate * (1.0 - sig)))
        ).astype(BF)
        grads_ref[rows, units : 2 * units] = (act_grad * silu_gate).astype(BF)
        gate, up = pre[:, 2 * units : 2 * units + shared], pre[:, 2 * units + shared : in_units]
        sig = jax.nn.sigmoid(gate)
        silu_gate = gate * sig
        acts_ref[rows, units:] = (silu_gate * up).astype(BF)
        act_grad = back[:, units:]
        grads_ref[rows, 2 * units : 2 * units + shared] = (
            act_grad * up * (sig * (1.0 + gate * (1.0 - sig)))
        ).astype(BF)
        grads_ref[rows, 2 * units + shared :] = (act_grad * silu_gate).astype(BF)
        in_dst[...] = nt(grads_ref[rows, :], w_ref[:, :in_units]).astype(BF)
        out_dst[...] = nt(acts_ref[rows, :], w_ref[:, down_at:down_end]).astype(BF)


def expert_products(
    own_ref, other_ref, cot_own_ref, cot_other_ref, grads_ref, acts_ref, sums_ref
):
    half_tokens, width = cot_own_ref.shape
    split = grads_ref.shape[1]
    first, second = slice(0, half_tokens), slice(half_tokens, 2 * half_tokens)
    block = 256
    for at in range(0, width, block):
        here = slice(at, at + block)
        sums_ref[here, :split] = (
            tn(own_ref[:, here], grads_ref[first, :]) + tn(other_ref[:, here], grads_ref[second, :])
        ).astype(BF)
        sums_ref[here, split:] = (
            tn(cot_own_ref[:, here], acts_ref[first, :])
            + tn(cot_other_ref[:, here], acts_ref[second, :])
        ).astype(BF)


def tail_sums(
    inner,
    heads,
    got_ref,
    out_ref,
    z_ref,
    x_ref,
    dt_ref,
    router_ref,
    conv_ref,
    gain_ref,
    head_ref,
    sent_ref,
):
    count, rows = got_ref.shape[0], out_ref.shape[0]
    experts = router_ref.shape[1]
    bc_at = 2 * inner
    small_at = got_ref.shape[2] - 128
    dt_at = small_at - 64
    out_at = dt_at - inner
    totals = []
    for core in range(2):
        total = got_ref[core].astype(F32)
        for at in range(core + 2, count, 2):
            total = total + got_ref[at].astype(F32)
        totals.append(total)
        here = slice(core * inner, (core + 1) * inner)
        x_ref[:, here] = total[:, :inner]
        z_ref[:, here] = total[:, inner:bc_at]
        out_ref[:, here] = total[:, out_at:dt_at]
        dt_ref[:, core * heads : (core + 1) * heads] = total[:, dt_at : dt_at + heads]
        small = total[:SMALL_ROWS, small_at:]

        def row_of(at):
            return jnp.concatenate([small[at : at + 1], small[at + 1 : at + 2, : inner - 128]], 1)

        for k in range(conv_ref.shape[0]):
            conv_ref[k : k + 1, here] = row_of(TAPS_X_ROW + 2 * k)
        gain_ref[:, here] = row_of(GATE_ROW)
        for k in range(3):
            head_ref[k : k + 1, core * heads : (core + 1) * heads] = small[
                HEAD_ROW + k : HEAD_ROW + k + 1, :heads
            ]
    router_ref[...] = totals[0][:, dt_at + 16 : dt_at + 16 + experts]
    sent_ref[:rows, :] = (totals[0][:, bc_at:out_at] + totals[1][:, bc_at:out_at]).astype(BF)
    small = totals[0][:TAPS_X_ROW, small_at:] + totals[1][:TAPS_X_ROW, small_at:]
    high = small.astype(BF)
    sent_ref[rows:, :128] = high
    sent_ref[rows:, 128:] = (small - high.astype(F32)).astype(BF)


def last_sums(got_ref, bc_ref, mix_ref, moe_ref, conv_ref):
    rows = bc_ref.shape[0]
    total = got_ref[0].astype(F32)
    for at in range(1, got_ref.shape[0]):
        total = total + got_ref[at].astype(F32)
    bc_ref[...] = total[:rows]
    small = total[rows:, :128] + total[rows:, 128:]
    half_rows = TAPS_BC_ROW // 2
    mix_ref[...] = small[:half_rows]
    moe_ref[...] = small[half_rows:TAPS_BC_ROW]
    for k in range(conv_ref.shape[0]):
        for part in range(2):
            at = TAPS_BC_ROW + 2 * k + part
            conv_ref[k : k + 1, part * 128 : (part + 1) * 128] = small[at : at + 1]


def chip_sum(own_ref, other_ref, extra_own_ref, extra_other_ref, sum_ref):
    width, more = own_ref.shape[1], extra_own_ref.shape[1]
    sum_ref[:, :width] = (own_ref[...].astype(F32) + other_ref[...].astype(F32)).astype(BF)
    extra = extra_own_ref[...] + extra_other_ref[...]
    high = extra.astype(BF)
    sum_ref[:, width:] = jnp.zeros((own_ref.shape[0], sum_ref.shape[1] - width), BF)
    sum_ref[:, width : width + more] = high
    sum_ref[:, width + more : width + 2 * more] = (extra - high.astype(F32)).astype(BF)


def second_shard(
    got_ref,
    residual_ref,
    mix_out_ref,
    cot_ref,
    gates_ref,
    router_ref,
    inv_ref,
    gain_ref,
    sent_ref,
    grad_ref,
    gain_grad_ref,
):
    width, experts = residual_ref.shape[1], gates_ref.shape[1]
    total = got_ref[0].astype(F32)
    for at in range(1, got_ref.shape[0]):
        total = total + got_ref[at].astype(F32)
    gates = gates_ref[...]
    gates_grad = total[:, width : width + experts] + total[:, width + experts : width + 2 * experts]
    logits_grad = (
        gates * (gates_grad - jnp.sum(gates * gates_grad, axis=1, keepdims=True))
    ).astype(BF)
    moe_in_grad = total[:, :width] + nt(logits_grad, router_ref[...])
    residual, inv = residual_ref[...], inv_ref[...]
    scaled = moe_in_grad * gain_ref[...]
    mean = jnp.sum(scaled * residual, axis=1, keepdims=True) * (1.0 / width)
    grad = cot_ref[...].astype(F32) + inv * scaled - residual * (inv * inv * inv * mean)
    grad_ref[...] = grad
    gain_grad_ref[...] = jnp.sum(moe_in_grad * residual * inv, axis=0, keepdims=True)
    grad_low = grad.astype(BF)
    gate_dot = jnp.sum(grad_low.astype(F32) * mix_out_ref[...], axis=1, keepdims=True)
    high = gate_dot.astype(BF)
    sent_ref[:, :width] = grad_low
    sent_ref[:, width:] = jnp.zeros((residual.shape[0], sent_ref.shape[1] - width), BF)
    sent_ref[:, width : width + experts] = logits_grad
    sent_ref[:, width + experts : width + experts + 1] = high
    sent_ref[:, width + experts + 1 : width + experts + 2] = (
        gate_dot - high.astype(F32)
    ).astype(BF)


def mixer_rows(
    inner,
    heads,
    x_src,
    z_src,
    bc_src,
    out_src,
    dt_src,
    rows_ref,
    x_ref,
    z_ref,
    bc_ref,
    out_ref,
    dt_ref,
    sems,
):
    copies = fetched(
        (
            (x_src, x_ref),
            (z_src, z_ref),
            (bc_src, bc_ref),
            (out_src, out_ref),
            (dt_src, dt_ref),
        ),
        sems,
    )
    for copy in copies:
        copy.wait()
    bc_at = 2 * inner
    out_at = bc_at + bc_ref.shape[1]
    dt_at = out_at + inner
    lanes = rows_ref.shape[2] - dt_at
    for core in range(2):
        here = slice(core * inner, (core + 1) * inner)
        down = lax.broadcasted_iota(jnp.int32, (2 * heads, lanes), 0) - core * heads
        across = lax.broadcasted_iota(jnp.int32, (2 * heads, lanes), 1)
        pick = jnp.where((down == across) & (across < heads), 1.0, 0.0).astype(BF)
        parts = (
            (0, x_ref[:, here]),
            (inner, z_ref[:, here]),
            (bc_at, bc_ref[...]),
            (out_at, out_ref[:, here]),
            (dt_at, tn(dt_ref[...], pick).astype(BF)),
        )
        for at, value in parts:
            rows_ref[core, :, at : at + value.shape[1]] = value
        for at in range(core + 2, rows_ref.shape[0], 2):
            rows_ref[at] = rows_ref[core]


def expert_packs(
    units, shared, flag_ref, gate_ref, up_ref, sg_ref, su_ref, router_ref, down_ref, sd_ref, *packs
):
    first = flag_ref[0] == 0
    router_at = 2 * (units + shared)
    down_at = router_at + 128
    for which, dst in enumerate(packs):
        dst[...] = jnp.zeros_like(dst)
        lead = first if which == 0 else jnp.logical_not(first)

        def pick(a, b):
            return jnp.where(lead, a.astype(F32), b.astype(F32)).astype(BF)

        for ref, at in ((gate_ref, 0), (up_ref, units), (down_ref, down_at)):
            dst[:, at : at + units] = pick(ref[:, :units], ref[:, units:])
        for ref, at in (
            (sg_ref, 2 * units),
            (su_ref, 2 * units + shared),
            (sd_ref, down_at + units),
        ):
            dst[:, at : at + shared] = pick(ref[:, :shared], ref[:, shared:])
        dst[:, router_at : router_at + router_ref.shape[1]] = router_ref[...]


def joined(flag_ref, own_ref, other_ref, rows_ref):
    first = flag_ref[0] == 0
    rows = own_ref.shape[0]
    own, other = own_ref[...].astype(F32), other_ref[...].astype(F32)
    rows_ref[:rows] = jnp.where(first, own, other).astype(BF)
    rows_ref[rows:] = jnp.where(first, other, own).astype(BF)


def small_set(
    inner,
    heads,
    head_width,
    flag_ref,
    bias_ref,
    log_ref,
    skip_ref,
    seg_own_ref,
    seg_other_ref,
    taps_ref,
    gain_ref,
    marks_ref,
    row_ref,
    taps_x_ref,
    head_ref,
    wide_ref,
):
    first = flag_ref[0] == 0
    half_tokens = seg_own_ref.shape[1]
    tokens = 2 * half_tokens
    seg = jnp.concatenate([seg_own_ref[...], seg_other_ref[...]], 1).astype(F32)
    seg = jnp.broadcast_to(seg, (8, tokens))
    place = lax.broadcasted_iota(jnp.int32, (8, tokens), 1)
    turned = jnp.where(place < half_tokens, place + half_tokens, place - half_tokens)
    place = jnp.where(first, place, turned).astype(F32)
    before = pltpu.roll(seg, 1, 1)
    hold = jnp.where((seg == before) & (place > 0.0), 1.0, 0.0)
    kept_two = hold * pltpu.roll(hold, 1, 1)
    kept_three = kept_two * pltpu.roll(hold, 2, 1)
    which = lax.broadcasted_iota(jnp.int32, (8, tokens), 0)
    rows = jnp.where(which == 0, seg, 0.0)
    for k, value in enumerate((place, hold, kept_two, kept_three)):
        rows = jnp.where(which == k + 1, value, rows)
    row_ref[...] = rows
    tall = jnp.concatenate([rows, jnp.zeros((120, tokens), F32)], 0)
    marks_ref[...] = tall.T[:, :8]
    taps_x_ref[...] = jnp.where(first, taps_ref[:, :inner], taps_ref[:, inner:])
    lanes = head_ref.shape[1]
    lane = lax.broadcasted_iota(jnp.int32, (1, lanes), 1)
    bias, log, on = jnp.zeros((1, lanes), F32), jnp.zeros((1, lanes), F32), lane < heads
    across = lax.broadcasted_iota(jnp.int32, (1, inner), 1)
    skip = jnp.zeros((1, inner), F32)
    for h in range(heads):
        own = lambda ref: jnp.where(first, ref[h], ref[heads + h])
        bias = jnp.where(lane == h, own(bias_ref), bias)
        log = jnp.where(lane == h, own(log_ref), log)
        skip = jnp.where(
            (across >= h * head_width) & (across < (h + 1) * head_width), own(skip_ref), skip
        )
    head_ref[0:1, :] = bias
    head_ref[1:2, :] = jnp.where(on, jnp.exp(log), 0.0)
    wide_ref[0:1, :] = skip
    wide_ref[1:2, :] = jnp.where(first, gain_ref[:, :inner], gain_ref[:, inner:])


def exchange_rows(part, axis):
    count = lax.axis_size(axis)
    blocks = part.reshape(count, part.shape[0] // count, part.shape[1])
    return lax.all_to_all(blocks, axis, 0, 0, tiled=False)


def chip(own, other, extra_own, extra_other):
    rows, width = own.shape
    extra = call(
        chip_sum,
        [((rows, width + 128), BF)],
        (own, swap(other), extra_own, swap(extra_other)),
        10**6,
        "chip_sum",
    )
    return extra[0]


def from_tokens(own):
    return lax.all_gather(own, "col", axis=0, tiled=True)


def on_device(
    hidden,
    cotangent,
    segments,
    routes,
    gain_mix,
    w_z,
    w_x,
    w_bc,
    w_dt,
    conv_x,
    conv_bc,
    dt_bias,
    a_log,
    d_skip,
    gain_gate,
    out_t,
    gain_moe,
    w_router,
    w_gate_t,
    w_up_t,
    w_down_t,
    ws_gate,
    ws_up,
    ws_down_t,
):
    half_tokens, width = hidden.shape
    rows = lax.axis_size("row")
    cols = lax.axis_size("col")
    seq = lax.axis_index("seq")
    col = lax.axis_index("col")
    tokens = 2 * half_tokens
    inner = conv_x.shape[1] // 2
    heads = dt_bias.shape[0] // 2
    head_width = inner // heads
    state = conv_bc.shape[1] // 2
    experts = w_router.shape[1]
    hidden_units = w_gate_t.shape[2]
    shared_units = ws_gate.shape[1] // 2
    lanes = 64
    inner_all = conv_x.shape[1] * cols
    shard = half_tokens // cols

    out_at = 2 * inner + 2 * state
    dt_at = out_at + inner
    mixer_width = dt_at + lanes
    (spread_rows,) = call(
        functools.partial(mixer_rows, inner, heads),
        [((2 * rows, w_z.shape[0], mixer_width), BF)],
        (w_x, w_z, w_bc, out_t, w_dt.T),
        10**6,
        "mixer_rows",
        56,
        (),
        (0, 1, 2, 3, 4),
    )
    (
        spread_rows,
        hidden,
        cotangent,
        w_gate_t,
        w_up_t,
        w_down_t,
        ws_gate,
        ws_up,
        ws_down_t,
        w_router,
        conv_x,
        gain_gate,
        segments,
        routes,
    ) = lax.optimization_barrier(
        (
            spread_rows,
            hidden,
            cotangent,
            w_gate_t,
            w_up_t,
            w_down_t,
            ws_gate,
            ws_up,
            ws_down_t,
            w_router,
            conv_x,
            gain_gate,
            segments,
            routes,
        )
    )
    mixer_whole = lax.all_to_all(spread_rows, ("row", "seq"), 0, 0).reshape(width, mixer_width)

    inv_mix = lax.rsqrt(jnp.mean(hidden * hidden, axis=1) + EPS)
    mix_own = (hidden * inv_mix[:, None] * gain_mix).astype(BF)
    mix_other = swap(mix_own)
    cot_other = swap(cotangent)
    routes_other = swap(routes)
    flag = seq.astype(jnp.int32)[None]

    down_units = hidden_units + shared_units
    in_units = 2 * down_units
    down_at = in_units + 128
    weight_rows = w_z.shape[0]
    packed = -(-(down_at + down_units) // 128) * 128
    flat = lambda a: a.reshape(weight_rows, 2 * hidden_units)
    pack_own, pack_other = call(
        functools.partial(expert_packs, hidden_units, shared_units),
        [((weight_rows, packed), BF)] * 2,
        (
            flag,
            flat(w_gate_t),
            flat(w_up_t),
            ws_gate,
            ws_up,
            w_router,
            flat(w_down_t),
            ws_down_t,
        ),
        10**6,
        "expert_packs",
        scalars=(0,),
    )
    (expert_rows,) = call(
        joined,
        [((2 * weight_rows, packed), BF)],
        (flag, pack_own, swap(pack_other)),
        10**6,
        "expert_rows",
        scalars=(0,),
    )
    seg_own = segments[None]
    marks, marks_row, taps_x, head_rows, wide_rows = call(
        functools.partial(small_set, inner, heads, head_width),
        [
            ((tokens, 8), F32),
            ((8, tokens), F32),
            ((4, inner), F32),
            ((2, lanes), F32),
            ((2, inner), F32),
        ],
        (flag, dt_bias, a_log, d_skip, seg_own, swap(seg_own), conv_x, gain_gate[None]),
        10**6,
        "small_set",
        scalars=(0, 1, 2, 3),
    )
    expert_rows, mixer_whole, mix_own, mix_other, cot_other, routes_other, marks, marks_row = (
        lax.optimization_barrier(
            (
                expert_rows,
                mixer_whole,
                mix_own,
                mix_other,
                cot_other,
                routes_other,
                marks,
                marks_row,
            )
        )
    )
    expert_whole = lax.all_gather(expert_rows, "row", axis=0, tiled=True)

    fixed = (mixer_whole, marks, marks_row, taps_x, conv_bc, head_rows, wide_rows)
    pre, dt_in, cum, scanned, part_own, part_other, square_own, square_other = call(
        functools.partial(mixer_forward, inner, head_width),
        [
            ((tokens, out_at), F32),
            ((tokens, lanes), F32),
            ((tokens, lanes), F32),
            ((tokens, inner), F32),
            ((half_tokens, width), BF),
            ((half_tokens, width), BF),
            ((half_tokens, 1), F32),
            ((half_tokens, 1), F32),
        ],
        (mix_own, mix_other, *fixed),
        4 * 10**9,
        "mixer_forward",
        28,
        [((tokens, inner), BF)],
        (2,),
    )
    mix_sum = exchange_rows(chip(part_own, part_other, square_own, square_other), "col")
    mix_sum = jnp.sum(mix_sum.astype(F32), axis=0)
    square = mix_sum[:, width : width + 1] + mix_sum[:, width + 1 : width + 2]
    mix_sum = mix_sum[:, :width]

    here = lax.dynamic_slice_in_dim(hidden, col * shard, shard, 0)
    inv_gate_here = lax.rsqrt(square / inner_all + EPS)
    mix_out = mix_sum * inv_gate_here
    residual = here + mix_out
    inv_moe_here = lax.rsqrt(jnp.mean(residual * residual, axis=1, keepdims=True) + EPS)
    moe_here = (residual * inv_moe_here * gain_moe).astype(BF)
    moe_own = from_tokens(
        jnp.concatenate(
            [moe_here, *two(inv_gate_here), *two(inv_moe_here), jnp.zeros((shard, 124), BF)], 1
        )
    )
    moe_own, expert_whole = lax.optimization_barrier((moe_own, expert_whole))
    inv_moe = one(moe_own[:, width + 2], moe_own[:, width + 3])
    moe_other = swap(moe_own)

    mine = (jnp.arange(experts) == 2 * col + seq).astype(F32)[None, :]
    in_own, in_other, out_own, out_other, in_grads, acts, gates, *gates_grad = call(
        functools.partial(experts_both_ways, hidden_units, shared_units),
        [
            ((half_tokens, width), BF),
            ((half_tokens, width), BF),
            ((half_tokens, width), BF),
            ((half_tokens, width), BF),
            ((tokens, in_units), BF),
            ((tokens, down_units), BF),
            ((tokens, experts), F32),
            ((half_tokens, experts), F32),
            ((half_tokens, experts), F32),
        ],
        (moe_own, moe_other, cotangent, cot_other, expert_whole, routes, routes_other, mine),
        6 * 10**9,
        "experts_both_ways",
        30,
    )
    moe_got = exchange_rows(chip(in_own, in_other, *gates_grad), "col")
    (expert_sums,) = call(
        expert_products,
        [((width, in_units + down_units), BF)],
        (moe_own, moe_other, cotangent, cot_other, in_grads, acts),
        3 * 10**9,
        "expert_products",
        28,
    )
    chip_out = (out_own.astype(F32) + swap(out_other).astype(F32)).astype(BF)
    moe_got, expert_sums, chip_out, cot_here, gates_here, router, gain_row = (
        lax.optimization_barrier(
            (
                moe_got,
                expert_sums,
                chip_out,
                lax.dynamic_slice_in_dim(cotangent, col * shard, shard, 0),
                lax.dynamic_slice_in_dim(gates, col * shard, shard, 0),
                expert_whole[:, in_units : in_units + experts],
                gain_moe[None],
            )
        )
    )
    expert_sums = lax.psum_scatter(expert_sums, "row", scatter_dimension=0, tiled=True)

    sent, residual_grad, gain_moe_grad = call(
        second_shard,
        [((shard, width + 128), BF), ((shard, width), F32), ((1, width), F32)],
        (
            moe_got,
            residual,
            mix_out,
            cot_here,
            gates_here,
            router,
            inv_moe_here,
            gain_row,
        ),
        10**7,
        "second_shard",
    )
    grad_own = from_tokens(sent)

    out_got = exchange_rows(chip_out, "col")
    grad_own, out_got = lax.optimization_barrier((grad_own, out_got))
    grad_other = swap(grad_own)

    grads, dt_grad, normed_gate, part_own, part_other, small = call(
        functools.partial(mixer_backward, inner, inner_all, head_width, experts),
        [
            ((tokens, out_at), BF),
            ((tokens, lanes), BF),
            ((tokens, inner), BF),
            ((half_tokens, width), BF),
            ((half_tokens, width), BF),
            ((SMALL_ROWS, 128), F32),
        ],
        (grad_own, grad_other, moe_own, moe_other, *fixed, pre, dt_in, cum, scanned),
        5 * 10**9,
        "mixer_backward",
        56,
        [
            ((tokens, inner), BF),
            ((tokens, inner), BF),
            ((tokens, inner), F32),
            ((tokens, state), F32),
            ((tokens, state), F32),
        ],
        tuple(range(15)),
    )
    chip_in = (part_own.astype(F32) + swap(part_other).astype(F32)).astype(BF)
    chip_in, out_got = lax.optimization_barrier((chip_in, out_got))
    output_here = residual + jnp.sum(out_got.astype(F32), axis=0)
    output = 2.0 * lax.all_gather(
        after(0.5 * output_here, expert_sums), "col", axis=0, tiled=True
    )
    mix_in_got = exchange_rows(chip_in, "col")
    (mixer_sums,) = call(
        functools.partial(mixer_products, inner, experts),
        [((2 * rows, w_z.shape[0], mixer_width + 128), BF)],
        (
            mix_own,
            mix_other,
            grad_own,
            grad_other,
            moe_own,
            moe_other,
            grads,
            dt_grad,
            normed_gate,
        ),
        2 * 10**9,
        "mixer_products",
        28,
    )
    mix_in_got, mixer_sums = lax.optimization_barrier((mix_in_got, mixer_sums))
    mix_in_grad = jnp.sum(mix_in_got.astype(F32), axis=0)

    inv_here = lax.dynamic_slice_in_dim(inv_mix, col * shard, shard, 0)[:, None]
    scaled_mix = mix_in_grad * gain_mix
    grad_hidden_here = (
        residual_grad
        + inv_here * scaled_mix
        - here * (inv_here**3 * jnp.mean(scaled_mix * here, axis=1, keepdims=True))
    )
    gain_mix_grad = jnp.sum(mix_in_grad * here * inv_here, axis=0)

    gains = jnp.concatenate([gain_mix_grad.reshape(-1, 128), gain_moe_grad.reshape(-1, 128)])
    small = jnp.concatenate([gains, small[TAPS_BC_ROW:]]).astype(BF)
    mixer_sums = lax.dynamic_update_slice(
        mixer_sums, jnp.broadcast_to(small[None], (2 * rows, *small.shape)), (0, 0, mixer_width)
    )
    got = lax.all_to_all(mixer_sums, ("row", "seq"), 0, 0)
    grad_hidden = from_tokens(grad_hidden_here.astype(BF))
    grad_hidden = grad_hidden.astype(F32)

    own = own_half(expert_sums, 0)
    other = swap(other_half(expert_sums, 0))

    def expert(at):
        a = own[:, None, at : at + hidden_units]
        return join(a, other[:, None, at : at + hidden_units], 1).astype(F32)

    def shared(at):
        return join(
            own[:, at : at + shared_units], other[:, at : at + shared_units], 1
        ).astype(F32)

    g_w_gate_t = expert(0)
    g_w_up_t = expert(hidden_units)
    g_w_down_t = expert(in_units)
    g_ws_gate = shared(2 * hidden_units)
    g_ws_up = shared(2 * hidden_units + shared_units)
    g_ws_down_t = shared(in_units + hidden_units)
    (
        got,
        grad_hidden,
        g_w_gate_t,
        g_w_up_t,
        g_w_down_t,
        g_ws_gate,
        g_ws_up,
        g_ws_down_t,
        inv_moe,
    ) = lax.optimization_barrier(
        (
            got,
            grad_hidden,
            g_w_gate_t,
            g_w_up_t,
            g_w_down_t,
            g_ws_gate,
            g_ws_up,
            g_ws_down_t,
            inv_moe,
        )
    )
    (
        g_out_t,
        g_w_z,
        g_w_x,
        g_w_dt,
        g_w_router,
        g_conv_x,
        g_gain_gate,
        by_heads,
        sent,
    ) = call(
        functools.partial(tail_sums, inner, heads),
        [
            ((weight_rows, 2 * inner), F32),
            ((weight_rows, 2 * inner), F32),
            ((weight_rows, 2 * inner), F32),
            ((weight_rows, 2 * heads), F32),
            ((weight_rows, experts), F32),
            ((4, 2 * inner), F32),
            ((1, 2 * inner), F32),
            ((3, 2 * heads), F32),
            ((weight_rows + 32, 2 * state), BF),
        ],
        (got,),
        10**7,
        "tail_sums",
        16,
    )
    g_gain_gate = g_gain_gate.reshape(-1)
    g_dt_bias, g_a_log, g_d_skip = by_heads[0], by_heads[1], by_heads[2]
    got = lax.all_to_all(jnp.broadcast_to(sent[None], (cols, *sent.shape)), "col", 0, 0)
    got, output = lax.optimization_barrier((got, output))
    g_w_bc, g_gain_mix, g_gain_moe, g_conv_bc = call(
        last_sums,
        [
            ((weight_rows, 2 * state), F32),
            ((width // 128, 128), F32),
            ((width // 128, 128), F32),
            ((4, 2 * state), F32),
        ],
        (got,),
        10**6,
        "last_sums",
    )
    g_gain_mix, g_gain_moe = g_gain_mix.reshape(-1), g_gain_moe.reshape(-1)

    return (
        output,
        grad_hidden,
        inv_mix,
        inv_moe,
        g_gain_mix,
        g_w_z,
        g_w_x,
        g_w_bc,
        g_w_dt,
        g_conv_x,
        g_conv_bc,
        g_dt_bias,
        g_a_log,
        g_d_skip,
        g_gain_gate,
        g_out_t,
        g_gain_moe,
        g_w_router,
        g_w_gate_t,
        g_w_up_t,
        g_w_down_t,
        g_ws_gate,
        g_ws_up,
        g_ws_down_t,
    )


def solution(mesh):
    placed = (
        P(("row", "seq"), None),
        P(("row", "seq"), None),
        P(("row", "seq")),
        P(("row", "seq"), None),
        P(),
        P(("row", "seq"), "col"),
        P(("row", "seq"), "col"),
        P(("row", "seq"), None),
        P(("row", "seq"), "col"),
        P(None, "col"),
        P(),
        P("col"),
        P("col"),
        P("col"),
        P("col"),
        P(("row", "seq"), "col"),
        P(),
        P(("row", "seq"), None),
        P(("row", "seq"), "col", None),
        P(("row", "seq"), "col", None),
        P(("row", "seq"), "col", None),
        P(("row", "seq"), "col"),
        P(("row", "seq"), "col"),
        P(("row", "seq"), "col"),
    )
    return jax.shard_map(
        on_device,
        mesh=mesh,
        in_specs=placed,
        out_specs=(
            P(("row", "seq"), None),
            P(("row", "seq"), None),
            P(("row", "seq")),
            P(("row", "seq")),
            P(),
            P(("row", "seq"), "col"),
            P(("row", "seq"), "col"),
            P(("row", "seq"), None),
            P(("row", "seq"), "col"),
            P(None, "col"),
            P(),
            P("col"),
            P("col"),
            P("col"),
            P("col"),
            P(("row", "seq"), "col"),
            P(),
            P(("row", "seq"), None),
            P(("row", "seq"), "col", None),
            P(("row", "seq"), "col", None),
            P(("row", "seq"), "col", None),
            P(("row", "seq"), "col"),
            P(("row", "seq"), "col"),
            P(("row", "seq"), "col"),
        ),
        check_vma=False,
    )
```

```python
import functools

import jax
import jax.numpy as jnp
from jax import lax
from jax.experimental import pallas as pl
from jax.experimental.pallas import tpu as pltpu
from jax.sharding import PartitionSpec as P

EPS = 1e-05
BF = jnp.bfloat16
F32 = jnp.float32
FAR = -1e30
TAPS_BC_ROW, TAPS_X_ROW, GATE_ROW, HEAD_ROW, SMALL_ROWS = 24, 32, 40, 42, 48


def silu(v):
    return v * jax.nn.sigmoid(v)


def nn(left, right):
    return lax.dot_general(left, right, (((1,), (0,)), ((), ())), preferred_element_type=F32)


def nt(left, right):
    return lax.dot_general(left, right, (((1,), (1,)), ((), ())), preferred_element_type=F32)


def tn(left, right):
    return lax.dot_general(left, right, (((0,), (0,)), ((), ())), preferred_element_type=F32)


def swap(value):
    return lax.ppermute(value, "seq", [(0, 1), (1, 0)])


def half(value, axis, which):
    size = value.shape[axis] // 2
    return lax.slice_in_dim(value, which * size, (which + 1) * size, axis=axis)


def own_half(value, axis):
    first = lax.axis_index("seq") == 0
    return jnp.where(first, half(value, axis, 0), half(value, axis, 1))


def other_half(value, axis):
    first = lax.axis_index("seq") == 0
    return jnp.where(first, half(value, axis, 1), half(value, axis, 0))


def join(own, other, axis):
    first = lax.axis_index("seq") == 0
    return jnp.where(
        first, jnp.concatenate([own, other], axis), jnp.concatenate([other, own], axis)
    )


def low(value):
    return lax.reduce_precision(value, 8, 7)


def two(value):
    high = low(value)
    return high.astype(BF), (value - high).astype(BF)


def three(value):
    high = value.astype(BF)
    rest = value - high.astype(F32)
    middle = rest.astype(BF)
    return high, middle, (rest - middle.astype(F32)).astype(BF)


def exact(left, value):
    high, middle, last = three(value)
    return (nn(left, last) + nn(left, middle)) + nn(left, high)


def one(high, low_term):
    return high.astype(F32) + low_term.astype(F32)


def after(value, *others):
    return lax.optimization_barrier((value, *others))[0]


def call(kernel, outs, args, flops, name, room=12, scratch=(), apart=(), scalars=()):
    whole = pl.BlockSpec(memory_space=pltpu.VMEM)
    spec = {i: pl.BlockSpec(memory_space=pltpu.HBM) for i in apart}
    spec.update({i: pl.BlockSpec(memory_space=pltpu.SMEM) for i in scalars})
    shapes = [jax.ShapeDtypeStruct(shape, kind) for shape, kind in outs]
    size = lambda a: a.size * jnp.dtype(a.dtype).itemsize
    held = [pltpu.VMEM(args[i].shape, args[i].dtype) for i in apart]
    if apart:
        held.append(pltpu.SemaphoreType.DMA((len(apart) + 1,)))
    return pl.pallas_call(
        kernel,
        out_shape=shapes,
        in_specs=[spec.get(i, whole) for i in range(len(args))],
        out_specs=[whole] * len(outs),
        scratch_shapes=[pltpu.VMEM(shape, kind) for shape, kind in scratch] + held,
        compiler_params=pltpu.CompilerParams(vmem_limit_bytes=room * 2**20),
        cost_estimate=pl.CostEstimate(
            flops=flops,
            bytes_accessed=sum(size(a) for a in args) + sum(size(a) for a in shapes),
            transcendentals=0,
        ),
        name=name,
    )(*args)


def fetched(pairs, sems):
    copies = [
        pltpu.make_async_copy(src, dst, sems.at[k]) for k, (src, dst) in enumerate(pairs)
    ]
    for copy in copies:
        copy.start()
    return copies


def causal(marks, marks_row, rows):
    return (marks[rows, 1:2] >= marks_row[1:2, :]) & (marks[rows, 0:1] == marks_row[0:1, :])


def convolved(value, taps, marks):
    total = taps[3:4, :] * value
    for lag in range(1, 4):
        rolled = pltpu.roll(value, lag, 0) * marks[:, 1 + lag : 2 + lag]
        total = total + taps[3 - lag : 4 - lag, :] * rolled
    return total


def head_columns(inner, lanes, head_width):
    down = lax.broadcasted_iota(jnp.int32, (inner, lanes), 0)
    across = lax.broadcasted_iota(jnp.int32, (inner, lanes), 1) * head_width
    return jnp.where((down >= across) & (down < across + head_width), 1.0, 0.0).astype(BF)


def by_head(value, columns):
    high, middle, last = three(value)
    return (nn(last, columns) + nn(middle, columns)) + nn(high, columns)


def softplus(v):
    return jnp.maximum(v, 0.0) + jnp.log1p(jnp.exp(-jnp.abs(v)))


def mixer_forward(
    inner,
    head_width,
    own_ref,
    other_ref,
    w_src,
    marks_ref,
    row_ref,
    taps_x_ref,
    taps_bc_ref,
    head_ref,
    wide_ref,
    pre_ref,
    dt_ref,
    cum_ref,
    scanned_ref,
    part_own_ref,
    part_other_ref,
    square_own_ref,
    square_other_ref,
    scaled_ref,
    w_ref,
    sems,
):
    half_tokens, width = own_ref.shape
    tokens = 2 * half_tokens
    heads = inner // head_width
    bc_at, out_at, dt_at = 2 * inner, pre_ref.shape[1], pre_ref.shape[1] + inner
    state = (out_at - bc_at) // 2
    copies = fetched(
        (
            (w_src.at[:, :out_at], w_ref.at[:, :out_at]),
            (w_src.at[:, out_at:], w_ref.at[:, out_at:]),
        ),
        sems,
    )
    for part, src in ((0, own_ref), (1, other_ref)):
        rows = slice(part * half_tokens, (part + 1) * half_tokens)
        if part == 0:
            copies[0].wait()
        pre_ref[rows, :] = nn(src[...], w_ref[:, :out_at])
        if part == 0:
            copies[1].wait()
        dt_ref[rows, :] = nn(src[...], w_ref[:, dt_at:]) + head_ref[0:1, :]
    marks, marks_row = marks_ref[...], row_ref[...]
    x_conv = silu(convolved(pre_ref[:, :inner], taps_x_ref[...], marks))
    bc = silu(convolved(pre_ref[:, bc_at:out_at], taps_bc_ref[...], marks)).astype(BF)
    b_map, c_map = bc[:, :state], bc[:, state:]
    step = softplus(dt_ref[...])
    lower = jnp.where(marks[:, 1:2] >= marks_row[1:2, :], 1.0, 0.0).astype(BF)
    cum = exact(lower, -step * head_ref[1:2, :])
    cum_ref[...] = cum
    cum_row = jnp.concatenate([cum, jnp.zeros_like(cum)], 1).T
    for h in range(heads):
        here = slice(h * head_width, (h + 1) * head_width)
        scaled_ref[:, here] = (x_conv[:, here] * step[:, h : h + 1]).astype(BF)
    block = 128
    for at in range(0, tokens, block):
        rows = slice(at, at + block)
        scores = nt(c_map[rows, :], b_map)
        mask = causal(marks, marks_row, rows)
        for h in range(heads):
            here = slice(h * head_width, (h + 1) * head_width)
            gap = cum[rows, h : h + 1] - cum_row[h : h + 1, :]
            mix = (jnp.exp(jnp.where(mask, gap, FAR)) * scores).astype(BF)
            scanned_ref[rows, here] = nn(mix, scaled_ref[:, here])
    mixer_out = scanned_ref[...] + wide_ref[0:1, :] * x_conv
    gated = mixer_out * silu(pre_ref[:, inner:bc_at])
    square = jnp.sum(gated * gated, axis=1, keepdims=True)
    square_own_ref[...] = square[:half_tokens]
    square_other_ref[...] = square[half_tokens:]
    sent = (gated * wide_ref[1:2, :]).astype(BF)
    out_w = w_ref[:, out_at:dt_at]
    part_own_ref[...] = nt(sent[:half_tokens], out_w).astype(BF)
    part_other_ref[...] = nt(sent[half_tokens:], out_w).astype(BF)


def mixer_backward(
    inner,
    inner_all,
    head_width,
    experts,
    own_src,
    other_src,
    moe_own_src,
    moe_other_src,
    w_src,
    marks_src,
    row_src,
    taps_x_src,
    taps_bc_src,
    head_src,
    wide_src,
    pre_src,
    dt_src,
    cum_src,
    scanned_src,
    grads_ref,
    dt_grad_ref,
    normed_ref,
    part_own_ref,
    part_other_ref,
    small_ref,
    scaled_ref,
    low_ref,
    spread_ref,
    c_grad_ref,
    b_grad_ref,
    own_ref,
    other_ref,
    moe_own_ref,
    moe_other_ref,
    w_ref,
    marks_ref,
    row_ref,
    taps_x_ref,
    taps_bc_ref,
    head_ref,
    wide_ref,
    pre_ref,
    dt_ref,
    cum_ref,
    scanned_ref,
    sems,
):
    half_tokens = own_ref.shape[0]
    width = w_ref.shape[0]
    split = pre_ref.shape[1]
    copies = fetched(
        (
            (w_src.at[:, split:], w_ref.at[:, split:]),
            (own_src, own_ref),
            (other_src, other_ref),
            (moe_own_src.at[:, width:], moe_own_ref.at[:, width:]),
            (moe_other_src.at[:, width:], moe_other_ref.at[:, width:]),
            (pre_src, pre_ref),
            (scanned_src, scanned_ref),
            (dt_src, dt_ref),
            (cum_src, cum_ref),
            (marks_src, marks_ref),
            (row_src, row_ref),
            (taps_x_src, taps_x_ref),
            (taps_bc_src, taps_bc_ref),
            (head_src, head_ref),
            (wide_src, wide_ref),
            (w_src.at[:, :split], w_ref.at[:, :split]),
        ),
        sems,
    )
    tokens = 2 * half_tokens
    heads = inner // head_width
    bc_at, out_at, dt_at = 2 * inner, pre_ref.shape[1], pre_ref.shape[1] + inner
    state = (out_at - bc_at) // 2
    stack = lambda a, b: jnp.concatenate([a, b], 0)
    for copy in copies[:3]:
        copy.wait()
    out_w = w_ref[:, out_at:dt_at]
    gate_norm_grad = stack(
        nn(own_ref[:, :width], out_w), nn(other_ref[:, :width], out_w)
    )
    for copy in copies[3:15]:
        copy.wait()
    marks, marks_row = marks_ref[...], row_ref[...]
    conv_x = convolved(pre_ref[:, :inner], taps_x_ref[...], marks)
    conv_bc = convolved(pre_ref[:, bc_at:out_at], taps_bc_ref[...], marks)
    x_conv = silu(conv_x)
    bc = silu(conv_bc).astype(BF)
    b_map, c_map = bc[:, :state], bc[:, state:]
    z_pre = pre_ref[:, inner:bc_at]
    step = softplus(dt_ref[...])
    rate = head_ref[1:2, :]
    skip_wide, gain = wide_ref[0:1, :], wide_ref[1:2, :]
    at = width + experts
    dots = lambda ref: one(ref[:, at : at + 1], ref[:, at + 1 : at + 2])
    gate_dot = stack(dots(own_ref), dots(other_ref))
    gates = lambda ref: one(ref[:, width : width + 1], ref[:, width + 1 : width + 2])
    inv_gate = stack(gates(moe_own_ref), gates(moe_other_ref))
    sig = jax.nn.sigmoid(z_pre)
    silu_z = z_pre * sig
    mixer_out = scanned_ref[...] + skip_wide * x_conv
    gated = mixer_out * silu_z
    normed = gated * inv_gate
    small_ref[...] = jnp.zeros_like(small_ref)

    def keep_small(row, value):
        for at in range(0, value.shape[1], 128):
            piece = value[:, at : at + 128]
            small_ref[row : row + 1, : piece.shape[1]] = piece
            row = row + 1

    keep_small(GATE_ROW, jnp.sum(gate_norm_grad * normed, axis=0, keepdims=True))
    normed_ref[...] = (normed * gain).astype(BF)
    gated_grad = inv_gate * (gate_norm_grad * gain) - gated * (
        inv_gate * inv_gate * gate_dot * (1.0 / inner_all)
    )
    ssm_grad = gated_grad * silu_z
    grads_ref[:, inner:bc_at] = (
        gated_grad * mixer_out * (sig * (1.0 + z_pre * (1.0 - sig)))
    ).astype(BF)
    columns = head_columns(inner, dt_ref.shape[1], head_width)
    skips = by_head(
        jnp.broadcast_to(jnp.sum(ssm_grad * x_conv, axis=0, keepdims=True), (8, inner)), columns
    )
    keep_small(HEAD_ROW + 2, skips[0:1, :heads])
    low_ref[...] = ssm_grad.astype(BF)
    for h in range(heads):
        here = slice(h * head_width, (h + 1) * head_width)
        scaled_ref[:, here] = (x_conv[:, here] * step[:, h : h + 1]).astype(BF)
    cum = cum_ref[...]
    cum_row = jnp.concatenate([cum, jnp.zeros_like(cum)], 1).T
    c_grad_ref[...] = jnp.zeros_like(c_grad_ref)
    block = 128
    for start in range(0, tokens, block):
        rows = slice(start, start + block)
        scores = nt(b_map[rows, :], c_map)
        mask = (marks_row[1:2, :] >= marks[rows, 1:2]) & (
            marks_row[0:1, :] == marks[rows, 0:1]
        )
        scores_grad = jnp.zeros((block, tokens), F32)
        for h in range(heads):
            here = slice(h * head_width, (h + 1) * head_width)
            gap = cum_row[h : h + 1, :] - cum[rows, h : h + 1]
            decay = jnp.exp(jnp.where(mask, gap, FAR))
            spread_ref[rows, here] = nn((decay * scores).astype(BF), low_ref[:, here])
            scores_grad = scores_grad + decay * nt(scaled_ref[rows, here], low_ref[:, here])
        scores_low = scores_grad.astype(BF)
        b_grad_ref[rows, :] = nn(scores_low, c_map)
        c_grad_ref[...] += tn(scores_low, b_map[rows, :])
    spread = spread_ref[...]
    step_grad = by_head(x_conv * spread, columns)
    cum_grad = by_head(
        low_ref[...].astype(F32) * scanned_ref[...] - scaled_ref[...].astype(F32) * spread, columns
    )
    upper = jnp.where(marks_row[1:2, :] >= marks[:, 1:2], 1.0, 0.0).astype(BF)
    decay_grad = exact(upper, cum_grad)
    dt_float = (step_grad - decay_grad * rate) * jax.nn.sigmoid(dt_ref[...])
    keep_small(HEAD_ROW, jnp.sum(dt_float, axis=0, keepdims=True)[:, :heads])
    keep_small(
        HEAD_ROW + 1, jnp.sum(decay_grad * (-step * rate), axis=0, keepdims=True)[:, :heads]
    )
    dt_low = dt_float.astype(BF)
    dt_grad_ref[...] = dt_low
    for h in range(heads):
        here = slice(h * head_width, (h + 1) * head_width)
        spread_ref[:, here] = spread[:, here] * step[:, h : h + 1]

    def back(value_grad, total, value, taps, small_row, to):
        sig_c = jax.nn.sigmoid(total)
        grad = value_grad * (sig_c * (1.0 + total * (1.0 - sig_c)))
        keep_small(small_row + 6, jnp.sum(grad * value, axis=0, keepdims=True))
        result = taps[3:4, :] * grad
        for lag in range(1, 4):
            kept = grad * marks[:, 1 + lag : 2 + lag]
            keep_small(
                small_row + 2 * (3 - lag),
                jnp.sum(kept * pltpu.roll(value, lag, 0), axis=0, keepdims=True),
            )
            result = result + taps[3 - lag : 4 - lag, :] * pltpu.roll(kept, tokens - lag, 0)
        grads_ref[:, to] = result.astype(BF)

    back(
        spread_ref[...] + ssm_grad * skip_wide,
        conv_x,
        pre_ref[:, :inner],
        taps_x_ref[...],
        TAPS_X_ROW,
        slice(0, inner),
    )
    back(
        jnp.concatenate([b_grad_ref[...], c_grad_ref[...]], 1),
        conv_bc,
        pre_ref[:, bc_at:out_at],
        taps_bc_ref[...],
        TAPS_BC_ROW,
        slice(bc_at, out_at),
    )
    copies[15].wait()
    for part, dst in ((0, part_own_ref), (1, part_other_ref)):
        rows = slice(part * half_tokens, (part + 1) * half_tokens)
        dst[...] = (
            nt(grads_ref[rows, :], w_ref[:, :out_at]) + nt(dt_low[rows, :], w_ref[:, dt_at:])
        ).astype(BF)


def mixer_products(
    inner,
    experts,
    own_ref,
    other_ref,
    mix_own_ref,
    mix_other_ref,
    moe_own_ref,
    moe_other_ref,
    grads_ref,
    dt_grad_ref,
    normed_ref,
    sums_ref,
):
    half_tokens, width = own_ref.shape
    out_at = grads_ref.shape[1]
    dt_at = out_at + inner
    count = sums_ref.shape[0]
    rows = width // count
    group = min(8, count)
    first, second = slice(0, half_tokens), slice(half_tokens, 2 * half_tokens)
    logits = slice(width, width + experts)
    for at in range(0, count, group):
        here = slice(at * rows, (at + group) * rows)
        mine, others = own_ref[:, here], other_ref[:, here]
        a = tn(mine, grads_ref[first, :]) + tn(others, grads_ref[second, :])
        b = tn(mix_own_ref[:, here], normed_ref[first, :]) + tn(
            mix_other_ref[:, here], normed_ref[second, :]
        )
        c = tn(mine, dt_grad_ref[first, :]) + tn(others, dt_grad_ref[second, :])
        d = tn(moe_own_ref[:, here], mix_own_ref[:, logits]) + tn(
            moe_other_ref[:, here], mix_other_ref[:, logits]
        )
        a, b, c, d = a.astype(BF), b.astype(BF), c.astype(BF), d.astype(BF)
        for k in range(group):
            part = slice(k * rows, (k + 1) * rows)
            sums_ref[at + k, :, :out_at] = a[part]
            sums_ref[at + k, :, out_at:dt_at] = b[part]
            sums_ref[at + k, :, dt_at : dt_at + 64] = c[part]
            sums_ref[at + k, :, dt_at + 16 : dt_at + 16 + experts] = d[part]
            sums_ref[at + k, :, dt_at + 64 :] = jnp.zeros((rows, 128), BF)


def experts_both_ways(
    units,
    shared,
    own_ref,
    other_ref,
    cot_own_src,
    cot_other_src,
    w_src,
    routes_own_ref,
    routes_other_ref,
    mine_ref,
    in_own_ref,
    in_other_ref,
    out_own_ref,
    out_other_ref,
    grads_ref,
    acts_ref,
    gates_ref,
    gates_grad_own_ref,
    gates_grad_other_ref,
    cot_own_ref,
    cot_other_ref,
    w_ref,
    sems,
):
    half_tokens = own_ref.shape[0]
    width = w_ref.shape[0]
    experts = mine_ref.shape[1]
    in_units = 2 * (units + shared)
    down_at = in_units + 128
    late, cot_one, first, cot_two = fetched(
        (
            (w_src.at[:, down_at:], w_ref.at[:, down_at:]),
            (cot_own_src, cot_own_ref),
            (w_src.at[:, :down_at], w_ref.at[:, :down_at]),
            (cot_other_src, cot_other_ref),
        ),
        sems,
    )
    mine = mine_ref[...]
    number = lax.broadcasted_iota(jnp.int32, (half_tokens, experts), 1)
    down_end = down_at + units + shared
    parts = (
        (own_ref, cot_own_ref, routes_own_ref, in_own_ref, out_own_ref, gates_grad_own_ref),
        (
            other_ref,
            cot_other_ref,
            routes_other_ref,
            in_other_ref,
            out_other_ref,
            gates_grad_other_ref,
        ),
    )
    for part, (src, cot, routes, in_dst, out_dst, gates_dst) in enumerate(parts):
        rows = slice(part * half_tokens, (part + 1) * half_tokens)
        if part == 0:
            late.wait()
        (cot_one, cot_two)[part].wait()
        back = nn(cot[...], w_ref[:, down_at:down_end])
        if part == 0:
            first.wait()
        pre = nn(src[:, :width], w_ref[:, :down_at])
        named = number == routes[:, 0:1]
        for k in range(1, routes.shape[1]):
            named = named | (number == routes[:, k : k + 1])
        logits = jnp.where(named, pre[:, in_units : in_units + experts], FAR)
        raised = jnp.exp(logits - jnp.max(logits, axis=1, keepdims=True))
        gates = raised / jnp.sum(raised, axis=1, keepdims=True)
        gates_ref[rows, :] = gates
        weight = jnp.sum(gates * mine, axis=1, keepdims=True)
        gate, up = pre[:, :units], pre[:, units : 2 * units]
        sig = jax.nn.sigmoid(gate)
        silu_gate = gate * sig
        act = silu_gate * up
        acts_ref[rows, :units] = (act * weight).astype(BF)
        act_back = back[:, :units]
        gates_dst[...] = jnp.sum(act * act_back, axis=1, keepdims=True) * mine
        act_grad = act_back * weight
        grads_ref[rows, :units] = (
            act_grad * up * (sig * (1.0 + gate * (1.0 - sig)))
        ).astype(BF)
        grads_ref[rows, units : 2 * units] = (act_grad * silu_gate).astype(BF)
        gate, up = pre[:, 2 * units : 2 * units + shared], pre[:, 2 * units + shared : in_units]
        sig = jax.nn.sigmoid(gate)
        silu_gate = gate * sig
        acts_ref[rows, units:] = (silu_gate * up).astype(BF)
        act_grad = back[:, units:]
        grads_ref[rows, 2 * units : 2 * units + shared] = (
            act_grad * up * (sig * (1.0 + gate * (1.0 - sig)))
        ).astype(BF)
        grads_ref[rows, 2 * units + shared :] = (act_grad * silu_gate).astype(BF)
        in_dst[...] = nt(grads_ref[rows, :], w_ref[:, :in_units]).astype(BF)
        out_dst[...] = nt(acts_ref[rows, :], w_ref[:, down_at:down_end]).astype(BF)


def expert_products(
    own_ref, other_ref, cot_own_ref, cot_other_ref, grads_ref, acts_ref, sums_ref
):
    half_tokens, width = cot_own_ref.shape
    split = grads_ref.shape[1]
    first, second = slice(0, half_tokens), slice(half_tokens, 2 * half_tokens)
    block = 256
    for at in range(0, width, block):
        here = slice(at, at + block)
        sums_ref[here, :split] = (
            tn(own_ref[:, here], grads_ref[first, :]) + tn(other_ref[:, here], grads_ref[second, :])
        ).astype(BF)
        sums_ref[here, split:] = (
            tn(cot_own_ref[:, here], acts_ref[first, :])
            + tn(cot_other_ref[:, here], acts_ref[second, :])
        ).astype(BF)


def tail_sums(
    inner,
    heads,
    got_ref,
    out_ref,
    z_ref,
    x_ref,
    dt_ref,
    router_ref,
    conv_ref,
    gain_ref,
    head_ref,
    sent_ref,
):
    count, rows = got_ref.shape[0], out_ref.shape[0]
    experts = router_ref.shape[1]
    bc_at = 2 * inner
    small_at = got_ref.shape[2] - 128
    dt_at = small_at - 64
    out_at = dt_at - inner
    totals = []
    for core in range(2):
        total = got_ref[core].astype(F32)
        for at in range(core + 2, count, 2):
            total = total + got_ref[at].astype(F32)
        totals.append(total)
        here = slice(core * inner, (core + 1) * inner)
        x_ref[:, here] = total[:, :inner]
        z_ref[:, here] = total[:, inner:bc_at]
        out_ref[:, here] = total[:, out_at:dt_at]
        dt_ref[:, core * heads : (core + 1) * heads] = total[:, dt_at : dt_at + heads]
        small = total[:SMALL_ROWS, small_at:]

        def row_of(at):
            return jnp.concatenate([small[at : at + 1], small[at + 1 : at + 2, : inner - 128]], 1)

        for k in range(conv_ref.shape[0]):
            conv_ref[k : k + 1, here] = row_of(TAPS_X_ROW + 2 * k)
        gain_ref[:, here] = row_of(GATE_ROW)
        for k in range(3):
            head_ref[k : k + 1, core * heads : (core + 1) * heads] = small[
                HEAD_ROW + k : HEAD_ROW + k + 1, :heads
            ]
    router_ref[...] = totals[0][:, dt_at + 16 : dt_at + 16 + experts]
    sent_ref[:rows, :] = (totals[0][:, bc_at:out_at] + totals[1][:, bc_at:out_at]).astype(BF)
    small = totals[0][:TAPS_X_ROW, small_at:] + totals[1][:TAPS_X_ROW, small_at:]
    high = small.astype(BF)
    sent_ref[rows:, :128] = high
    sent_ref[rows:, 128:] = (small - high.astype(F32)).astype(BF)


def last_sums(got_ref, bc_ref, mix_ref, moe_ref, conv_ref):
    rows = bc_ref.shape[0]
    total = got_ref[0].astype(F32)
    for at in range(1, got_ref.shape[0]):
        total = total + got_ref[at].astype(F32)
    bc_ref[...] = total[:rows]
    small = total[rows:, :128] + total[rows:, 128:]
    half_rows = TAPS_BC_ROW // 2
    mix_ref[...] = small[:half_rows]
    moe_ref[...] = small[half_rows:TAPS_BC_ROW]
    for k in range(conv_ref.shape[0]):
        for part in range(2):
            at = TAPS_BC_ROW + 2 * k + part
            conv_ref[k : k + 1, part * 128 : (part + 1) * 128] = small[at : at + 1]


def chip_sum(own_ref, other_ref, extra_own_ref, extra_other_ref, sum_ref):
    width, more = own_ref.shape[1], extra_own_ref.shape[1]
    sum_ref[:, :width] = (own_ref[...].astype(F32) + other_ref[...].astype(F32)).astype(BF)
    extra = extra_own_ref[...] + extra_other_ref[...]
    high = extra.astype(BF)
    sum_ref[:, width:] = jnp.zeros((own_ref.shape[0], sum_ref.shape[1] - width), BF)
    sum_ref[:, width : width + more] = high
    sum_ref[:, width + more : width + 2 * more] = (extra - high.astype(F32)).astype(BF)


def second_shard(
    got_ref,
    residual_ref,
    mix_out_ref,
    cot_ref,
    gates_ref,
    router_ref,
    inv_ref,
    gain_ref,
    sent_ref,
    grad_ref,
    gain_grad_ref,
):
    width, experts = residual_ref.shape[1], gates_ref.shape[1]
    total = got_ref[0].astype(F32)
    for at in range(1, got_ref.shape[0]):
        total = total + got_ref[at].astype(F32)
    gates = gates_ref[...]
    gates_grad = total[:, width : width + experts] + total[:, width + experts : width + 2 * experts]
    logits_grad = (
        gates * (gates_grad - jnp.sum(gates * gates_grad, axis=1, keepdims=True))
    ).astype(BF)
    moe_in_grad = total[:, :width] + nt(logits_grad, router_ref[...])
    residual, inv = residual_ref[...], inv_ref[...]
    scaled = moe_in_grad * gain_ref[...]
    mean = jnp.sum(scaled * residual, axis=1, keepdims=True) * (1.0 / width)
    grad = cot_ref[...].astype(F32) + inv * scaled - residual * (inv * inv * inv * mean)
    grad_ref[...] = grad
    gain_grad_ref[...] = jnp.sum(moe_in_grad * residual * inv, axis=0, keepdims=True)
    grad_low = grad.astype(BF)
    gate_dot = jnp.sum(grad_low.astype(F32) * mix_out_ref[...], axis=1, keepdims=True)
    high = gate_dot.astype(BF)
    sent_ref[:, :width] = grad_low
    sent_ref[:, width:] = jnp.zeros((residual.shape[0], sent_ref.shape[1] - width), BF)
    sent_ref[:, width : width + experts] = logits_grad
    sent_ref[:, width + experts : width + experts + 1] = high
    sent_ref[:, width + experts + 1 : width + experts + 2] = (
        gate_dot - high.astype(F32)
    ).astype(BF)


def mixer_rows(
    inner,
    heads,
    x_src,
    z_src,
    bc_src,
    out_src,
    dt_src,
    rows_ref,
    x_ref,
    z_ref,
    bc_ref,
    out_ref,
    dt_ref,
    sems,
):
    copies = fetched(
        (
            (x_src, x_ref),
            (z_src, z_ref),
            (bc_src, bc_ref),
            (out_src, out_ref),
            (dt_src, dt_ref),
        ),
        sems,
    )
    for copy in copies:
        copy.wait()
    bc_at = 2 * inner
    out_at = bc_at + bc_ref.shape[1]
    dt_at = out_at + inner
    lanes = rows_ref.shape[2] - dt_at
    for core in range(2):
        here = slice(core * inner, (core + 1) * inner)
        down = lax.broadcasted_iota(jnp.int32, (2 * heads, lanes), 0) - core * heads
        across = lax.broadcasted_iota(jnp.int32, (2 * heads, lanes), 1)
        pick = jnp.where((down == across) & (across < heads), 1.0, 0.0).astype(BF)
        parts = (
            (0, x_ref[:, here]),
            (inner, z_ref[:, here]),
            (bc_at, bc_ref[...]),
            (out_at, out_ref[:, here]),
            (dt_at, tn(dt_ref[...], pick).astype(BF)),
        )
        for at, value in parts:
            rows_ref[core, :, at : at + value.shape[1]] = value
        for at in range(core + 2, rows_ref.shape[0], 2):
            rows_ref[at] = rows_ref[core]


def expert_packs(
    units, shared, flag_ref, gate_ref, up_ref, sg_ref, su_ref, router_ref, down_ref, sd_ref, *packs
):
    first = flag_ref[0] == 0
    router_at = 2 * (units + shared)
    down_at = router_at + 128
    for which, dst in enumerate(packs):
        dst[...] = jnp.zeros_like(dst)
        lead = first if which == 0 else jnp.logical_not(first)

        def pick(a, b):
            return jnp.where(lead, a.astype(F32), b.astype(F32)).astype(BF)

        for ref, at in ((gate_ref, 0), (up_ref, units), (down_ref, down_at)):
            dst[:, at : at + units] = pick(ref[:, :units], ref[:, units:])
        for ref, at in (
            (sg_ref, 2 * units),
            (su_ref, 2 * units + shared),
            (sd_ref, down_at + units),
        ):
            dst[:, at : at + shared] = pick(ref[:, :shared], ref[:, shared:])
        dst[:, router_at : router_at + router_ref.shape[1]] = router_ref[...]


def joined(flag_ref, own_ref, other_ref, rows_ref):
    first = flag_ref[0] == 0
    rows = own_ref.shape[0]
    own, other = own_ref[...].astype(F32), other_ref[...].astype(F32)
    rows_ref[:rows] = jnp.where(first, own, other).astype(BF)
    rows_ref[rows:] = jnp.where(first, other, own).astype(BF)


def small_set(
    inner,
    heads,
    head_width,
    flag_ref,
    bias_ref,
    log_ref,
    skip_ref,
    seg_own_ref,
    seg_other_ref,
    taps_ref,
    gain_ref,
    marks_ref,
    row_ref,
    taps_x_ref,
    head_ref,
    wide_ref,
):
    first = flag_ref[0] == 0
    half_tokens = seg_own_ref.shape[1]
    tokens = 2 * half_tokens
    seg = jnp.concatenate([seg_own_ref[...], seg_other_ref[...]], 1).astype(F32)
    seg = jnp.broadcast_to(seg, (8, tokens))
    place = lax.broadcasted_iota(jnp.int32, (8, tokens), 1)
    turned = jnp.where(place < half_tokens, place + half_tokens, place - half_tokens)
    place = jnp.where(first, place, turned).astype(F32)
    before = pltpu.roll(seg, 1, 1)
    hold = jnp.where((seg == before) & (place > 0.0), 1.0, 0.0)
    kept_two = hold * pltpu.roll(hold, 1, 1)
    kept_three = kept_two * pltpu.roll(hold, 2, 1)
    which = lax.broadcasted_iota(jnp.int32, (8, tokens), 0)
    rows = jnp.where(which == 0, seg, 0.0)
    for k, value in enumerate((place, hold, kept_two, kept_three)):
        rows = jnp.where(which == k + 1, value, rows)
    row_ref[...] = rows
    tall = jnp.concatenate([rows, jnp.zeros((120, tokens), F32)], 0)
    marks_ref[...] = tall.T[:, :8]
    taps_x_ref[...] = jnp.where(first, taps_ref[:, :inner], taps_ref[:, inner:])
    lanes = head_ref.shape[1]
    lane = lax.broadcasted_iota(jnp.int32, (1, lanes), 1)
    bias, log, on = jnp.zeros((1, lanes), F32), jnp.zeros((1, lanes), F32), lane < heads
    across = lax.broadcasted_iota(jnp.int32, (1, inner), 1)
    skip = jnp.zeros((1, inner), F32)
    for h in range(heads):
        own = lambda ref: jnp.where(first, ref[h], ref[heads + h])
        bias = jnp.where(lane == h, own(bias_ref), bias)
        log = jnp.where(lane == h, own(log_ref), log)
        skip = jnp.where(
            (across >= h * head_width) & (across < (h + 1) * head_width), own(skip_ref), skip
        )
    head_ref[0:1, :] = bias
    head_ref[1:2, :] = jnp.where(on, jnp.exp(log), 0.0)
    wide_ref[0:1, :] = skip
    wide_ref[1:2, :] = jnp.where(first, gain_ref[:, :inner], gain_ref[:, inner:])


def exchange_rows(part, axis):
    count = lax.axis_size(axis)
    blocks = part.reshape(count, part.shape[0] // count, part.shape[1])
    return lax.all_to_all(blocks, axis, 0, 0, tiled=False)


def chip(own, other, extra_own, extra_other):
    rows, width = own.shape
    extra = call(
        chip_sum,
        [((rows, width + 128), BF)],
        (own, swap(other), extra_own, swap(extra_other)),
        10**6,
        "chip_sum",
    )
    return extra[0]


def from_tokens(own):
    return lax.all_gather(own, "col", axis=0, tiled=True)


def on_device(
    hidden,
    cotangent,
    segments,
    routes,
    gain_mix,
    w_z,
    w_x,
    w_bc,
    w_dt,
    conv_x,
    conv_bc,
    dt_bias,
    a_log,
    d_skip,
    gain_gate,
    out_t,
    gain_moe,
    w_router,
    w_gate_t,
    w_up_t,
    w_down_t,
    ws_gate,
    ws_up,
    ws_down_t,
):
    half_tokens, width = hidden.shape
    rows = lax.axis_size("row")
    cols = lax.axis_size("col")
    seq = lax.axis_index("seq")
    col = lax.axis_index("col")
    tokens = 2 * half_tokens
    inner = conv_x.shape[1] // 2
    heads = dt_bias.shape[0] // 2
    head_width = inner // heads
    state = conv_bc.shape[1] // 2
    experts = w_router.shape[1]
    hidden_units = w_gate_t.shape[2]
    shared_units = ws_gate.shape[1] // 2
    lanes = 64
    inner_all = conv_x.shape[1] * cols
    shard = half_tokens // cols

    out_at = 2 * inner + 2 * state
    dt_at = out_at + inner
    mixer_width = dt_at + lanes
    (spread_rows,) = call(
        functools.partial(mixer_rows, inner, heads),
        [((2 * rows, w_z.shape[0], mixer_width), BF)],
        (w_x, w_z, w_bc, out_t, w_dt.T),
        10**6,
        "mixer_rows",
        56,
        (),
        (0, 1, 2, 3, 4),
    )
    (
        spread_rows,
        hidden,
        cotangent,
        w_gate_t,
        w_up_t,
        w_down_t,
        ws_gate,
        ws_up,
        ws_down_t,
        w_router,
        conv_x,
        gain_gate,
        segments,
        routes,
    ) = lax.optimization_barrier(
        (
            spread_rows,
            hidden,
            cotangent,
            w_gate_t,
            w_up_t,
            w_down_t,
            ws_gate,
            ws_up,
            ws_down_t,
            w_router,
            conv_x,
            gain_gate,
            segments,
            routes,
        )
    )
    mixer_whole = lax.all_to_all(spread_rows, ("row", "seq"), 0, 0).reshape(width, mixer_width)

    inv_mix = lax.rsqrt(jnp.mean(hidden * hidden, axis=1) + EPS)
    mix_own = (hidden * inv_mix[:, None] * gain_mix).astype(BF)
    mix_other = swap(mix_own)
    cot_other = swap(cotangent)
    routes_other = swap(routes)
    flag = seq.astype(jnp.int32)[None]

    down_units = hidden_units + shared_units
    in_units = 2 * down_units
    down_at = in_units + 128
    weight_rows = w_z.shape[0]
    packed = -(-(down_at + down_units) // 128) * 128
    flat = lambda a: a.reshape(weight_rows, 2 * hidden_units)
    pack_own, pack_other = call(
        functools.partial(expert_packs, hidden_units, shared_units),
        [((weight_rows, packed), BF)] * 2,
        (
            flag,
            flat(w_gate_t),
            flat(w_up_t),
            ws_gate,
            ws_up,
            w_router,
            flat(w_down_t),
            ws_down_t,
        ),
        10**6,
        "expert_packs",
        scalars=(0,),
    )
    (expert_rows,) = call(
        joined,
        [((2 * weight_rows, packed), BF)],
        (flag, pack_own, swap(pack_other)),
        10**6,
        "expert_rows",
        scalars=(0,),
    )
    seg_own = segments[None]
    marks, marks_row, taps_x, head_rows, wide_rows = call(
        functools.partial(small_set, inner, heads, head_width),
        [
            ((tokens, 8), F32),
            ((8, tokens), F32),
            ((4, inner), F32),
            ((2, lanes), F32),
            ((2, inner), F32),
        ],
        (flag, dt_bias, a_log, d_skip, seg_own, swap(seg_own), conv_x, gain_gate[None]),
        10**6,
        "small_set",
        scalars=(0, 1, 2, 3),
    )
    expert_rows, mixer_whole, mix_own, mix_other, cot_other, routes_other, marks, marks_row = (
        lax.optimization_barrier(
            (
                expert_rows,
                mixer_whole,
                mix_own,
                mix_other,
                cot_other,
                routes_other,
                marks,
                marks_row,
            )
        )
    )
    expert_whole = lax.all_gather(expert_rows, "row", axis=0, tiled=True)

    fixed = (mixer_whole, marks, marks_row, taps_x, conv_bc, head_rows, wide_rows)
    pre, dt_in, cum, scanned, part_own, part_other, square_own, square_other = call(
        functools.partial(mixer_forward, inner, head_width),
        [
            ((tokens, out_at), F32),
            ((tokens, lanes), F32),
            ((tokens, lanes), F32),
            ((tokens, inner), F32),
            ((half_tokens, width), BF),
            ((half_tokens, width), BF),
            ((half_tokens, 1), F32),
            ((half_tokens, 1), F32),
        ],
        (mix_own, mix_other, *fixed),
        4 * 10**9,
        "mixer_forward",
        28,
        [((tokens, inner), BF)],
        (2,),
    )
    mix_sum = exchange_rows(chip(part_own, part_other, square_own, square_other), "col")
    mix_sum = jnp.sum(mix_sum.astype(F32), axis=0)
    square = mix_sum[:, width : width + 1] + mix_sum[:, width + 1 : width + 2]
    mix_sum = mix_sum[:, :width]

    here = lax.dynamic_slice_in_dim(hidden, col * shard, shard, 0)
    inv_gate_here = lax.rsqrt(square / inner_all + EPS)
    mix_out = mix_sum * inv_gate_here
    residual = here + mix_out
    inv_moe_here = lax.rsqrt(jnp.mean(residual * residual, axis=1, keepdims=True) + EPS)
    moe_here = (residual * inv_moe_here * gain_moe).astype(BF)
    moe_own = from_tokens(
        jnp.concatenate(
            [moe_here, *two(inv_gate_here), *two(inv_moe_here), jnp.zeros((shard, 124), BF)], 1
        )
    )
    moe_own, expert_whole = lax.optimization_barrier((moe_own, expert_whole))
    inv_moe = one(moe_own[:, width + 2], moe_own[:, width + 3])
    moe_other = swap(moe_own)

    mine = (jnp.arange(experts) == 2 * col + seq).astype(F32)[None, :]
    in_own, in_other, out_own, out_other, in_grads, acts, gates, *gates_grad = call(
        functools.partial(experts_both_ways, hidden_units, shared_units),
        [
            ((half_tokens, width), BF),
            ((half_tokens, width), BF),
            ((half_tokens, width), BF),
            ((half_tokens, width), BF),
            ((tokens, in_units), BF),
            ((tokens, down_units), BF),
            ((tokens, experts), F32),
            ((half_tokens, experts), F32),
            ((half_tokens, experts), F32),
        ],
        (moe_own, moe_other, cotangent, cot_other, expert_whole, routes, routes_other, mine),
        6 * 10**9,
        "experts_both_ways",
        46,
        (),
        (2, 3, 4),
    )
    moe_got = exchange_rows(chip(in_own, in_other, *gates_grad), "col")
    (expert_sums,) = call(
        expert_products,
        [((width, in_units + down_units), BF)],
        (moe_own, moe_other, cotangent, cot_other, in_grads, acts),
        3 * 10**9,
        "expert_products",
        28,
    )
    chip_out = (out_own.astype(F32) + swap(out_other).astype(F32)).astype(BF)
    moe_got, expert_sums, chip_out, cot_here, gates_here, router, gain_row = (
        lax.optimization_barrier(
            (
                moe_got,
                expert_sums,
                chip_out,
                lax.dynamic_slice_in_dim(cotangent, col * shard, shard, 0),
                lax.dynamic_slice_in_dim(gates, col * shard, shard, 0),
                expert_whole[:, in_units : in_units + experts],
                gain_moe[None],
            )
        )
    )
    expert_sums = lax.psum_scatter(expert_sums, "row", scatter_dimension=0, tiled=True)

    sent, residual_grad, gain_moe_grad = call(
        second_shard,
        [((shard, width + 128), BF), ((shard, width), F32), ((1, width), F32)],
        (
            moe_got,
            residual,
            mix_out,
            cot_here,
            gates_here,
            router,
            inv_moe_here,
            gain_row,
        ),
        10**7,
        "second_shard",
    )
    grad_own = from_tokens(sent)

    grad_own, chip_out = lax.optimization_barrier((grad_own, chip_out))
    grad_other = swap(grad_own)
    out_got = exchange_rows(chip_out, "col")

    grads, dt_grad, normed_gate, part_own, part_other, small = call(
        functools.partial(mixer_backward, inner, inner_all, head_width, experts),
        [
            ((tokens, out_at), BF),
            ((tokens, lanes), BF),
            ((tokens, inner), BF),
            ((half_tokens, width), BF),
            ((half_tokens, width), BF),
            ((SMALL_ROWS, 128), F32),
        ],
        (grad_own, grad_other, moe_own, moe_other, *fixed, pre, dt_in, cum, scanned),
        5 * 10**9,
        "mixer_backward",
        56,
        [
            ((tokens, inner), BF),
            ((tokens, inner), BF),
            ((tokens, inner), F32),
            ((tokens, state), F32),
            ((tokens, state), F32),
        ],
        tuple(range(15)),
    )
    chip_in = (part_own.astype(F32) + swap(part_other).astype(F32)).astype(BF)
    chip_in, out_got = lax.optimization_barrier((chip_in, out_got))
    output_here = residual + jnp.sum(out_got.astype(F32), axis=0)
    output = 2.0 * lax.all_gather(
        after(0.5 * output_here, expert_sums), "col", axis=0, tiled=True
    )
    mix_in_got = exchange_rows(chip_in, "col")
    (mixer_sums,) = call(
        functools.partial(mixer_products, inner, experts),
        [((2 * rows, w_z.shape[0], mixer_width + 128), BF)],
        (
            mix_own,
            mix_other,
            grad_own,
            grad_other,
            moe_own,
            moe_other,
            grads,
            dt_grad,
            normed_gate,
        ),
        2 * 10**9,
        "mixer_products",
        28,
    )
    mix_in_got, mixer_sums = lax.optimization_barrier((mix_in_got, mixer_sums))
    mix_in_grad = jnp.sum(mix_in_got.astype(F32), axis=0)

    inv_here = lax.dynamic_slice_in_dim(inv_mix, col * shard, shard, 0)[:, None]
    scaled_mix = mix_in_grad * gain_mix
    grad_hidden_here = (
        residual_grad
        + inv_here * scaled_mix
        - here * (inv_here**3 * jnp.mean(scaled_mix * here, axis=1, keepdims=True))
    )
    gain_mix_grad = jnp.sum(mix_in_grad * here * inv_here, axis=0)

    gains = jnp.concatenate([gain_mix_grad.reshape(-1, 128), gain_moe_grad.reshape(-1, 128)])
    small = jnp.concatenate([gains, small[TAPS_BC_ROW:]]).astype(BF)
    mixer_sums = lax.dynamic_update_slice(
        mixer_sums, jnp.broadcast_to(small[None], (2 * rows, *small.shape)), (0, 0, mixer_width)
    )
    got = lax.all_to_all(mixer_sums, ("row", "seq"), 0, 0)
    grad_hidden = from_tokens(grad_hidden_here.astype(BF))
    grad_hidden = grad_hidden.astype(F32)

    own = own_half(expert_sums, 0)
    other = swap(other_half(expert_sums, 0))

    def expert(at):
        a = own[:, None, at : at + hidden_units]
        return join(a, other[:, None, at : at + hidden_units], 1).astype(F32)

    def shared(at):
        return join(
            own[:, at : at + shared_units], other[:, at : at + shared_units], 1
        ).astype(F32)

    g_w_gate_t = expert(0)
    g_w_up_t = expert(hidden_units)
    g_w_down_t = expert(in_units)
    g_ws_gate = shared(2 * hidden_units)
    g_ws_up = shared(2 * hidden_units + shared_units)
    g_ws_down_t = shared(in_units + hidden_units)
    (
        got,
        grad_hidden,
        g_w_gate_t,
        g_w_up_t,
        g_w_down_t,
        g_ws_gate,
        g_ws_up,
        g_ws_down_t,
        inv_moe,
    ) = lax.optimization_barrier(
        (
            got,
            grad_hidden,
            g_w_gate_t,
            g_w_up_t,
            g_w_down_t,
            g_ws_gate,
            g_ws_up,
            g_ws_down_t,
            inv_moe,
        )
    )
    (
        g_out_t,
        g_w_z,
        g_w_x,
        g_w_dt,
        g_w_router,
        g_conv_x,
        g_gain_gate,
        by_heads,
        sent,
    ) = call(
        functools.partial(tail_sums, inner, heads),
        [
            ((weight_rows, 2 * inner), F32),
            ((weight_rows, 2 * inner), F32),
            ((weight_rows, 2 * inner), F32),
            ((weight_rows, 2 * heads), F32),
            ((weight_rows, experts), F32),
            ((4, 2 * inner), F32),
            ((1, 2 * inner), F32),
            ((3, 2 * heads), F32),
            ((weight_rows + 32, 2 * state), BF),
        ],
        (got,),
        10**7,
        "tail_sums",
        16,
    )
    g_gain_gate = g_gain_gate.reshape(-1)
    g_dt_bias, g_a_log, g_d_skip = by_heads[0], by_heads[1], by_heads[2]
    got = lax.all_to_all(jnp.broadcast_to(sent[None], (cols, *sent.shape)), "col", 0, 0)
    got, output = lax.optimization_barrier((got, output))
    g_w_bc, g_gain_mix, g_gain_moe, g_conv_bc = call(
        last_sums,
        [
            ((weight_rows, 2 * state), F32),
            ((width // 128, 128), F32),
            ((width // 128, 128), F32),
            ((4, 2 * state), F32),
        ],
        (got,),
        10**6,
        "last_sums",
    )
    g_gain_mix, g_gain_moe = g_gain_mix.reshape(-1), g_gain_moe.reshape(-1)

    return (
        output,
        grad_hidden,
        inv_mix,
        inv_moe,
        g_gain_mix,
        g_w_z,
        g_w_x,
        g_w_bc,
        g_w_dt,
        g_conv_x,
        g_conv_bc,
        g_dt_bias,
        g_a_log,
        g_d_skip,
        g_gain_gate,
        g_out_t,
        g_gain_moe,
        g_w_router,
        g_w_gate_t,
        g_w_up_t,
        g_w_down_t,
        g_ws_gate,
        g_ws_up,
        g_ws_down_t,
    )


def solution(mesh):
    placed = (
        P(("row", "seq"), None),
        P(("row", "seq"), None),
        P(("row", "seq")),
        P(("row", "seq"), None),
        P(),
        P(("row", "seq"), "col"),
        P(("row", "seq"), "col"),
        P(("row", "seq"), None),
        P(("row", "seq"), "col"),
        P(None, "col"),
        P(),
        P("col"),
        P("col"),
        P("col"),
        P("col"),
        P(("row", "seq"), "col"),
        P(),
        P(("row", "seq"), None),
        P(("row", "seq"), "col", None),
        P(("row", "seq"), "col", None),
        P(("row", "seq"), "col", None),
        P(("row", "seq"), "col"),
        P(("row", "seq"), "col"),
        P(("row", "seq"), "col"),
    )
    return jax.shard_map(
        on_device,
        mesh=mesh,
        in_specs=placed,
        out_specs=(
            P(("row", "seq"), None),
            P(("row", "seq"), None),
            P(("row", "seq")),
            P(("row", "seq")),
            P(),
            P(("row", "seq"), "col"),
            P(("row", "seq"), "col"),
            P(("row", "seq"), None),
            P(("row", "seq"), "col"),
            P(None, "col"),
            P(),
            P("col"),
            P("col"),
            P("col"),
            P("col"),
            P(("row", "seq"), "col"),
            P(),
            P(("row", "seq"), None),
            P(("row", "seq"), "col", None),
            P(("row", "seq"), "col", None),
            P(("row", "seq"), "col", None),
            P(("row", "seq"), "col"),
            P(("row", "seq"), "col"),
            P(("row", "seq"), "col"),
        ),
        check_vma=False,
    )
```

```python
import functools

import jax
import jax.numpy as jnp
from jax import lax
from jax.experimental import pallas as pl
from jax.experimental.pallas import tpu as pltpu
from jax.sharding import PartitionSpec as P

EPS = 1e-05
BF = jnp.bfloat16
F32 = jnp.float32
FAR = -1e30
TAPS_BC_ROW, TAPS_X_ROW, GATE_ROW, HEAD_ROW, SMALL_ROWS = 24, 32, 40, 42, 48


def silu(v):
    return v * jax.nn.sigmoid(v)


def nn(left, right):
    return lax.dot_general(left, right, (((1,), (0,)), ((), ())), preferred_element_type=F32)


def nt(left, right):
    return lax.dot_general(left, right, (((1,), (1,)), ((), ())), preferred_element_type=F32)


def tn(left, right):
    return lax.dot_general(left, right, (((0,), (0,)), ((), ())), preferred_element_type=F32)


def swap(value):
    return lax.ppermute(value, "seq", [(0, 1), (1, 0)])


def half(value, axis, which):
    size = value.shape[axis] // 2
    return lax.slice_in_dim(value, which * size, (which + 1) * size, axis=axis)


def own_half(value, axis):
    first = lax.axis_index("seq") == 0
    return jnp.where(first, half(value, axis, 0), half(value, axis, 1))


def other_half(value, axis):
    first = lax.axis_index("seq") == 0
    return jnp.where(first, half(value, axis, 1), half(value, axis, 0))


def join(own, other, axis):
    first = lax.axis_index("seq") == 0
    return jnp.where(
        first, jnp.concatenate([own, other], axis), jnp.concatenate([other, own], axis)
    )


def low(value):
    return lax.reduce_precision(value, 8, 7)


def two(value):
    high = low(value)
    return high.astype(BF), (value - high).astype(BF)


def three(value):
    high = value.astype(BF)
    rest = value - high.astype(F32)
    middle = rest.astype(BF)
    return high, middle, (rest - middle.astype(F32)).astype(BF)


def exact(left, value):
    high, middle, last = three(value)
    return (nn(left, last) + nn(left, middle)) + nn(left, high)


def one(high, low_term):
    return high.astype(F32) + low_term.astype(F32)


def after(value, *others):
    return lax.optimization_barrier((value, *others))[0]


def call(kernel, outs, args, flops, name, room=12, scratch=(), apart=(), scalars=()):
    whole = pl.BlockSpec(memory_space=pltpu.VMEM)
    spec = {i: pl.BlockSpec(memory_space=pltpu.HBM) for i in apart}
    spec.update({i: pl.BlockSpec(memory_space=pltpu.SMEM) for i in scalars})
    shapes = [jax.ShapeDtypeStruct(shape, kind) for shape, kind in outs]
    size = lambda a: a.size * jnp.dtype(a.dtype).itemsize
    held = [pltpu.VMEM(args[i].shape, args[i].dtype) for i in apart]
    if apart:
        held.append(pltpu.SemaphoreType.DMA((len(apart) + 1,)))
    return pl.pallas_call(
        kernel,
        out_shape=shapes,
        in_specs=[spec.get(i, whole) for i in range(len(args))],
        out_specs=[whole] * len(outs),
        scratch_shapes=[pltpu.VMEM(shape, kind) for shape, kind in scratch] + held,
        compiler_params=pltpu.CompilerParams(vmem_limit_bytes=room * 2**20),
        cost_estimate=pl.CostEstimate(
            flops=flops,
            bytes_accessed=sum(size(a) for a in args) + sum(size(a) for a in shapes),
            transcendentals=0,
        ),
        name=name,
    )(*args)


def fetched(pairs, sems):
    copies = [
        pltpu.make_async_copy(src, dst, sems.at[k]) for k, (src, dst) in enumerate(pairs)
    ]
    for copy in copies:
        copy.start()
    return copies


def saved_parts(saved_ref, out_at):
    end = saved_ref.shape[1]
    return (
        saved_ref.at[:, :out_at],
        saved_ref.at[:, out_at : end - 256],
        saved_ref.at[:, end - 256 : end - 128],
        saved_ref.at[:, end - 128 :],
    )


def causal(marks, marks_row, rows):
    return (marks[rows, 1:2] >= marks_row[1:2, :]) & (marks[rows, 0:1] == marks_row[0:1, :])


def convolved(value, taps, marks):
    total = taps[3:4, :] * value
    for lag in range(1, 4):
        rolled = pltpu.roll(value, lag, 0) * marks[:, 1 + lag : 2 + lag]
        total = total + taps[3 - lag : 4 - lag, :] * rolled
    return total


def head_columns(inner, lanes, head_width):
    down = lax.broadcasted_iota(jnp.int32, (inner, lanes), 0)
    across = lax.broadcasted_iota(jnp.int32, (inner, lanes), 1) * head_width
    return jnp.where((down >= across) & (down < across + head_width), 1.0, 0.0).astype(BF)


def by_head(value, columns):
    high, middle, last = three(value)
    return (nn(last, columns) + nn(middle, columns)) + nn(high, columns)


def softplus(v):
    return jnp.maximum(v, 0.0) + jnp.log1p(jnp.exp(-jnp.abs(v)))


def mixer_forward(
    inner,
    head_width,
    own_ref,
    other_ref,
    w_src,
    marks_ref,
    row_ref,
    taps_x_ref,
    taps_bc_ref,
    head_ref,
    wide_ref,
    saved_ref,
    part_own_ref,
    part_other_ref,
    square_own_ref,
    square_other_ref,
    scaled_ref,
    w_ref,
    sems,
):
    half_tokens, width = own_ref.shape
    tokens = 2 * half_tokens
    heads = inner // head_width
    lanes = head_ref.shape[1]
    dt_at = w_ref.shape[1] - lanes
    bc_at, out_at = 2 * inner, dt_at - inner
    pre_ref, scanned_ref, dt_ref, cum_ref = saved_parts(saved_ref, out_at)
    state = (out_at - bc_at) // 2
    copies = fetched(
        (
            (w_src.at[:, :out_at], w_ref.at[:, :out_at]),
            (w_src.at[:, out_at:], w_ref.at[:, out_at:]),
        ),
        sems,
    )
    for part, src in ((0, own_ref), (1, other_ref)):
        rows = slice(part * half_tokens, (part + 1) * half_tokens)
        if part == 0:
            copies[0].wait()
        pre_ref[rows, :] = nn(src[...], w_ref[:, :out_at])
        if part == 0:
            copies[1].wait()
        dt_ref[rows, :lanes] = nn(src[...], w_ref[:, dt_at:]) + head_ref[0:1, :]
    marks, marks_row = marks_ref[...], row_ref[...]
    x_conv = silu(convolved(pre_ref[:, :inner], taps_x_ref[...], marks))
    bc = silu(convolved(pre_ref[:, bc_at:out_at], taps_bc_ref[...], marks)).astype(BF)
    b_map, c_map = bc[:, :state], bc[:, state:]
    step = softplus(dt_ref[:, :lanes])
    lower = jnp.where(marks[:, 1:2] >= marks_row[1:2, :], 1.0, 0.0).astype(BF)
    cum = exact(lower, -step * head_ref[1:2, :])
    cum_ref[:, :lanes] = cum
    cum_row = jnp.concatenate([cum, jnp.zeros_like(cum)], 1).T
    for h in range(heads):
        here = slice(h * head_width, (h + 1) * head_width)
        scaled_ref[:, here] = (x_conv[:, here] * step[:, h : h + 1]).astype(BF)
    block = 128
    for at in range(0, tokens, block):
        rows = slice(at, at + block)
        scores = nt(c_map[rows, :], b_map)
        mask = causal(marks, marks_row, rows)
        for h in range(heads):
            here = slice(h * head_width, (h + 1) * head_width)
            gap = cum[rows, h : h + 1] - cum_row[h : h + 1, :]
            mix = (jnp.exp(jnp.where(mask, gap, FAR)) * scores).astype(BF)
            scanned_ref[rows, here] = nn(mix, scaled_ref[:, here])
    mixer_out = scanned_ref[:, :inner] + wide_ref[0:1, :] * x_conv
    gated = mixer_out * silu(pre_ref[:, inner:bc_at])
    square = jnp.sum(gated * gated, axis=1, keepdims=True)
    square_own_ref[...] = square[:half_tokens]
    square_other_ref[...] = square[half_tokens:]
    sent = (gated * wide_ref[1:2, :]).astype(BF)
    out_w = w_ref[:, out_at:dt_at]
    part_own_ref[...] = nt(sent[:half_tokens], out_w).astype(BF)
    part_other_ref[...] = nt(sent[half_tokens:], out_w).astype(BF)


def mixer_backward(
    inner,
    inner_all,
    head_width,
    experts,
    own_src,
    other_src,
    moe_own_src,
    moe_other_src,
    w_src,
    marks_src,
    row_src,
    taps_x_src,
    taps_bc_src,
    head_src,
    wide_src,
    saved_src,
    grads_ref,
    dt_grad_ref,
    normed_ref,
    part_own_ref,
    part_other_ref,
    small_ref,
    scaled_ref,
    low_ref,
    spread_ref,
    c_grad_ref,
    b_grad_ref,
    own_ref,
    other_ref,
    moe_own_ref,
    moe_other_ref,
    w_ref,
    marks_ref,
    row_ref,
    taps_x_ref,
    taps_bc_ref,
    head_ref,
    wide_ref,
    saved_ref,
    sems,
):
    half_tokens = own_ref.shape[0]
    width = w_ref.shape[0]
    lanes = head_ref.shape[1]
    dt_at = w_ref.shape[1] - lanes
    bc_at, out_at = 2 * inner, dt_at - inner
    split = out_at
    pre_ref, scanned_ref, dt_ref, cum_ref = saved_parts(saved_ref, out_at)
    copies = fetched(
        (
            (w_src.at[:, split:], w_ref.at[:, split:]),
            (own_src, own_ref),
            (other_src, other_ref),
            (moe_own_src.at[:, width:], moe_own_ref.at[:, width:]),
            (moe_other_src.at[:, width:], moe_other_ref.at[:, width:]),
            (saved_src, saved_ref),
            (marks_src, marks_ref),
            (row_src, row_ref),
            (taps_x_src, taps_x_ref),
            (taps_bc_src, taps_bc_ref),
            (head_src, head_ref),
            (wide_src, wide_ref),
            (w_src.at[:, :split], w_ref.at[:, :split]),
        ),
        sems,
    )
    tokens = 2 * half_tokens
    heads = inner // head_width
    state = (out_at - bc_at) // 2
    stack = lambda a, b: jnp.concatenate([a, b], 0)
    for copy in copies[:3]:
        copy.wait()
    out_w = w_ref[:, out_at:dt_at]
    gate_norm_grad = stack(
        nn(own_ref[:, :width], out_w), nn(other_ref[:, :width], out_w)
    )
    for copy in copies[3:12]:
        copy.wait()
    marks, marks_row = marks_ref[...], row_ref[...]
    conv_x = convolved(pre_ref[:, :inner], taps_x_ref[...], marks)
    conv_bc = convolved(pre_ref[:, bc_at:out_at], taps_bc_ref[...], marks)
    x_conv = silu(conv_x)
    bc = silu(conv_bc).astype(BF)
    b_map, c_map = bc[:, :state], bc[:, state:]
    z_pre = pre_ref[:, inner:bc_at]
    step = softplus(dt_ref[:, :lanes])
    rate = head_ref[1:2, :]
    skip_wide, gain = wide_ref[0:1, :], wide_ref[1:2, :]
    at = width + experts
    dots = lambda ref: one(ref[:, at : at + 1], ref[:, at + 1 : at + 2])
    gate_dot = stack(dots(own_ref), dots(other_ref))
    gates = lambda ref: one(ref[:, width : width + 1], ref[:, width + 1 : width + 2])
    inv_gate = stack(gates(moe_own_ref), gates(moe_other_ref))
    sig = jax.nn.sigmoid(z_pre)
    silu_z = z_pre * sig
    mixer_out = scanned_ref[:, :inner] + skip_wide * x_conv
    gated = mixer_out * silu_z
    normed = gated * inv_gate
    small_ref[...] = jnp.zeros_like(small_ref)

    def keep_small(row, value):
        for at in range(0, value.shape[1], 128):
            piece = value[:, at : at + 128]
            small_ref[row : row + 1, : piece.shape[1]] = piece
            row = row + 1

    keep_small(GATE_ROW, jnp.sum(gate_norm_grad * normed, axis=0, keepdims=True))
    normed_ref[...] = (normed * gain).astype(BF)
    gated_grad = inv_gate * (gate_norm_grad * gain) - gated * (
        inv_gate * inv_gate * gate_dot * (1.0 / inner_all)
    )
    ssm_grad = gated_grad * silu_z
    grads_ref[:, inner:bc_at] = (
        gated_grad * mixer_out * (sig * (1.0 + z_pre * (1.0 - sig)))
    ).astype(BF)
    columns = head_columns(inner, lanes, head_width)
    skips = by_head(
        jnp.broadcast_to(jnp.sum(ssm_grad * x_conv, axis=0, keepdims=True), (8, inner)), columns
    )
    keep_small(HEAD_ROW + 2, skips[0:1, :heads])
    low_ref[...] = ssm_grad.astype(BF)
    for h in range(heads):
        here = slice(h * head_width, (h + 1) * head_width)
        scaled_ref[:, here] = (x_conv[:, here] * step[:, h : h + 1]).astype(BF)
    cum = cum_ref[:, :lanes]
    cum_row = jnp.concatenate([cum, jnp.zeros_like(cum)], 1).T
    c_grad_ref[...] = jnp.zeros_like(c_grad_ref)
    block = 128
    for start in range(0, tokens, block):
        rows = slice(start, start + block)
        scores = nt(b_map[rows, :], c_map)
        mask = (marks_row[1:2, :] >= marks[rows, 1:2]) & (
            marks_row[0:1, :] == marks[rows, 0:1]
        )
        scores_grad = jnp.zeros((block, tokens), F32)
        for h in range(heads):
            here = slice(h * head_width, (h + 1) * head_width)
            gap = cum_row[h : h + 1, :] - cum[rows, h : h + 1]
            decay = jnp.exp(jnp.where(mask, gap, FAR))
            spread_ref[rows, here] = nn((decay * scores).astype(BF), low_ref[:, here])
            scores_grad = scores_grad + decay * nt(scaled_ref[rows, here], low_ref[:, here])
        scores_low = scores_grad.astype(BF)
        b_grad_ref[rows, :] = nn(scores_low, c_map)
        c_grad_ref[...] += tn(scores_low, b_map[rows, :])
    spread = spread_ref[...]
    step_grad = by_head(x_conv * spread, columns)
    cum_grad = by_head(
        low_ref[...].astype(F32) * scanned_ref[:, :inner] - scaled_ref[...].astype(F32) * spread, columns
    )
    upper = jnp.where(marks_row[1:2, :] >= marks[:, 1:2], 1.0, 0.0).astype(BF)
    decay_grad = exact(upper, cum_grad)
    dt_float = (step_grad - decay_grad * rate) * jax.nn.sigmoid(dt_ref[:, :lanes])
    keep_small(HEAD_ROW, jnp.sum(dt_float, axis=0, keepdims=True)[:, :heads])
    keep_small(
        HEAD_ROW + 1, jnp.sum(decay_grad * (-step * rate), axis=0, keepdims=True)[:, :heads]
    )
    dt_low = dt_float.astype(BF)
    dt_grad_ref[...] = dt_low
    for h in range(heads):
        here = slice(h * head_width, (h + 1) * head_width)
        spread_ref[:, here] = spread[:, here] * step[:, h : h + 1]

    def back(value_grad, total, value, taps, small_row, to):
        sig_c = jax.nn.sigmoid(total)
        grad = value_grad * (sig_c * (1.0 + total * (1.0 - sig_c)))
        keep_small(small_row + 6, jnp.sum(grad * value, axis=0, keepdims=True))
        result = taps[3:4, :] * grad
        for lag in range(1, 4):
            kept = grad * marks[:, 1 + lag : 2 + lag]
            keep_small(
                small_row + 2 * (3 - lag),
                jnp.sum(kept * pltpu.roll(value, lag, 0), axis=0, keepdims=True),
            )
            result = result + taps[3 - lag : 4 - lag, :] * pltpu.roll(kept, tokens - lag, 0)
        grads_ref[:, to] = result.astype(BF)

    back(
        spread_ref[...] + ssm_grad * skip_wide,
        conv_x,
        pre_ref[:, :inner],
        taps_x_ref[...],
        TAPS_X_ROW,
        slice(0, inner),
    )
    back(
        jnp.concatenate([b_grad_ref[...], c_grad_ref[...]], 1),
        conv_bc,
        pre_ref[:, bc_at:out_at],
        taps_bc_ref[...],
        TAPS_BC_ROW,
        slice(bc_at, out_at),
    )
    copies[12].wait()
    for part, dst in ((0, part_own_ref), (1, part_other_ref)):
        rows = slice(part * half_tokens, (part + 1) * half_tokens)
        dst[...] = (
            nt(grads_ref[rows, :], w_ref[:, :out_at]) + nt(dt_low[rows, :], w_ref[:, dt_at:])
        ).astype(BF)


def mixer_products(
    inner,
    experts,
    own_ref,
    other_ref,
    mix_own_ref,
    mix_other_ref,
    moe_own_ref,
    moe_other_ref,
    grads_ref,
    dt_grad_ref,
    normed_ref,
    sums_ref,
):
    half_tokens, width = own_ref.shape
    out_at = grads_ref.shape[1]
    dt_at = out_at + inner
    count = sums_ref.shape[0]
    rows = width // count
    group = min(8, count)
    first, second = slice(0, half_tokens), slice(half_tokens, 2 * half_tokens)
    logits = slice(width, width + experts)
    for at in range(0, count, group):
        here = slice(at * rows, (at + group) * rows)
        mine, others = own_ref[:, here], other_ref[:, here]
        a = tn(mine, grads_ref[first, :]) + tn(others, grads_ref[second, :])
        b = tn(mix_own_ref[:, here], normed_ref[first, :]) + tn(
            mix_other_ref[:, here], normed_ref[second, :]
        )
        c = tn(mine, dt_grad_ref[first, :]) + tn(others, dt_grad_ref[second, :])
        d = tn(moe_own_ref[:, here], mix_own_ref[:, logits]) + tn(
            moe_other_ref[:, here], mix_other_ref[:, logits]
        )
        a, b, c, d = a.astype(BF), b.astype(BF), c.astype(BF), d.astype(BF)
        for k in range(group):
            part = slice(k * rows, (k + 1) * rows)
            sums_ref[at + k, :, :out_at] = a[part]
            sums_ref[at + k, :, out_at:dt_at] = b[part]
            sums_ref[at + k, :, dt_at : dt_at + 64] = c[part]
            sums_ref[at + k, :, dt_at + 16 : dt_at + 16 + experts] = d[part]
            sums_ref[at + k, :, dt_at + 64 :] = jnp.zeros((rows, 128), BF)


def experts_both_ways(
    units,
    shared,
    src_ref,
    cot_ref,
    w_ref,
    routes_ref,
    mine_ref,
    in_ref,
    out_ref,
    grads_ref,
    acts_ref,
    gates_ref,
    gates_grad_ref,
):
    tokens, width = cot_ref.shape
    experts = mine_ref.shape[1]
    in_units = 2 * (units + shared)
    down_at = in_units + 128
    down_end = down_at + units + shared
    mine = mine_ref[...]
    number = lax.broadcasted_iota(jnp.int32, (tokens, experts), 1)
    back = nn(cot_ref[...], w_ref[:, down_at:down_end])
    pre = nn(src_ref[:, :width], w_ref[:, :down_at])
    named = number == routes_ref[:, 0:1]
    for k in range(1, routes_ref.shape[1]):
        named = named | (number == routes_ref[:, k : k + 1])
    logits = jnp.where(named, pre[:, in_units : in_units + experts], FAR)
    raised = jnp.exp(logits - jnp.max(logits, axis=1, keepdims=True))
    gates = raised / jnp.sum(raised, axis=1, keepdims=True)
    gates_ref[...] = gates
    weight = jnp.sum(gates * mine, axis=1, keepdims=True)
    gate, up = pre[:, :units], pre[:, units : 2 * units]
    sig = jax.nn.sigmoid(gate)
    silu_gate = gate * sig
    act = silu_gate * up
    acts_ref[:, :units] = (act * weight).astype(BF)
    act_back = back[:, :units]
    gates_grad_ref[...] = jnp.sum(act * act_back, axis=1, keepdims=True) * mine
    act_grad = act_back * weight
    grads_ref[:, :units] = (act_grad * up * (sig * (1.0 + gate * (1.0 - sig)))).astype(BF)
    grads_ref[:, units : 2 * units] = (act_grad * silu_gate).astype(BF)
    gate, up = pre[:, 2 * units : 2 * units + shared], pre[:, 2 * units + shared : in_units]
    sig = jax.nn.sigmoid(gate)
    silu_gate = gate * sig
    acts_ref[:, units:] = (silu_gate * up).astype(BF)
    act_grad = back[:, units:]
    grads_ref[:, 2 * units : 2 * units + shared] = (
        act_grad * up * (sig * (1.0 + gate * (1.0 - sig)))
    ).astype(BF)
    grads_ref[:, 2 * units + shared :] = (act_grad * silu_gate).astype(BF)
    in_ref[...] = nt(grads_ref[...], w_ref[:, :in_units]).astype(BF)
    out_ref[...] = nt(acts_ref[...], w_ref[:, down_at:down_end]).astype(BF)


def expert_products(
    own_ref,
    other_ref,
    cot_own_ref,
    cot_other_ref,
    grads_own_ref,
    grads_other_ref,
    acts_own_ref,
    acts_other_ref,
    sums_ref,
):
    width = cot_own_ref.shape[1]
    split = grads_own_ref.shape[1]
    block = 256
    for at in range(0, width, block):
        here = slice(at, at + block)
        sums_ref[here, :split] = (
            tn(own_ref[:, here], grads_own_ref[...]) + tn(other_ref[:, here], grads_other_ref[...])
        ).astype(BF)
        sums_ref[here, split:] = (
            tn(cot_own_ref[:, here], acts_own_ref[...])
            + tn(cot_other_ref[:, here], acts_other_ref[...])
        ).astype(BF)


def tail_sums(
    inner,
    heads,
    got_ref,
    out_ref,
    z_ref,
    x_ref,
    dt_ref,
    router_ref,
    conv_ref,
    gain_ref,
    head_ref,
    sent_ref,
):
    count, rows = got_ref.shape[0], out_ref.shape[0]
    experts = router_ref.shape[1]
    bc_at = 2 * inner
    small_at = got_ref.shape[2] - 128
    dt_at = small_at - 64
    out_at = dt_at - inner
    totals = []
    for core in range(2):
        total = got_ref[core].astype(F32)
        for at in range(core + 2, count, 2):
            total = total + got_ref[at].astype(F32)
        totals.append(total)
        here = slice(core * inner, (core + 1) * inner)
        x_ref[:, here] = total[:, :inner]
        z_ref[:, here] = total[:, inner:bc_at]
        out_ref[:, here] = total[:, out_at:dt_at]
        dt_ref[:, core * heads : (core + 1) * heads] = total[:, dt_at : dt_at + heads]
        small = total[:SMALL_ROWS, small_at:]

        def row_of(at):
            return jnp.concatenate([small[at : at + 1], small[at + 1 : at + 2, : inner - 128]], 1)

        for k in range(conv_ref.shape[0]):
            conv_ref[k : k + 1, here] = row_of(TAPS_X_ROW + 2 * k)
        gain_ref[:, here] = row_of(GATE_ROW)
        for k in range(3):
            head_ref[k : k + 1, core * heads : (core + 1) * heads] = small[
                HEAD_ROW + k : HEAD_ROW + k + 1, :heads
            ]
    router_ref[...] = totals[0][:, dt_at + 16 : dt_at + 16 + experts]
    bc = (totals[0][:, bc_at:out_at] + totals[1][:, bc_at:out_at]).astype(BF)
    small = totals[0][:TAPS_X_ROW, small_at:] + totals[1][:TAPS_X_ROW, small_at:]
    small = small.astype(BF)
    for to in range(sent_ref.shape[0]):
        sent_ref[to, :rows, :] = bc
        sent_ref[to, rows:, :128] = small[: TAPS_X_ROW // 2]
        sent_ref[to, rows:, 128:] = small[TAPS_X_ROW // 2 :]


def last_sums(got_ref, bc_ref, mix_ref, moe_ref, conv_ref):
    rows = bc_ref.shape[0]
    total = got_ref[0].astype(F32)
    for at in range(1, got_ref.shape[0]):
        total = total + got_ref[at].astype(F32)
    bc_ref[...] = total[:rows]
    small = jnp.concatenate([total[rows:, :128], total[rows:, 128:]], 0)
    half_rows = TAPS_BC_ROW // 2
    mix_ref[...] = small[:half_rows]
    moe_ref[...] = small[half_rows:TAPS_BC_ROW]
    for k in range(conv_ref.shape[0]):
        for part in range(2):
            at = TAPS_BC_ROW + 2 * k + part
            conv_ref[k : k + 1, part * 128 : (part + 1) * 128] = small[at : at + 1]


def chip_sum(own_ref, other_ref, extra_own_ref, extra_other_ref, sum_ref):
    width, more = own_ref.shape[1], extra_own_ref.shape[1]
    sum_ref[:, :width] = (own_ref[...].astype(F32) + other_ref[...].astype(F32)).astype(BF)
    extra = extra_own_ref[...] + extra_other_ref[...]
    high = extra.astype(BF)
    sum_ref[:, width:] = jnp.zeros((own_ref.shape[0], sum_ref.shape[1] - width), BF)
    sum_ref[:, width : width + more] = high
    sum_ref[:, width + more : width + 2 * more] = (extra - high.astype(F32)).astype(BF)


def second_shard(
    got_ref,
    residual_ref,
    mix_out_ref,
    cot_ref,
    gates_ref,
    router_ref,
    inv_ref,
    gain_ref,
    sent_ref,
    grad_ref,
    gain_grad_ref,
):
    width, experts = residual_ref.shape[1], gates_ref.shape[1]
    total = got_ref[0].astype(F32)
    for at in range(1, got_ref.shape[0]):
        total = total + got_ref[at].astype(F32)
    gates = gates_ref[...]
    gates_grad = total[:, width : width + experts] + total[:, width + experts : width + 2 * experts]
    logits_grad = (
        gates * (gates_grad - jnp.sum(gates * gates_grad, axis=1, keepdims=True))
    ).astype(BF)
    moe_in_grad = total[:, :width] + nt(logits_grad, router_ref[...])
    residual, inv = residual_ref[...], inv_ref[...]
    scaled = moe_in_grad * gain_ref[...]
    mean = jnp.sum(scaled * residual, axis=1, keepdims=True) * (1.0 / width)
    grad = cot_ref[...].astype(F32) + inv * scaled - residual * (inv * inv * inv * mean)
    grad_ref[...] = grad
    gain_grad_ref[...] = jnp.sum(moe_in_grad * residual * inv, axis=0, keepdims=True)
    grad_low = grad.astype(BF)
    gate_dot = jnp.sum(grad_low.astype(F32) * mix_out_ref[...], axis=1, keepdims=True)
    high = gate_dot.astype(BF)
    sent_ref[:, :width] = grad_low
    sent_ref[:, width:] = jnp.zeros((residual.shape[0], sent_ref.shape[1] - width), BF)
    sent_ref[:, width : width + experts] = logits_grad
    sent_ref[:, width + experts : width + experts + 1] = high
    sent_ref[:, width + experts + 1 : width + experts + 2] = (
        gate_dot - high.astype(F32)
    ).astype(BF)


def third_shard(
    got_src,
    here_src,
    residual_grad_src,
    gain_src,
    gain_moe_src,
    small_src,
    grad_ref,
    sent_ref,
    got_ref,
    here_ref,
    residual_grad_ref,
    gain_ref,
    gain_moe_ref,
    small_ref,
    sems,
):
    width = here_ref.shape[1]
    copies = fetched(
        (
            (got_src, got_ref),
            (here_src, here_ref),
            (residual_grad_src, residual_grad_ref),
            (gain_src, gain_ref),
            (gain_moe_src, gain_moe_ref),
            (small_src, small_ref),
        ),
        sems,
    )
    for copy in copies:
        copy.wait()
    total = got_ref[0].astype(F32)
    for at in range(1, got_ref.shape[0]):
        total = total + got_ref[at].astype(F32)
    here = here_ref[...]
    inv = lax.rsqrt(jnp.sum(here * here, axis=1, keepdims=True) * (1.0 / width) + EPS)
    scaled = total * gain_ref[...]
    mean = jnp.sum(scaled * here, axis=1, keepdims=True) * (1.0 / width)
    grad = residual_grad_ref[...] + inv * scaled - here * (inv * inv * inv * mean)
    grad_ref[...] = grad.astype(BF)
    gain_mix = jnp.sum(total * here * inv, axis=0, keepdims=True)
    sent_ref[...] = small_ref[...].astype(BF)
    for part, value in enumerate((gain_mix, gain_moe_ref[...])):
        rows = [value[:, at : at + 128] for at in range(0, width, 128)]
        count = len(rows)
        sent_ref[part * count : (part + 1) * count, :] = jnp.concatenate(rows, 0).astype(BF)


def mixer_rows(
    inner,
    heads,
    x_src,
    z_src,
    bc_src,
    out_src,
    dt_src,
    rows_ref,
    x_ref,
    z_ref,
    bc_ref,
    out_ref,
    dt_ref,
    sems,
):
    copies = fetched(
        (
            (x_src, x_ref),
            (z_src, z_ref),
            (bc_src, bc_ref),
            (out_src, out_ref),
            (dt_src, dt_ref),
        ),
        sems,
    )
    for copy in copies:
        copy.wait()
    bc_at = 2 * inner
    out_at = bc_at + bc_ref.shape[1]
    dt_at = out_at + inner
    lanes = rows_ref.shape[2] - dt_at
    for core in range(2):
        here = slice(core * inner, (core + 1) * inner)
        down = lax.broadcasted_iota(jnp.int32, (2 * heads, lanes), 0) - core * heads
        across = lax.broadcasted_iota(jnp.int32, (2 * heads, lanes), 1)
        pick = jnp.where((down == across) & (across < heads), 1.0, 0.0).astype(BF)
        parts = (
            (0, x_ref[:, here]),
            (inner, z_ref[:, here]),
            (bc_at, bc_ref[...]),
            (out_at, out_ref[:, here]),
            (dt_at, tn(dt_ref[...], pick).astype(BF)),
        )
        for at, value in parts:
            rows_ref[core, :, at : at + value.shape[1]] = value
        for at in range(core + 2, rows_ref.shape[0], 2):
            rows_ref[at] = rows_ref[core]


def expert_packs(
    units, shared, flag_ref, gate_ref, up_ref, sg_ref, su_ref, router_ref, down_ref, sd_ref, *packs
):
    first = flag_ref[0] == 0
    router_at = 2 * (units + shared)
    down_at = router_at + 128
    for which, dst in enumerate(packs):
        dst[...] = jnp.zeros_like(dst)
        lead = first if which == 0 else jnp.logical_not(first)

        def pick(a, b):
            return jnp.where(lead, a.astype(F32), b.astype(F32)).astype(BF)

        for ref, at in ((gate_ref, 0), (up_ref, units), (down_ref, down_at)):
            dst[:, at : at + units] = pick(ref[:, :units], ref[:, units:])
        for ref, at in (
            (sg_ref, 2 * units),
            (su_ref, 2 * units + shared),
            (sd_ref, down_at + units),
        ):
            dst[:, at : at + shared] = pick(ref[:, :shared], ref[:, shared:])
        dst[:, router_at : router_at + router_ref.shape[1]] = router_ref[...]


def joined(flag_ref, own_ref, other_ref, rows_ref):
    first = flag_ref[0] == 0
    rows = own_ref.shape[0]
    own, other = own_ref[...].astype(F32), other_ref[...].astype(F32)
    rows_ref[:rows] = jnp.where(first, own, other).astype(BF)
    rows_ref[rows:] = jnp.where(first, other, own).astype(BF)


def small_set(
    inner,
    heads,
    head_width,
    flag_ref,
    bias_ref,
    log_ref,
    skip_ref,
    seg_own_ref,
    seg_other_ref,
    taps_ref,
    gain_ref,
    marks_ref,
    row_ref,
    taps_x_ref,
    head_ref,
    wide_ref,
):
    first = flag_ref[0] == 0
    half_tokens = seg_own_ref.shape[1]
    tokens = 2 * half_tokens
    seg = jnp.concatenate([seg_own_ref[...], seg_other_ref[...]], 1).astype(F32)
    seg = jnp.broadcast_to(seg, (8, tokens))
    place = lax.broadcasted_iota(jnp.int32, (8, tokens), 1)
    turned = jnp.where(place < half_tokens, place + half_tokens, place - half_tokens)
    place = jnp.where(first, place, turned).astype(F32)
    before = pltpu.roll(seg, 1, 1)
    hold = jnp.where((seg == before) & (place > 0.0), 1.0, 0.0)
    kept_two = hold * pltpu.roll(hold, 1, 1)
    kept_three = kept_two * pltpu.roll(hold, 2, 1)
    which = lax.broadcasted_iota(jnp.int32, (8, tokens), 0)
    rows = jnp.where(which == 0, seg, 0.0)
    for k, value in enumerate((place, hold, kept_two, kept_three)):
        rows = jnp.where(which == k + 1, value, rows)
    row_ref[...] = rows
    tall = jnp.concatenate([rows, jnp.zeros((120, tokens), F32)], 0)
    marks_ref[...] = tall.T[:, :8]
    taps_x_ref[...] = jnp.where(first, taps_ref[:, :inner], taps_ref[:, inner:])
    lanes = head_ref.shape[1]
    lane = lax.broadcasted_iota(jnp.int32, (1, lanes), 1)
    bias, log, on = jnp.zeros((1, lanes), F32), jnp.zeros((1, lanes), F32), lane < heads
    across = lax.broadcasted_iota(jnp.int32, (1, inner), 1)
    skip = jnp.zeros((1, inner), F32)
    for h in range(heads):
        own = lambda ref: jnp.where(first, ref[h], ref[heads + h])
        bias = jnp.where(lane == h, own(bias_ref), bias)
        log = jnp.where(lane == h, own(log_ref), log)
        skip = jnp.where(
            (across >= h * head_width) & (across < (h + 1) * head_width), own(skip_ref), skip
        )
    head_ref[0:1, :] = bias
    head_ref[1:2, :] = jnp.where(on, jnp.exp(log), 0.0)
    wide_ref[0:1, :] = skip
    wide_ref[1:2, :] = jnp.where(first, gain_ref[:, :inner], gain_ref[:, inner:])


def exchange_rows(part, axis):
    count = lax.axis_size(axis)
    blocks = part.reshape(count, part.shape[0] // count, part.shape[1])
    return lax.all_to_all(blocks, axis, 0, 0, tiled=False)


def chip(own, other, extra_own, extra_other):
    rows, width = own.shape
    extra = call(
        chip_sum,
        [((rows, width + 128), BF)],
        (own, swap(other), extra_own, swap(extra_other)),
        10**6,
        "chip_sum",
    )
    return extra[0]


def from_tokens(own):
    return lax.all_gather(own, "col", axis=0, tiled=True)


def on_device(
    hidden,
    cotangent,
    segments,
    routes,
    gain_mix,
    w_z,
    w_x,
    w_bc,
    w_dt,
    conv_x,
    conv_bc,
    dt_bias,
    a_log,
    d_skip,
    gain_gate,
    out_t,
    gain_moe,
    w_router,
    w_gate_t,
    w_up_t,
    w_down_t,
    ws_gate,
    ws_up,
    ws_down_t,
):
    half_tokens, width = hidden.shape
    rows = lax.axis_size("row")
    cols = lax.axis_size("col")
    seq = lax.axis_index("seq")
    col = lax.axis_index("col")
    tokens = 2 * half_tokens
    inner = conv_x.shape[1] // 2
    heads = dt_bias.shape[0] // 2
    head_width = inner // heads
    state = conv_bc.shape[1] // 2
    experts = w_router.shape[1]
    hidden_units = w_gate_t.shape[2]
    shared_units = ws_gate.shape[1] // 2
    lanes = 64
    inner_all = conv_x.shape[1] * cols
    shard = half_tokens // cols

    out_at = 2 * inner + 2 * state
    dt_at = out_at + inner
    mixer_width = dt_at + lanes
    (spread_rows,) = call(
        functools.partial(mixer_rows, inner, heads),
        [((2 * rows, w_z.shape[0], mixer_width), BF)],
        (w_x, w_z, w_bc, out_t, w_dt.T),
        10**6,
        "mixer_rows",
        56,
        (),
        (0, 1, 2, 3, 4),
    )
    (
        spread_rows,
        hidden,
        cotangent,
        w_gate_t,
        w_up_t,
        w_down_t,
        ws_gate,
        ws_up,
        ws_down_t,
        w_router,
        conv_x,
        gain_gate,
        segments,
        routes,
    ) = lax.optimization_barrier(
        (
            spread_rows,
            hidden,
            cotangent,
            w_gate_t,
            w_up_t,
            w_down_t,
            ws_gate,
            ws_up,
            ws_down_t,
            w_router,
            conv_x,
            gain_gate,
            segments,
            routes,
        )
    )
    mixer_whole = lax.all_to_all(spread_rows, ("row", "seq"), 0, 0).reshape(width, mixer_width)

    inv_mix = lax.rsqrt(jnp.mean(hidden * hidden, axis=1) + EPS)
    mix_own = (hidden * inv_mix[:, None] * gain_mix).astype(BF)
    mix_other = swap(mix_own)
    cot_other = swap(cotangent)
    routes_other = swap(routes)
    flag = seq.astype(jnp.int32)[None]

    down_units = hidden_units + shared_units
    in_units = 2 * down_units
    down_at = in_units + 128
    weight_rows = w_z.shape[0]
    packed = -(-(down_at + down_units) // 128) * 128
    flat = lambda a: a.reshape(weight_rows, 2 * hidden_units)
    pack_own, pack_other = call(
        functools.partial(expert_packs, hidden_units, shared_units),
        [((weight_rows, packed), BF)] * 2,
        (
            flag,
            flat(w_gate_t),
            flat(w_up_t),
            ws_gate,
            ws_up,
            w_router,
            flat(w_down_t),
            ws_down_t,
        ),
        10**6,
        "expert_packs",
        scalars=(0,),
    )
    (expert_rows,) = call(
        joined,
        [((2 * weight_rows, packed), BF)],
        (flag, pack_own, swap(pack_other)),
        10**6,
        "expert_rows",
        scalars=(0,),
    )
    seg_own = segments[None]
    marks, marks_row, taps_x, head_rows, wide_rows = call(
        functools.partial(small_set, inner, heads, head_width),
        [
            ((tokens, 8), F32),
            ((8, tokens), F32),
            ((4, inner), F32),
            ((2, lanes), F32),
            ((2, inner), F32),
        ],
        (flag, dt_bias, a_log, d_skip, seg_own, swap(seg_own), conv_x, gain_gate[None]),
        10**6,
        "small_set",
        scalars=(0, 1, 2, 3),
    )
    expert_rows, mixer_whole, mix_own, mix_other, cot_other, routes_other, marks, marks_row = (
        lax.optimization_barrier(
            (
                expert_rows,
                mixer_whole,
                mix_own,
                mix_other,
                cot_other,
                routes_other,
                marks,
                marks_row,
            )
        )
    )
    expert_whole = lax.all_gather(expert_rows, "row", axis=0, tiled=True)

    fixed = (mixer_whole, marks, marks_row, taps_x, conv_bc, head_rows, wide_rows)
    saved, part_own, part_other, square_own, square_other = call(
        functools.partial(mixer_forward, inner, head_width),
        [
            ((tokens, -(-(out_at + inner) // 128) * 128 + 256), F32),
            ((half_tokens, width), BF),
            ((half_tokens, width), BF),
            ((half_tokens, 1), F32),
            ((half_tokens, 1), F32),
        ],
        (mix_own, mix_other, *fixed),
        4 * 10**9,
        "mixer_forward",
        28,
        [((tokens, inner), BF)],
        (2,),
    )
    mix_sum = exchange_rows(chip(part_own, part_other, square_own, square_other), "col")
    mix_sum = jnp.sum(mix_sum.astype(F32), axis=0)
    square = mix_sum[:, width : width + 1] + mix_sum[:, width + 1 : width + 2]
    mix_sum = mix_sum[:, :width]

    here = lax.dynamic_slice_in_dim(hidden, col * shard, shard, 0)
    inv_gate_here = lax.rsqrt(square / inner_all + EPS)
    mix_out = mix_sum * inv_gate_here
    residual = here + mix_out
    inv_moe_here = lax.rsqrt(jnp.mean(residual * residual, axis=1, keepdims=True) + EPS)
    moe_here = (residual * inv_moe_here * gain_moe).astype(BF)
    moe_own = from_tokens(
        jnp.concatenate(
            [moe_here, *two(inv_gate_here), *two(inv_moe_here), jnp.zeros((shard, 124), BF)], 1
        )
    )
    moe_own, expert_whole = lax.optimization_barrier((moe_own, expert_whole))
    inv_moe = one(moe_own[:, width + 2], moe_own[:, width + 3])
    moe_other = swap(moe_own)

    mine = (jnp.arange(experts) == 2 * col + seq).astype(F32)[None, :]

    def experts_half(src, cot, routes_here):
        return call(
            functools.partial(experts_both_ways, hidden_units, shared_units),
            [
                ((half_tokens, width), BF),
                ((half_tokens, width), BF),
                ((half_tokens, in_units), BF),
                ((half_tokens, down_units), BF),
                ((half_tokens, experts), F32),
                ((half_tokens, experts), F32),
            ],
            (src, cot, expert_whole, routes_here, mine),
            3 * 10**9,
            "experts_both_ways",
            22,
        )

    in_own, out_own, grads_own, acts_own, gates, gates_grad_own = experts_half(
        moe_own, cotangent, routes
    )
    in_other, out_other, grads_other, acts_other, _, gates_grad_other = experts_half(
        moe_other, cot_other, routes_other
    )
    moe_got = exchange_rows(chip(in_own, in_other, gates_grad_own, gates_grad_other), "col")
    (expert_sums,) = call(
        expert_products,
        [((width, in_units + down_units), BF)],
        (
            moe_own,
            moe_other,
            cotangent,
            cot_other,
            grads_own,
            grads_other,
            acts_own,
            acts_other,
        ),
        3 * 10**9,
        "expert_products",
        28,
    )
    chip_out = (out_own.astype(F32) + swap(out_other).astype(F32)).astype(BF)
    moe_got, expert_sums, chip_out, cot_here, gates_here, router, gain_row = (
        lax.optimization_barrier(
            (
                moe_got,
                expert_sums,
                chip_out,
                lax.dynamic_slice_in_dim(cotangent, col * shard, shard, 0),
                lax.dynamic_slice_in_dim(gates, col * shard, shard, 0),
                expert_whole[:, in_units : in_units + experts],
                gain_moe[None],
            )
        )
    )
    expert_sums = lax.psum_scatter(expert_sums, "row", scatter_dimension=0, tiled=True)

    sent, residual_grad, gain_moe_grad = call(
        second_shard,
        [((shard, width + 128), BF), ((shard, width), F32), ((1, width), F32)],
        (
            moe_got,
            residual,
            mix_out,
            cot_here,
            gates_here,
            router,
            inv_moe_here,
            gain_row,
        ),
        10**7,
        "second_shard",
    )
    grad_own = from_tokens(sent)

    grad_own, chip_out = lax.optimization_barrier((grad_own, chip_out))
    grad_other = swap(grad_own)
    out_got = exchange_rows(chip_out, "col")

    grads, dt_grad, normed_gate, part_own, part_other, small = call(
        functools.partial(mixer_backward, inner, inner_all, head_width, experts),
        [
            ((tokens, out_at), BF),
            ((tokens, lanes), BF),
            ((tokens, inner), BF),
            ((half_tokens, width), BF),
            ((half_tokens, width), BF),
            ((SMALL_ROWS, 128), F32),
        ],
        (grad_own, grad_other, moe_own, moe_other, *fixed, saved),
        5 * 10**9,
        "mixer_backward",
        56,
        [
            ((tokens, inner), BF),
            ((tokens, inner), BF),
            ((tokens, inner), F32),
            ((tokens, state), F32),
            ((tokens, state), F32),
        ],
        tuple(range(12)),
    )
    chip_in = (part_own.astype(F32) + swap(part_other).astype(F32)).astype(BF)
    chip_in, out_got = lax.optimization_barrier((chip_in, out_got))
    output_here = residual + jnp.sum(out_got.astype(F32), axis=0)
    output = 2.0 * lax.all_gather(
        after(0.5 * output_here, expert_sums), "col", axis=0, tiled=True
    )
    mix_in_got = exchange_rows(chip_in, "col")
    (mixer_sums,) = call(
        functools.partial(mixer_products, inner, experts),
        [((2 * rows, w_z.shape[0], mixer_width + 128), BF)],
        (
            mix_own,
            mix_other,
            grad_own,
            grad_other,
            moe_own,
            moe_other,
            grads,
            dt_grad,
            normed_gate,
        ),
        2 * 10**9,
        "mixer_products",
        28,
    )
    mix_in_got, mixer_sums, gain_row = lax.optimization_barrier(
        (mix_in_got, mixer_sums, gain_mix[None])
    )

    grad_hidden_here, small = call(
        third_shard,
        [((shard, width), BF), ((SMALL_ROWS, 128), BF)],
        (mix_in_got, here, residual_grad, gain_row, gain_moe_grad, small),
        10**7,
        "third_shard",
        56,
        (),
        tuple(range(6)),
    )
    mixer_sums = lax.dynamic_update_slice(
        mixer_sums, jnp.broadcast_to(small[None], (2 * rows, *small.shape)), (0, 0, mixer_width)
    )
    got = lax.all_to_all(mixer_sums, ("row", "seq"), 0, 0)
    grad_hidden = from_tokens(grad_hidden_here)
    grad_hidden = grad_hidden.astype(F32)

    own = own_half(expert_sums, 0)
    other = swap(other_half(expert_sums, 0))

    def expert(at):
        a = own[:, None, at : at + hidden_units]
        return join(a, other[:, None, at : at + hidden_units], 1).astype(F32)

    def shared(at):
        return join(
            own[:, at : at + shared_units], other[:, at : at + shared_units], 1
        ).astype(F32)

    g_w_gate_t = expert(0)
    g_w_up_t = expert(hidden_units)
    g_w_down_t = expert(in_units)
    g_ws_gate = shared(2 * hidden_units)
    g_ws_up = shared(2 * hidden_units + shared_units)
    g_ws_down_t = shared(in_units + hidden_units)
    (
        got,
        grad_hidden,
        g_w_gate_t,
        g_w_up_t,
        g_w_down_t,
        g_ws_gate,
        g_ws_up,
        g_ws_down_t,
        inv_moe,
    ) = lax.optimization_barrier(
        (
            got,
            grad_hidden,
            g_w_gate_t,
            g_w_up_t,
            g_w_down_t,
            g_ws_gate,
            g_ws_up,
            g_ws_down_t,
            inv_moe,
        )
    )
    (
        g_out_t,
        g_w_z,
        g_w_x,
        g_w_dt,
        g_w_router,
        g_conv_x,
        g_gain_gate,
        by_heads,
        sent,
    ) = call(
        functools.partial(tail_sums, inner, heads),
        [
            ((weight_rows, 2 * inner), F32),
            ((weight_rows, 2 * inner), F32),
            ((weight_rows, 2 * inner), F32),
            ((weight_rows, 2 * heads), F32),
            ((weight_rows, experts), F32),
            ((4, 2 * inner), F32),
            ((1, 2 * inner), F32),
            ((3, 2 * heads), F32),
            ((cols, weight_rows + 16, 2 * state), BF),
        ],
        (got,),
        10**7,
        "tail_sums",
        16,
    )
    g_gain_gate = g_gain_gate.reshape(-1)
    g_dt_bias, g_a_log, g_d_skip = by_heads[0], by_heads[1], by_heads[2]
    got = lax.all_to_all(sent, "col", 0, 0)
    got, output = lax.optimization_barrier((got, output))
    g_w_bc, g_gain_mix, g_gain_moe, g_conv_bc = call(
        last_sums,
        [
            ((weight_rows, 2 * state), F32),
            ((width // 128, 128), F32),
            ((width // 128, 128), F32),
            ((4, 2 * state), F32),
        ],
        (got,),
        10**6,
        "last_sums",
    )
    g_gain_mix, g_gain_moe = g_gain_mix.reshape(-1), g_gain_moe.reshape(-1)

    return (
        output,
        grad_hidden,
        inv_mix,
        inv_moe,
        g_gain_mix,
        g_w_z,
        g_w_x,
        g_w_bc,
        g_w_dt,
        g_conv_x,
        g_conv_bc,
        g_dt_bias,
        g_a_log,
        g_d_skip,
        g_gain_gate,
        g_out_t,
        g_gain_moe,
        g_w_router,
        g_w_gate_t,
        g_w_up_t,
        g_w_down_t,
        g_ws_gate,
        g_ws_up,
        g_ws_down_t,
    )


def solution(mesh):
    placed = (
        P(("row", "seq"), None),
        P(("row", "seq"), None),
        P(("row", "seq")),
        P(("row", "seq"), None),
        P(),
        P(("row", "seq"), "col"),
        P(("row", "seq"), "col"),
        P(("row", "seq"), None),
        P(("row", "seq"), "col"),
        P(None, "col"),
        P(),
        P("col"),
        P("col"),
        P("col"),
        P("col"),
        P(("row", "seq"), "col"),
        P(),
        P(("row", "seq"), None),
        P(("row", "seq"), "col", None),
        P(("row", "seq"), "col", None),
        P(("row", "seq"), "col", None),
        P(("row", "seq"), "col"),
        P(("row", "seq"), "col"),
        P(("row", "seq"), "col"),
    )
    return jax.shard_map(
        on_device,
        mesh=mesh,
        in_specs=placed,
        out_specs=(
            P(("row", "seq"), None),
            P(("row", "seq"), None),
            P(("row", "seq")),
            P(("row", "seq")),
            P(),
            P(("row", "seq"), "col"),
            P(("row", "seq"), "col"),
            P(("row", "seq"), None),
            P(("row", "seq"), "col"),
            P(None, "col"),
            P(),
            P("col"),
            P("col"),
            P("col"),
            P("col"),
            P(("row", "seq"), "col"),
            P(),
            P(("row", "seq"), None),
            P(("row", "seq"), "col", None),
            P(("row", "seq"), "col", None),
            P(("row", "seq"), "col", None),
            P(("row", "seq"), "col"),
            P(("row", "seq"), "col"),
            P(("row", "seq"), "col"),
        ),
        check_vma=False,
    )
```
